128 devices in a mesh: dp: 8 (over x, core), seq: 16 (over y, z).
Axes of the slice: x: 4, y: 4, z: 4, core: 2. Of those that a mesh axis runs over, the one named last changes fastest.
Arguments:
- inputs: bfloat16 [16, 3072, 1024], P('dp', 'seq'), may hold values from -6 to 6
- first_gain: float32 [1024], replicated, may hold values from 0.1 to 1.9
- first_shift: float32 [1024], replicated, may hold values from -3 to 3
- qkv_weight: bfloat16 [1024, 3072], replicated, may hold values from -0.1875 to 0.1875
- out_weight: bfloat16 [1024, 1024], replicated, may hold values from -4 to 4
- second_gain: float32 [1024], replicated, may hold values from 0.1 to 1.9
- second_shift: float32 [1024], replicated, may hold values from -3 to 3
- up_weight: bfloat16 [1024, 4096], replicated, may hold values from -0.1875 to 0.1875
- down_weight: bfloat16 [4096, 1024], replicated, may hold values from -0.09375 to 0.09375
- cotangent: bfloat16 [16, 3072, 1024], P('dp', 'seq'), may hold values from -6 to 6
Outputs:
- output: bfloat16 [16, 3072, 1024], P('dp', 'seq')
- grad_input: float32 [16, 3072, 1024], P('dp', 'seq')
- grad_qkv: float32 [1024, 3072], P(('dp', 'seq'))
- grad_out: float32 [1024, 1024], P(('dp', 'seq'))
- grad_up: float32 [1024, 4096], P(('dp', 'seq'))
- grad_down: float32 [4096, 1024], P(('dp', 'seq'))
- grad_first_gain: float32 [1024], P(('dp', 'seq'))
- grad_first_shift: float32 [1024], P(('dp', 'seq'))
- grad_second_gain: float32 [1024], P(('dp', 'seq'))
- grad_second_shift: float32 [1024], P(('dp', 'seq'))
The draws below stay inside these ranges and needn't reach their ends.
All inputs are finite; a program needn't handle non-finite values.
Results may differ from the reference program's by a relative error of at most 0.0065.
Values sent between devices are 32-bit elements; how exact they have to be, the bound alone decides.
A program may use at most 192 MiB of HBM per device.

```python
import jax
import jax.numpy as jnp
from jax import lax

D = 1024
HEADS = 16
HEAD = 64
FF = 4096
GROUP = 192
LENGTH = 3072
IMAGES = 16


def shard_levels(stream_key, extent, cuts, smallest, high):
    level, own = 1.0, jax.random.fold_in(stream_key, 6)
    for position, parts in cuts:
        draws = jnp.exp(jax.random.uniform(jax.random.fold_in(own, position), (parts,), jnp.float32, smallest / len(cuts), high / len(cuts)))
        level = level * jnp.repeat(draws, extent[position] // parts).reshape([-1 if axis == position else 1 for axis in range(len(extent))])
    return level


def centred(own_key, extent, width, most, cuts=(), held_as=jnp.bfloat16):
    loudness = shard_levels(own_key, extent, cuts, -0.22, 0.18) if cuts else 1.0
    array = jax.random.normal(own_key, extent, jnp.float32) * width * loudness
    return jnp.minimum(jnp.maximum(array, -most), most).astype(held_as)


def setup_inputs(seed: int = 0) -> dict:
    arg_keys = jax.random.split(jax.random.key(seed), 11)
    return {
        "inputs": centred(arg_keys[0], (IMAGES, LENGTH, D), 1.0, 6.0, ((0, 8), (1, 16))),
        "first_gain": jnp.clip(1.0 + 0.18 * jax.random.normal(arg_keys[1], (D,), jnp.float32), 0.1, 1.9),
        "first_shift": centred(arg_keys[2], (D,), 0.5, 3.0, (), jnp.float32),
        "qkv_weight": centred(arg_keys[3], (D, 3 * D), D ** -0.5, 0.1875),
        "out_weight": centred(arg_keys[4], (D, D), 2 ** -0.5, 4.0),
        "second_gain": jnp.clip(1.0 + 0.18 * jax.random.normal(arg_keys[5], (D,), jnp.float32), 0.1, 1.9),
        "second_shift": centred(arg_keys[6], (D,), 0.5, 3.0, (), jnp.float32),
        "up_weight": centred(arg_keys[7], (D, FF), D ** -0.5, 0.1875),
        "down_weight": centred(arg_keys[8], (FF, D), FF ** -0.5, 0.09375),
        "cotangent": centred(arg_keys[9], (IMAGES, LENGTH, D), 1.0, 6.0, ((0, 8), (1, 16))),
    }


@jax.custom_vjp
def low(v):
    return lax.optimization_barrier(v.astype(jnp.bfloat16)).astype(jnp.float32)

@jax.custom_vjp
def low_back(v):
    return v

def low_keep(v):
    return (low(v), None)

def low_pass(kept, grad):
    return (grad,)

def back_keep(v):
    return (v, None)

def back_low(kept, grad):
    return (low(grad),)
low.defvjp(low_keep, low_pass)
low_back.defvjp(back_keep, back_low)

def precise_dot(left, right):
    return jnp.dot(left, right, precision=lax.Precision.HIGHEST, preferred_element_type=jnp.float32)

def layer_norm(values, gain, shift):
    center = lax.optimization_barrier(jnp.mean(values, axis=-1, keepdims=True))
    centered = values - center
    variance = lax.optimization_barrier(jnp.mean(centered * centered, axis=-1, keepdims=True))
    return centered * lax.rsqrt(variance + 1e-05) * gain + shift

def one_sequence(single, params):
    first_gain, first_shift, qkv_weight, out_weight, second_gain, second_shift, up_weight, down_weight = params
    length = single.shape[0]
    block_count = length // GROUP
    highest = lax.Precision.HIGHEST
    normed = low(layer_norm(single, first_gain, first_shift))
    qkv = low_back(low(precise_dot(normed, qkv_weight)))
    qkv = qkv.reshape(block_count, GROUP, 3, HEADS, HEAD)
    queries = qkv[:, :, 0]
    keys = qkv[:, :, 1]
    values = qkv[:, :, 2]
    feat_query = low(jax.nn.elu(queries) + 1.0)
    feat_key = low(jax.nn.elu(keys) + 1.0)
    positions = jnp.arange(GROUP)
    causal = (positions[:, None] >= positions[None, :]).astype(jnp.float32)

    def attend_block(carry, pieces):
        key_state, key_total = carry
        block_query, block_key, block_value = pieces
        scores = jnp.einsum('the,she->hts', block_query, block_key, precision=highest) * causal
        numer = jnp.einsum('hts,shf->thf', scores, block_value, precision=highest)
        numer = numer + jnp.einsum('the,hef->thf', block_query, key_state, precision=highest)
        denom = lax.optimization_barrier(jnp.sum(scores, axis=-1)).T + jnp.einsum('the,he->th', block_query, key_total, precision=highest)
        attended = numer / denom[..., None]
        key_state = key_state + jnp.einsum('she,shf->hef', block_key, block_value, precision=highest)
        key_total = key_total + lax.optimization_barrier(jnp.sum(block_key, axis=0))
        return ((key_state, key_total), attended)
    start = (jnp.zeros((HEADS, HEAD, HEAD), jnp.float32), jnp.zeros((HEADS, HEAD), jnp.float32))
    finish, attended = lax.scan(jax.checkpoint(attend_block), start, (feat_query, feat_key, values))
    attended = low(attended.reshape(length, HEADS * HEAD))
    mixed = single + low_back(precise_dot(attended, out_weight))
    normed_two = low(layer_norm(mixed, second_gain, second_shift))
    pre_act = low_back(precise_dot(normed_two, up_weight))
    hidden = low(jax.nn.gelu(pre_act, approximate=False))
    return mixed + low_back(precise_dot(hidden, down_weight))

def forward(inputs, first_gain, first_shift, qkv_weight, out_weight, second_gain, second_shift, up_weight, down_weight):
    params = (first_gain, first_shift, qkv_weight, out_weight, second_gain, second_shift, up_weight, down_weight)
    return lax.map(lambda single: one_sequence(single, params), inputs)

def reference(inputs, first_gain, first_shift, qkv_weight, out_weight, second_gain, second_shift, up_weight, down_weight, cotangent):
    wide = (inputs.astype(jnp.float32), first_gain.astype(jnp.float32), first_shift.astype(jnp.float32), qkv_weight.astype(jnp.float32), out_weight.astype(jnp.float32), second_gain.astype(jnp.float32), second_shift.astype(jnp.float32), up_weight.astype(jnp.float32), down_weight.astype(jnp.float32))
    output, pullback = jax.vjp(forward, *wide)
    grads = pullback(cotangent.astype(jnp.float32))
    return (output.astype(jnp.bfloat16), grads[0], grads[3], grads[4], grads[7], grads[8], grads[1], grads[2], grads[5], grads[6])
```

```python
import math

import jax
import jax.numpy as jnp
from jax import lax
from jax.experimental import pallas as pl
from jax.experimental.pallas import tpu as pltpu
from jax.sharding import PartitionSpec as P

HEADS = 16
MESH = pl.DeviceIdType.MESH
F32 = jnp.float32
BF16 = jnp.bfloat16
RING = 4
MIB = 2**20

highest = lax.Precision.HIGHEST


class Place:
    def __init__(self):
        dp, seq = lax.axis_index("dp"), lax.axis_index("seq")
        self.core = lax.rem(dp, 2)
        self.at = (lax.div(dp, 2), lax.div(seq, RING), lax.rem(seq, RING))

    def id_of(self, x, y, z, core):
        return (x * 2 + core, y * RING + z)

    def ring(self, axis, step):
        return lax.rem(self.at[axis] + (step + RING), RING)

    def neighbour(self, axis, step):
        at = list(self.at)
        at[axis] = self.ring(axis, step)
        return self.id_of(*at, self.core)

    def partner(self):
        return self.id_of(*self.at, 1 - self.core)


def greet(place):
    barrier = pltpu.get_barrier_semaphore()
    others = [place.neighbour(axis, step) for axis in range(3) for step in (1, -1)]
    others.append(place.partner())
    for other in others:
        pl.semaphore_signal(barrier, inc=1, device_id=other, device_id_type=MESH)
    pl.semaphore_wait(barrier, len(others))


ORDERS = ((0, 1, 2), (1, 2, 0), (2, 0, 1))
MESSAGES = 18


def stream_scratch(length):
    wide = (length // 256) * 128 + (128 if (length // 128) % 2 else 0)
    return [
        pltpu.VMEM((2, 4, 4, 8, length), F32),
        pltpu.VMEM((2, 2, 4, 8, length), F32),
        pltpu.VMEM((2, 4, 8, length), F32),
        pltpu.VMEM((2, 2, 8, length), F32),
        pltpu.VMEM((2, 8, length), F32),
        pltpu.VMEM((2, 8, wide), F32),
        pltpu.SemaphoreType.DMA((MESSAGES,)),
        pltpu.SemaphoreType.DMA((MESSAGES,)),
    ]


class Stream:
    def __init__(self, place, slab, order, scratch):
        self.place, self.slab, self.order = place, slab, order
        self.full = (scratch[0], scratch[2], scratch[4])
        self.half = (scratch[1], scratch[3], scratch[5])
        self.sent, self.came = scratch[6], scratch[7]
        self.length = slab.shape[-1]
        self.cut = scratch[5].shape[-1]
        self.flying = []

    def chunk(self, phase, target):
        index = [slice(None)] * 3
        for done in self.order[:phase]:
            index[done] = self.place.at[done]
        index[self.order[phase]] = target
        return self.slab.at[tuple(index)]

    def part(self, ref, phase, which):
        if phase < 2:
            return ref.at[pl.ds(2 * which, 2)]
        if which == 0:
            return ref.at[:, pl.ds(0, self.cut)]
        return ref.at[:, pl.ds(self.cut, self.length - self.cut)]

    def through(self, phase, way):
        ref = self.half[phase].at[way]
        if phase == 2 and way == 1:
            return ref.at[:, pl.ds(0, self.length - self.cut)]
        return ref

    def send(self, phase, kind, way, source, target):
        number = phase * 6 + kind * 2 + way
        copy = pltpu.make_async_remote_copy(
            src_ref=source,
            dst_ref=target,
            send_sem=self.sent.at[number],
            recv_sem=self.came.at[number],
            device_id=self.place.neighbour(self.order[phase], 1 - 2 * way),
            device_id_type=MESH,
        )
        copy.start()
        self.flying.append(copy)

    def ring(self, phase, step):
        return self.place.ring(self.order[phase], step)

    def begin(self, phase):
        opposite = self.chunk(phase, self.ring(phase, 2))
        for way in range(2):
            self.send(phase, 0, way, self.part(opposite, phase, way), self.through(phase, way))
        for way in range(2):
            beside = self.chunk(phase, self.ring(phase, 1 - 2 * way))
            self.send(
                phase,
                1,
                way,
                self.part(beside, phase, 1 - way),
                self.part(self.full[phase].at[way], phase, 1 - way),
            )

    def arrived(self, phase, kind, way, target):
        number = phase * 6 + kind * 2 + way
        pltpu.make_async_remote_copy(
            src_ref=target,
            dst_ref=target,
            send_sem=self.sent.at[number],
            recv_sem=self.came.at[number],
            device_id=self.place.neighbour(self.order[phase], 2 * way - 1),
            device_id_type=MESH,
        ).wait_recv()

    def forward(self, phase):
        for way in range(2):
            came = self.through(phase, way)
            self.arrived(phase, 0, way, came)
            own = self.part(self.chunk(phase, self.ring(phase, 1 - 2 * way)), phase, way)
            add_into(own, came)
            self.send(phase, 2, way, own, self.part(self.full[phase].at[way], phase, way))

    def finish(self, phase):
        own = self.chunk(phase, self.place.at[self.order[phase]])
        for way in range(2):
            for kind, which in ((1, 1 - way), (2, way)):
                self.arrived(phase, kind, way, self.part(self.full[phase].at[way], phase, which))
        add_into(own, self.full[phase].at[0], self.full[phase].at[1])

    def result(self):
        return self.slab.at[self.place.at]

    def drain(self):
        for copy in self.flying:
            copy.wait_send()


def add_into(own, *others):
    if len(own.shape) > 2:

        def row(index, carry):
            add_into(own.at[index], *[other.at[index] for other in others])
            return carry

        if len(own.shape) == 4:
            lax.fori_loop(0, own.shape[0], row, 0)
        else:
            for index in range(own.shape[0]):
                row(index, 0)
        return
    total = own[...]
    for other in others:
        total = total + other[...]
    own[...] = total


def run_streams(streams):
    for phase in range(3):
        for stream in streams:
            stream.begin(phase)
        for stream in streams:
            stream.forward(phase)
        for stream in streams:
            stream.finish(phase)


def tn_dot(left, right):
    return lax.dot_general(left, right, (((0,), (0,)), ((), ())), preferred_element_type=F32)


class Exchange:
    def __init__(self, place, sent, came):
        self.place, self.sent, self.came, self.count, self.flying = place, sent, came, 0, []

    def send(self, source, target):
        copy = pltpu.make_async_remote_copy(
            src_ref=source,
            dst_ref=target,
            send_sem=self.sent.at[self.count],
            recv_sem=self.came.at[self.count],
            device_id=self.place.partner(),
            device_id_type=MESH,
        )
        copy.start()
        self.count += 1
        self.flying.append(copy)
        return copy

    def drain(self):
        for copy in self.flying:
            copy.wait_send()


def half_columns(block, core, quarter):
    half = quarter // 2
    return pl.ds(pl.multiple_of(block * quarter + core * half, half), half)


def stage_left(place, exchange, left, stage, land, pieces):
    quarter = left.shape[1] // 4
    copies = []
    for block in range(4):
        columns = pl.ds(block * quarter // 2, quarter // 2)
        stage[:, columns] = left[:, half_columns(block, 1 - place.core, quarter)].astype(F32)
        copies.append(exchange.send(stage.at[:, columns], land.at[:, columns]))
    return copies


def stage_right(exchange, right, stage, land, tile):
    copies = []
    for start in range(0, right.shape[1], tile):
        columns = pl.ds(start, tile)
        stage[:, columns] = right[:, columns].astype(F32)
        copies.append(exchange.send(stage.at[:, columns], land.at[:, columns]))
    return copies


def gather_left(place, left, land, both, copies):
    rows, quarter = left.shape[0], left.shape[1] // 4
    for block in range(4):
        columns = pl.ds(block * quarter // 2, quarter // 2)
        both[pl.ds(0, rows), columns] = left[:, half_columns(block, place.core, quarter)]
        copies[block].wait_recv()
        both[pl.ds(rows, rows), columns] = land[:, columns].astype(BF16)


def gather_right(right, land, both, copies, tile, index):
    rows = right.shape[0]
    columns = pl.ds(index * tile, tile)
    both[pl.ds(0, rows), columns] = right[:, columns]
    copies[index].wait_recv()
    both[pl.ds(rows, rows), columns] = land[:, columns].astype(BF16)


TILE = 512


def down_kernel(left, right, out, stage_l, land_l, both_l, stage_r, land_r, both_r, sent, came, *rest):
    place = Place()
    greet(place)
    slabs, scratch = rest[:3], rest[3:]
    exchange = Exchange(place, sent, came)
    right_copies = stage_right(exchange, right, stage_r, land_r, TILE)
    left_copies = stage_left(place, exchange, left, stage_l, land_l, None)
    for index in range(right.shape[1] // TILE):
        gather_right(right, land_r, both_r, right_copies, TILE, index)
    gather_left(place, left, land_l, both_l, left_copies)
    cuts = ((0, 384), (384, 384), (768, 256))

    def block_product(block, carry):
        rows = both_l[:, pl.ds(pl.multiple_of(block * 512, 512), 512)]
        for piece, (start, width) in enumerate(cuts):
            product = tn_dot(rows, both_r[:, pl.ds(start, width)]).reshape(4, 4, 4, 8, width)
            for stream in range(3):
                slabs[stream][block, :, :, :, pl.ds(start, width)] = product[:, :, stream]
            slabs[piece][block, :, :, :, pl.ds(1024, width)] = product[:, :, 3]
        return carry

    lax.fori_loop(0, 4, block_product, 0)
    streams = [
        Stream(place, slabs[k], ORDERS[k], scratch[8 * k : 8 * k + 8]) for k in range(3)
    ]
    run_streams(streams)
    for stream in range(3):
        result = streams[stream].result()
        out[pl.ds(8 * stream, 8), :] = result[:, pl.ds(0, 1024)]
        start, width = cuts[stream]
        out[pl.ds(24, 8), pl.ds(start, width)] = result[:, pl.ds(1024, width)]
    exchange.drain()
    for stream in streams:
        stream.drain()


def wide_kernel(widths, left, right, out, stage_l, land_l, both_l, stage_r, land_r, both_r, sent, came, *rest):
    place = Place()
    greet(place)
    slabs, scratch = rest[:3], rest[3:]
    exchange = Exchange(place, sent, came)
    left_copies = stage_left(place, exchange, left, stage_l, land_l, None)
    right_copies = stage_right(exchange, right, stage_r, land_r, TILE)
    gather_left(place, left, land_l, both_l, left_copies)
    for index in range(right.shape[1] // TILE):
        gather_right(right, land_r, both_r, right_copies, TILE, index)
    starts = (0, widths[0], widths[0] + widths[1])
    for stream in range(3):
        for start in range(0, widths[stream], TILE):
            width = min(TILE, widths[stream] - start)
            product = tn_dot(both_l[...], both_r[:, pl.ds(starts[stream] + start, width)])
            slabs[stream][:, :, :, :, pl.ds(start, width)] = product.reshape(4, 4, 4, 8, width)
    streams = [
        Stream(place, slabs[k], ORDERS[k], scratch[8 * k : 8 * k + 8]) for k in range(3)
    ]
    run_streams(streams)
    for stream in range(3):
        out[:, pl.ds(starts[stream], widths[stream])] = streams[stream].result()[...]
    exchange.drain()
    for stream in streams:
        stream.drain()


def grad_call(kernel, left, right, out_shape, widths, collective_id):
    rows, half, columns = left.shape[0], left.shape[1] // 2, right.shape[1]
    pieces = 4 + columns // TILE
    vmem = pl.BlockSpec(memory_space=pltpu.VMEM)
    return pl.pallas_call(
        kernel,
        out_shape=jax.ShapeDtypeStruct(out_shape, F32),
        in_specs=[vmem, vmem],
        out_specs=vmem,
        scratch_shapes=[
            pltpu.VMEM((rows, half), F32),
            pltpu.VMEM((rows, half), F32),
            pltpu.VMEM((2 * rows, half), BF16),
            pltpu.VMEM((rows, columns), F32),
            pltpu.VMEM((rows, columns), F32),
            pltpu.VMEM((2 * rows, columns), BF16),
            pltpu.SemaphoreType.DMA((pieces,)),
            pltpu.SemaphoreType.DMA((pieces,)),
            *[pltpu.VMEM((4, 4, 4, 8, width), F32) for width in widths],
            *[item for width in widths for item in stream_scratch(width)],
        ],
        compiler_params=pltpu.CompilerParams(
            collective_id=collective_id, has_side_effects=True, vmem_limit_bytes=62 * MIB
        ),
    )(left, right)


def grad_down_sum(hidden, cotangent):
    return grad_call(down_kernel, hidden, cotangent, (32, 1024), (1408, 1408, 1280), 1)


def grad_wide_sum(left, right, widths, collective_id):
    def kernel(*refs):
        wide_kernel(widths, *refs)

    return grad_call(kernel, left, right, (8, right.shape[1]), widths, collective_id)
def carried_in(shard, axis, combine, identity, reverse):
    devices, place = (lax.axis_size(axis), lax.axis_index(axis))
    everything = jax.tree.map(lambda part: lax.all_gather(part, axis), shard)
    start = jax.tree.map(
        lambda part, zero: jnp.broadcast_to(jnp.asarray(zero, part.dtype), part.shape),
        shard,
        identity,
    )

    def lap(k, before):
        at = devices - 1 - k if reverse else k
        reached = at > place if reverse else at < place
        new = combine(before, jax.tree.map(lambda part: part[at], everything))
        return jax.tree.map(lambda a, b: jnp.where(reached, a, b), new, before)

    return lax.fori_loop(0, devices, lap, start)


def rounded(values):
    return lax.optimization_barrier(values.astype(jnp.bfloat16)).astype(jnp.float32)


def layer_norm(values, gain, shift):
    center = jnp.mean(values, axis=-1, keepdims=True)
    centered = values - center
    variance = jnp.mean(centered * centered, axis=-1, keepdims=True)
    inverse = lax.rsqrt(variance + 1e-05)
    scaled = centered * inverse
    return (scaled * gain + shift, scaled, inverse)


def norm_back(grad_out, gain, scaled, inverse):
    grad_scaled = grad_out * gain
    first_mean = jnp.mean(grad_scaled, axis=-1, keepdims=True)
    second_mean = jnp.mean(grad_scaled * scaled, axis=-1, keepdims=True)
    return inverse * (grad_scaled - first_mean - scaled * second_mean)


def rows_dot(left, right):
    return lax.dot_general(
        left, right, (((0,), (0,)), ((), ())), preferred_element_type=jnp.float32
    )


def back_dot(left, right):
    return lax.dot_general(
        left, right, (((1,), (1,)), ((), ())), preferred_element_type=jnp.float32
    )


def add_pair(earlier, later):
    return (earlier[0] + later[0], earlier[1] + later[1])


def body(
    inputs,
    first_gain,
    first_shift,
    qkv_weight,
    out_weight,
    second_gain,
    second_shift,
    up_weight,
    down_weight,
    cotangent,
):
    seq_count, block_len, width = inputs.shape
    head_size = width // HEADS
    row_count = seq_count * block_len
    flat_input = inputs.astype(jnp.float32).reshape(row_count, width)
    normed, scaled_one, inverse_one = layer_norm(flat_input, first_gain, first_shift)
    normed_low = normed.astype(jnp.bfloat16)
    qkv_low = jnp.dot(normed_low, qkv_weight, preferred_element_type=jnp.float32).astype(
        jnp.bfloat16
    )
    qkv_wide = qkv_low.astype(jnp.float32).reshape(seq_count, block_len, 3, HEADS, head_size)
    queries = qkv_wide[:, :, 0]
    keys = qkv_wide[:, :, 1]
    values = qkv_wide[:, :, 2]
    feat_query = rounded(jax.nn.elu(queries) + 1.0)
    feat_key = rounded(jax.nn.elu(keys) + 1.0)
    causal = (
        lax.broadcasted_iota(jnp.int32, (block_len, block_len), 0)
        >= lax.broadcasted_iota(jnp.int32, (block_len, block_len), 1)
    ).astype(jnp.float32)
    scores = jnp.einsum("nthe,nshe->nhts", feat_query, feat_key, precision=highest) * causal
    numer_local = jnp.einsum("nhts,nshf->nthf", scores, values, precision=highest)
    denom_local = jnp.transpose(jnp.sum(scores, axis=-1), (0, 2, 1))
    state_local = jnp.einsum("nshe,nshf->nhef", feat_key, values, precision=highest)
    total_local = jnp.sum(feat_key, axis=1)
    state_in, total_in = carried_in(
        (state_local, total_local),
        "seq",
        add_pair,
        (jnp.zeros_like(state_local), jnp.zeros_like(total_local)),
        False,
    )
    numer = numer_local + jnp.einsum("nthe,nhef->nthf", feat_query, state_in, precision=highest)
    denom = denom_local + jnp.einsum("nthe,nhe->nth", feat_query, total_in, precision=highest)
    attended = numer / denom[..., None]
    attended_low = attended.reshape(row_count, width).astype(jnp.bfloat16)
    mixed = flat_input + jnp.dot(attended_low, out_weight, preferred_element_type=jnp.float32)
    normed_two, scaled_two, inverse_two = layer_norm(mixed, second_gain, second_shift)
    normed_two_low = normed_two.astype(jnp.bfloat16)
    pre_act = jnp.dot(normed_two_low, up_weight, preferred_element_type=jnp.float32)
    hidden_low = jax.nn.gelu(pre_act, approximate=False).astype(jnp.bfloat16)
    result = mixed + jnp.dot(hidden_low, down_weight, preferred_element_type=jnp.float32)
    output = result.astype(jnp.bfloat16).reshape(seq_count, block_len, width)
    grad_result = cotangent.reshape(row_count, width)
    grad_down = grad_down_sum(hidden_low, grad_result)
    grad_hidden = back_dot(grad_result, down_weight)
    cumulative = 0.5 * (1.0 + lax.erf(pre_act * (1.0 / math.sqrt(2.0))))
    density = jnp.exp(-0.5 * pre_act * pre_act) * (1.0 / math.sqrt(2.0 * math.pi))
    grad_pre_low = (grad_hidden * (cumulative + pre_act * density)).astype(jnp.bfloat16)
    grad_up = grad_wide_sum(normed_two_low, grad_pre_low, (1408, 1408, 1280), 2)
    grad_normed_two = back_dot(grad_pre_low, up_weight)
    grad_second_gain = jnp.sum(grad_normed_two * scaled_two, axis=0)
    grad_second_shift = jnp.sum(grad_normed_two, axis=0)
    grad_mixed = grad_result.astype(jnp.float32) + norm_back(
        grad_normed_two, second_gain, scaled_two, inverse_two
    )
    grad_mixed_low = grad_mixed.astype(jnp.bfloat16)
    grad_out = grad_wide_sum(attended_low, grad_mixed_low, (384, 384, 256), 3)
    grad_att = back_dot(grad_mixed_low, out_weight).reshape(seq_count, block_len, HEADS, head_size)
    grad_numer = grad_att / denom[..., None]
    grad_denom = -jnp.sum(grad_att * attended, axis=-1) / denom
    mixing = (
        jnp.einsum("nthf,nshf->nhts", grad_numer, values, precision=highest)
        + jnp.transpose(grad_denom, (0, 2, 1))[..., None]
    ) * causal
    grad_query = (
        jnp.einsum("nhts,nshe->nthe", mixing, feat_key, precision=highest)
        + jnp.einsum("nthf,nhef->nthe", grad_numer, state_in, precision=highest)
        + grad_denom[..., None] * total_in[:, None]
    )
    grad_state_in = jnp.einsum("nthe,nthf->nhef", feat_query, grad_numer, precision=highest)
    grad_total_in = jnp.einsum("nthe,nth->nhe", feat_query, grad_denom, precision=highest)
    grad_state, grad_total = carried_in(
        (grad_state_in, grad_total_in),
        "seq",
        add_pair,
        (jnp.zeros_like(grad_state_in), jnp.zeros_like(grad_total_in)),
        True,
    )
    grad_key = (
        jnp.einsum("nhts,nthe->nshe", mixing, feat_query, precision=highest)
        + jnp.einsum("nshf,nhef->nshe", values, grad_state, precision=highest)
        + grad_total[:, None]
    )
    grad_value = jnp.einsum("nhts,nthf->nshf", scores, grad_numer, precision=highest) + jnp.einsum(
        "nshe,nhef->nshf", feat_key, grad_state, precision=highest
    )
    grad_query = grad_query * jnp.where(queries > 0, 1.0, jnp.exp(jnp.minimum(queries, 0.0)))
    grad_key = grad_key * jnp.where(keys > 0, 1.0, jnp.exp(jnp.minimum(keys, 0.0)))
    grad_qkv_low = (
        jnp.stack([grad_query, grad_key, grad_value], axis=2)
        .reshape(row_count, 3 * width)
        .astype(jnp.bfloat16)
    )
    grad_qkv = grad_wide_sum(normed_low, grad_qkv_low, (1024, 1024, 1024), 4)
    grad_normed = back_dot(grad_qkv_low, qkv_weight)
    grad_first_gain = jnp.sum(grad_normed * scaled_one, axis=0)
    grad_first_shift = jnp.sum(grad_normed, axis=0)
    grad_input = (grad_mixed + norm_back(grad_normed, first_gain, scaled_one, inverse_one)).reshape(
        seq_count, block_len, width
    )
    summed = (
        grad_qkv,
        grad_out,
        grad_up,
        grad_down,
        lax.psum_scatter(grad_first_gain, ("dp", "seq"), scatter_dimension=0, tiled=True),
        lax.psum_scatter(grad_first_shift, ("dp", "seq"), scatter_dimension=0, tiled=True),
        lax.psum_scatter(grad_second_gain, ("dp", "seq"), scatter_dimension=0, tiled=True),
        lax.psum_scatter(grad_second_shift, ("dp", "seq"), scatter_dimension=0, tiled=True),
    )
    return (
        output,
        grad_input,
        summed[0],
        summed[1],
        summed[2],
        summed[3],
        summed[4],
        summed[5],
        summed[6],
        summed[7],
    )


def solution(mesh):
    return jax.shard_map(
        body,
        mesh=mesh,
        in_specs=(
            P("dp", "seq", None),
            P(),
            P(),
            P(),
            P(),
            P(),
            P(),
            P(),
            P(),
            P("dp", "seq", None),
        ),
        out_specs=(
            P("dp", "seq", None),
            P("dp", "seq", None),
            P(("dp", "seq"), None),
            P(("dp", "seq"), None),
            P(("dp", "seq"), None),
            P(("dp", "seq"), None),
            P(("dp", "seq")),
            P(("dp", "seq")),
            P(("dp", "seq")),
            P(("dp", "seq")),
        ),
        check_vma=False,
    )
```

```python
import math

import jax
import jax.numpy as jnp
from jax import lax
from jax.experimental import pallas as pl
from jax.experimental.pallas import tpu as pltpu
from jax.sharding import PartitionSpec as P

MESH = pl.DeviceIdType.MESH
F32 = jnp.float32
BF16 = jnp.bfloat16
RING = 4
MIB = 2**20


class Place:
    def __init__(self):
        dp, seq = lax.axis_index("dp"), lax.axis_index("seq")
        self.core = lax.rem(dp, 2)
        self.at = (lax.div(dp, 2), lax.div(seq, RING), lax.rem(seq, RING))

    def id_of(self, x, y, z, core):
        return (x * 2 + core, y * RING + z)

    def ring(self, axis, step):
        return lax.rem(self.at[axis] + (step + RING), RING)

    def neighbour(self, axis, step):
        at = list(self.at)
        at[axis] = self.ring(axis, step)
        return self.id_of(*at, self.core)

    def partner(self):
        return self.id_of(*self.at, 1 - self.core)


def greet(place):
    barrier = pltpu.get_barrier_semaphore()
    others = [place.neighbour(axis, step) for axis in range(3) for step in (1, -1)]
    others.append(place.partner())
    for other in others:
        pl.semaphore_signal(barrier, inc=1, device_id=other, device_id_type=MESH)
    pl.semaphore_wait(barrier, len(others))


ORDERS = ((0, 1, 2), (1, 2, 0), (2, 0, 1))
MESSAGES = 18


def stream_scratch(length):
    wide = (length // 256) * 128 + (128 if (length // 128) % 2 else 0)
    return [
        pltpu.VMEM((2, 4, 4, 8, length), F32),
        pltpu.VMEM((2, 2, 4, 8, length), F32),
        pltpu.VMEM((2, 4, 8, length), F32),
        pltpu.VMEM((2, 2, 8, length), F32),
        pltpu.VMEM((2, 8, length), F32),
        pltpu.VMEM((2, 8, wide), F32),
        pltpu.SemaphoreType.DMA((MESSAGES,)),
        pltpu.SemaphoreType.DMA((MESSAGES,)),
    ]


class Stream:
    def __init__(self, place, slab, order, scratch):
        self.place, self.slab, self.order = place, slab, order
        self.full = (scratch[0], scratch[2], scratch[4])
        self.half = (scratch[1], scratch[3], scratch[5])
        self.sent, self.came = scratch[6], scratch[7]
        self.length = slab.shape[-1]
        self.cut = scratch[5].shape[-1]
        self.flying = []

    def chunk(self, phase, target):
        index = [slice(None)] * 3
        for done in self.order[:phase]:
            index[done] = self.place.at[done]
        index[self.order[phase]] = target
        return self.slab.at[tuple(index)]

    def part(self, ref, phase, which):
        if phase < 2:
            return ref.at[pl.ds(2 * which, 2)]
        if which == 0:
            return ref.at[:, pl.ds(0, self.cut)]
        return ref.at[:, pl.ds(self.cut, self.length - self.cut)]

    def through(self, phase, way):
        ref = self.half[phase].at[way]
        if phase == 2 and way == 1:
            return ref.at[:, pl.ds(0, self.length - self.cut)]
        return ref

    def send(self, phase, kind, way, source, target):
        number = phase * 6 + kind * 2 + way
        copy = pltpu.make_async_remote_copy(
            src_ref=source,
            dst_ref=target,
            send_sem=self.sent.at[number],
            recv_sem=self.came.at[number],
            device_id=self.place.neighbour(self.order[phase], 1 - 2 * way),
            device_id_type=MESH,
        )
        copy.start()
        self.flying.append(copy)

    def ring(self, phase, step):
        return self.place.ring(self.order[phase], step)

    def begin(self, phase):
        opposite = self.chunk(phase, self.ring(phase, 2))
        for way in range(2):
            self.send(phase, 0, way, self.part(opposite, phase, way), self.through(phase, way))
        for way in range(2):
            beside = self.chunk(phase, self.ring(phase, 1 - 2 * way))
            self.send(
                phase,
                1,
                way,
                self.part(beside, phase, 1 - way),
                self.part(self.full[phase].at[way], phase, 1 - way),
            )

    def arrived(self, phase, kind, way, target):
        number = phase * 6 + kind * 2 + way
        pltpu.make_async_remote_copy(
            src_ref=target,
            dst_ref=target,
            send_sem=self.sent.at[number],
            recv_sem=self.came.at[number],
            device_id=self.place.neighbour(self.order[phase], 2 * way - 1),
            device_id_type=MESH,
        ).wait_recv()

    def forward(self, phase):
        for way in range(2):
            came = self.through(phase, way)
            self.arrived(phase, 0, way, came)
            own = self.part(self.chunk(phase, self.ring(phase, 1 - 2 * way)), phase, way)
            add_into(own, came)
            self.send(phase, 2, way, own, self.part(self.full[phase].at[way], phase, way))

    def finish(self, phase):
        own = self.chunk(phase, self.place.at[self.order[phase]])
        for way in range(2):
            for kind, which in ((1, 1 - way), (2, way)):
                self.arrived(phase, kind, way, self.part(self.full[phase].at[way], phase, which))
        add_into(own, self.full[phase].at[0], self.full[phase].at[1])

    def result(self):
        return self.slab.at[self.place.at]

    def drain(self):
        for copy in self.flying:
            copy.wait_send()


def add_into(own, *others):
    if len(own.shape) > 2:

        def row(index, carry):
            add_into(own.at[index], *[other.at[index] for other in others])
            return carry

        if len(own.shape) == 4:
            lax.fori_loop(0, own.shape[0], row, 0)
        else:
            for index in range(own.shape[0]):
                row(index, 0)
        return
    total = own[...]
    for other in others:
        total = total + other[...]
    own[...] = total


def run_streams(streams):
    for phase in range(3):
        for stream in streams:
            stream.begin(phase)
        for stream in streams:
            stream.forward(phase)
        for stream in streams:
            stream.finish(phase)


def tn_dot(left, right):
    return lax.dot_general(left, right, (((0,), (0,)), ((), ())), preferred_element_type=F32)


class Exchange:
    def __init__(self, place, sent, came):
        self.place, self.sent, self.came, self.count, self.flying = place, sent, came, 0, []

    def send(self, source, target):
        copy = pltpu.make_async_remote_copy(
            src_ref=source,
            dst_ref=target,
            send_sem=self.sent.at[self.count],
            recv_sem=self.came.at[self.count],
            device_id=self.place.partner(),
            device_id_type=MESH,
        )
        copy.start()
        self.count += 1
        self.flying.append(copy)
        return copy

    def drain(self):
        for copy in self.flying:
            copy.wait_send()


def half_columns(block, core, quarter):
    half = quarter // 2
    return pl.ds(pl.multiple_of(block * quarter + core * half, half), half)


def stage_left(place, exchange, left, stage, land, pieces):
    quarter = left.shape[1] // 4
    copies = []
    for block in range(4):
        columns = pl.ds(block * quarter // 2, quarter // 2)
        stage[:, columns] = left[:, half_columns(block, 1 - place.core, quarter)].astype(F32)
        copies.append(exchange.send(stage.at[:, columns], land.at[:, columns]))
    return copies


def stage_right(exchange, right, stage, land, tile):
    copies = []
    for start in range(0, right.shape[1], tile):
        columns = pl.ds(start, tile)
        stage[:, columns] = right[:, columns].astype(F32)
        copies.append(exchange.send(stage.at[:, columns], land.at[:, columns]))
    return copies


def gather_left(place, left, land, both, copies):
    rows, quarter = left.shape[0], left.shape[1] // 4
    for block in range(4):
        columns = pl.ds(block * quarter // 2, quarter // 2)
        both[pl.ds(0, rows), columns] = left[:, half_columns(block, place.core, quarter)]
        copies[block].wait_recv()
        both[pl.ds(rows, rows), columns] = land[:, columns].astype(BF16)


def gather_right(right, land, both, copies, tile, index):
    rows = right.shape[0]
    columns = pl.ds(index * tile, tile)
    both[pl.ds(0, rows), columns] = right[:, columns]
    copies[index].wait_recv()
    both[pl.ds(rows, rows), columns] = land[:, columns].astype(BF16)


TILE = 512


def down_kernel(left, right, out, stage_l, land_l, both_l, stage_r, land_r, both_r, sent, came, *rest):
    place = Place()
    greet(place)
    slabs, scratch = rest[:3], rest[3:]
    exchange = Exchange(place, sent, came)
    right_copies = stage_right(exchange, right, stage_r, land_r, TILE)
    left_copies = stage_left(place, exchange, left, stage_l, land_l, None)
    for index in range(right.shape[1] // TILE):
        gather_right(right, land_r, both_r, right_copies, TILE, index)
    gather_left(place, left, land_l, both_l, left_copies)
    cuts = ((0, 384), (384, 384), (768, 256))

    def block_product(block, carry):
        rows = both_l[:, pl.ds(pl.multiple_of(block * 512, 512), 512)]
        for piece, (start, width) in enumerate(cuts):
            product = tn_dot(rows, both_r[:, pl.ds(start, width)]).reshape(4, 4, 4, 8, width)
            for stream in range(3):
                slabs[stream][block, :, :, :, pl.ds(start, width)] = product[:, :, stream]
            slabs[piece][block, :, :, :, pl.ds(1024, width)] = product[:, :, 3]
        return carry

    lax.fori_loop(0, 4, block_product, 0)
    streams = [
        Stream(place, slabs[k], ORDERS[k], scratch[8 * k : 8 * k + 8]) for k in range(3)
    ]
    run_streams(streams)
    for stream in range(3):
        result = streams[stream].result()
        out[pl.ds(8 * stream, 8), :] = result[:, pl.ds(0, 1024)]
        start, width = cuts[stream]
        out[pl.ds(24, 8), pl.ds(start, width)] = result[:, pl.ds(1024, width)]
    exchange.drain()
    for stream in streams:
        stream.drain()


def wide_kernel(widths, left, right, out, stage_l, land_l, both_l, stage_r, land_r, both_r, sent, came, *rest):
    place = Place()
    greet(place)
    slabs, scratch = rest[:3], rest[3:]
    exchange = Exchange(place, sent, came)
    left_copies = stage_left(place, exchange, left, stage_l, land_l, None)
    right_copies = stage_right(exchange, right, stage_r, land_r, TILE)
    gather_left(place, left, land_l, both_l, left_copies)
    for index in range(right.shape[1] // TILE):
        gather_right(right, land_r, both_r, right_copies, TILE, index)
    starts = (0, widths[0], widths[0] + widths[1])
    for stream in range(3):
        for start in range(0, widths[stream], TILE):
            width = min(TILE, widths[stream] - start)
            product = tn_dot(both_l[...], both_r[:, pl.ds(starts[stream] + start, width)])
            slabs[stream][:, :, :, :, pl.ds(start, width)] = product.reshape(4, 4, 4, 8, width)
    streams = [
        Stream(place, slabs[k], ORDERS[k], scratch[8 * k : 8 * k + 8]) for k in range(3)
    ]
    run_streams(streams)
    for stream in range(3):
        out[:, pl.ds(starts[stream], widths[stream])] = streams[stream].result()[...]
    exchange.drain()
    for stream in streams:
        stream.drain()


def grad_call(kernel, left, right, out_shape, widths, collective_id):
    rows, half, columns = left.shape[0], left.shape[1] // 2, right.shape[1]
    pieces = 4 + columns // TILE
    vmem = pl.BlockSpec(memory_space=pltpu.VMEM)
    return pl.pallas_call(
        kernel,
        out_shape=jax.ShapeDtypeStruct(out_shape, F32),
        in_specs=[vmem, vmem],
        out_specs=vmem,
        scratch_shapes=[
            pltpu.VMEM((rows, half), F32),
            pltpu.VMEM((rows, half), F32),
            pltpu.VMEM((2 * rows, half), BF16),
            pltpu.VMEM((rows, columns), F32),
            pltpu.VMEM((rows, columns), F32),
            pltpu.VMEM((2 * rows, columns), BF16),
            pltpu.SemaphoreType.DMA((pieces,)),
            pltpu.SemaphoreType.DMA((pieces,)),
            *[pltpu.VMEM((4, 4, 4, 8, width), F32) for width in widths],
            *[item for width in widths for item in stream_scratch(width)],
        ],
        compiler_params=pltpu.CompilerParams(
            collective_id=collective_id, has_side_effects=True, vmem_limit_bytes=62 * MIB
        ),
    )(left, right)


def grad_down_sum(hidden, cotangent):
    return grad_call(down_kernel, hidden, cotangent, (32, 1024), (1408, 1408, 1280), 1)


def grad_wide_sum(left, right, widths, collective_id):
    def kernel(*refs):
        wide_kernel(widths, *refs)

    return grad_call(kernel, left, right, (8, right.shape[1]), widths, collective_id)

SEQ = 16
PAIR = 128
NT = (((1,), (1,)), ((), ()))
TN = (((0,), (0,)), ((), ()))


def dot_nt(left, right):
    return lax.dot_general(left, right, NT, preferred_element_type=F32)


def dot_nn(left, right):
    return jnp.dot(left, right, preferred_element_type=F32)


def split(values):
    high = values.astype(BF16)
    return high, (values - high.astype(F32)).astype(BF16)


def features(raw):
    return jnp.where(raw > 0, raw + 1.0, jnp.exp(jnp.minimum(raw, 0.0))).astype(BF16)


def feature_slope(raw):
    return jnp.where(raw > 0, 1.0, jnp.exp(jnp.minimum(raw, 0.0)))


def head_masks():
    lane = lax.broadcasted_iota(jnp.int32, (1, PAIR), 1)
    first = jnp.where(lane < 64, 1.0, 0.0)
    return first.astype(BF16), (1.0 - first).astype(BF16)


def first_head(rows):
    return lax.broadcasted_iota(jnp.int32, (rows, PAIR), 1) < 64


def pack_state(square, total):
    blocks = jnp.where(first_head(64), square[:64], square[64:])
    return blocks, jnp.broadcast_to(total, (8, PAIR))


def unpack_state(packed):
    first = first_head(64)
    square = jnp.concatenate(
        [jnp.where(first, packed[:64], 0.0), jnp.where(first, 0.0, packed[:64])], axis=0
    )
    return square, packed[64:65]


def same_head():
    row = lax.broadcasted_iota(jnp.int32, (PAIR, PAIR), 0)
    lane = lax.broadcasted_iota(jnp.int32, (PAIR, PAIR), 1)
    return (row < 64) == (lane < 64)


class Scan:
    def __init__(self, terms, landed, sums, result, sems, reverse):
        self.terms, self.landed, self.sums, self.result = terms, landed, sums, result
        self.sems, self.reverse = sems, reverse
        self.dp, self.me = lax.axis_index("dp"), lax.axis_index("seq")

    def greet(self):
        barrier = pltpu.get_barrier_semaphore()
        for step in range(1, SEQ):
            pl.semaphore_signal(
                barrier,
                inc=1,
                device_id=(self.dp, lax.rem(self.me + step, SEQ)),
                device_id_type=MESH,
            )

    def send_all(self, source, target, sent, came):
        def one(step, carry):
            other = lax.rem(self.me + step, SEQ)
            pltpu.make_async_remote_copy(
                src_ref=source.at[other],
                dst_ref=target.at[self.me],
                send_sem=sent.at[step],
                recv_sem=came.at[step],
                device_id=(self.dp, other),
                device_id_type=MESH,
            ).start()
            return carry

        lax.fori_loop(1, SEQ, one, 0)
        target[self.me] = source[self.me]

    def wait_all(self, source, target, sent, came):
        def one(step, carry):
            other = lax.rem(self.me + (SEQ - step), SEQ)
            pltpu.make_async_remote_copy(
                src_ref=source.at[other],
                dst_ref=target.at[other],
                send_sem=sent.at[step],
                recv_sem=came.at[step],
                device_id=(self.dp, other),
                device_id_type=MESH,
            ).wait_recv()
            return carry

        lax.fori_loop(1, SEQ, one, 0)

    def wait_sent(self, source, target, sent, came):
        def one(step, carry):
            other = lax.rem(self.me + step, SEQ)
            pltpu.make_async_remote_copy(
                src_ref=source.at[other],
                dst_ref=target.at[self.me],
                send_sem=sent.at[step],
                recv_sem=came.at[step],
                device_id=(self.dp, other),
                device_id_type=MESH,
            ).wait_send()
            return carry

        lax.fori_loop(1, SEQ, one, 0)

    def start(self):
        self.send_all(self.terms, self.landed, self.sems[0], self.sems[1])

    def middle(self):
        self.wait_all(self.terms, self.landed, self.sems[0], self.sems[1])
        total = jnp.zeros(self.landed.shape[1:], F32)
        for k in range(SEQ):
            at = SEQ - 1 - k if self.reverse else k
            self.sums[at] = total
            total = total + self.landed[at]
        self.send_all(self.sums, self.result, self.sems[2], self.sems[3])

    def finish(self):
        self.wait_all(self.sums, self.result, self.sems[2], self.sems[3])

    def drain(self):
        self.wait_sent(self.terms, self.landed, self.sems[0], self.sems[1])
        self.wait_sent(self.sums, self.result, self.sems[2], self.sems[3])


SCAN_SCRATCH = [
    pltpu.VMEM((SEQ, 72, PAIR), F32),
    pltpu.VMEM((SEQ, 72, PAIR), F32),
    pltpu.VMEM((SEQ, 72, PAIR), F32),
    *[pltpu.SemaphoreType.DMA((SEQ,)) for _ in range(4)],
]


def unit_slices(unit, block):
    rows = pl.ds(pl.multiple_of(lax.div(unit, 8) * block, block), block)
    columns = pl.ds(pl.multiple_of(lax.rem(unit, 8) * PAIR, PAIR), PAIR)
    return rows, columns


def for_units(step, together):
    def several(index, carry):
        for offset in range(together):
            step(index * together + offset)
        return carry

    lax.fori_loop(0, SEQ // together, several, 0)


def causal_mask(block, transposed=False):
    row = lax.broadcasted_iota(jnp.int32, (block, block), 0)
    column = lax.broadcasted_iota(jnp.int32, (block, block), 1)
    return (row <= column) if transposed else (row >= column)


def norm_rows(values):
    center = jnp.mean(values, axis=-1, keepdims=True)
    centered = values - center
    variance = jnp.mean(centered * centered, axis=-1, keepdims=True)
    inverse = lax.rsqrt(variance + 1e-05)
    return centered * inverse, inverse


ROWS = 64


def for_rows(count, step):
    def one(index, carry):
        step(pl.ds(pl.multiple_of(index * ROWS, ROWS), ROWS))
        return carry

    lax.fori_loop(0, count // ROWS, one, 0)


def for_columns(count, width, step):
    def one(index, carry):
        step(pl.ds(pl.multiple_of(index * width, width), width))
        return carry

    lax.fori_loop(0, count // width, one, 0)


def attention_forward_kernel(
    block, x, gain, shift, weight, normed, qkv, att, den, state,
    w, fq, fk, terms, landed, sums, s0, s1, s2, s3, wsem,
):
    scan = Scan(terms, landed, sums, state, (s0, s1, s2, s3), False)
    scan.greet()
    loads = []
    for slot, third in enumerate((1, 2, 0)):
        load = pltpu.make_async_copy(
            weight.at[:, pl.ds(third * 1024, 1024)], w.at[slot], wsem.at[slot]
        )
        load.start()
        loads.append(load)

    def norm_step(rows):
        scaled, _ = norm_rows(x[rows, :].astype(F32))
        normed[rows, :] = (scaled * gain[...] + shift[...]).astype(BF16)

    for_rows(x.shape[0], norm_step)

    def project(slot, third, feature):
        loads[slot].wait()

        def step(columns):
            raw = dot_nn(normed[...], w[slot, :, columns]).astype(BF16)
            qkv[third, :, columns] = raw
            if feature is not None:
                feature[:, columns] = features(raw.astype(F32))

        for_columns(1024, 512, step)

    project(0, 1, fk)
    project(1, 2, None)

    def local_state(unit):
        rows, columns = unit_slices(unit, block)
        keys = fk[rows, columns]
        square = tn_dot(qkv[2, rows, columns], keys)
        total = jnp.sum(keys.astype(F32), axis=0, keepdims=True)
        blocks, row = pack_state(square, total)
        terms[unit, pl.ds(0, 64)] = blocks
        terms[unit, pl.ds(64, 8)] = row

    for_units(local_state, 4)
    pl.semaphore_wait(pltpu.get_barrier_semaphore(), SEQ - 1)
    scan.start()
    project(2, 0, fq)
    first, second = head_masks()
    causal = causal_mask(block)

    def local_part(unit):
        rows, columns = unit_slices(unit, block)
        query, key, value = fq[rows, columns], fk[rows, columns], qkv[2, rows, columns]
        scores = dot_nt(jnp.concatenate([query * first, query * second], axis=0), key)
        both = 0.0
        for head, mask in enumerate((first, second)):
            own = jnp.where(causal, scores[head * block : (head + 1) * block], 0.0).astype(BF16)
            right = jnp.concatenate([value * mask, jnp.broadcast_to(mask, value.shape)], axis=1)
            both = both + dot_nn(own, right)
        att[rows, columns] = both[:, :PAIR]
        den[rows, columns] = both[:, PAIR:]

    for_units(local_part, 2)
    scan.middle()
    scan.finish()
    together = same_head()

    def incoming(unit):
        rows, columns = unit_slices(unit, block)
        square, total = unpack_state(state[unit])
        totals = jnp.where(together, jnp.broadcast_to(total, (PAIR, PAIR)), 0.0)
        high, low = split(jnp.concatenate([square, totals], axis=0))
        query = fq[rows, columns]
        both = dot_nt(
            jnp.concatenate([query, query], axis=1), jnp.concatenate([high, low], axis=1)
        )
        denom = den[rows, columns] + both[:, PAIR:]
        den[rows, columns] = denom
        att[rows, columns] = (att[rows, columns] + both[:, :PAIR]) / denom

    for_units(incoming, 2)
    scan.drain()


def attention_forward(x, gain, shift, weight, block):
    rows, width = x.shape
    vmem = pl.BlockSpec(memory_space=pltpu.VMEM)

    def kernel(*refs):
        attention_forward_kernel(block, *refs)

    return pl.pallas_call(
        kernel,
        out_shape=[
            jax.ShapeDtypeStruct((rows, width), BF16),
            jax.ShapeDtypeStruct((3, rows, width), BF16),
            jax.ShapeDtypeStruct((rows, width), F32),
            jax.ShapeDtypeStruct((rows, width), F32),
            jax.ShapeDtypeStruct((SEQ, 72, PAIR), F32),
        ],
        in_specs=[vmem, vmem, vmem, pl.BlockSpec(memory_space=pl.ANY)],
        out_specs=[vmem] * 5,
        scratch_shapes=[
            pltpu.VMEM((3, width, width), BF16),
            pltpu.VMEM((rows, width), BF16),
            pltpu.VMEM((rows, width), BF16),
            *SCAN_SCRATCH,
            pltpu.SemaphoreType.DMA((3,)),
        ],
        compiler_params=pltpu.CompilerParams(
            collective_id=5, has_side_effects=True, vmem_limit_bytes=62 * MIB
        ),
    )(x, gain.reshape(1, width), shift.reshape(1, width), weight)


def attention_backward_kernel(
    block, qkv, att, den, state, gatt, gqkv,
    fq, fk, gn, grads, terms, landed, sums, result, s0, s1, s2, s3,
):
    scan = Scan(terms, landed, sums, result, (s0, s1, s2, s3), True)
    scan.greet()
    first, second = head_masks()
    first_wide = first_head(block)
    fq[...] = features(qkv[0].astype(F32))
    fk[...] = features(qkv[1].astype(F32))

    def slopes(rows, columns):
        numer = gn[rows, columns]
        product = numer * att[rows, columns]
        ours = jnp.sum(jnp.where(first_wide, product, 0.0), axis=1, keepdims=True)
        theirs = jnp.sum(jnp.where(first_wide, 0.0, product), axis=1, keepdims=True)
        return numer, -ours, -theirs

    def local_state(unit):
        rows, columns = unit_slices(unit, block)
        gn[rows, columns] = gatt[rows, columns] / den[rows, columns]
        numer, one, two = slopes(rows, columns)
        query = fq[rows, columns]
        high, low = split(numer)
        wide = tn_dot(query, jnp.concatenate([high, low], axis=1))
        spread = jnp.where(first_wide, one, two)
        total = jnp.sum(query.astype(F32) * spread, axis=0, keepdims=True)
        blocks, row = pack_state(wide[:, :PAIR] + wide[:, PAIR:], total)
        terms[unit, pl.ds(0, 64)] = blocks
        terms[unit, pl.ds(64, 8)] = row

    for_units(local_state, 2)
    pl.semaphore_wait(pltpu.get_barrier_semaphore(), SEQ - 1)
    scan.start()
    causal = causal_mask(block)
    causal_t = causal_mask(block, True)

    def local_part(unit):
        rows, columns = unit_slices(unit, block)
        query, key, value = fq[rows, columns], fk[rows, columns], qkv[2, rows, columns]
        numer, one, two = slopes(rows, columns)
        high, low = split(numer)
        scores = dot_nt(jnp.concatenate([key * first, key * second], axis=0), query)
        wide = jnp.concatenate([high, low], axis=1)
        values = jnp.concatenate([value, value], axis=1)
        grad_query, grad_key, grad_value = 0.0, 0.0, 0.0
        for head, (mask, slope) in enumerate(((first, one), (second, two))):
            mask_wide = jnp.concatenate([mask, mask], axis=1)
            mixing = jnp.where(causal, dot_nt(wide * mask_wide, values) + slope, 0.0).astype(BF16)
            turned = jnp.where(causal_t, scores[head * block : (head + 1) * block], 0.0)
            grad_query = grad_query + dot_nn(mixing, key * mask)
            grad_key = grad_key + tn_dot(mixing, query * mask)
            grad_value = grad_value + dot_nn(turned.astype(BF16), high * mask)
        square, total = unpack_state(state[unit])
        state_high, state_low = split(square)
        grad_query = grad_query + dot_nn(
            jnp.concatenate([high, low], axis=1),
            jnp.concatenate([state_high, state_high], axis=0),
        )
        grad_query = grad_query + dot_nn(high, state_low)
        grad_query = grad_query + jnp.where(first_wide, one, two) * total
        raw = qkv[0, rows, columns].astype(F32)
        gqkv[0, rows, columns] = (grad_query * feature_slope(raw)).astype(BF16)
        grads[0, rows, columns] = grad_key
        grads[1, rows, columns] = grad_value

    for_units(local_part, 1)
    scan.middle()
    scan.finish()

    def incoming(unit):
        rows, columns = unit_slices(unit, block)
        square, total = unpack_state(result[unit])
        high, low = split(square)
        key, value = fk[rows, columns], qkv[2, rows, columns]
        grad_key = grads[0, rows, columns] + total
        grad_key = grad_key + dot_nt(
            jnp.concatenate([value, value], axis=1), jnp.concatenate([high, low], axis=1)
        )
        grad_value = grads[1, rows, columns] + dot_nn(
            jnp.concatenate([key, key], axis=1), jnp.concatenate([high, low], axis=0)
        )
        raw = qkv[1, rows, columns].astype(F32)
        gqkv[1, rows, columns] = (grad_key * feature_slope(raw)).astype(BF16)
        gqkv[2, rows, columns] = grad_value.astype(BF16)

    for_units(incoming, 2)
    scan.drain()


def attention_backward(qkv, att, den, state, gatt, block):
    _, rows, width = qkv.shape
    vmem = pl.BlockSpec(memory_space=pltpu.VMEM)

    def kernel(*refs):
        attention_backward_kernel(block, *refs)

    return pl.pallas_call(
        kernel,
        out_shape=jax.ShapeDtypeStruct((3, rows, width), BF16),
        in_specs=[vmem] * 5,
        out_specs=vmem,
        scratch_shapes=[
            pltpu.VMEM((rows, width), BF16),
            pltpu.VMEM((rows, width), BF16),
            pltpu.VMEM((rows, width), F32),
            pltpu.VMEM((2, rows, width), F32),
            SCAN_SCRATCH[0],
            *SCAN_SCRATCH,
        ],
        compiler_params=pltpu.CompilerParams(
            collective_id=6, has_side_effects=True, vmem_limit_bytes=62 * MIB
        ),
    )(qkv, att, den, state, gatt)


def layer_norm(values, gain, shift):
    center = jnp.mean(values, axis=-1, keepdims=True)
    centered = values - center
    variance = jnp.mean(centered * centered, axis=-1, keepdims=True)
    inverse = lax.rsqrt(variance + 1e-05)
    scaled = centered * inverse
    return (scaled * gain + shift, scaled, inverse)


def norm_back(grad_out, gain, scaled, inverse):
    grad_scaled = grad_out * gain
    first_mean = jnp.mean(grad_scaled, axis=-1, keepdims=True)
    second_mean = jnp.mean(grad_scaled * scaled, axis=-1, keepdims=True)
    return inverse * (grad_scaled - first_mean - scaled * second_mean)


def rows_dot(left, right):
    return lax.dot_general(
        left, right, (((0,), (0,)), ((), ())), preferred_element_type=jnp.float32
    )


def back_dot(left, right):
    return lax.dot_general(
        left, right, (((1,), (1,)), ((), ())), preferred_element_type=jnp.float32
    )


def body(
    inputs,
    first_gain,
    first_shift,
    qkv_weight,
    out_weight,
    second_gain,
    second_shift,
    up_weight,
    down_weight,
    cotangent,
):
    seq_count, block_len, width = inputs.shape
    row_count = seq_count * block_len
    flat_input = inputs.astype(jnp.float32).reshape(row_count, width)
    _, scaled_one, inverse_one = layer_norm(flat_input, first_gain, first_shift)
    normed_low, qkv_low, attended, denom, state_in = attention_forward(
        inputs.reshape(row_count, width), first_gain, first_shift, qkv_weight, block_len
    )
    attended_low = attended.astype(jnp.bfloat16)
    mixed = flat_input + jnp.dot(attended_low, out_weight, preferred_element_type=jnp.float32)
    normed_two, scaled_two, inverse_two = layer_norm(mixed, second_gain, second_shift)
    normed_two_low = normed_two.astype(jnp.bfloat16)
    pre_act = jnp.dot(normed_two_low, up_weight, preferred_element_type=jnp.float32)
    hidden_low = jax.nn.gelu(pre_act, approximate=False).astype(jnp.bfloat16)
    result = mixed + jnp.dot(hidden_low, down_weight, preferred_element_type=jnp.float32)
    output = result.astype(jnp.bfloat16).reshape(seq_count, block_len, width)
    grad_result = cotangent.reshape(row_count, width)
    grad_down = grad_down_sum(hidden_low, grad_result)
    grad_hidden = back_dot(grad_result, down_weight)
    cumulative = 0.5 * (1.0 + lax.erf(pre_act * (1.0 / math.sqrt(2.0))))
    density = jnp.exp(-0.5 * pre_act * pre_act) * (1.0 / math.sqrt(2.0 * math.pi))
    grad_pre_low = (grad_hidden * (cumulative + pre_act * density)).astype(jnp.bfloat16)
    grad_up = grad_wide_sum(normed_two_low, grad_pre_low, (1408, 1408, 1280), 2)
    grad_normed_two = back_dot(grad_pre_low, up_weight)
    grad_second_gain = jnp.sum(grad_normed_two * scaled_two, axis=0)
    grad_second_shift = jnp.sum(grad_normed_two, axis=0)
    grad_mixed = grad_result.astype(jnp.float32) + norm_back(
        grad_normed_two, second_gain, scaled_two, inverse_two
    )
    grad_mixed_low = grad_mixed.astype(jnp.bfloat16)
    grad_out = grad_wide_sum(attended_low, grad_mixed_low, (384, 384, 256), 3)
    grad_att = back_dot(grad_mixed_low, out_weight)
    grad_qkv_three = attention_backward(qkv_low, attended, denom, state_in, grad_att, block_len)
    grad_qkv_low = jnp.concatenate([grad_qkv_three[0], grad_qkv_three[1], grad_qkv_three[2]], axis=1)
    grad_qkv = grad_wide_sum(normed_low, grad_qkv_low, (1024, 1024, 1024), 4)
    grad_normed = back_dot(grad_qkv_low, qkv_weight)
    grad_first_gain = jnp.sum(grad_normed * scaled_one, axis=0)
    grad_first_shift = jnp.sum(grad_normed, axis=0)
    grad_input = (grad_mixed + norm_back(grad_normed, first_gain, scaled_one, inverse_one)).reshape(
        seq_count, block_len, width
    )
    summed = (
        grad_qkv,
        grad_out,
        grad_up,
        grad_down,
        lax.psum_scatter(grad_first_gain, ("dp", "seq"), scatter_dimension=0, tiled=True),
        lax.psum_scatter(grad_first_shift, ("dp", "seq"), scatter_dimension=0, tiled=True),
        lax.psum_scatter(grad_second_gain, ("dp", "seq"), scatter_dimension=0, tiled=True),
        lax.psum_scatter(grad_second_shift, ("dp", "seq"), scatter_dimension=0, tiled=True),
    )
    return (
        output,
        grad_input,
        summed[0],
        summed[1],
        summed[2],
        summed[3],
        summed[4],
        summed[5],
        summed[6],
        summed[7],
    )


def solution(mesh):
    return jax.shard_map(
        body,
        mesh=mesh,
        in_specs=(
            P("dp", "seq", None),
            P(),
            P(),
            P(),
            P(),
            P(),
            P(),
            P(),
            P(),
            P("dp", "seq", None),
        ),
        out_specs=(
            P("dp", "seq", None),
            P("dp", "seq", None),
            P(("dp", "seq"), None),
            P(("dp", "seq"), None),
            P(("dp", "seq"), None),
            P(("dp", "seq"), None),
            P(("dp", "seq")),
            P(("dp", "seq")),
            P(("dp", "seq")),
            P(("dp", "seq")),
        ),
        check_vma=False,
    )
```

```python
import math

import jax
import jax.numpy as jnp
from jax import lax
from jax.experimental import pallas as pl
from jax.experimental.pallas import tpu as pltpu
from jax.sharding import PartitionSpec as P

MESH = pl.DeviceIdType.MESH
F32 = jnp.float32
BF16 = jnp.bfloat16
RING = 4
MIB = 2**20


class Place:
    def __init__(self):
        dp, seq = lax.axis_index("dp"), lax.axis_index("seq")
        self.core = lax.rem(dp, 2)
        self.at = (lax.div(dp, 2), lax.div(seq, RING), lax.rem(seq, RING))

    def id_of(self, x, y, z, core):
        return (x * 2 + core, y * RING + z)

    def ring(self, axis, step):
        return lax.rem(self.at[axis] + (step + RING), RING)

    def neighbour(self, axis, step):
        at = list(self.at)
        at[axis] = self.ring(axis, step)
        return self.id_of(*at, self.core)

    def partner(self):
        return self.id_of(*self.at, 1 - self.core)


def greet(others):
    barrier = pltpu.get_barrier_semaphore()
    for other in others:
        pl.semaphore_signal(barrier, inc=1, device_id=other, device_id_type=MESH)


def met(count):
    pl.semaphore_wait(pltpu.get_barrier_semaphore(), count)


def link_neighbours(place):
    others = [place.neighbour(axis, step) for axis in range(3) for step in (1, -1)]
    return [*others, place.partner()]


ORDERS = ((0, 1, 2), (1, 2, 0), (2, 0, 1))


def phase_scratch(remaining, length):
    if remaining:
        half = (2, 2, *[4] * (remaining - 1), 8, length)
    else:
        half = (2, 8, (length // 128 + 1) // 2 * 128)
    return [
        pltpu.VMEM((2, *[4] * remaining, 8, length), F32),
        pltpu.VMEM(half, F32),
        pltpu.SemaphoreType.DMA((6,)),
        pltpu.SemaphoreType.DMA((6,)),
    ]


class Phase:
    def __init__(self, place, data, axes, axis, scratch):
        self.place, self.data, self.axis = place, data, axis
        self.where = axes.index(axis)
        self.full, self.half, self.sent, self.came = scratch
        self.flying = []
        self.flat = len(axes) == 1
        self.length = data.shape[-1]
        self.cut = (self.length // 128 + 1) // 2 * 128
        self.whole = self.flat and self.cut == self.length

    def empty(self, which):
        return self.whole and which == 1

    def chunk(self, target):
        index = [slice(None)] * self.where + [target]
        return self.data.at[tuple(index)]

    def part(self, ref, which):
        if not self.flat:
            return ref.at[pl.ds(2 * which, 2)]
        if which == 0:
            return ref.at[:, pl.ds(0, self.cut)]
        return ref.at[:, pl.ds(self.cut, self.length - self.cut)]

    def through(self, way):
        ref = self.half.at[way]
        if self.flat and way == 1:
            return ref.at[:, pl.ds(0, self.length - self.cut)]
        return ref

    def copy(self, kind, way, source, target):
        number = kind * 2 + way
        return pltpu.make_async_remote_copy(
            src_ref=source,
            dst_ref=target,
            send_sem=self.sent.at[number],
            recv_sem=self.came.at[number],
            device_id=self.place.neighbour(self.axis, 1 - 2 * way),
            device_id_type=MESH,
        )

    def send(self, kind, way, source, target):
        copy = self.copy(kind, way, source, target)
        copy.start()
        self.flying.append(copy)

    def beside(self, way):
        return self.chunk(self.place.ring(self.axis, 1 - 2 * way))

    def begin(self):
        opposite = self.chunk(self.place.ring(self.axis, 2))
        for way in range(2):
            if not self.empty(way):
                self.send(0, way, self.part(opposite, way), self.through(way))
        for way in range(2):
            if self.empty(1 - way):
                continue
            target = self.part(self.full.at[way], 1 - way)
            self.send(1, way, self.part(self.beside(way), 1 - way), target)

    def forward(self):
        for way in range(2):
            if self.empty(way):
                continue
            came = self.through(way)
            self.copy(0, way, came, came).wait_recv()
            own = self.part(self.beside(way), way)
            add_into(own, own, came)
            self.send(2, way, own, self.part(self.full.at[way], way))

    def finish(self, out=None):
        own = self.chunk(self.place.at[self.axis])
        for way in range(2):
            for kind, which in ((1, 1 - way), (2, way)):
                if self.empty(which):
                    continue
                target = self.part(self.full.at[way], which)
                self.copy(kind, way, target, target).wait_recv()
        add_into(own if out is None else out, own, self.full.at[0], self.full.at[1])
        return own

    def drain(self):
        for copy in self.flying:
            copy.wait_send()


class Sum:
    def __init__(self, place, pieces, scratch, first=0, last=2):
        self.place, self.pieces, self.scratch = place, list(pieces), scratch
        self.at, self.last, self.old = first, last, []
        self.now = None
        self.axes = [sorted(order[first:]) for order in ORDERS[: len(self.pieces)]]

    def begin(self):
        self.now = []
        for k, piece in enumerate(self.pieces):
            axis = ORDERS[k][self.at]
            scratch = self.scratch[self.at][k]
            self.now.append(Phase(self.place, piece, self.axes[k], axis, scratch))
        for phase in self.now:
            phase.begin()

    def forward(self):
        for phase in self.now:
            phase.forward()

    def finish(self, outs=None):
        for k, phase in enumerate(self.now):
            self.pieces[k] = phase.finish(None if outs is None else outs[k])
            self.axes[k] = [axis for axis in self.axes[k] if axis != phase.axis]
        self.old += self.now
        self.at += 1
        if self.at <= self.last:
            self.begin()

    def drain(self):
        for phase in self.old:
            phase.drain()


def sum_scratch(widths, first=0, last=2):
    return {
        at: [phase_scratch(2 - at, width) for width in widths] for at in range(first, last + 1)
    }


def add_into(out, *terms):
    if len(out.shape) > 2:

        def row(index, carry):
            add_into(out.at[index], *[term.at[index] for term in terms])
            return carry

        if len(out.shape) == 4:
            lax.fori_loop(0, out.shape[0], row, 0)
        else:
            for index in range(out.shape[0]):
                row(index, 0)
        return
    total = terms[0][...]
    for term in terms[1:]:
        total = total + term[...]
    out[...] = total


def tn_dot(left, right):
    return lax.dot_general(left, right, (((0,), (0,)), ((), ())), preferred_element_type=F32)


TILE = 512


class Swap:
    def __init__(self, place, stage, sent, came):
        self.place, self.stage, self.sent, self.came = place, stage, sent, came

    def copy(self, number, slot, target):
        return pltpu.make_async_remote_copy(
            src_ref=self.stage.at[slot],
            dst_ref=target,
            send_sem=self.sent.at[number],
            recv_sem=self.came.at[number],
            device_id=self.place.partner(),
            device_id_type=MESH,
        )

    def put(self, number, slot, values, target, before=None):
        if before is not None:
            self.copy(before, slot, target).wait_send()
        self.stage[slot] = values.astype(F32)
        self.copy(number, slot, target).start()

    def get(self, number, target):
        self.copy(number, 0, target).wait_recv()
        return target[...].astype(BF16)

    def drain(self, numbers, target):
        for number in numbers:
            self.copy(number, number % 4, target).wait_send()


def half_columns(block, core, quarter):
    half = quarter // 2
    return pl.ds(pl.multiple_of(block * quarter + core * half, half), half)


def half_tile(index, core):
    return pl.ds(pl.multiple_of((2 * index + core) * TILE, TILE), TILE)


def shared_widths(columns):
    tiles = columns // 128
    main = (2 * tiles + 2) // 3
    return main * 128, main * 128, (2 * tiles - 2 * main) * 128


def shared_product(left, right, slabs, columns):
    main, _, tail = shared_widths(columns)
    rest = tail // 2
    start = 0
    while start < columns:
        width = min(TILE, main - start) if start < main else rest
        product = tn_dot(left[...], right[:, pl.ds(start, width)]).reshape(4, 2, 4, 4, 8, width)
        for core in range(2):
            if start < main:
                slabs[core][:, :, :, :, pl.ds(start, width)] = product[:, core]
            else:
                slabs[2][:, :, :, :, pl.ds(core * rest, rest)] = product[:, core]
        start += width


def shared_rows(pieces, columns, rows):
    main, _, tail = shared_widths(columns)
    rest = tail // 2
    for core in range(2):
        rows[core, :, pl.ds(0, main)] = pieces[core][...]
        rows[core, :, pl.ds(main, rest)] = pieces[2][:, pl.ds(core * rest, rest)]


def row_swap(place, rows, land, sems):
    return pltpu.make_async_remote_copy(
        src_ref=rows.at[1 - place.core],
        dst_ref=land,
        send_sem=sems.at[0],
        recv_sem=sems.at[1],
        device_id=place.partner(),
        device_id_type=MESH,
    )


def lay_rows(place, rows, land, out):
    for tile in range(land.shape[1] // TILE):
        columns = pl.ds(tile * TILE, TILE)
        out[:, half_tile(tile, place.core)] = rows[place.core, :, columns]
        out[:, half_tile(tile, 1 - place.core)] = land[:, columns]


DOWN_CUTS = ((0, 384), (384, 384), (768, 256))
DOWN_WIDTHS = (1408, 1408, 1280)


SEQ = 16
PAIR = 128
NT = (((1,), (1,)), ((), ()))
TN = (((0,), (0,)), ((), ()))


def dot_nt(left, right):
    return lax.dot_general(left, right, NT, preferred_element_type=F32)


def dot_nn(left, right):
    return jnp.dot(left, right, preferred_element_type=F32)


def split(values):
    high = values.astype(BF16)
    return high, (values - high.astype(F32)).astype(BF16)


def features(raw):
    return jnp.where(raw > 0, raw + 1.0, jnp.exp(jnp.minimum(raw, 0.0))).astype(BF16)


def feature_slope(raw):
    return jnp.where(raw > 0, 1.0, jnp.exp(jnp.minimum(raw, 0.0)))


def head_masks():
    lane = lax.broadcasted_iota(jnp.int32, (1, PAIR), 1)
    first = jnp.where(lane < 64, 1.0, 0.0)
    return first.astype(BF16), (1.0 - first).astype(BF16)


def first_head(rows):
    return lax.broadcasted_iota(jnp.int32, (rows, PAIR), 1) < 64


def pack_state(square, total):
    blocks = jnp.where(first_head(64), square[:64], square[64:])
    return blocks, jnp.broadcast_to(total, (8, PAIR))


def unpack_state(packed):
    first = first_head(64)
    square = jnp.concatenate(
        [jnp.where(first, packed[:64], 0.0), jnp.where(first, 0.0, packed[:64])], axis=0
    )
    return square, packed[64:65]


def same_head():
    row = lax.broadcasted_iota(jnp.int32, (PAIR, PAIR), 0)
    lane = lax.broadcasted_iota(jnp.int32, (PAIR, PAIR), 1)
    return (row < 64) == (lane < 64)


class Scan:
    def __init__(self, terms, landed, sums, result, sems, reverse):
        self.terms, self.landed, self.sums, self.result = terms, landed, sums, result
        self.sems, self.reverse = sems, reverse
        self.dp, self.me = lax.axis_index("dp"), lax.axis_index("seq")

    def others(self):
        return [(self.dp, lax.rem(self.me + step, SEQ)) for step in range(1, SEQ)]

    def send_all(self, source, target, sent, came):
        def one(step, carry):
            other = lax.rem(self.me + step, SEQ)
            pltpu.make_async_remote_copy(
                src_ref=source.at[other],
                dst_ref=target.at[self.me],
                send_sem=sent.at[step],
                recv_sem=came.at[step],
                device_id=(self.dp, other),
                device_id_type=MESH,
            ).start()
            return carry

        lax.fori_loop(1, SEQ, one, 0)
        target[self.me] = source[self.me]

    def wait_all(self, source, target, sent, came):
        def one(step, carry):
            other = lax.rem(self.me + (SEQ - step), SEQ)
            pltpu.make_async_remote_copy(
                src_ref=source.at[other],
                dst_ref=target.at[other],
                send_sem=sent.at[step],
                recv_sem=came.at[step],
                device_id=(self.dp, other),
                device_id_type=MESH,
            ).wait_recv()
            return carry

        lax.fori_loop(1, SEQ, one, 0)

    def wait_sent(self, source, target, sent, came):
        def one(step, carry):
            other = lax.rem(self.me + step, SEQ)
            pltpu.make_async_remote_copy(
                src_ref=source.at[other],
                dst_ref=target.at[self.me],
                send_sem=sent.at[step],
                recv_sem=came.at[step],
                device_id=(self.dp, other),
                device_id_type=MESH,
            ).wait_send()
            return carry

        lax.fori_loop(1, SEQ, one, 0)

    def start(self):
        self.send_all(self.terms, self.landed, self.sems[0], self.sems[1])

    def middle(self):
        self.wait_all(self.terms, self.landed, self.sems[0], self.sems[1])
        total = jnp.zeros(self.landed.shape[1:], F32)
        for k in range(SEQ):
            at = SEQ - 1 - k if self.reverse else k
            self.sums[at] = total
            total = total + self.landed[at]
        self.send_all(self.sums, self.result, self.sems[2], self.sems[3])

    def finish(self):
        self.wait_all(self.sums, self.result, self.sems[2], self.sems[3])

    def drain(self):
        self.wait_sent(self.terms, self.landed, self.sems[0], self.sems[1])
        self.wait_sent(self.sums, self.result, self.sems[2], self.sems[3])


SCAN_SCRATCH = [
    pltpu.VMEM((SEQ, 72, PAIR), F32),
    pltpu.VMEM((SEQ, 72, PAIR), F32),
    pltpu.VMEM((SEQ, 72, PAIR), F32),
    *[pltpu.SemaphoreType.DMA((SEQ,)) for _ in range(4)],
]


def unit_slices(unit, block):
    rows = pl.ds(pl.multiple_of(lax.div(unit, 8) * block, block), block)
    columns = pl.ds(pl.multiple_of(lax.rem(unit, 8) * PAIR, PAIR), PAIR)
    return rows, columns


def for_units(step, together):
    def several(index, carry):
        for offset in range(together):
            step(index * together + offset)
        return carry

    lax.fori_loop(0, SEQ // together, several, 0)


def causal_mask(block, transposed=False):
    row = lax.broadcasted_iota(jnp.int32, (block, block), 0)
    column = lax.broadcasted_iota(jnp.int32, (block, block), 1)
    return (row <= column) if transposed else (row >= column)


def norm_rows(values):
    center = jnp.mean(values, axis=-1, keepdims=True)
    centered = values - center
    variance = jnp.mean(centered * centered, axis=-1, keepdims=True)
    inverse = lax.rsqrt(variance + 1e-05)
    return centered * inverse, inverse


ROWS = 64


def for_rows(count, step):
    def one(index, carry):
        step(pl.ds(pl.multiple_of(index * ROWS, ROWS), ROWS))
        return carry

    lax.fori_loop(0, count // ROWS, one, 0)


def for_columns(count, width, step):
    def one(index, carry):
        step(pl.ds(pl.multiple_of(index * width, width), width))
        return carry

    lax.fori_loop(0, count // width, one, 0)


def attention_forward_kernel(
    block, x, gain, shift, weight, normed, qkv, att, att_low, den, state,
    w, fq, fk, terms, landed, sums, s0, s1, s2, s3, wsem,
):
    scan = Scan(terms, landed, sums, state, (s0, s1, s2, s3), False)
    greet(scan.others())
    loads = []
    for slot, third in enumerate((1, 2, 0)):
        load = pltpu.make_async_copy(
            weight.at[:, pl.ds(third * 1024, 1024)], w.at[slot], wsem.at[slot]
        )
        load.start()
        loads.append(load)

    def norm_step(rows):
        scaled, _ = norm_rows(x[rows, :].astype(F32))
        normed[rows, :] = (scaled * gain[...] + shift[...]).astype(BF16)

    for_rows(x.shape[0], norm_step)

    def project(slot, third, feature):
        loads[slot].wait()

        def step(columns):
            raw = dot_nn(normed[...], w[slot, :, columns]).astype(BF16)
            qkv[third, :, columns] = raw
            if feature is not None:
                feature[:, columns] = features(raw.astype(F32))

        for_columns(1024, 512, step)

    project(0, 1, fk)
    project(1, 2, None)

    def local_state(unit):
        rows, columns = unit_slices(unit, block)
        keys = fk[rows, columns]
        square = tn_dot(qkv[2, rows, columns], keys)
        total = jnp.sum(keys.astype(F32), axis=0, keepdims=True)
        blocks, row = pack_state(square, total)
        terms[unit, pl.ds(0, 64)] = blocks
        terms[unit, pl.ds(64, 8)] = row

    for_units(local_state, 4)
    met(SEQ - 1)
    scan.start()
    project(2, 0, fq)
    first, second = head_masks()
    causal = causal_mask(block)

    def local_part(unit):
        rows, columns = unit_slices(unit, block)
        query, key, value = fq[rows, columns], fk[rows, columns], qkv[2, rows, columns]
        scores = dot_nt(jnp.concatenate([query * first, query * second], axis=0), key)
        both = 0.0
        for head, mask in enumerate((first, second)):
            own = jnp.where(causal, scores[head * block : (head + 1) * block], 0.0).astype(BF16)
            right = jnp.concatenate([value * mask, jnp.broadcast_to(mask, value.shape)], axis=1)
            both = both + dot_nn(own, right)
        att[rows, columns] = both[:, :PAIR]
        den[rows, columns] = both[:, PAIR:]

    for_units(local_part, 2)
    scan.middle()
    scan.finish()
    together = same_head()

    def incoming(unit):
        rows, columns = unit_slices(unit, block)
        square, total = unpack_state(state[unit])
        totals = jnp.where(together, jnp.broadcast_to(total, (PAIR, PAIR)), 0.0)
        high, low = split(jnp.concatenate([square, totals], axis=0))
        query = fq[rows, columns]
        both = dot_nt(
            jnp.concatenate([query, query], axis=1), jnp.concatenate([high, low], axis=1)
        )
        denom = den[rows, columns] + both[:, PAIR:]
        den[rows, columns] = denom
        attended = (att[rows, columns] + both[:, :PAIR]) / denom
        att[rows, columns] = attended
        att_low[rows, columns] = attended.astype(BF16)

    for_units(incoming, 2)
    scan.drain()


def attention_forward(x, gain, shift, weight, block):
    rows, width = x.shape
    vmem = pl.BlockSpec(memory_space=pltpu.VMEM)

    def kernel(*refs):
        attention_forward_kernel(block, *refs)

    return pl.pallas_call(
        kernel,
        out_shape=[
            jax.ShapeDtypeStruct((rows, width), BF16),
            jax.ShapeDtypeStruct((3, rows, width), BF16),
            jax.ShapeDtypeStruct((rows, width), F32),
            jax.ShapeDtypeStruct((rows, width), BF16),
            jax.ShapeDtypeStruct((rows, width), F32),
            jax.ShapeDtypeStruct((SEQ, 72, PAIR), F32),
        ],
        in_specs=[vmem, vmem, vmem, pl.BlockSpec(memory_space=pl.ANY)],
        out_specs=[vmem] * 6,
        scratch_shapes=[
            pltpu.VMEM((3, width, width), BF16),
            pltpu.VMEM((rows, width), BF16),
            pltpu.VMEM((rows, width), BF16),
            *SCAN_SCRATCH,
            pltpu.SemaphoreType.DMA((3,)),
        ],
        compiler_params=pltpu.CompilerParams(
            collective_id=5, has_side_effects=True, vmem_limit_bytes=62 * MIB
        ),
    )(x, gain.reshape(1, width), shift.reshape(1, width), weight)


def gelu_both(pre):
    cumulative = 0.5 * (1.0 + lax.erf(pre * (1.0 / math.sqrt(2.0))))
    density = jnp.exp(-0.5 * pre * pre) * (1.0 / math.sqrt(2.0 * math.pi))
    return (pre * cumulative).astype(BF16), (cumulative + pre * density).astype(BF16)


def norm_back(grad, gain, scaled, inverse):
    spread = grad * gain
    first_mean = jnp.mean(spread, axis=-1, keepdims=True)
    second_mean = jnp.mean(spread * scaled, axis=-1, keepdims=True)
    return inverse * (spread - first_mean - scaled * second_mean)


def norm_back_rows(values, grad, base, gain, sums, store):
    sums[...] = jnp.zeros_like(sums)

    def step(rows):
        scaled, inverse = norm_rows(values[rows, :].astype(F32))
        part = grad[rows, :]
        sums[0:1, :] += jnp.sum(part * scaled, axis=0, keepdims=True)
        sums[1:2, :] += jnp.sum(part, axis=0, keepdims=True)
        store(rows, base[rows, :].astype(F32) + norm_back(part, gain[...], scaled, inverse))

    for_rows(grad.shape[0], step)


def feed_forward_kernel(
    x, att_low, gain, shift, cot_in, w_out, w_up, w_down,
    output, gmixed, gatt, sums, norm_cat, pre_cat, down_a, down_b, down_c,
    wo, wu, wd, wsem, hidden, slope, cot_cat, stage, land, land_cot, land_norm,
    slab_a, slab_b, slab_c, swap_sent, swap_came, free, *scratch,
):
    place = Place()
    core = place.core
    rows = x.shape[0]
    others = link_neighbours(place)
    greet(others)
    own, other = pl.ds(0, rows), pl.ds(rows, rows)
    mixed = gatt
    loads = []
    moves = ((w_out, wo), (w_up, wu), (w_down, wd), (cot_in, cot_cat.at[own]))
    for slot in (3, 0, 1, 2):
        loads.append(pltpu.make_async_copy(*moves[slot], wsem.at[slot]))
        loads[-1].start()
    loads.append(loads.pop(0))
    cot = cot_cat.at[own]
    swap = Swap(place, stage, swap_sent, swap_came)
    met(len(others))
    loads[3].wait()
    for tile in range(2):
        columns = pl.ds(tile * TILE, TILE)
        swap.put(tile, tile, cot[:, columns], land_cot.at[tile])
    loads[0].wait()

    def mix(columns):
        mixed[:, columns] = x[:, columns].astype(F32) + dot_nn(att_low[...], wo[:, columns])

    for_columns(1024, TILE, mix)

    def norm_step(index):
        scaled, _ = norm_rows(mixed[index, :])
        norm_cat[index, :] = (scaled * gain[...] + shift[...]).astype(BF16)

    for_rows(rows, norm_step)
    for tile in range(2):
        columns = pl.ds(tile * TILE, TILE)
        swap.put(2 + tile, 2 + tile, norm_cat[own, columns], land_norm.at[tile])
    loads[1].wait()

    def up(columns):
        ours, ours_slope = gelu_both(dot_nn(norm_cat[own, :], wu[:, columns]))
        hidden[:, columns] = ours
        slope[:, columns] = ours_slope
        return ours

    def give(block, carry):
        theirs = up(half_columns(block, 1 - core, 1024))
        swap.put(4 + block, block, theirs, land.at[block], before=block)
        return carry

    lax.fori_loop(0, 4, give, 0)
    for tile in range(2):
        cot_cat[other, pl.ds(tile * TILE, TILE)] = swap.get(tile, land_cot.at[tile])
    slabs = (slab_a, slab_b, slab_c)

    def take(block, carry):
        ours = up(half_columns(block, core, 1024))
        both = jnp.concatenate([ours, swap.get(4 + block, land.at[block])], axis=0)
        for piece, (start, width) in enumerate(DOWN_CUTS):
            product = tn_dot(both, cot_cat[:, pl.ds(start, width)]).reshape(4, 4, 4, 8, width)
            for stream in range(3):
                slabs[stream][block, :, :, :, pl.ds(start, width)] = product[:, :, stream]
            slabs[piece][block, :, :, :, pl.ds(1024, width)] = product[:, :, 3]
        return carry

    lax.fori_loop(0, 4, take, 0)
    pl.semaphore_signal(free, inc=1, device_id=place.partner(), device_id_type=MESH)
    down = Sum(place, slabs, {0: [scratch[4 * k : 4 * k + 4] for k in range(3)]}, 0, 0)
    down.begin()
    loads[2].wait()

    def finish_forward(columns):
        output[:, columns] = (mixed[:, columns] + dot_nn(hidden[...], wd[:, columns])).astype(BF16)

    for_columns(1024, 256, finish_forward)

    def back(columns):
        grad = dot_nt(cot[...], wd[columns, :]) * slope[:, columns].astype(F32)
        low = grad.astype(BF16)
        hidden[:, columns] = low
        return low

    pl.semaphore_wait(free, 1)

    def give_back(block, carry):
        theirs = back(half_columns(block, 1 - core, 1024))
        swap.put(8 + block, block, theirs, land.at[block], before=4 + block)
        return carry

    lax.fori_loop(0, 4, give_back, 0)

    def take_back(block, carry):
        columns = pl.ds(pl.multiple_of(block * TILE, TILE), TILE)
        pre_cat[own, columns] = back(half_columns(block, core, 1024))
        pre_cat[other, columns] = swap.get(8 + block, land.at[block])
        return carry

    lax.fori_loop(0, 4, take_back, 0)
    down.forward()
    for tile in range(2):
        norm_cat[other, pl.ds(tile * TILE, TILE)] = swap.get(2 + tile, land_norm.at[tile])

    def back_up(columns):
        gmixed[:, columns] = dot_nt(hidden[...], wu[columns, :])

    for_columns(1024, 256, back_up)

    def store(index, values):
        gmixed[index, :] = values
        hidden[index, pl.ds(0, 1024)] = values.astype(BF16)

    norm_back_rows(mixed, gmixed, cot, gain, sums, store)

    def back_out(columns):
        gatt[:, columns] = dot_nt(hidden[:, pl.ds(0, 1024)], wo[columns, :])

    for_columns(1024, TILE, back_out)
    down.finish((down_a, down_b, down_c))
    swap.drain(range(8, 12), land.at[0])
    down.drain()


def slab_shapes(widths):
    return [pltpu.VMEM((4, 4, 4, 8, width), F32) for width in widths]


def flat_scratch(by_phase):
    return [item for at in sorted(by_phase) for stream in by_phase[at] for item in stream]


def nest(flat, phases, streams=3):
    nested = {}
    for at in phases:
        nested[at] = [[flat.pop(0) for _ in range(4)] for _ in range(streams)]
    return nested


def struct(shape, dtype=F32):
    return jax.ShapeDtypeStruct(shape, dtype)


VMEM_SPEC = pl.BlockSpec(memory_space=pltpu.VMEM)
ANY_SPEC = pl.BlockSpec(memory_space=pl.ANY)


def call(kernel, outs, operands, in_specs, scratch, collective_id):
    return pl.pallas_call(
        kernel,
        out_shape=outs,
        in_specs=in_specs,
        out_specs=[VMEM_SPEC] * len(outs),
        scratch_shapes=scratch,
        compiler_params=pltpu.CompilerParams(
            collective_id=collective_id, has_side_effects=True, vmem_limit_bytes=63 * MIB
        ),
    )(*operands)


def feed_forward(x, att_low, gain, shift, cot, w_out, w_up, w_down):
    rows, width = x.shape
    wide = w_up.shape[1]
    outs = [
        struct((rows, width), BF16),
        struct((rows, width)),
        struct((rows, width)),
        struct((8, width)),
        struct((2 * rows, width), BF16),
        struct((2 * rows, wide // 2), BF16),
        *[struct((4, 4, 8, length)) for length in DOWN_WIDTHS],
    ]
    scratch = [
        pltpu.VMEM((width, width), BF16),
        pltpu.VMEM((width, wide), BF16),
        pltpu.VMEM((wide, width), BF16),
        pltpu.SemaphoreType.DMA((4,)),
        pltpu.VMEM((rows, wide), BF16),
        pltpu.VMEM((rows, wide), BF16),
        pltpu.VMEM((2 * rows, width), BF16),
        pltpu.VMEM((4, rows, TILE), F32),
        pltpu.VMEM((4, rows, TILE), F32),
        pltpu.VMEM((2, rows, TILE), F32),
        pltpu.VMEM((2, rows, TILE), F32),
        *slab_shapes(DOWN_WIDTHS),
        pltpu.SemaphoreType.DMA((12,)),
        pltpu.SemaphoreType.DMA((12,)),
        pltpu.SemaphoreType.REGULAR,
        *flat_scratch(sum_scratch(DOWN_WIDTHS, 0, 0)),
    ]
    specs = [VMEM_SPEC] * 4 + [ANY_SPEC] * 4
    operands = (x, att_low, gain, shift, cot, w_out, w_up, w_down)
    return call(feed_forward_kernel, outs, operands, specs, scratch, 1)


UP_WIDTHS = shared_widths(2048)
OUT_WIDTHS = shared_widths(512)
QKV_WIDTHS = shared_widths(1536)


def attention_backward_kernel(
    block, qkv, att, den, state, gatt, gmixed, normed, norm_cat, pre_cat, down_in_a, down_in_b, down_in_c,
    gqkv, norm_one_cat, gqkv_cat, grad_down, up_a, up_b, up_c, out_a, out_b, out_c,
    grads, terms, landed, sums, result, s0, s1, s2, s3,
    att_cat, mixed_cat, stage, land_att, land_mixed, land_norm, land_gqkv, swap_sent, swap_came,
    slab_a, slab_b, slab_c, down_a, down_b, down_c, *scratch,
):
    place = Place()
    core = place.core
    rows = gatt.shape[0]
    scratch = list(scratch)
    scan = Scan(terms, landed, sums, result, (s0, s1, s2, s3), True)
    others = link_neighbours(place) + scan.others()
    greet(others)
    down_work = (down_a, down_b, down_c)
    for source, target in zip((down_in_a, down_in_b, down_in_c), down_work):
        add_into(target, source)
    down = Sum(place, down_work, nest(scratch, (1, 2)), 1, 2)
    slabs = (slab_a, slab_b, slab_c)
    up = Sum(place, slabs, nest(scratch, (0,)), 0, 0)
    swap = Swap(place, stage, swap_sent, swap_came)
    met(len(others))
    down.begin()
    own, other = pl.ds(0, rows), pl.ds(rows, rows)
    att_cat[own, :] = att[...].astype(BF16)
    norm_one_cat[own, :] = normed[...]
    for tile in range(2):
        columns = pl.ds(tile * TILE, TILE)
        swap.put(tile, tile, att_cat[own, columns], land_att.at[tile])
        swap.put(2 + tile, 2 + tile, normed[:, columns], land_norm.at[tile])
    shared_product(norm_cat, pre_cat, slabs, 2048)
    up.begin()
    mixed_cat[own, :] = gmixed[:, half_tile(0, core)].astype(BF16)
    swap.put(4, 0, gmixed[:, half_tile(0, 1 - core)].astype(BF16), land_mixed, before=0)
    first, second = head_masks()
    first_wide = first_head(block)

    def slopes(index, columns):
        numer = gatt[index, columns] / den[index, columns]
        product = numer * att[index, columns]
        ours = jnp.sum(jnp.where(first_wide, product, 0.0), axis=1, keepdims=True)
        theirs = jnp.sum(jnp.where(first_wide, 0.0, product), axis=1, keepdims=True)
        return numer, -ours, -theirs

    def local_state(unit):
        index, columns = unit_slices(unit, block)
        numer, one, two = slopes(index, columns)
        query = features(qkv[0, index, columns].astype(F32))
        high, low = split(numer)
        wide = tn_dot(query, jnp.concatenate([high, low], axis=1))
        spread = jnp.where(first_wide, one, two)
        total = jnp.sum(query.astype(F32) * spread, axis=0, keepdims=True)
        blocks, row = pack_state(wide[:, :PAIR] + wide[:, PAIR:], total)
        terms[unit, pl.ds(0, 64)] = blocks
        terms[unit, pl.ds(64, 8)] = row

    for_units(local_state, 2)
    scan.start()
    down.forward()
    causal = causal_mask(block)
    causal_t = causal_mask(block, True)

    def local_part(unit):
        index, columns = unit_slices(unit, block)
        raw_query = qkv[0, index, columns].astype(F32)
        query, value = features(raw_query), qkv[2, index, columns]
        key = features(qkv[1, index, columns].astype(F32))
        numer, one, two = slopes(index, columns)
        high, low = split(numer)
        scores = dot_nt(jnp.concatenate([key * first, key * second], axis=0), query)
        wide = jnp.concatenate([high, low], axis=1)
        values = jnp.concatenate([value, value], axis=1)
        grad_query, grad_key, grad_value = 0.0, 0.0, 0.0
        for head, (mask, slope) in enumerate(((first, one), (second, two))):
            mask_wide = jnp.concatenate([mask, mask], axis=1)
            mixing = jnp.where(causal, dot_nt(wide * mask_wide, values) + slope, 0.0).astype(BF16)
            turned = jnp.where(causal_t, scores[head * block : (head + 1) * block], 0.0)
            grad_query = grad_query + dot_nn(mixing, key * mask)
            grad_key = grad_key + tn_dot(mixing, query * mask)
            grad_value = grad_value + dot_nn(turned.astype(BF16), high * mask)
        square, total = unpack_state(state[unit])
        state_high, state_low = split(square)
        grad_query = grad_query + dot_nn(
            jnp.concatenate([high, low], axis=1),
            jnp.concatenate([state_high, state_high], axis=0),
        )
        grad_query = grad_query + dot_nn(high, state_low)
        grad_query = grad_query + jnp.where(first_wide, one, two) * total
        gqkv[0, index, columns] = (grad_query * feature_slope(raw_query)).astype(BF16)
        grads[0, index, columns] = grad_key
        grads[1, index, columns] = grad_value

    def local_parts(start, count):
        def one(index, carry):
            local_part(start + index)
            return carry

        lax.fori_loop(0, count, one, 0)

    local_parts(0, 4)
    down.finish()
    local_parts(4, 3)
    down.forward()
    scan.middle()
    local_parts(7, 4)
    down.finish()
    up.forward()
    for stream in range(3):
        piece = down.pieces[stream]
        grad_down[pl.ds(8 * stream, 8), :] = piece[:, pl.ds(0, 1024)]
        start, width = DOWN_CUTS[stream]
        grad_down[pl.ds(24, 8), pl.ds(start, width)] = piece[:, pl.ds(1024, width)]
    local_parts(11, 5)
    for tile in range(2):
        columns = pl.ds(tile * TILE, TILE)
        att_cat[other, columns] = swap.get(tile, land_att.at[tile])
        norm_one_cat[other, columns] = swap.get(2 + tile, land_norm.at[tile])
    mixed_cat[other, :] = swap.get(4, land_mixed)
    shared_product(att_cat, mixed_cat, (out_a, out_b, out_c), 512)
    scan.finish()

    def incoming(unit):
        index, columns = unit_slices(unit, block)
        square, total = unpack_state(result[unit])
        high, low = split(square)
        raw_key = qkv[1, index, columns].astype(F32)
        key, value = features(raw_key), qkv[2, index, columns]
        grad_key = grads[0, index, columns] + total
        grad_key = grad_key + dot_nt(
            jnp.concatenate([value, value], axis=1), jnp.concatenate([high, low], axis=1)
        )
        grad_value = grads[1, index, columns] + dot_nn(
            jnp.concatenate([key, key], axis=1), jnp.concatenate([high, low], axis=0)
        )
        gqkv[1, index, columns] = (grad_key * feature_slope(raw_key)).astype(BF16)
        gqkv[2, index, columns] = grad_value.astype(BF16)

    for_units(incoming, 2)
    before = (1, 2, 3)
    for third in range(3):
        theirs = gqkv[third, :, half_tile(0, 1 - core)]
        swap.put(5 + third, 1 + third, theirs, land_gqkv.at[third], before=before[third])
    for third in range(3):
        columns = pl.ds(third * TILE, TILE)
        gqkv_cat[own, columns] = gqkv[third, :, half_tile(0, core)]
        gqkv_cat[other, columns] = swap.get(5 + third, land_gqkv.at[third])
    up.finish((up_a, up_b, up_c))
    swap.copy(4, 0, land_mixed).wait_send()
    for third in range(3):
        swap.copy(5 + third, 1 + third, land_gqkv.at[third]).wait_send()
    scan.drain()
    up.drain()
    down.drain()


def attention_backward(qkv, att, den, state, gatt, gmixed, normed, norm_cat, pre_cat, down, block):
    _, rows, width = qkv.shape

    def kernel(*refs):
        attention_backward_kernel(block, *refs)

    outs = [
        struct((3, rows, width), BF16),
        struct((2 * rows, width), BF16),
        struct((2 * rows, 3 * TILE), BF16),
        struct((32, width)),
        *[struct((4, 4, 8, length)) for length in UP_WIDTHS],
        *[struct((4, 4, 4, 8, length)) for length in OUT_WIDTHS],
    ]
    scratch = [
        pltpu.VMEM((2, rows, width), F32),
        SCAN_SCRATCH[0],
        *SCAN_SCRATCH,
        pltpu.VMEM((2 * rows, width), BF16),
        pltpu.VMEM((2 * rows, TILE), BF16),
        pltpu.VMEM((4, rows, TILE), F32),
        pltpu.VMEM((2, rows, TILE), F32),
        pltpu.VMEM((rows, TILE), F32),
        pltpu.VMEM((2, rows, TILE), F32),
        pltpu.VMEM((3, rows, TILE), F32),
        pltpu.SemaphoreType.DMA((8,)),
        pltpu.SemaphoreType.DMA((8,)),
        *slab_shapes(UP_WIDTHS),
        *[pltpu.VMEM((4, 4, 8, length), F32) for length in DOWN_WIDTHS],
        *flat_scratch(sum_scratch(DOWN_WIDTHS, 1, 2)),
        *flat_scratch(sum_scratch(UP_WIDTHS, 0, 0)),
    ]
    operands = (qkv, att, den, state, gatt, gmixed, normed, norm_cat, pre_cat, *down)
    return call(kernel, outs, operands, [VMEM_SPEC] * len(operands), scratch, 2)


def last_kernel(
    x, gain, norm_one_cat, gqkv, gqkv_cat, gmixed, sums_two, weight,
    up_in_a, up_in_b, up_in_c, out_in_a, out_in_b, out_in_c,
    grad_input, grad_up, grad_out, grad_qkv, grad_gains,
    w, wsem, sums, up_rows, up_land, out_rows, out_land, qkv_rows, qkv_land, row_sems,
    vec_slab, vec_land, vec_sems,
    up_a, up_b, up_c, out_a, out_b, out_c, qkv_a, qkv_b, qkv_c, *scratch,
):
    place = Place()
    scratch = list(scratch)
    others = link_neighbours(place)
    greet(others)
    load = pltpu.make_async_copy(weight, w, wsem.at[0])
    load.start()
    up_work, out_work, qkv_work = (up_a, up_b, up_c), (out_a, out_b, out_c), (qkv_a, qkv_b, qkv_c)
    for source, target in zip((up_in_a, up_in_b, up_in_c), up_work):
        add_into(target, source)
    for source, target in zip((out_in_a, out_in_b, out_in_c), out_work):
        for index in range(4):
            add_into(target.at[index], source.at[index])
    up = Sum(place, up_work, nest(scratch, (1, 2)), 1, 2)
    out = Sum(place, out_work, nest(scratch, (0, 1, 2)))
    qkv = Sum(place, qkv_work, nest(scratch, (0, 1, 2)))
    vec = Sum(place, (vec_slab,), nest(scratch, (0, 1, 2), 1))
    met(len(others))
    up.begin()
    out.begin()
    shared_product(norm_one_cat, gqkv_cat, qkv_work, 3 * TILE)
    qkv.begin()
    load.wait()

    def back_norm(columns):
        total = 0.0
        for third in range(3):
            total = total + dot_nt(gqkv[third], w[columns, pl.ds(third * 1024, 1024)])
        grad_input[:, columns] = total

    for_columns(1024, 256, back_norm)
    up.forward()

    def store(index, values):
        grad_input[index, :] = values

    norm_back_rows(x, grad_input, gmixed, gain, sums, store)
    row = lax.broadcasted_iota(jnp.int32, (8, 1), 0)
    four = jnp.concatenate([sums[0:2, :], sums_two[0:2, :]], axis=0)
    eight = jnp.concatenate([four, four], axis=0)
    turned = jnp.transpose(jnp.concatenate([eight, jnp.zeros((120, 1024), F32)], axis=0))
    turned = turned.reshape(4, 2, 4, 4, 8, 128)
    lane = lax.broadcasted_iota(jnp.int32, (8, 128), 1)
    vec_slab[...] = jnp.where(lane < 4, turned[:, 0], jnp.where(lane < 8, turned[:, 1], 0.0))
    vec.begin()
    up.finish()
    out.forward()
    vec.forward()
    up.forward()
    out.finish()
    vec.finish()
    out.forward()
    up.finish()
    vec.forward()
    qkv.forward()
    out.finish()
    vec.finish()
    out.forward()
    vec.forward()
    out.finish()
    vec.finish()
    swaps = []

    def swap_rows(pieces, columns, rows, land, slot):
        shared_rows(pieces, columns, rows)
        copy = row_swap(place, rows, land, row_sems.at[slot])
        copy.start()
        swaps.append(copy)

    swap_rows(up.pieces, 2048, up_rows, up_land, 0)
    swap_rows(out.pieces, 512, out_rows, out_land, 1)
    vec_tile = vec.pieces[0]
    vec_copy = pltpu.make_async_remote_copy(
        src_ref=vec_tile,
        dst_ref=vec_land,
        send_sem=vec_sems.at[0],
        recv_sem=vec_sems.at[1],
        device_id=place.partner(),
        device_id_type=MESH,
    )
    vec_copy.start()
    swaps[0].wait()
    lay_rows(place, up_rows, up_land, grad_up)
    swaps[1].wait()
    lay_rows(place, out_rows, out_land, grad_out)
    vec_copy.wait()
    grad_gains[...] = vec_tile[...] + vec_land[...]
    qkv.finish()
    qkv.forward()
    qkv.finish()
    qkv.forward()
    qkv.finish()
    swap_rows(qkv.pieces, 3 * TILE, qkv_rows, qkv_land, 2)
    swaps[2].wait()
    lay_rows(place, qkv_rows, qkv_land, grad_qkv)
    for each in (up, out, qkv, vec):
        each.drain()


def last_part(x, gain, norm_one_cat, gqkv, gqkv_cat, gmixed, sums_two, weight, up, out):
    rows, width = x.shape
    outs = [
        struct((rows, width)),
        struct((8, 4096)),
        struct((8, width)),
        struct((8, 3 * width)),
        struct((8, 128)),
    ]
    scratch = [
        pltpu.VMEM((width, 3 * width), BF16),
        pltpu.SemaphoreType.DMA((1,)),
        pltpu.VMEM((8, width), F32),
        pltpu.VMEM((2, 8, 2048), F32),
        pltpu.VMEM((8, 2048), F32),
        pltpu.VMEM((2, 8, 512), F32),
        pltpu.VMEM((8, 512), F32),
        pltpu.VMEM((2, 8, 1536), F32),
        pltpu.VMEM((8, 1536), F32),
        pltpu.SemaphoreType.DMA((3, 2)),
        pltpu.VMEM((4, 4, 4, 8, 128), F32),
        pltpu.VMEM((8, 128), F32),
        pltpu.SemaphoreType.DMA((2,)),
        *[pltpu.VMEM((4, 4, 8, length), F32) for length in UP_WIDTHS],
        *slab_shapes(OUT_WIDTHS),
        *slab_shapes(QKV_WIDTHS),
        *flat_scratch(sum_scratch(UP_WIDTHS, 1, 2)),
        *flat_scratch(sum_scratch(OUT_WIDTHS)),
        *flat_scratch(sum_scratch(QKV_WIDTHS)),
        *flat_scratch(sum_scratch((128,))),
    ]
    operands = (x, gain, norm_one_cat, gqkv, gqkv_cat, gmixed, sums_two, weight, *up, *out)
    specs = [VMEM_SPEC] * len(operands)
    specs[7] = ANY_SPEC
    return call(last_kernel, outs, operands, specs, scratch, 3)


def body(
    inputs,
    first_gain,
    first_shift,
    qkv_weight,
    out_weight,
    second_gain,
    second_shift,
    up_weight,
    down_weight,
    cotangent,
):
    sequences, block, width = inputs.shape
    rows = sequences * block
    x = inputs.reshape(rows, width)
    cot = cotangent.reshape(rows, width)
    gain_one, gain_two = first_gain.reshape(1, width), second_gain.reshape(1, width)
    shift_two = second_shift.reshape(1, width)
    normed, qkv, att, att_low, den, state = attention_forward(
        x, first_gain, first_shift, qkv_weight, block
    )
    output, gmixed, gatt, sums_two, norm_cat, pre_cat, *down = feed_forward(
        x, att_low, gain_two, shift_two, cot, out_weight, up_weight, down_weight
    )
    gqkv, norm_one_cat, gqkv_cat, grad_down, *rest = attention_backward(
        qkv, att, den, state, gatt, gmixed, normed, norm_cat, pre_cat, down, block
    )
    grad_input, grad_up, grad_out, grad_qkv, gains = last_part(
        x, gain_one, norm_one_cat, gqkv, gqkv_cat, gmixed, sums_two, qkv_weight, rest[:3], rest[3:]
    )
    core = lax.rem(lax.axis_index("dp"), 2)
    gains = lax.dynamic_slice(gains, (0, 4 * core), (8, 4))
    return (
        output.reshape(inputs.shape),
        grad_input.reshape(inputs.shape),
        grad_qkv,
        grad_out,
        grad_up,
        grad_down,
        *[gains[:, k] for k in range(4)],
    )


def solution(mesh):
    return jax.shard_map(
        body,
        mesh=mesh,
        in_specs=(
            P("dp", "seq", None),
            P(),
            P(),
            P(),
            P(),
            P(),
            P(),
            P(),
            P(),
            P("dp", "seq", None),
        ),
        out_specs=(
            P("dp", "seq", None),
            P("dp", "seq", None),
            P(("dp", "seq"), None),
            P(("dp", "seq"), None),
            P(("dp", "seq"), None),
            P(("dp", "seq"), None),
            P(("dp", "seq")),
            P(("dp", "seq")),
            P(("dp", "seq")),
            P(("dp", "seq")),
        ),
        check_vma=False,
    )
```

```python
import math

import jax
import jax.numpy as jnp
from jax import lax
from jax.experimental import pallas as pl
from jax.experimental.pallas import tpu as pltpu
from jax.sharding import PartitionSpec as P

MESH = pl.DeviceIdType.MESH
F32 = jnp.float32
BF16 = jnp.bfloat16
RING = 4
MIB = 2**20


class Place:
    def __init__(self):
        dp, seq = lax.axis_index("dp"), lax.axis_index("seq")
        self.core = lax.rem(dp, 2)
        self.at = (lax.div(dp, 2), lax.div(seq, RING), lax.rem(seq, RING))

    def id_of(self, x, y, z, core):
        return (x * 2 + core, y * RING + z)

    def ring(self, axis, step):
        return lax.rem(self.at[axis] + (step + RING), RING)

    def neighbour(self, axis, step):
        at = list(self.at)
        at[axis] = self.ring(axis, step)
        return self.id_of(*at, self.core)

    def partner(self):
        return self.id_of(*self.at, 1 - self.core)


def greet(others):
    barrier = pltpu.get_barrier_semaphore()
    for other in others:
        pl.semaphore_signal(barrier, inc=1, device_id=other, device_id_type=MESH)


def met(count):
    pl.semaphore_wait(pltpu.get_barrier_semaphore(), count)


def link_neighbours(place):
    others = [place.neighbour(axis, step) for axis in range(3) for step in (1, -1)]
    return [*others, place.partner()]


ORDERS = ((0, 1, 2), (1, 2, 0), (2, 0, 1))


def phase_scratch(remaining, length):
    if remaining:
        half = (2, 2, *[4] * (remaining - 1), 8, length)
    else:
        half = (2, 8, (length // 128 + 1) // 2 * 128)
    return [
        pltpu.VMEM((2, *[4] * remaining, 8, length), F32),
        pltpu.VMEM(half, F32),
        pltpu.SemaphoreType.DMA((6,)),
        pltpu.SemaphoreType.DMA((6,)),
    ]


class Phase:
    def __init__(self, place, data, axes, axis, scratch):
        self.place, self.data, self.axis = place, data, axis
        self.where = axes.index(axis)
        self.full, self.half, self.sent, self.came = scratch
        self.flying = []
        self.flat = len(axes) == 1
        self.length = data.shape[-1]
        self.cut = (self.length // 128 + 1) // 2 * 128
        self.whole = self.flat and self.cut == self.length

    def empty(self, which):
        return self.whole and which == 1

    def chunk(self, target):
        index = [slice(None)] * self.where + [target]
        return self.data.at[tuple(index)]

    def part(self, ref, which):
        if not self.flat:
            return ref.at[pl.ds(2 * which, 2)]
        if which == 0:
            return ref.at[:, pl.ds(0, self.cut)]
        return ref.at[:, pl.ds(self.cut, self.length - self.cut)]

    def through(self, way):
        ref = self.half.at[way]
        if self.flat and way == 1:
            return ref.at[:, pl.ds(0, self.length - self.cut)]
        return ref

    def copy(self, kind, way, source, target):
        number = kind * 2 + way
        return pltpu.make_async_remote_copy(
            src_ref=source,
            dst_ref=target,
            send_sem=self.sent.at[number],
            recv_sem=self.came.at[number],
            device_id=self.place.neighbour(self.axis, 1 - 2 * way),
            device_id_type=MESH,
        )

    def send(self, kind, way, source, target):
        copy = self.copy(kind, way, source, target)
        copy.start()
        self.flying.append(copy)

    def beside(self, way):
        return self.chunk(self.place.ring(self.axis, 1 - 2 * way))

    def begin_far(self):
        opposite = self.chunk(self.place.ring(self.axis, 2))
        for way in range(2):
            if not self.empty(way):
                self.send(0, way, self.part(opposite, way), self.through(way))

    def begin_near(self):
        for way in range(2):
            if self.empty(1 - way):
                continue
            target = self.part(self.full.at[way], 1 - way)
            self.send(1, way, self.part(self.beside(way), 1 - way), target)

    def begin(self):
        self.begin_far()
        self.begin_near()

    def forward(self):
        for way in range(2):
            if self.empty(way):
                continue
            came = self.through(way)
            self.copy(0, way, came, came).wait_recv()
            own = self.part(self.beside(way), way)
            add_into(own, own, came)
            self.send(2, way, own, self.part(self.full.at[way], way))

    def finish(self, out=None):
        own = self.chunk(self.place.at[self.axis])
        for way in range(2):
            for kind, which in ((1, 1 - way), (2, way)):
                if self.empty(which):
                    continue
                target = self.part(self.full.at[way], which)
                self.copy(kind, way, target, target).wait_recv()
        add_into(own if out is None else out, own, self.full.at[0], self.full.at[1])
        return own

    def drain(self):
        for copy in self.flying:
            copy.wait_send()


class Direct:
    def __init__(self, place, data, axes, axis, scratch):
        self.place, self.data, self.axis = place, data, axis
        self.where = axes.index(axis)
        self.full, self.sent, self.came = scratch
        self.flying = []

    def chunk(self, target):
        index = [slice(None)] * self.where + [target]
        return self.data.at[tuple(index)]

    def copy(self, step, source):
        return pltpu.make_async_remote_copy(
            src_ref=source,
            dst_ref=self.full.at[step - 1],
            send_sem=self.sent.at[step - 1],
            recv_sem=self.came.at[step - 1],
            device_id=self.place.neighbour(self.axis, step),
            device_id_type=MESH,
        )

    def begin(self):
        for step in (2, 1, 3):
            copy = self.copy(step, self.chunk(self.place.ring(self.axis, step)))
            copy.start()
            self.flying.append(copy)

    def forward(self):
        pass

    def finish(self, out=None):
        own = self.chunk(self.place.at[self.axis])
        for step in (1, 2, 3):
            self.copy(step, self.full.at[step - 1]).wait_recv()
        add_into(own if out is None else out, own, *[self.full.at[k] for k in range(3)])
        return own

    def drain(self):
        for copy in self.flying:
            copy.wait_send()


class Stream:
    def __init__(self, place, data, order, scratch):
        self.place, self.data, self.scratch = place, data, scratch
        self.todo, self.old = [axis for axis in order], []
        self.axes = sorted(order)
        self.phase = None

    def prepare(self):
        scratch = self.scratch.pop(0)
        kind = Phase if len(scratch) == 4 else Direct
        self.phase = kind(self.place, self.data, self.axes, self.todo[0], scratch)
        return self.phase

    def begin(self):
        self.prepare().begin()

    def forward(self):
        self.phase.forward()

    def finish(self, out=None):
        own = self.phase.finish(out)
        self.data = own if out is None else out
        self.axes.remove(self.todo.pop(0))
        self.old.append(self.phase)

    def proceed(self):
        self.finish()
        self.begin()

    def drain(self):
        for phase in self.old:
            phase.drain()
        self.old = []


def direct_scratch(remaining, length):
    return [
        pltpu.VMEM((3, *[4] * remaining, 8, length), F32),
        pltpu.SemaphoreType.DMA((3,)),
        pltpu.SemaphoreType.DMA((3,)),
    ]


def stream_scratch(length, phases, direct=()):
    return [
        (direct_scratch if phase in direct else phase_scratch)(2 - phase, length)
        for phase in phases
    ]


class Taker:
    def __init__(self, refs):
        self.refs = list(refs)

    def __call__(self, like):
        if isinstance(like, list):
            return [self(item) for item in like]
        return self.refs.pop(0)


def flatten(items):
    if isinstance(items, list):
        return [leaf for item in items for leaf in flatten(item)]
    return [items]


def add_into(out, *terms):
    if len(out.shape) > 2:

        def row(index, carry):
            add_into(out.at[index], *[term.at[index] for term in terms])
            return carry

        if len(out.shape) == 4:
            lax.fori_loop(0, out.shape[0], row, 0)
        else:
            for index in range(out.shape[0]):
                row(index, 0)
        return
    total = terms[0][...]
    for term in terms[1:]:
        total = total + term[...]
    out[...] = total


def tn_dot(left, right):
    return lax.dot_general(left, right, (((0,), (0,)), ((), ())), preferred_element_type=F32)


TILE = 512


class Swap:
    def __init__(self, place, stage, sent, came):
        self.place, self.stage, self.sent, self.came = place, stage, sent, came

    def copy(self, number, slot, target):
        return pltpu.make_async_remote_copy(
            src_ref=self.stage.at[slot],
            dst_ref=target,
            send_sem=self.sent.at[number],
            recv_sem=self.came.at[number],
            device_id=self.place.partner(),
            device_id_type=MESH,
        )

    def put(self, number, slot, values, target, before=None):
        if before is not None:
            self.copy(before, slot, target).wait_send()
        self.stage[slot] = values.astype(F32)
        self.copy(number, slot, target).start()

    def get(self, number, target):
        self.copy(number, 0, target).wait_recv()
        return target[...].astype(BF16)

    def drain(self, numbers, target):
        for number in numbers:
            self.copy(number, number % 4, target).wait_send()


def half_columns(block, core, quarter):
    half = quarter // 2
    return pl.ds(pl.multiple_of(block * quarter + core * half, half), half)


def half_tile(index, core):
    return pl.ds(pl.multiple_of((2 * index + core) * TILE, TILE), TILE)


def core_product(left, core, right, start, width, slab, at):
    done = 0
    while done < width:
        step = min(TILE, width - done)
        product = tn_dot(left[core], right[:, pl.ds(start + done, step)])
        slab[:, :, :, :, pl.ds(at + done, step)] = product.reshape(4, 4, 4, 8, step)
        done += step


UP_WIDTHS = (1536, 1280, 1280)
OUT_WIDTHS = (512, 256, 256)
QKV_WIDTHS = (1152, 896, 1024)


def stream_pieces(stream, widths, columns):
    if stream < 2:
        return [(stream, 0, widths[stream], 0)]
    pieces, at = [], 0
    for core in range(2):
        width = columns - widths[core]
        if width:
            pieces.append((core, widths[core], width, at))
        at += width
    return pieces


def stream_product(stream, left, right, slab, widths, columns):
    for core, start, width, at in stream_pieces(stream, widths, columns):
        core_product(left, core, right, start, width, slab, at)


def shared_rows(streams, widths, columns, rows):
    for stream in range(3):
        for core, start, width, at in stream_pieces(stream, widths, columns):
            rows[core, :, pl.ds(start, width)] = streams[stream].data[:, pl.ds(at, width)]


def row_swap(place, rows, land, sems):
    return pltpu.make_async_remote_copy(
        src_ref=rows.at[1 - place.core],
        dst_ref=land,
        send_sem=sems.at[0],
        recv_sem=sems.at[1],
        device_id=place.partner(),
        device_id_type=MESH,
    )


def lay_rows(place, rows, land, out):
    for tile in range(land.shape[1] // TILE):
        columns = pl.ds(tile * TILE, TILE)
        out[:, half_tile(tile, place.core)] = rows[place.core, :, columns]
        out[:, half_tile(tile, 1 - place.core)] = land[:, columns]


DOWN_CUTS = ((0, 384), (384, 384), (768, 256))
DOWN_WIDTHS = (1408, 1408, 1280)


SEQ = 16
PAIR = 128
NT = (((1,), (1,)), ((), ()))
TN = (((0,), (0,)), ((), ()))


def dot_nt(left, right):
    return lax.dot_general(left, right, NT, preferred_element_type=F32)


def dot_nn(left, right):
    return jnp.dot(left, right, preferred_element_type=F32)


def split(values):
    high = values.astype(BF16)
    return high, (values - high.astype(F32)).astype(BF16)


def features(raw):
    return jnp.where(raw > 0, raw + 1.0, jnp.exp(jnp.minimum(raw, 0.0))).astype(BF16)


def feature_slope(raw):
    return jnp.where(raw > 0, 1.0, jnp.exp(jnp.minimum(raw, 0.0)))


def head_masks():
    lane = lax.broadcasted_iota(jnp.int32, (1, PAIR), 1)
    first = jnp.where(lane < 64, 1.0, 0.0)
    return first.astype(BF16), (1.0 - first).astype(BF16)


def first_head(rows):
    return lax.broadcasted_iota(jnp.int32, (rows, PAIR), 1) < 64


def pack_state(square, total):
    blocks = jnp.where(first_head(64), square[:64], square[64:])
    return blocks, jnp.broadcast_to(total, (8, PAIR))


def unpack_state(packed):
    first = first_head(64)
    square = jnp.concatenate(
        [jnp.where(first, packed[:64], 0.0), jnp.where(first, 0.0, packed[:64])], axis=0
    )
    return square, packed[64:65]


def same_head():
    row = lax.broadcasted_iota(jnp.int32, (PAIR, PAIR), 0)
    lane = lax.broadcasted_iota(jnp.int32, (PAIR, PAIR), 1)
    return (row < 64) == (lane < 64)


class Scan:
    def __init__(self, terms, landed, sums, result, sems, reverse):
        self.terms, self.landed, self.sums, self.result = terms, landed, sums, result
        self.sems, self.reverse = sems, reverse
        self.dp, self.me = lax.axis_index("dp"), lax.axis_index("seq")

    def others(self):
        return [(self.dp, lax.rem(self.me + step, SEQ)) for step in range(1, SEQ)]

    def send_all(self, source, target, sent, came):
        def one(step, carry):
            other = lax.rem(self.me + step, SEQ)
            pltpu.make_async_remote_copy(
                src_ref=source.at[other],
                dst_ref=target.at[self.me],
                send_sem=sent.at[step],
                recv_sem=came.at[step],
                device_id=(self.dp, other),
                device_id_type=MESH,
            ).start()
            return carry

        lax.fori_loop(1, SEQ, one, 0)
        target[self.me] = source[self.me]

    def wait_all(self, source, target, sent, came):
        def one(step, carry):
            other = lax.rem(self.me + (SEQ - step), SEQ)
            pltpu.make_async_remote_copy(
                src_ref=source.at[other],
                dst_ref=target.at[other],
                send_sem=sent.at[step],
                recv_sem=came.at[step],
                device_id=(self.dp, other),
                device_id_type=MESH,
            ).wait_recv()
            return carry

        lax.fori_loop(1, SEQ, one, 0)

    def wait_sent(self, source, target, sent, came):
        def one(step, carry):
            other = lax.rem(self.me + step, SEQ)
            pltpu.make_async_remote_copy(
                src_ref=source.at[other],
                dst_ref=target.at[self.me],
                send_sem=sent.at[step],
                recv_sem=came.at[step],
                device_id=(self.dp, other),
                device_id_type=MESH,
            ).wait_send()
            return carry

        lax.fori_loop(1, SEQ, one, 0)

    def start(self):
        self.send_all(self.terms, self.landed, self.sems[0], self.sems[1])

    def middle(self):
        total = jnp.zeros(self.landed.shape[1:], F32)
        for k in range(SEQ):
            at = SEQ - 1 - k if self.reverse else k
            mine = self.me == at
            ahead = lax.rem(at - self.me + SEQ, SEQ)
            behind = lax.rem(self.me - at + SEQ, SEQ)
            self.sums[at] = total

            @pl.when(mine)
            def _():
                self.result[at] = self.sums[at]

            @pl.when(jnp.logical_not(mine))
            def _():
                pltpu.make_async_remote_copy(
                    src_ref=self.sums.at[at],
                    dst_ref=self.result.at[self.me],
                    send_sem=self.sems[2].at[ahead],
                    recv_sem=self.sems[3].at[ahead],
                    device_id=(self.dp, at),
                    device_id_type=MESH,
                ).start()
                pltpu.make_async_remote_copy(
                    src_ref=self.terms.at[at],
                    dst_ref=self.landed.at[at],
                    send_sem=self.sems[0].at[behind],
                    recv_sem=self.sems[1].at[behind],
                    device_id=(self.dp, at),
                    device_id_type=MESH,
                ).wait_recv()

            total = total + self.landed[at]

    def finish(self):
        self.wait_all(self.sums, self.result, self.sems[2], self.sems[3])

    def drain(self):
        self.wait_sent(self.terms, self.landed, self.sems[0], self.sems[1])
        self.wait_sent(self.sums, self.result, self.sems[2], self.sems[3])


SCAN_SCRATCH = [
    pltpu.VMEM((SEQ, 72, PAIR), F32),
    pltpu.VMEM((SEQ, 72, PAIR), F32),
    pltpu.VMEM((SEQ, 72, PAIR), F32),
    *[pltpu.SemaphoreType.DMA((SEQ,)) for _ in range(4)],
]


def unit_slices(unit, block):
    rows = pl.ds(pl.multiple_of(lax.div(unit, 8) * block, block), block)
    columns = pl.ds(pl.multiple_of(lax.rem(unit, 8) * PAIR, PAIR), PAIR)
    return rows, columns


def for_units(step, together):
    def several(index, carry):
        for offset in range(together):
            step(index * together + offset)
        return carry

    lax.fori_loop(0, SEQ // together, several, 0)


def causal_mask(block, transposed=False):
    row = lax.broadcasted_iota(jnp.int32, (block, block), 0)
    column = lax.broadcasted_iota(jnp.int32, (block, block), 1)
    return (row <= column) if transposed else (row >= column)


def norm_rows(values):
    center = jnp.mean(values, axis=-1, keepdims=True)
    centered = values - center
    variance = jnp.mean(centered * centered, axis=-1, keepdims=True)
    inverse = lax.rsqrt(variance + 1e-05)
    return centered * inverse, inverse


ROWS = 64


def for_rows(count, step):
    def one(index, carry):
        step(pl.ds(pl.multiple_of(index * ROWS, ROWS), ROWS))
        return carry

    lax.fori_loop(0, count // ROWS, one, 0)


def for_columns(count, width, step):
    def one(index, carry):
        step(pl.ds(pl.multiple_of(index * width, width), width))
        return carry

    lax.fori_loop(0, count // width, one, 0)


def attention_forward_kernel(
    block, x, gain, shift, weight, cot_in, cat_out, cot_out, qkv_out, att_out, att_low_out, den_out, state,
    w, cot, normed, qkv, att, att_low, den, cat, fq, fk, stage, land, terms, landed, sums, s0, s1, s2, s3,
    wsem, osem, swap_sent, swap_came,
):
    place = Place()
    rows_all = x.shape[0]
    own, other = pl.ds(0, rows_all), pl.ds(rows_all, rows_all)
    outs = []

    def leave(source, target):
        outs.append(pltpu.make_async_copy(source, target, osem.at[len(outs)]))
        outs[-1].start()

    scan = Scan(terms, landed, sums, state, (s0, s1, s2, s3), False)
    others = [*scan.others(), place.partner()]
    greet(others)
    loads = []
    cot_load = pltpu.make_async_copy(cot_in, cot.at[own], wsem.at[3])
    for slot, third in enumerate((1, 2, 0)):
        load = pltpu.make_async_copy(
            weight.at[:, pl.ds(third * 1024, 1024)], w.at[slot], wsem.at[slot]
        )
        load.start()
        loads.append(load)
    cot_load.start()

    def norm_step(rows):
        scaled, _ = norm_rows(x[rows, :].astype(F32))
        normed[rows, :] = (scaled * gain[...] + shift[...]).astype(BF16)

    for_rows(x.shape[0], norm_step)

    def project(slot, third, feature):
        loads[slot].wait()

        def step(columns):
            raw = dot_nn(normed[...], w[slot, :, columns]).astype(BF16)
            qkv[third, :, columns] = raw
            if feature is not None:
                feature[:, columns] = features(raw.astype(F32))

        for_columns(1024, 512, step)

    project(0, 1, fk)
    project(1, 2, None)

    def local_state(unit):
        rows, columns = unit_slices(unit, block)
        keys = fk[rows, columns]
        square = tn_dot(qkv[2, rows, columns], keys)
        total = jnp.sum(keys.astype(F32), axis=0, keepdims=True)
        blocks, row = pack_state(square, total)
        terms[unit, pl.ds(0, 64)] = blocks
        terms[unit, pl.ds(64, 8)] = row

    for_units(local_state, 4)
    met(len(others))
    scan.start()
    swap = Swap(place, stage, swap_sent, swap_came)
    for core in range(2):
        for block_x in range(4):
            columns = pl.ds(block_x * 256 + core * 128, 128)
            cat[core, own, pl.ds(block_x * 128, 128)] = normed[:, columns]
        swap.put(core, core, cat[core, own, :], land.at[core])
    cot_load.wait()
    for tile in range(2):
        swap.put(2 + tile, 2 + tile, cot[own, pl.ds(tile * TILE, TILE)], land.at[2 + tile])
    leave(qkv.at[pl.ds(1, 2)], qkv_out.at[pl.ds(1, 2)])
    project(2, 0, fq)
    leave(qkv.at[0], qkv_out.at[0])
    first, second = head_masks()
    causal = causal_mask(block)

    def local_part(unit):
        rows, columns = unit_slices(unit, block)
        query, key, value = fq[rows, columns], fk[rows, columns], qkv[2, rows, columns]
        scores = dot_nt(jnp.concatenate([query * first, query * second], axis=0), key)
        both = 0.0
        for head, mask in enumerate((first, second)):
            own = jnp.where(causal, scores[head * block : (head + 1) * block], 0.0).astype(BF16)
            right = jnp.concatenate([value * mask, jnp.broadcast_to(mask, value.shape)], axis=1)
            both = both + dot_nn(own, right)
        att[rows, columns] = both[:, :PAIR]
        den[rows, columns] = both[:, PAIR:]

    for_units(local_part, 2)
    for core in range(2):
        cat[core, other, :] = swap.get(core, land.at[core])
        cot[other, pl.ds(core * TILE, TILE)] = swap.get(2 + core, land.at[2 + core])
    leave(cat, cat_out)
    leave(cot, cot_out)
    scan.middle()
    scan.finish()
    together = same_head()

    def incoming(unit):
        rows, columns = unit_slices(unit, block)
        square, total = unpack_state(state[unit])
        totals = jnp.where(together, jnp.broadcast_to(total, (PAIR, PAIR)), 0.0)
        high, low = split(jnp.concatenate([square, totals], axis=0))
        query = fq[rows, columns]
        both = dot_nt(
            jnp.concatenate([query, query], axis=1), jnp.concatenate([high, low], axis=1)
        )
        denom = den[rows, columns] + both[:, PAIR:]
        den[rows, columns] = denom
        attended = (att[rows, columns] + both[:, :PAIR]) / denom
        att[rows, columns] = attended
        att_low[rows, columns] = attended.astype(BF16)

    for half in range(2):

        def several(index, carry):
            incoming(half * 8 + 2 * index)
            incoming(half * 8 + 2 * index + 1)
            return carry

        lax.fori_loop(0, 4, several, 0)
        part = pl.ds(half * block, block)
        leave(att.at[part], att_out.at[part])
        leave(den.at[part], den_out.at[part])
        leave(att_low.at[part], att_low_out.at[part])
    scan.drain()
    swap.drain(range(4), land.at[0])
    for copy in outs:
        copy.wait()


def attention_forward(x, gain, shift, weight, cot, block):
    rows, width = x.shape
    vmem = pl.BlockSpec(memory_space=pltpu.VMEM)

    def kernel(*refs):
        attention_forward_kernel(block, *refs)

    return pl.pallas_call(
        kernel,
        out_shape=[
            struct((2, 2 * rows, width // 2), BF16),
            struct((2 * rows, width), BF16),
            struct((3, rows, width), BF16),
            struct((rows, width)),
            struct((rows, width), BF16),
            struct((rows, width)),
            struct((SEQ, 72, PAIR)),
        ],
        in_specs=[vmem, vmem, vmem, ANY_SPEC, ANY_SPEC],
        out_specs=[ANY_SPEC] * 6 + [vmem],
        scratch_shapes=[
            pltpu.VMEM((3, width, width), BF16),
            pltpu.VMEM((2 * rows, width), BF16),
            pltpu.VMEM((rows, width), BF16),
            pltpu.VMEM((3, rows, width), BF16),
            pltpu.VMEM((rows, width), F32),
            pltpu.VMEM((rows, width), BF16),
            pltpu.VMEM((rows, width), F32),
            pltpu.VMEM((2, 2 * rows, width // 2), BF16),
            pltpu.VMEM((rows, width), BF16),
            pltpu.VMEM((rows, width), BF16),
            pltpu.VMEM((4, rows, TILE), F32),
            pltpu.VMEM((4, rows, TILE), F32),
            *SCAN_SCRATCH,
            pltpu.SemaphoreType.DMA((4,)),
            pltpu.SemaphoreType.DMA((10,)),
            pltpu.SemaphoreType.DMA((4,)),
            pltpu.SemaphoreType.DMA((4,)),
        ],
        compiler_params=pltpu.CompilerParams(
            collective_id=5, has_side_effects=True, vmem_limit_bytes=62 * MIB
        ),
    )(x, gain.reshape(1, width), shift.reshape(1, width), weight, cot)


def gelu_both(pre):
    cumulative = 0.5 * (1.0 + lax.erf(pre * (1.0 / math.sqrt(2.0))))
    density = jnp.exp(-0.5 * pre * pre) * (1.0 / math.sqrt(2.0 * math.pi))
    return (pre * cumulative).astype(BF16), (cumulative + pre * density).astype(BF16)


def norm_back(grad, gain, scaled, inverse):
    spread = grad * gain
    first_mean = jnp.mean(spread, axis=-1, keepdims=True)
    second_mean = jnp.mean(spread * scaled, axis=-1, keepdims=True)
    return inverse * (spread - first_mean - scaled * second_mean)


def norm_back_rows(values, grad, base, gain, sums, store):
    sums[...] = jnp.zeros_like(sums)

    def step(rows):
        scaled, inverse = norm_rows(values[rows, :].astype(F32))
        part = grad[rows, :]
        sums[0:1, :] += jnp.sum(part * scaled, axis=0, keepdims=True)
        sums[1:2, :] += jnp.sum(part, axis=0, keepdims=True)
        store(rows, base[rows, :].astype(F32) + norm_back(part, gain[...], scaled, inverse))

    for_rows(grad.shape[0], step)


def feed_forward_kernel(
    x, att_low, gain, shift, cot_in, w_out, w_up, w_down,
    output_out, gmixed_out, gatt_out, sums, norm_out, pre_out, out_out, down_a, down_b, down_c,
    wo, wu, wd, wsem, osem, output, gmixed, gatt, norm_cat, pre_cat, hidden, slope, cot_cat,
    stage, land, land_att, land_norm, swap_sent, swap_came, free, *scratch,
):
    take_scratch = Taker(scratch)
    slabs = take_scratch(slab_shapes(DOWN_WIDTHS))
    slab_a, slab_b, slab_c = slabs
    phases = take_scratch([stream_scratch(length, (0,)) for length in DOWN_WIDTHS])
    place = Place()
    core = place.core
    rows = x.shape[0]
    others = link_neighbours(place)
    greet(others)
    own, other = pl.ds(0, rows), pl.ds(rows, rows)
    mixed = gatt
    loads = []
    moves = ((w_out, wo), (w_up, wu), (w_down, wd), (cot_in, cot_cat))
    for slot in (0, 1, 3, 2):
        loads.append(pltpu.make_async_copy(*moves[slot], wsem.at[slot]))
        loads[-1].start()
    outs = []

    def leave(source, target):
        outs.append(pltpu.make_async_copy(source, target, osem.at[len(outs)]))
        outs[-1].start()

    cot = cot_cat.at[own]
    swap = Swap(place, stage, swap_sent, swap_came)
    loads[0].wait()

    def mix(columns):
        mixed[:, columns] = x[:, columns].astype(F32) + dot_nn(att_low[...], wo[:, columns])

    for_columns(1024, TILE, mix)

    def norm_step(index):
        scaled, _ = norm_rows(mixed[index, :])
        norm_cat[index, :] = (scaled * gain[...] + shift[...]).astype(BF16)

    for_rows(rows, norm_step)
    met(len(others))
    loads[1].wait()

    def up(columns):
        ours, ours_slope = gelu_both(dot_nn(norm_cat[own, :], wu[:, columns]))
        hidden[:, columns] = ours
        slope[:, columns] = ours_slope
        return ours

    def give(block, carry):
        theirs = up(half_columns(block, 1 - core, 1024))
        swap.put(block, block, theirs, land.at[block])
        return carry

    lax.fori_loop(0, 4, give, 0)
    loads[2].wait()

    def take(block, carry):
        ours = up(half_columns(block, core, 1024))
        both = jnp.concatenate([ours, swap.get(block, land.at[block])], axis=0)
        for half in range(2):
            columns = pl.ds(half * TILE, TILE)
            product = tn_dot(both, cot_cat[:, columns]).reshape(4, 4, 4, 8, TILE)
            for stream in range(3):
                slabs[stream][block, :, :, :, columns] = product[:, :, stream]
            last = product[:, :, 3]
            if half == 0:
                slab_a[block, :, :, :, pl.ds(1024, 384)] = last[..., :384]
                slab_b[block, :, :, :, pl.ds(1024, 128)] = last[..., 384:]
            else:
                slab_b[block, :, :, :, pl.ds(1152, 256)] = last[..., :256]
                slab_c[block, :, :, :, pl.ds(1024, 256)] = last[..., 256:]
        return carry

    lax.fori_loop(0, 4, take, 0)
    pl.semaphore_signal(free, inc=1, device_id=place.partner(), device_id_type=MESH)
    down = [Stream(place, slabs[k], ORDERS[k], phases[k]) for k in range(3)]
    for stream in down:
        stream.prepare().begin_far()
    for stream in down:
        stream.phase.begin_near()
    for tile in range(2):
        columns = pl.ds(tile * TILE, TILE)
        swap.put(4 + tile, tile, norm_cat[own, columns], land_norm.at[tile], before=tile)
    loads[3].wait()

    def finish_forward(columns):
        output[:, columns] = (mixed[:, columns] + dot_nn(hidden[...], wd[:, columns])).astype(BF16)

    for_columns(1024, 256, finish_forward)
    leave(output, output_out)

    def back(columns):
        grad = dot_nt(cot[...], wd[columns, :]) * slope[:, columns].astype(F32)
        low = grad.astype(BF16)
        hidden[:, columns] = low
        return low

    pl.semaphore_wait(free, 1)

    def give_back(block, carry):
        theirs = back(half_columns(block, 1 - core, 1024))
        before = jnp.where(block < 2, 4 + block, block)
        swap.put(6 + block, block, theirs, land.at[block], before=before)
        return carry

    lax.fori_loop(0, 4, give_back, 0)

    def take_back(block, carry):
        columns = pl.ds(pl.multiple_of(block * TILE, TILE), TILE)
        pre_cat[own, columns] = back(half_columns(block, core, 1024))
        pre_cat[other, columns] = swap.get(6 + block, land.at[block])
        return carry

    lax.fori_loop(0, 4, take_back, 0)
    leave(pre_cat, pre_out)
    for tile in range(2):
        columns = pl.ds(tile * TILE, TILE)
        norm_cat[other, columns] = swap.get(4 + tile, land_norm.at[tile])
        swap.put(10 + tile, tile, att_low[:, columns], land_att.at[tile], before=6 + tile)
    leave(norm_cat, norm_out)
    pl.semaphore_signal(free, inc=1, device_id=place.partner(), device_id_type=MESH)
    for stream in down:
        stream.forward()

    def back_up(columns):
        gmixed[:, columns] = dot_nt(hidden[...], wu[columns, :])

    for_columns(1024, 256, back_up)

    def store(index, values):
        gmixed[index, :] = values
        hidden[index, pl.ds(0, 1024)] = values.astype(BF16)

    norm_back_rows(mixed, gmixed, cot, gain, sums, store)
    leave(gmixed, gmixed_out)
    pl.semaphore_wait(free, 1)
    swap.put(12, 2, hidden[:, half_tile(0, 1 - core)], land_norm.at[0], before=8)

    def back_out(columns):
        gatt[:, columns] = dot_nt(hidden[:, pl.ds(0, 1024)], wo[columns, :])

    for_columns(1024, TILE, back_out)
    leave(gatt, gatt_out)
    ours = hidden[:, half_tile(0, core)]
    theirs = swap.get(12, land_norm.at[0])
    for tile in range(2):
        swap.copy(10 + tile, tile, land_att.at[tile]).wait_recv()
        for part, (start, width) in enumerate(((0, 384), (384, 128))):
            product = tn_dot(att_low[:, pl.ds(tile * TILE + start, width)], ours)
            theirs_att = land_att[tile, :, pl.ds(start, width)].astype(BF16)
            land[2 * tile + part, pl.ds(0, width), :] = product + tn_dot(theirs_att, theirs)
            leave(land.at[2 * tile + part, pl.ds(0, width)], out_out.at[pl.ds(tile * TILE + start, width)])
    for stream, out in zip(down, (down_a, down_b, down_c)):
        stream.finish(out)
    for number, slot in ((9, 3), (10, 0), (11, 1), (12, 2)):
        swap.copy(number, slot, land_norm.at[0]).wait_send()
    for stream in down:
        stream.drain()
    for copy in outs:
        copy.wait()


def slab_shapes(widths):
    return [pltpu.VMEM((4, 4, 4, 8, width), F32) for width in widths]


def struct(shape, dtype=F32):
    return jax.ShapeDtypeStruct(shape, dtype)


VMEM_SPEC = pl.BlockSpec(memory_space=pltpu.VMEM)
ANY_SPEC = pl.BlockSpec(memory_space=pl.ANY)


def call(kernel, outs, out_specs, operands, in_specs, scratch, collective_id):
    return pl.pallas_call(
        kernel,
        out_shape=outs,
        in_specs=in_specs,
        out_specs=out_specs,
        scratch_shapes=scratch,
        compiler_params=pltpu.CompilerParams(
            collective_id=collective_id, has_side_effects=True, vmem_limit_bytes=63 * MIB
        ),
    )(*operands)


def feed_forward(x, att_low, gain, shift, cot_cat, w_out, w_up, w_down):
    rows, width = x.shape
    wide = w_up.shape[1]
    outs = [
        struct((rows, width), BF16),
        struct((rows, width)),
        struct((rows, width)),
        struct((8, width)),
        struct((2 * rows, width), BF16),
        struct((2 * rows, wide // 2), BF16),
        struct((width, TILE)),
        *[struct((4, 4, 8, length)) for length in DOWN_WIDTHS],
    ]
    scratch = [
        pltpu.VMEM((width, width), BF16),
        pltpu.VMEM((width, wide), BF16),
        pltpu.VMEM((wide, width), BF16),
        pltpu.SemaphoreType.DMA((4,)),
        pltpu.SemaphoreType.DMA((9,)),
        pltpu.VMEM((rows, width), BF16),
        pltpu.VMEM((rows, width), F32),
        pltpu.VMEM((rows, width), F32),
        pltpu.VMEM((2 * rows, width), BF16),
        pltpu.VMEM((2 * rows, wide // 2), BF16),
        pltpu.VMEM((rows, wide), BF16),
        pltpu.VMEM((rows, wide), BF16),
        pltpu.VMEM((2 * rows, width), BF16),
        pltpu.VMEM((4, rows, TILE), F32),
        pltpu.VMEM((4, rows, TILE), F32),
        pltpu.VMEM((2, rows, TILE), F32),
        pltpu.VMEM((2, rows, TILE), F32),
        pltpu.SemaphoreType.DMA((13,)),
        pltpu.SemaphoreType.DMA((13,)),
        pltpu.SemaphoreType.REGULAR,
        *slab_shapes(DOWN_WIDTHS),
        *flatten([stream_scratch(length, (0,)) for length in DOWN_WIDTHS]),
    ]
    specs = [VMEM_SPEC] * 4 + [ANY_SPEC] * 4
    out_specs = [ANY_SPEC] * 3 + [VMEM_SPEC] + [ANY_SPEC] * 3 + [VMEM_SPEC] * 3
    operands = (x, att_low, gain, shift, cot_cat, w_out, w_up, w_down)
    return call(feed_forward_kernel, outs, out_specs, operands, specs, scratch, 1)


def last_scratch(rows, width):
    return {
        "qkv": pltpu.VMEM((3, rows, width), BF16),
        "att": pltpu.VMEM((rows, width), F32),
        "gn": pltpu.VMEM((rows, width), F32),
        "state": pltpu.VMEM((SEQ, 72, PAIR), F32),
        "x": pltpu.VMEM((rows, width), BF16),
        "grads": pltpu.VMEM((2, rows, width), F32),
        "scan": list(SCAN_SCRATCH[:3]) + [SCAN_SCRATCH[0]] + list(SCAN_SCRATCH[3:]),
        "norm_cat": pltpu.VMEM((2, 2 * rows, width // 2), BF16),
        "pre_cat": pltpu.VMEM((2 * rows, 2 * width), BF16),
        "w": pltpu.VMEM((width, 3 * width), BF16),
        "stage": pltpu.VMEM((3, rows, TILE), F32),
        "land": pltpu.VMEM((3, rows, TILE), F32),
        "swap": [pltpu.SemaphoreType.DMA((3,)), pltpu.SemaphoreType.DMA((3,))],
        "slabs": slab_shapes(UP_WIDTHS),
        "chunks": [pltpu.VMEM((4, 4, 8, length), F32) for length in DOWN_WIDTHS],
        "up_chunks": [pltpu.VMEM((4, 4, 8, length), F32) for length in UP_WIDTHS],
        "out_slabs": slab_shapes(OUT_WIDTHS),
        "vec_slab": pltpu.VMEM((4, 4, 4, 8, 128), F32),
        "sums": pltpu.VMEM((8, width), F32),
        "down": [stream_scratch(length, (1, 2), (2,)) for length in DOWN_WIDTHS],
        "up": [stream_scratch(length, (0, 1, 2), (2,)) for length in UP_WIDTHS],
        "out": [stream_scratch(length, (0, 1, 2), (1, 2)) for length in OUT_WIDTHS],
        "qkv_sems": [[pltpu.SemaphoreType.DMA((6,))] * 2 for _ in QKV_WIDTHS],
        "qkv_sum": [stream_scratch(length, (1, 2), (2,)) for length in QKV_WIDTHS],
        "vec": stream_scratch(128, (0, 1, 2), (0, 1, 2)),
        "up_rows": [pltpu.VMEM((2, 8, 2048), F32), pltpu.VMEM((8, 2048), F32)],
        "out_rows": [pltpu.VMEM((2, 8, 512), F32), pltpu.VMEM((8, 512), F32)],
        "qkv_rows": [pltpu.VMEM((2, 8, 1536), F32), pltpu.VMEM((8, 1536), F32)],
        "row_sems": pltpu.SemaphoreType.DMA((3, 2)),
        "vec_land": pltpu.VMEM((8, 128), F32),
        "vec_sems": pltpu.SemaphoreType.DMA((2,)),
        "credit": pltpu.SemaphoreType.REGULAR((3,)),
        "loads": pltpu.SemaphoreType.DMA((32,)),
    }


def last_kernel(
    block, qkv_in, att_in, den_in, state_in, gatt_in, gmixed_in, norm_one_in, norm_in, pre_in,
    down_in_a, down_in_b, down_in_c, out_in, x_in, weight, gain, sums_two,
    grad_input, grad_up, grad_out, grad_qkv, grad_down, grad_gains, *scratch,
):
    place = Place()
    core = place.core
    rows, width = att_in.shape
    like = last_scratch(rows, width)
    take = Taker(scratch)
    s = {name: take(like[name]) for name in like}
    qkv, att, gn, grads = s["qkv"], s["att"], s["gn"], s["grads"]
    slabs = s["slabs"]
    scan = Scan(*s["scan"][:4], s["scan"][4:], True)
    across = [place.neighbour(0, step) for step in (1, -1, 2)]
    others = [*across, place.partner(), *scan.others()]
    greet(others)
    loads = []

    def load(source, target):
        copy = pltpu.make_async_copy(source, target, s["loads"].at[len(loads)])
        copy.start()
        loads.append(copy)
        return copy

    down_in = (down_in_a, down_in_b, down_in_c)
    down_loads = [load(source, target) for source, target in zip(down_in, s["chunks"])]
    started = [
        load(qkv_in.at[0], qkv.at[0]),
        load(gatt_in, gn),
        load(den_in, grads.at[0]),
        load(att_in, att),
    ]
    up_loads = [load(pre_in, s["pre_cat"])]
    for which in range(2):
        for block_x in range(4):
            source = norm_in.at[:, pl.ds(block_x * 256 + which * 128, 128)]
            target = s["norm_cat"].at[which, :, pl.ds(block_x * 128, 128)]
            up_loads.append(load(source, target))
    qkv_loads = [load(qkv_in.at[pl.ds(1, 2)], qkv.at[pl.ds(1, 2)]), load(state_in, s["state"])]
    out_loads = []
    for k in range(3):
        for which, start, length, at in stream_pieces(k, OUT_WIDTHS, TILE):
            source = out_in.at[:, which, :, :, :, pl.ds(start, length)]
            target = s["out_slabs"][k].at[:, :, :, :, pl.ds(at, length)]
            out_loads.append(load(source, target))
    late_loads = [load(weight, s["w"]), load(x_in, s["x"])]

    def settle(copies):
        for copy in copies:
            copy.wait()

    first, second = head_masks()
    first_wide = first_head(block)

    def slopes(index, columns, numer):
        product = numer * att[index, columns]
        ours = jnp.sum(jnp.where(first_wide, product, 0.0), axis=1, keepdims=True)
        theirs = jnp.sum(jnp.where(first_wide, 0.0, product), axis=1, keepdims=True)
        return -ours, -theirs

    up_first = [phases[0] for phases in s["up"]]
    down = [Stream(place, s["chunks"][k], ORDERS[k][1:], s["down"][k]) for k in range(3)]
    up = [Stream(place, slabs[k], ORDERS[k], s["up"][k]) for k in range(3)]
    out = [Stream(place, s["out_slabs"][k], ORDERS[k], s["out"][k]) for k in range(3)]
    qkv_sum = [None] * 3
    vec = [Stream(place, s["vec_slab"], ORDERS[0], s["vec"])]
    begin, forward, proceed, finish = Stream.begin, Stream.forward, Stream.proceed, Stream.finish

    def go(*steps):
        for step, streams, k in steps:
            step(streams[k])

    settle(down_loads)
    met(len(others))
    for stream in down:
        stream.begin()
    settle(started)

    def local_state(unit):
        index, columns = unit_slices(unit, block)
        numer = gn[index, columns] / grads[0, index, columns]
        gn[index, columns] = numer
        one, two = slopes(index, columns, numer)
        query = features(qkv[0, index, columns].astype(F32))
        high, low = split(numer)
        wide = tn_dot(query, jnp.concatenate([high, low], axis=1))
        spread = jnp.where(first_wide, one, two)
        total = jnp.sum(query.astype(F32) * spread, axis=0, keepdims=True)
        blocks, row = pack_state(wide[:, :PAIR] + wide[:, PAIR:], total)
        scan.terms[unit, pl.ds(0, 64)] = blocks
        scan.terms[unit, pl.ds(64, 8)] = row

    for_units(local_state, 2)
    scan.start()
    go((forward, down, 0), (forward, down, 1), (forward, down, 2))
    settle(up_loads)
    for k in range(3):
        stream_product(k, s["norm_cat"], s["pre_cat"], slabs[k], UP_WIDTHS, 2048)
        if k == 0:
            up[0].begin()
    norm_load = load(norm_one_in, s["norm_cat"])
    go((proceed, down, 2))
    settle(qkv_loads)
    causal = causal_mask(block)
    causal_t = causal_mask(block, True)

    def local_part(unit):
        index, columns = unit_slices(unit, block)
        raw_query = qkv[0, index, columns].astype(F32)
        query, value = features(raw_query), qkv[2, index, columns]
        key = features(qkv[1, index, columns].astype(F32))
        numer = gn[index, columns]
        one, two = slopes(index, columns, numer)
        high, low = split(numer)
        scores = dot_nt(jnp.concatenate([key * first, key * second], axis=0), query)
        wide = jnp.concatenate([high, low], axis=1)
        values = jnp.concatenate([value, value], axis=1)
        grad_query, grad_key, grad_value = 0.0, 0.0, 0.0
        for head, (mask, slope) in enumerate(((first, one), (second, two))):
            mask_wide = jnp.concatenate([mask, mask], axis=1)
            mixing = jnp.where(causal, dot_nt(wide * mask_wide, values) + slope, 0.0).astype(BF16)
            turned = jnp.where(causal_t, scores[head * block : (head + 1) * block], 0.0)
            grad_query = grad_query + dot_nn(mixing, key * mask)
            grad_key = grad_key + tn_dot(mixing, query * mask)
            grad_value = grad_value + dot_nn(turned.astype(BF16), high * mask)
        square, total = unpack_state(s["state"][unit])
        state_high, state_low = split(square)
        grad_query = grad_query + dot_nn(wide, jnp.concatenate([state_high, state_high], axis=0))
        grad_query = grad_query + dot_nn(high, state_low)
        grad_query = grad_query + jnp.where(first_wide, one, two) * total
        qkv[0, index, columns] = (grad_query * feature_slope(raw_query)).astype(BF16)
        grads[0, index, columns] = grad_key
        grads[1, index, columns] = grad_value

    def local_parts(start, count):
        def one(index, carry):
            local_part(start + index)
            return carry

        lax.fori_loop(0, count, one, 0)

    local_parts(0, 4)
    scan.middle()
    up[1].begin()
    up[2].begin()
    go((proceed, down, 0), (proceed, down, 1))
    local_parts(4, 4)
    go((finish, down, 2))
    local_parts(8, 1)
    go((forward, up, 0))
    local_parts(9, 7)
    settle(out_loads)
    swap = Swap(place, s["stage"], *s["swap"])
    land, cat = s["land"], s["pre_cat"]
    own, other = pl.ds(0, rows), pl.ds(rows, rows)
    swap.put(0, 0, qkv[0, :, half_tile(0, 1 - core)], land.at[0])
    mixed_load = load(gmixed_in, att)
    scan.finish()

    def incoming(unit):
        index, columns = unit_slices(unit, block)
        square, total = unpack_state(scan.result[unit])
        high, low = split(square)
        raw_key = qkv[1, index, columns].astype(F32)
        key, value = features(raw_key), qkv[2, index, columns]
        grad_key = grads[0, index, columns] + total
        grad_key = grad_key + dot_nt(
            jnp.concatenate([value, value], axis=1), jnp.concatenate([high, low], axis=1)
        )
        grad_value = grads[1, index, columns] + dot_nn(
            jnp.concatenate([key, key], axis=1), jnp.concatenate([high, low], axis=0)
        )
        qkv[1, index, columns] = (grad_key * feature_slope(raw_key)).astype(BF16)
        qkv[2, index, columns] = grad_value.astype(BF16)

    for_units(incoming, 2)
    for third in (1, 2):
        swap.put(third, third, qkv[third, :, half_tile(0, 1 - core)], land.at[third])
    go((forward, up, 2))
    settle(late_loads)

    def back_norm(columns):
        total = 0.0
        for third in range(3):
            total = total + dot_nt(qkv[third], s["w"][columns, pl.ds(third * 1024, 1024)])
        gn[:, columns] = total

    for start in (0, 256, 512, 768):
        back_norm(pl.ds(start, 256))
        if start == 0:
            go((forward, up, 1), (finish, down, 1))
    for third in range(3):
        columns = pl.ds(third * TILE, TILE)
        cat[own, columns] = qkv[third, :, half_tile(0, core)]
        cat[other, columns] = swap.get(third, land.at[third])
    norm_load.wait()
    mixed_load.wait()
    def turn(k):
        up[k].finish(s["up_chunks"][k])
        up[k].drain()
        for step in (1, -1):
            pl.semaphore_signal(
                s["credit"].at[k],
                inc=1,
                device_id=place.neighbour(ORDERS[k][0], step),
                device_id_type=MESH,
            )
        narrow = (slice(None),) * 4 + (pl.ds(0, QKV_WIDTHS[k]),)
        data = slabs[k].at[narrow]
        stream_product(k, s["norm_cat"], cat, data, QKV_WIDTHS, 3 * TILE)
        pl.semaphore_wait(s["credit"].at[k], 2)
        phases = [[up_first[k][0].at[narrow], up_first[k][1].at[narrow], *s["qkv_sems"][k]]]
        qkv_sum[k] = Stream(place, data, ORDERS[k], phases + s["qkv_sum"][k])
        qkv_sum[k].begin()

    def store(index, values):
        gn[index, :] = values

    sums = s["sums"]
    norm_back_rows(s["x"], gn, att, gain, sums, store)
    leave = load(gn, grad_input)
    four = jnp.concatenate([sums[0:2, :], sums_two[0:2, :]], axis=0)
    eight = jnp.concatenate([four, four], axis=0)
    turned = jnp.transpose(jnp.concatenate([eight, jnp.zeros((120, 1024), F32)], axis=0))
    turned = turned.reshape(4, 2, 4, 4, 8, 128)
    lane = lax.broadcasted_iota(jnp.int32, (8, 128), 1)
    s["vec_slab"][...] = jnp.where(lane < 4, turned[:, 0], jnp.where(lane < 8, turned[:, 1], 0.0))
    for stream in out:
        stream.begin()
    turn(0)
    go((forward, out, 0), (finish, down, 0))
    turn(1)
    go((forward, out, 1), (forward, out, 2))
    turn(2)
    go(
        (forward, qkv_sum, 0), (proceed, out, 2), (begin, vec, 0), (forward, qkv_sum, 1), (forward, qkv_sum, 2),
        (begin, up, 0), (begin, up, 1), (begin, up, 2), (proceed, out, 0), (proceed, out, 1), (proceed, qkv_sum, 1),
        (proceed, qkv_sum, 0), (forward, up, 0), (proceed, out, 2), (proceed, qkv_sum, 2), (proceed, vec, 0),
        (forward, up, 1), (proceed, out, 0), (forward, up, 2), (forward, qkv_sum, 0), (proceed, out, 1),
        (forward, qkv_sum, 2), (forward, qkv_sum, 1), (proceed, up, 0), (proceed, up, 2), (finish, out, 2),
        (proceed, up, 1), (proceed, vec, 0), (proceed, qkv_sum, 0), (proceed, qkv_sum, 2), (proceed, qkv_sum, 1),
        (finish, out, 1), (finish, out, 0), (finish, up, 0), (finish, up, 2), (finish, up, 1), (finish, vec, 0),
    )
    for k in range(3):
        piece = down[k].data
        grad_down[pl.ds(8 * k, 8), :] = piece[:, pl.ds(0, 1024)]
        start, width_k = DOWN_CUTS[k]
        grad_down[pl.ds(24, 8), pl.ds(start, width_k)] = piece[:, pl.ds(1024, width_k)]
    swaps = []

    def swap_rows(streams, widths, columns, rows_land, slot):
        shared_rows(streams, widths, columns, rows_land[0])
        copy = row_swap(place, *rows_land, s["row_sems"].at[slot])
        copy.start()
        swaps.append(copy)

    swap_rows(up, UP_WIDTHS, 2048, s["up_rows"], 0)
    vec_tile = vec[0].data
    vec_copy = pltpu.make_async_remote_copy(
        src_ref=vec_tile,
        dst_ref=s["vec_land"],
        send_sem=s["vec_sems"].at[0],
        recv_sem=s["vec_sems"].at[1],
        device_id=place.partner(),
        device_id_type=MESH,
    )
    vec_copy.start()
    swap_rows(out, OUT_WIDTHS, TILE, s["out_rows"], 1)
    go((finish, qkv_sum, 2), (finish, qkv_sum, 0), (finish, qkv_sum, 1))
    swap_rows(qkv_sum, QKV_WIDTHS, 3 * TILE, s["qkv_rows"], 2)
    scan.drain()
    for number in range(3):
        swap.copy(number, number, land.at[number]).wait_send()
    for stream in (*down, *up, *out, *qkv_sum, *vec):
        stream.drain()
    vec_copy.wait()
    grad_gains[...] = vec_tile[...] + s["vec_land"][...]
    leave.wait()
    swaps[0].wait()
    lay_rows(place, *s["up_rows"], grad_up)
    swaps[1].wait()
    lay_rows(place, *s["out_rows"], grad_out)
    swaps[2].wait()
    lay_rows(place, *s["qkv_rows"], grad_qkv)


def last_part(qkv, att, den, state, gatt, gmixed, norm_one, norm_cat, pre_cat, down, out, x, weight, gain, sums_two, block):
    rows, width = x.shape

    def kernel(*refs):
        last_kernel(block, *refs)

    outs = [
        struct((rows, width)),
        struct((8, 4096)),
        struct((8, width)),
        struct((8, 3 * width)),
        struct((32, width)),
        struct((8, 128)),
    ]
    like = last_scratch(rows, width)
    scratch = [leaf for name in like for leaf in flatten(like[name])]
    out = out.reshape(4, 2, 4, 4, 8, TILE)
    operands = (
        qkv, att, den, state, gatt, gmixed, norm_one, norm_cat, pre_cat, *down, out, x, weight, gain, sums_two,
    )
    specs = [ANY_SPEC] * 15 + [VMEM_SPEC] * 2
    out_specs = [ANY_SPEC] + [VMEM_SPEC] * 5
    return call(kernel, outs, out_specs, operands, specs, scratch, 2)


def lay_out_kernel(output, grad_input, up, out, qkv, down, gains, output_to, grad_to, up_to, out_to, qkv_to, down_to, a, b, c, d):
    pairs = (
        (output, output_to), (grad_input, grad_to), (up, up_to), (out, out_to), (qkv, qkv_to), (down, down_to),
    )
    for source, target in pairs:
        target[...] = source[...]
    core = lax.rem(lax.axis_index("dp"), 2)
    turned = jnp.transpose(jnp.concatenate([gains[...], jnp.zeros((120, 128), F32)], axis=0))
    for k, target in enumerate((a, b, c, d)):
        target[...] = jnp.where(core == 0, turned[k : k + 1, :8], turned[4 + k : 5 + k, :8])


def lay_out(output, *grads):
    arrays = (output, *grads[:-1])
    outs = [struct(array.shape, array.dtype) for array in arrays] + [struct((1, 8))] * 4
    return pl.pallas_call(
        lay_out_kernel,
        out_shape=outs,
        in_specs=[VMEM_SPEC] * 7,
        out_specs=[VMEM_SPEC] * 10,
        compiler_params=pltpu.CompilerParams(vmem_limit_bytes=62 * MIB),
    )(output, *grads)


def body(
    inputs,
    first_gain,
    first_shift,
    qkv_weight,
    out_weight,
    second_gain,
    second_shift,
    up_weight,
    down_weight,
    cotangent,
):
    sequences, block, width = inputs.shape
    rows = sequences * block
    x = inputs.reshape(rows, width)
    cot = cotangent.reshape(rows, width)
    gain_one, gain_two = first_gain.reshape(1, width), second_gain.reshape(1, width)
    shift_two = second_shift.reshape(1, width)
    norm_one, cot_cat, qkv, att, att_low, den, state = attention_forward(
        x, first_gain, first_shift, qkv_weight, cot, block
    )
    output, gmixed, gatt, sums_two, norm_cat, pre_cat, out, *down = feed_forward(
        x, att_low, gain_two, shift_two, cot_cat, out_weight, up_weight, down_weight
    )
    grads = last_part(
        qkv, att, den, state, gatt, gmixed, norm_one, norm_cat, pre_cat, down, out, x, qkv_weight,
        gain_one, sums_two, block,
    )
    output, grad_input, grad_up, grad_out, grad_qkv, grad_down, *gains = lay_out(output, *grads)
    return (
        output.reshape(inputs.shape),
        grad_input.reshape(inputs.shape),
        grad_qkv,
        grad_out,
        grad_up,
        grad_down,
        *[gain.reshape(8) for gain in gains],
    )


def solution(mesh):
    return jax.shard_map(
        body,
        mesh=mesh,
        in_specs=(
            P("dp", "seq", None),
            P(),
            P(),
            P(),
            P(),
            P(),
            P(),
            P(),
            P(),
            P("dp", "seq", None),
        ),
        out_specs=(
            P("dp", "seq", None),
            P("dp", "seq", None),
            P(("dp", "seq"), None),
            P(("dp", "seq"), None),
            P(("dp", "seq"), None),
            P(("dp", "seq"), None),
            P(("dp", "seq")),
            P(("dp", "seq")),
            P(("dp", "seq")),
            P(("dp", "seq")),
        ),
        check_vma=False,
    )
```

```python
import math

import jax
import jax.numpy as jnp
from jax import lax
from jax.experimental import pallas as pl
from jax.experimental.pallas import tpu as pltpu
from jax.sharding import PartitionSpec as P

MESH = pl.DeviceIdType.MESH
F32 = jnp.float32
BF16 = jnp.bfloat16
RING = 4
MIB = 2**20


class Place:
    def __init__(self):
        dp, seq = lax.axis_index("dp"), lax.axis_index("seq")
        self.core = lax.rem(dp, 2)
        self.at = (lax.div(dp, 2), lax.div(seq, RING), lax.rem(seq, RING))

    def id_of(self, x, y, z, core):
        return (x * 2 + core, y * RING + z)

    def ring(self, axis, step):
        return lax.rem(self.at[axis] + (step + RING), RING)

    def neighbour(self, axis, step):
        at = list(self.at)
        at[axis] = self.ring(axis, step)
        return self.id_of(*at, self.core)

    def partner(self):
        return self.id_of(*self.at, 1 - self.core)


def greet(others):
    barrier = pltpu.get_barrier_semaphore()
    for other in others:
        pl.semaphore_signal(barrier, inc=1, device_id=other, device_id_type=MESH)


def met(count):
    pl.semaphore_wait(pltpu.get_barrier_semaphore(), count)


def link_neighbours(place):
    others = [place.neighbour(axis, step) for axis in range(3) for step in (1, -1)]
    return [*others, place.partner()]


ORDERS = ((0, 1, 2), (1, 2, 0), (2, 0, 1))


def phase_scratch(remaining, length):
    if remaining:
        half = (2, 2, *[4] * (remaining - 1), 8, length)
    else:
        half = (2, 8, (length // 128 + 1) // 2 * 128)
    return [
        pltpu.VMEM((2, *[4] * remaining, 8, length), F32),
        pltpu.VMEM(half, F32),
        pltpu.SemaphoreType.DMA((6,)),
        pltpu.SemaphoreType.DMA((6,)),
    ]


class Phase:
    def __init__(self, place, data, axes, axis, scratch):
        self.place, self.data, self.axis = place, data, axis
        self.where = axes.index(axis)
        self.full, self.half, self.sent, self.came = scratch
        self.flying = []
        self.flat = len(axes) == 1
        self.length = data.shape[-1]
        self.cut = (self.length // 128 + 1) // 2 * 128
        self.whole = self.flat and self.cut == self.length

    def empty(self, which):
        return self.whole and which == 1

    def chunk(self, target):
        index = [slice(None)] * self.where + [target]
        return self.data.at[tuple(index)]

    def part(self, ref, which):
        if not self.flat:
            return ref.at[pl.ds(2 * which, 2)]
        if which == 0:
            return ref.at[:, pl.ds(0, self.cut)]
        return ref.at[:, pl.ds(self.cut, self.length - self.cut)]

    def through(self, way):
        ref = self.half.at[way]
        if self.flat and way == 1:
            return ref.at[:, pl.ds(0, self.length - self.cut)]
        return ref

    def copy(self, kind, way, source, target):
        number = kind * 2 + way
        return pltpu.make_async_remote_copy(
            src_ref=source,
            dst_ref=target,
            send_sem=self.sent.at[number],
            recv_sem=self.came.at[number],
            device_id=self.place.neighbour(self.axis, 1 - 2 * way),
            device_id_type=MESH,
        )

    def send(self, kind, way, source, target):
        copy = self.copy(kind, way, source, target)
        copy.start()
        self.flying.append(copy)

    def beside(self, way):
        return self.chunk(self.place.ring(self.axis, 1 - 2 * way))

    def begin_far(self):
        opposite = self.chunk(self.place.ring(self.axis, 2))
        for way in range(2):
            if not self.empty(way):
                self.send(0, way, self.part(opposite, way), self.through(way))

    def begin_near(self):
        for way in range(2):
            if self.empty(1 - way):
                continue
            target = self.part(self.full.at[way], 1 - way)
            self.send(1, way, self.part(self.beside(way), 1 - way), target)

    def begin(self):
        self.begin_far()
        self.begin_near()

    def forward(self):
        for way in range(2):
            if self.empty(way):
                continue
            came = self.through(way)
            self.copy(0, way, came, came).wait_recv()
            own = self.part(self.beside(way), way)
            add_into(own, own, came)
            self.send(2, way, own, self.part(self.full.at[way], way))

    def finish(self, out=None):
        own = self.chunk(self.place.at[self.axis])
        for way in range(2):
            for kind, which in ((1, 1 - way), (2, way)):
                if self.empty(which):
                    continue
                target = self.part(self.full.at[way], which)
                self.copy(kind, way, target, target).wait_recv()
        add_into(own if out is None else out, own, self.full.at[0], self.full.at[1])
        return own

    def drain(self):
        for copy in self.flying:
            copy.wait_send()


class Direct:
    def __init__(self, place, data, axes, axis, scratch):
        self.place, self.data, self.axis = place, data, axis
        self.where = axes.index(axis)
        self.full, self.sent, self.came = scratch
        self.flying = []

    def chunk(self, target):
        index = [slice(None)] * self.where + [target]
        return self.data.at[tuple(index)]

    def copy(self, step, source):
        return pltpu.make_async_remote_copy(
            src_ref=source,
            dst_ref=self.full.at[step - 1],
            send_sem=self.sent.at[step - 1],
            recv_sem=self.came.at[step - 1],
            device_id=self.place.neighbour(self.axis, step),
            device_id_type=MESH,
        )

    def begin(self):
        for step in (2, 1, 3):
            copy = self.copy(step, self.chunk(self.place.ring(self.axis, step)))
            copy.start()
            self.flying.append(copy)

    def forward(self):
        pass

    def finish(self, out=None):
        own = self.chunk(self.place.at[self.axis])
        for step in (1, 2, 3):
            self.copy(step, self.full.at[step - 1]).wait_recv()
        add_into(own if out is None else out, own, *[self.full.at[k] for k in range(3)])
        return own

    def drain(self):
        for copy in self.flying:
            copy.wait_send()


class Stream:
    def __init__(self, place, data, order, scratch):
        self.place, self.data, self.scratch = place, data, scratch
        self.todo, self.old = [axis for axis in order], []
        self.axes = sorted(order)
        self.phase = None

    def prepare(self):
        scratch = self.scratch.pop(0)
        kind = Phase if len(scratch) == 4 else Direct
        self.phase = kind(self.place, self.data, self.axes, self.todo[0], scratch)
        return self.phase

    def begin(self):
        self.prepare().begin()

    def forward(self):
        self.phase.forward()

    def finish(self, out=None):
        own = self.phase.finish(out)
        self.data = own if out is None else out
        self.axes.remove(self.todo.pop(0))
        self.old.append(self.phase)

    def proceed(self):
        self.finish()
        self.begin()

    def drain(self):
        for phase in self.old:
            phase.drain()
        self.old = []


def direct_scratch(remaining, length):
    return [
        pltpu.VMEM((3, *[4] * remaining, 8, length), F32),
        pltpu.SemaphoreType.DMA((3,)),
        pltpu.SemaphoreType.DMA((3,)),
    ]


def stream_scratch(length, phases, direct=()):
    return [
        (direct_scratch if phase in direct else phase_scratch)(2 - phase, length)
        for phase in phases
    ]


class Taker:
    def __init__(self, refs):
        self.refs = list(refs)

    def __call__(self, like):
        if isinstance(like, list):
            return [self(item) for item in like]
        return self.refs.pop(0)


def flatten(items):
    if isinstance(items, list):
        return [leaf for item in items for leaf in flatten(item)]
    return [items]


def add_into(out, *terms):
    if len(out.shape) > 2:

        def row(index, carry):
            add_into(out.at[index], *[term.at[index] for term in terms])
            return carry

        if len(out.shape) == 4:
            lax.fori_loop(0, out.shape[0], row, 0)
        else:
            for index in range(out.shape[0]):
                row(index, 0)
        return
    total = terms[0][...]
    for term in terms[1:]:
        total = total + term[...]
    out[...] = total


def tn_dot(left, right):
    return lax.dot_general(left, right, (((0,), (0,)), ((), ())), preferred_element_type=F32)


TILE = 512


class Swap:
    def __init__(self, place, stage, sent, came):
        self.place, self.stage, self.sent, self.came = place, stage, sent, came

    def copy(self, number, slot, target):
        return pltpu.make_async_remote_copy(
            src_ref=self.stage.at[slot],
            dst_ref=target,
            send_sem=self.sent.at[number],
            recv_sem=self.came.at[number],
            device_id=self.place.partner(),
            device_id_type=MESH,
        )

    def put(self, number, slot, values, target, before=None):
        if before is not None:
            self.copy(before, slot, target).wait_send()
        self.stage[slot] = values.astype(F32)
        self.copy(number, slot, target).start()

    def get(self, number, target):
        self.copy(number, 0, target).wait_recv()
        return target[...].astype(BF16)

    def drain(self, numbers, target):
        for number in numbers:
            self.copy(number, number % 4, target).wait_send()


def half_columns(block, core, quarter):
    half = quarter // 2
    return pl.ds(pl.multiple_of(block * quarter + core * half, half), half)


def half_tile(index, core):
    return pl.ds(pl.multiple_of((2 * index + core) * TILE, TILE), TILE)


def core_product(left, core, right, start, width, slab, at):
    done = 0
    while done < width:
        step = min(TILE, width - done)
        product = tn_dot(left[core], right[:, pl.ds(start + done, step)])
        slab[:, :, :, :, pl.ds(at + done, step)] = product.reshape(4, 4, 4, 8, step)
        done += step


UP_WIDTHS = (1536, 1280, 1280)
OUT_WIDTHS = (512, 256, 256)
QKV_WIDTHS = (1152, 896, 1024)


def stream_pieces(stream, widths, columns):
    if stream < 2:
        return [(stream, 0, widths[stream], 0)]
    pieces, at = [], 0
    for core in range(2):
        width = columns - widths[core]
        if width:
            pieces.append((core, widths[core], width, at))
        at += width
    return pieces


def stream_product(stream, left, right, slab, widths, columns):
    for core, start, width, at in stream_pieces(stream, widths, columns):
        core_product(left, core, right, start, width, slab, at)


def shared_rows(streams, widths, columns, rows):
    for stream in range(3):
        for core, start, width, at in stream_pieces(stream, widths, columns):
            rows[core, :, pl.ds(start, width)] = streams[stream].data[:, pl.ds(at, width)]


def row_swap(place, rows, land, sems):
    return pltpu.make_async_remote_copy(
        src_ref=rows.at[1 - place.core],
        dst_ref=land,
        send_sem=sems.at[0],
        recv_sem=sems.at[1],
        device_id=place.partner(),
        device_id_type=MESH,
    )


def lay_rows(place, rows, land, out):
    for tile in range(land.shape[1] // TILE):
        columns = pl.ds(tile * TILE, TILE)
        out[:, half_tile(tile, place.core)] = rows[place.core, :, columns]
        out[:, half_tile(tile, 1 - place.core)] = land[:, columns]


DOWN_CUTS = ((0, 384), (384, 384), (768, 256))
DOWN_WIDTHS = (1408, 1408, 1280)


SEQ = 16
PAIR = 128
NT = (((1,), (1,)), ((), ()))
TN = (((0,), (0,)), ((), ()))


def dot_nt(left, right):
    return lax.dot_general(left, right, NT, preferred_element_type=F32)


def dot_nn(left, right):
    return jnp.dot(left, right, preferred_element_type=F32)


def split(values):
    high = values.astype(BF16)
    return high, (values - high.astype(F32)).astype(BF16)


def features(raw):
    return jnp.where(raw > 0, raw + 1.0, jnp.exp(jnp.minimum(raw, 0.0))).astype(BF16)


def feature_slope(raw):
    return jnp.where(raw > 0, 1.0, jnp.exp(jnp.minimum(raw, 0.0)))


def head_masks():
    lane = lax.broadcasted_iota(jnp.int32, (1, PAIR), 1)
    first = jnp.where(lane < 64, 1.0, 0.0)
    return first.astype(BF16), (1.0 - first).astype(BF16)


def first_head(rows):
    return lax.broadcasted_iota(jnp.int32, (rows, PAIR), 1) < 64


def pack_state(square, total):
    blocks = jnp.where(first_head(64), square[:64], square[64:])
    return blocks, jnp.broadcast_to(total, (8, PAIR))


def unpack_state(packed):
    first = first_head(64)
    square = jnp.concatenate(
        [jnp.where(first, packed[:64], 0.0), jnp.where(first, 0.0, packed[:64])], axis=0
    )
    return square, packed[64:65]


def same_head():
    row = lax.broadcasted_iota(jnp.int32, (PAIR, PAIR), 0)
    lane = lax.broadcasted_iota(jnp.int32, (PAIR, PAIR), 1)
    return (row < 64) == (lane < 64)


def head_slopes(numer, attended, first_wide):
    product = numer * attended
    ours = jnp.sum(jnp.where(first_wide, product, 0.0), axis=1, keepdims=True)
    theirs = jnp.sum(jnp.where(first_wide, 0.0, product), axis=1, keepdims=True)
    return -ours, -theirs


def state_gradient(query, numer, attended, first_wide):
    one, two = head_slopes(numer, attended, first_wide)
    high, low = split(numer)
    wide = tn_dot(query, jnp.concatenate([high, low], axis=1))
    spread = jnp.where(first_wide, one, two)
    total = jnp.sum(query.astype(F32) * spread, axis=0, keepdims=True)
    return pack_state(wide[:, :PAIR] + wide[:, PAIR:], total)


OFFSETS = sorted(
    ((y, z) for y in range(RING) for z in range(RING) if y or z),
    key=lambda offset: -sum(min(step, RING - step) for step in offset),
)


class Scan:
    def __init__(self, terms, landed, sums, result, sems, reverse):
        self.terms, self.landed, self.sums, self.result = terms, landed, sums, result
        self.sems, self.reverse = sems, reverse
        self.dp, self.me = lax.axis_index("dp"), lax.axis_index("seq")
        self.y, self.z = lax.div(self.me, RING), lax.rem(self.me, RING)
        self.parity = lax.rem(self.y + self.z, 2)
        self.unit = self.unit_of(self.parity, self.me)

    def unit_of(self, parity, device):
        return parity * 8 + lax.div(device, 2)

    def at(self, y, z, sign=1):
        y = lax.rem(self.y + (sign * y + RING), RING)
        z = lax.rem(self.z + (sign * z + RING), RING)
        return y * RING + z

    def others(self):
        return [(self.dp, self.at(*offset)) for offset in OFFSETS]

    def half_offsets(self, half):
        for y in (2, 1, 3, 0):
            for step in (1, 0):
                yield y, 2 * step + lax.rem(self.parity + (y + half), 2)

    def copy(self, number, source, target, sems, other):
        return pltpu.make_async_remote_copy(
            src_ref=source,
            dst_ref=target,
            send_sem=sems[0].at[number],
            recv_sem=sems[1].at[number],
            device_id=(self.dp, other),
            device_id_type=MESH,
        )

    def start(self):
        for half in range(2):
            for y, z in self.half_offsets(half):
                other = self.at(y, z)
                source = self.terms.at[self.unit_of(half, other)]
                copy = self.copy(y * RING + z, source, self.landed.at[self.me], self.sems[:2], other)
                if y:
                    copy.start()
                else:
                    pl.when(z > 0)(copy.start)
        self.landed[self.me] = self.terms[self.unit]

    def middle(self):
        for y, z in OFFSETS:
            other = self.at(y, z, -1)
            came = self.landed.at[other]
            self.copy(y * RING + z, came, came, self.sems[:2], other).wait_recv()
        total = jnp.zeros(self.landed.shape[1:], F32)
        for k in range(SEQ):
            at = SEQ - 1 - k if self.reverse else k
            self.sums[at] = total
            total = total + self.landed[at]
        for y, z in OFFSETS:
            other = self.at(y, z)
            target = self.result.at[self.unit]
            self.copy(y * RING + z, self.sums.at[other], target, self.sems[2:], other).start()
        self.result[self.unit] = self.sums[self.me]

    def finish(self, half):
        for y, z in self.half_offsets(half):
            other = self.at(y, z, -1)
            came = self.result.at[self.unit_of(half, other)]
            copy = self.copy(y * RING + z, came, came, self.sems[2:], other)
            if y:
                copy.wait_recv()
            else:
                pl.when(z > 0)(copy.wait_recv)

    def drain(self):
        for y, z in OFFSETS:
            number, other = y * RING + z, self.at(y, z)
            self.copy(number, self.terms.at[0], self.landed.at[0], self.sems[:2], other).wait_send()
            self.copy(number, self.sums.at[0], self.result.at[0], self.sems[2:], other).wait_send()


SCAN_SCRATCH = [
    pltpu.VMEM((SEQ, 72, PAIR), F32),
    pltpu.VMEM((SEQ, 72, PAIR), F32),
    pltpu.VMEM((SEQ, 72, PAIR), F32),
    *[pltpu.SemaphoreType.DMA((SEQ,)) for _ in range(4)],
]


def unit_slices(unit, block):
    rows = pl.ds(pl.multiple_of(lax.div(unit, 8) * block, block), block)
    columns = pl.ds(pl.multiple_of(lax.rem(unit, 8) * PAIR, PAIR), PAIR)
    return rows, columns


def for_units(step, together):
    def several(index, carry):
        for offset in range(together):
            step(index * together + offset)
        return carry

    lax.fori_loop(0, SEQ // together, several, 0)


def causal_mask(block, transposed=False):
    row = lax.broadcasted_iota(jnp.int32, (block, block), 0)
    column = lax.broadcasted_iota(jnp.int32, (block, block), 1)
    return (row <= column) if transposed else (row >= column)


def norm_rows(values):
    center = jnp.mean(values, axis=-1, keepdims=True)
    centered = values - center
    variance = jnp.mean(centered * centered, axis=-1, keepdims=True)
    inverse = lax.rsqrt(variance + 1e-05)
    return centered * inverse, inverse


ROWS = 64


def for_rows(count, step):
    def one(index, carry):
        step(pl.ds(pl.multiple_of(index * ROWS, ROWS), ROWS))
        return carry

    lax.fori_loop(0, count // ROWS, one, 0)


def for_columns(count, width, step):
    def one(index, carry):
        step(pl.ds(pl.multiple_of(index * width, width), width))
        return carry

    lax.fori_loop(0, count // width, one, 0)


def attention_forward_kernel(
    block, x, gain, shift, weight, cot_in, cat_out, cot_out, qkv_out, att_out, att_low_out, den_out, state_out,
    w, cot, normed, qkv, att, att_low, den, cat, fq, fk, stage, land, state, terms, landed, sums, s0, s1, s2, s3,
    wsem, osem, swap_sent, swap_came,
):
    place = Place()
    rows_all = x.shape[0]
    own, other = pl.ds(0, rows_all), pl.ds(rows_all, rows_all)
    outs = []

    def leave(source, target):
        outs.append(pltpu.make_async_copy(source, target, osem.at[len(outs)]))
        outs[-1].start()

    scan = Scan(terms, landed, sums, state, (s0, s1, s2, s3), False)
    others = [*scan.others(), place.partner()]
    greet(others)
    loads = []
    cot_load = pltpu.make_async_copy(cot_in, cot.at[own], wsem.at[3])
    for slot, third in enumerate((1, 2, 0)):
        load = pltpu.make_async_copy(
            weight.at[:, pl.ds(third * 1024, 1024)], w.at[slot], wsem.at[slot]
        )
        load.start()
        loads.append(load)
    cot_load.start()

    def norm_step(rows):
        scaled, _ = norm_rows(x[rows, :].astype(F32))
        normed[rows, :] = (scaled * gain[...] + shift[...]).astype(BF16)

    for_rows(x.shape[0], norm_step)

    def project(slot, third, feature):
        loads[slot].wait()

        def step(columns):
            raw = dot_nn(normed[...], w[slot, :, columns]).astype(BF16)
            qkv[third, :, columns] = raw
            if feature is not None:
                feature[:, columns] = features(raw.astype(F32))

        for_columns(1024, 512, step)

    project(0, 1, fk)
    project(1, 2, None)

    def local_state(unit):
        rows, columns = unit_slices(unit, block)
        keys = fk[rows, columns]
        square = tn_dot(qkv[2, rows, columns], keys)
        total = jnp.sum(keys.astype(F32), axis=0, keepdims=True)
        blocks, row = pack_state(square, total)
        terms[unit, pl.ds(0, 64)] = blocks
        terms[unit, pl.ds(64, 8)] = row

    for_units(local_state, 4)
    met(len(others))
    scan.start()
    swap = Swap(place, stage, swap_sent, swap_came)
    for core in range(2):
        for block_x in range(4):
            columns = pl.ds(block_x * 256 + core * 128, 128)
            cat[core, own, pl.ds(block_x * 128, 128)] = normed[:, columns]
        swap.put(core, core, cat[core, own, :], land.at[core])
    cot_load.wait()
    for tile in range(2):
        swap.put(2 + tile, 2 + tile, cot[own, pl.ds(tile * TILE, TILE)], land.at[2 + tile])
    leave(qkv.at[pl.ds(1, 2)], qkv_out.at[pl.ds(1, 2)])
    project(2, 0, fq)
    leave(qkv.at[0], qkv_out.at[0])
    first, second = head_masks()
    causal = causal_mask(block)

    def local_part(unit):
        rows, columns = unit_slices(unit, block)
        query, key, value = fq[rows, columns], fk[rows, columns], qkv[2, rows, columns]
        scores = dot_nt(jnp.concatenate([query * first, query * second], axis=0), key)
        both = 0.0
        for head, mask in enumerate((first, second)):
            own = jnp.where(causal, scores[head * block : (head + 1) * block], 0.0).astype(BF16)
            right = jnp.concatenate([value * mask, jnp.broadcast_to(mask, value.shape)], axis=1)
            both = both + dot_nn(own, right)
        att[rows, columns] = both[:, :PAIR]
        den[rows, columns] = both[:, PAIR:]

    def local_parts(start, count):
        def two(index, carry):
            local_part(start + 2 * index)
            local_part(start + 2 * index + 1)
            return carry

        lax.fori_loop(0, count // 2, two, 0)

    local_parts(0, 10)
    scan.middle()
    local_parts(10, 6)
    for core in range(2):
        cat[core, other, :] = swap.get(core, land.at[core])
        cot[other, pl.ds(core * TILE, TILE)] = swap.get(2 + core, land.at[2 + core])
    leave(cat, cat_out)
    leave(cot, cot_out)
    together = same_head()

    def incoming(unit):
        rows, columns = unit_slices(unit, block)
        square, total = unpack_state(state[unit])
        totals = jnp.where(together, jnp.broadcast_to(total, (PAIR, PAIR)), 0.0)
        high, low = split(jnp.concatenate([square, totals], axis=0))
        query = fq[rows, columns]
        both = dot_nt(
            jnp.concatenate([query, query], axis=1), jnp.concatenate([high, low], axis=1)
        )
        denom = den[rows, columns] + both[:, PAIR:]
        den[rows, columns] = denom
        attended = (att[rows, columns] + both[:, :PAIR]) / denom
        att[rows, columns] = attended
        att_low[rows, columns] = attended.astype(BF16)

    for half in range(2):
        scan.finish(half)
        leave(state.at[pl.ds(half * 8, 8)], state_out.at[pl.ds(half * 8, 8)])

        def several(index, carry):
            incoming(half * 8 + 2 * index)
            incoming(half * 8 + 2 * index + 1)
            return carry

        lax.fori_loop(0, 4, several, 0)
        part = pl.ds(half * block, block)
        leave(att.at[part], att_out.at[part])
        leave(den.at[part], den_out.at[part])
        leave(att_low.at[part], att_low_out.at[part])
    scan.drain()
    swap.drain(range(4), land.at[0])
    for copy in outs:
        copy.wait()


def attention_forward(x, gain, shift, weight, cot, block):
    rows, width = x.shape
    vmem = pl.BlockSpec(memory_space=pltpu.VMEM)

    def kernel(*refs):
        attention_forward_kernel(block, *refs)

    return pl.pallas_call(
        kernel,
        out_shape=[
            struct((2, 2 * rows, width // 2), BF16),
            struct((2 * rows, width), BF16),
            struct((3, rows, width), BF16),
            struct((rows, width)),
            struct((rows, width), BF16),
            struct((rows, width)),
            struct((SEQ, 72, PAIR)),
        ],
        in_specs=[vmem, vmem, vmem, ANY_SPEC, ANY_SPEC],
        out_specs=[ANY_SPEC] * 7,
        scratch_shapes=[
            pltpu.VMEM((3, width, width), BF16),
            pltpu.VMEM((2 * rows, width), BF16),
            pltpu.VMEM((rows, width), BF16),
            pltpu.VMEM((3, rows, width), BF16),
            pltpu.VMEM((rows, width), F32),
            pltpu.VMEM((rows, width), BF16),
            pltpu.VMEM((rows, width), F32),
            pltpu.VMEM((2, 2 * rows, width // 2), BF16),
            pltpu.VMEM((rows, width), BF16),
            pltpu.VMEM((rows, width), BF16),
            pltpu.VMEM((4, rows, TILE), F32),
            pltpu.VMEM((4, rows, TILE), F32),
            SCAN_SCRATCH[0],
            *SCAN_SCRATCH,
            pltpu.SemaphoreType.DMA((4,)),
            pltpu.SemaphoreType.DMA((12,)),
            pltpu.SemaphoreType.DMA((4,)),
            pltpu.SemaphoreType.DMA((4,)),
        ],
        compiler_params=pltpu.CompilerParams(
            collective_id=5, has_side_effects=True, vmem_limit_bytes=62 * MIB
        ),
    )(x, gain.reshape(1, width), shift.reshape(1, width), weight, cot)


def gelu_both(pre):
    cumulative = 0.5 * (1.0 + lax.erf(pre * (1.0 / math.sqrt(2.0))))
    density = jnp.exp(-0.5 * pre * pre) * (1.0 / math.sqrt(2.0 * math.pi))
    return (pre * cumulative).astype(BF16), (cumulative + pre * density).astype(BF16)


def norm_back(grad, gain, scaled, inverse):
    spread = grad * gain
    first_mean = jnp.mean(spread, axis=-1, keepdims=True)
    second_mean = jnp.mean(spread * scaled, axis=-1, keepdims=True)
    return inverse * (spread - first_mean - scaled * second_mean)


def norm_back_rows(values, grad, base, gain, sums, store):
    sums[...] = jnp.zeros_like(sums)

    def step(rows):
        scaled, inverse = norm_rows(values[rows, :].astype(F32))
        part = grad[rows, :]
        sums[0:1, :] += jnp.sum(part * scaled, axis=0, keepdims=True)
        sums[1:2, :] += jnp.sum(part, axis=0, keepdims=True)
        store(rows, base[rows, :].astype(F32) + norm_back(part, gain[...], scaled, inverse))

    for_rows(grad.shape[0], step)


def feed_forward_kernel(
    block_rows, x, att_low, gain, shift, cot_in, w_out, w_up, w_down, qkv_in, att_in, den_in,
    output_out, gmixed_out, gn_out, sums, norm_out, pre_out, out_out, terms, down_a, down_b, down_c,
    wo, wu, wd, wsem, osem, output, gmixed, gatt, norm_cat, pre_cat, hidden, slope, cot_cat,
    stage, land, land_att, land_norm, swap_sent, swap_came, free, *scratch,
):
    take_scratch = Taker(scratch)
    slabs = take_scratch(slab_shapes(DOWN_WIDTHS))
    slab_a, slab_b, slab_c = slabs
    phases = take_scratch([stream_scratch(length, (0,)) for length in DOWN_WIDTHS])
    place = Place()
    core = place.core
    rows = x.shape[0]
    others = link_neighbours(place)
    greet(others)
    own, other = pl.ds(0, rows), pl.ds(rows, rows)
    mixed = gatt
    loads = []
    moves = ((w_out, wo), (w_up, wu), (w_down, wd), (cot_in, cot_cat))
    for slot in (0, 1, 3, 2):
        loads.append(pltpu.make_async_copy(*moves[slot], wsem.at[slot]))
        loads[-1].start()
    outs = []

    def leave(source, target):
        outs.append(pltpu.make_async_copy(source, target, osem.at[len(outs)]))
        outs[-1].start()

    cot = cot_cat.at[own]
    swap = Swap(place, stage, swap_sent, swap_came)
    loads[0].wait()

    def mix(columns):
        mixed[:, columns] = x[:, columns].astype(F32) + dot_nn(att_low[...], wo[:, columns])

    for_columns(1024, TILE, mix)

    def norm_step(index):
        scaled, _ = norm_rows(mixed[index, :])
        norm_cat[index, :] = (scaled * gain[...] + shift[...]).astype(BF16)

    for_rows(rows, norm_step)
    met(len(others))
    loads[1].wait()

    def up(columns):
        ours, ours_slope = gelu_both(dot_nn(norm_cat[own, :], wu[:, columns]))
        hidden[:, columns] = ours
        slope[:, columns] = ours_slope
        return ours

    def give(block, carry):
        theirs = up(half_columns(block, 1 - core, 1024))
        swap.put(block, block, theirs, land.at[block])
        return carry

    lax.fori_loop(0, 4, give, 0)
    loads[2].wait()

    def take(block, carry):
        ours = up(half_columns(block, core, 1024))
        both = jnp.concatenate([ours, swap.get(block, land.at[block])], axis=0)
        for half in range(2):
            columns = pl.ds(half * TILE, TILE)
            product = tn_dot(both, cot_cat[:, columns]).reshape(4, 4, 4, 8, TILE)
            for stream in range(3):
                slabs[stream][block, :, :, :, columns] = product[:, :, stream]
            last = product[:, :, 3]
            if half == 0:
                slab_a[block, :, :, :, pl.ds(1024, 384)] = last[..., :384]
                slab_b[block, :, :, :, pl.ds(1024, 128)] = last[..., 384:]
            else:
                slab_b[block, :, :, :, pl.ds(1152, 256)] = last[..., :256]
                slab_c[block, :, :, :, pl.ds(1024, 256)] = last[..., 256:]
        return carry

    lax.fori_loop(0, 4, take, 0)
    pl.semaphore_signal(free, inc=1, device_id=place.partner(), device_id_type=MESH)
    down = [Stream(place, slabs[k], ORDERS[k], phases[k]) for k in range(3)]
    for stream in down:
        stream.prepare().begin_far()
    for stream in down:
        stream.phase.begin_near()
    for tile in range(2):
        columns = pl.ds(tile * TILE, TILE)
        swap.put(4 + tile, tile, norm_cat[own, columns], land_norm.at[tile], before=tile)
    loads[3].wait()

    def finish_forward(columns):
        output[:, columns] = (mixed[:, columns] + dot_nn(hidden[...], wd[:, columns])).astype(BF16)

    for_columns(1024, 256, finish_forward)
    leave(output, output_out)

    def back(columns):
        grad = dot_nt(cot[...], wd[columns, :]) * slope[:, columns].astype(F32)
        low = grad.astype(BF16)
        hidden[:, columns] = low
        return low

    pl.semaphore_wait(free, 1)

    def give_back(block, carry):
        theirs = back(half_columns(block, 1 - core, 1024))
        before = jnp.where(block < 2, 4 + block, block)
        swap.put(6 + block, block, theirs, land.at[block], before=before)
        return carry

    lax.fori_loop(0, 4, give_back, 0)

    def take_back(block, carry):
        columns = pl.ds(pl.multiple_of(block * TILE, TILE), TILE)
        pre_cat[own, columns] = back(half_columns(block, core, 1024))
        pre_cat[other, columns] = swap.get(6 + block, land.at[block])
        return carry

    lax.fori_loop(0, 4, take_back, 0)
    leave(pre_cat, pre_out)
    for tile in range(2):
        columns = pl.ds(tile * TILE, TILE)
        norm_cat[other, columns] = swap.get(4 + tile, land_norm.at[tile])
        swap.put(10 + tile, tile, att_low[:, columns], land_att.at[tile], before=6 + tile)
    leave(norm_cat, norm_out)
    query_load = pltpu.make_async_copy(qkv_in.at[0], slope.at[:, pl.ds(0, 1024)], wsem.at[4])
    query_load.start()
    pl.semaphore_signal(free, inc=1, device_id=place.partner(), device_id_type=MESH)
    for stream in down:
        stream.forward()

    def back_up(columns):
        gmixed[:, columns] = dot_nt(hidden[...], wu[columns, :])

    for_columns(1024, 256, back_up)

    def store(index, values):
        gmixed[index, :] = values
        hidden[index, pl.ds(0, 1024)] = values.astype(BF16)

    norm_back_rows(mixed, gmixed, cot, gain, sums, store)
    leave(gmixed, gmixed_out)
    pl.semaphore_wait(free, 1)
    swap.put(12, 2, hidden[:, half_tile(0, 1 - core)], land_norm.at[0], before=8)

    def back_out(columns):
        gatt[:, columns] = dot_nt(hidden[:, pl.ds(0, 1024)], wo[columns, :])

    for_columns(1024, TILE, back_out)
    query_load.wait()
    ours = hidden[:, half_tile(0, core)]
    theirs = swap.get(12, land_norm.at[0])
    for tile in range(2):
        swap.copy(10 + tile, tile, land_att.at[tile]).wait_recv()
        for part, (start, width) in enumerate(((0, 384), (384, 128))):
            product = tn_dot(att_low[:, pl.ds(tile * TILE + start, width)], ours)
            theirs_att = land_att[tile, :, pl.ds(start, width)].astype(BF16)
            land[2 * tile + part, pl.ds(0, width), :] = product + tn_dot(theirs_att, theirs)
            leave(land.at[2 * tile + part, pl.ds(0, width)], out_out.at[pl.ds(tile * TILE + start, width)])
    for number, slot in ((9, 3), (10, 0), (11, 1), (12, 2)):
        swap.copy(number, slot, land_norm.at[0]).wait_send()
    state_loads = []
    for tile in range(2):
        columns = pl.ds(tile * TILE, TILE)
        for source, slot in ((att_in, tile), (den_in, 2 + tile)):
            state_loads.append(pltpu.make_async_copy(source.at[:, columns], stage.at[slot], wsem.at[5 + slot]))
            state_loads[-1].start()
    for copy in state_loads:
        copy.wait()
    first_wide = first_head(block_rows)

    def local_state(unit):
        index, columns = unit_slices(unit, block_rows)
        pair = lax.rem(unit, 8)
        within = pl.ds(pl.multiple_of(lax.rem(pair, 4) * PAIR, PAIR), PAIR)
        tile = lax.div(pair, 4)
        numer = gatt[index, columns] / stage[2 + tile, index, within]
        gatt[index, columns] = numer
        query = features(slope[index, columns].astype(F32))
        blocks, row = state_gradient(query, numer, stage[tile, index, within], first_wide)
        terms[unit, pl.ds(0, 64)] = blocks
        terms[unit, pl.ds(64, 8)] = row

    for_units(local_state, 2)
    leave(gatt, gn_out)
    for stream, target in zip(down, (down_a, down_b, down_c)):
        stream.finish()
        leave(stream.data, target)
    for stream in down:
        stream.drain()
    for copy in outs:
        copy.wait()


def slab_shapes(widths):
    return [pltpu.VMEM((4, 4, 4, 8, width), F32) for width in widths]


def struct(shape, dtype=F32):
    return jax.ShapeDtypeStruct(shape, dtype)


VMEM_SPEC = pl.BlockSpec(memory_space=pltpu.VMEM)
ANY_SPEC = pl.BlockSpec(memory_space=pl.ANY)


def call(kernel, outs, out_specs, operands, in_specs, scratch, collective_id):
    return pl.pallas_call(
        kernel,
        out_shape=outs,
        in_specs=in_specs,
        out_specs=out_specs,
        scratch_shapes=scratch,
        compiler_params=pltpu.CompilerParams(
            collective_id=collective_id, has_side_effects=True, vmem_limit_bytes=63 * MIB
        ),
    )(*operands)


def feed_forward(x, att_low, gain, shift, cot_cat, w_out, w_up, w_down, qkv, att, den, block):
    rows, width = x.shape
    wide = w_up.shape[1]
    outs = [
        struct((rows, width), BF16),
        struct((rows, width)),
        struct((rows, width)),
        struct((8, width)),
        struct((2 * rows, width), BF16),
        struct((2 * rows, wide // 2), BF16),
        struct((width, TILE)),
        struct((SEQ, 72, PAIR)),
        *[struct((4, 4, 8, length)) for length in DOWN_WIDTHS],
    ]
    scratch = [
        pltpu.VMEM((width, width), BF16),
        pltpu.VMEM((width, wide), BF16),
        pltpu.VMEM((wide, width), BF16),
        pltpu.SemaphoreType.DMA((9,)),
        pltpu.SemaphoreType.DMA((12,)),
        pltpu.VMEM((rows, width), BF16),
        pltpu.VMEM((rows, width), F32),
        pltpu.VMEM((rows, width), F32),
        pltpu.VMEM((2 * rows, width), BF16),
        pltpu.VMEM((2 * rows, wide // 2), BF16),
        pltpu.VMEM((rows, wide), BF16),
        pltpu.VMEM((rows, wide), BF16),
        pltpu.VMEM((2 * rows, width), BF16),
        pltpu.VMEM((4, rows, TILE), F32),
        pltpu.VMEM((4, rows, TILE), F32),
        pltpu.VMEM((2, rows, TILE), F32),
        pltpu.VMEM((2, rows, TILE), F32),
        pltpu.SemaphoreType.DMA((13,)),
        pltpu.SemaphoreType.DMA((13,)),
        pltpu.SemaphoreType.REGULAR,
        *slab_shapes(DOWN_WIDTHS),
        *flatten([stream_scratch(length, (0,)) for length in DOWN_WIDTHS]),
    ]
    specs = [VMEM_SPEC] * 4 + [ANY_SPEC] * 7
    out_specs = [ANY_SPEC] * 3 + [VMEM_SPEC] + [ANY_SPEC] * 3 + [VMEM_SPEC] + [ANY_SPEC] * 3
    operands = (x, att_low, gain, shift, cot_cat, w_out, w_up, w_down, qkv, att, den)

    def kernel(*refs):
        feed_forward_kernel(block, *refs)

    return call(kernel, outs, out_specs, operands, specs, scratch, 1)


def last_scratch(rows, width):
    return {
        "qkv": pltpu.VMEM((3, rows, width), BF16),
        "att": pltpu.VMEM((rows, width), F32),
        "gn": pltpu.VMEM((rows, width), F32),
        "state": pltpu.VMEM((SEQ, 72, PAIR), F32),
        "x": pltpu.VMEM((rows, width), BF16),
        "grads": pltpu.VMEM((2, rows, width), F32),
        "scan": list(SCAN_SCRATCH[:3]) + [SCAN_SCRATCH[0]] + list(SCAN_SCRATCH[3:]),
        "norm_cat": pltpu.VMEM((2, 2 * rows, width // 2), BF16),
        "pre_cat": pltpu.VMEM((2 * rows, 2 * width), BF16),
        "w": pltpu.VMEM((width, 3 * width), BF16),
        "stage": pltpu.VMEM((3, rows, TILE), F32),
        "land": pltpu.VMEM((3, rows, TILE), F32),
        "swap": [pltpu.SemaphoreType.DMA((3,)), pltpu.SemaphoreType.DMA((3,))],
        "slabs": slab_shapes(UP_WIDTHS),
        "chunks": [pltpu.VMEM((4, 4, 8, length), F32) for length in DOWN_WIDTHS],
        "up_chunks": [pltpu.VMEM((4, 4, 8, length), F32) for length in UP_WIDTHS],
        "out_slabs": slab_shapes(OUT_WIDTHS),
        "vec_slab": pltpu.VMEM((4, 4, 4, 8, 128), F32),
        "sums": pltpu.VMEM((8, width), F32),
        "down": [stream_scratch(length, (1, 2), (2,)) for length in DOWN_WIDTHS],
        "up": [stream_scratch(length, (0, 1, 2), (2,)) for length in UP_WIDTHS],
        "out": [stream_scratch(length, (0, 1, 2), (1, 2)) for length in OUT_WIDTHS],
        "qkv_sems": [[pltpu.SemaphoreType.DMA((6,))] * 2 for _ in QKV_WIDTHS],
        "qkv_sum": [stream_scratch(length, (1, 2), (2,)) for length in QKV_WIDTHS],
        "vec": stream_scratch(128, (0, 1, 2), (0, 1, 2)),
        "up_rows": [pltpu.VMEM((2, 8, 2048), F32), pltpu.VMEM((8, 2048), F32)],
        "out_rows": [pltpu.VMEM((2, 8, 512), F32), pltpu.VMEM((8, 512), F32)],
        "qkv_rows": [pltpu.VMEM((2, 8, 1536), F32), pltpu.VMEM((8, 1536), F32)],
        "row_sems": pltpu.SemaphoreType.DMA((3, 2)),
        "vec_land": pltpu.VMEM((8, 128), F32),
        "vec_sems": pltpu.SemaphoreType.DMA((2,)),
        "credit": pltpu.SemaphoreType.REGULAR((3,)),
        "loads": pltpu.SemaphoreType.DMA((32,)),
    }


def last_kernel(
    block, qkv_in, att_in, terms_in, state_in, gn_in, gmixed_in, norm_one_in, norm_in, pre_in,
    down_in_a, down_in_b, down_in_c, out_in, x_in, weight, gain, sums_two,
    grad_input, grad_up, grad_out, grad_qkv, grad_down, grad_gains, *scratch,
):
    place = Place()
    core = place.core
    rows, width = att_in.shape
    like = last_scratch(rows, width)
    take = Taker(scratch)
    s = {name: take(like[name]) for name in like}
    qkv, att, gn, grads = s["qkv"], s["att"], s["gn"], s["grads"]
    slabs = s["slabs"]
    scan = Scan(*s["scan"][:4], s["scan"][4:], True)
    across = [place.neighbour(0, step) for step in (1, -1, 2)]
    others = [*across, place.partner(), *scan.others()]
    greet(others)
    loads = []

    def load(source, target):
        copy = pltpu.make_async_copy(source, target, s["loads"].at[len(loads)])
        copy.start()
        loads.append(copy)
        return copy

    started = load(terms_in, scan.terms)
    down_in = (down_in_a, down_in_b, down_in_c)
    down_loads = [load(source, target) for source, target in zip(down_in, s["chunks"])]
    up_loads = [load(pre_in, s["pre_cat"])]
    for which in range(2):
        for block_x in range(4):
            source = norm_in.at[:, pl.ds(block_x * 256 + which * 128, 128)]
            target = s["norm_cat"].at[which, :, pl.ds(block_x * 128, 128)]
            up_loads.append(load(source, target))
    qkv_loads = [load(qkv_in, qkv), load(state_in, s["state"]), load(gn_in, gn), load(att_in, att)]
    out_loads = []
    for k in range(3):
        for which, start, length, at in stream_pieces(k, OUT_WIDTHS, TILE):
            source = out_in.at[:, which, :, :, :, pl.ds(start, length)]
            target = s["out_slabs"][k].at[:, :, :, :, pl.ds(at, length)]
            out_loads.append(load(source, target))
    late_loads = [load(weight, s["w"]), load(x_in, s["x"])]

    def settle(copies):
        for copy in copies:
            copy.wait()

    first, second = head_masks()
    first_wide = first_head(block)

    up_first = [phases[0] for phases in s["up"]]
    down = [Stream(place, s["chunks"][k], ORDERS[k][1:], s["down"][k]) for k in range(3)]
    up = [Stream(place, slabs[k], ORDERS[k], s["up"][k]) for k in range(3)]
    out = [Stream(place, s["out_slabs"][k], ORDERS[k], s["out"][k]) for k in range(3)]
    qkv_sum = [None] * 3
    vec = [Stream(place, s["vec_slab"], ORDERS[0], s["vec"])]
    begin, forward, proceed, finish = Stream.begin, Stream.forward, Stream.proceed, Stream.finish

    def go(*steps):
        for step, streams, k in steps:
            step(streams[k])

    started.wait()
    met(len(others))
    scan.start()
    settle(down_loads)
    for stream in down:
        stream.begin()
    settle(up_loads)
    for k in range(3):
        stream_product(k, s["norm_cat"], s["pre_cat"], slabs[k], UP_WIDTHS, 2048)
        if k == 0:
            up[0].begin()
        if k == 1:
            go((forward, down, 2))
    norm_load = load(norm_one_in, s["norm_cat"])
    settle(qkv_loads)
    causal = causal_mask(block)
    causal_t = causal_mask(block, True)

    def local_part(unit):
        index, columns = unit_slices(unit, block)
        raw_query = qkv[0, index, columns].astype(F32)
        query, value = features(raw_query), qkv[2, index, columns]
        key = features(qkv[1, index, columns].astype(F32))
        numer = gn[index, columns]
        one, two = head_slopes(numer, att[index, columns], first_wide)
        high, low = split(numer)
        scores = dot_nt(jnp.concatenate([key * first, key * second], axis=0), query)
        wide = jnp.concatenate([high, low], axis=1)
        values = jnp.concatenate([value, value], axis=1)
        grad_query, grad_key, grad_value = 0.0, 0.0, 0.0
        for head, (mask, slope) in enumerate(((first, one), (second, two))):
            mask_wide = jnp.concatenate([mask, mask], axis=1)
            mixing = jnp.where(causal, dot_nt(wide * mask_wide, values) + slope, 0.0).astype(BF16)
            turned = jnp.where(causal_t, scores[head * block : (head + 1) * block], 0.0)
            grad_query = grad_query + dot_nn(mixing, key * mask)
            grad_key = grad_key + tn_dot(mixing, query * mask)
            grad_value = grad_value + dot_nn(turned.astype(BF16), high * mask)
        square, total = unpack_state(s["state"][unit])
        state_high, state_low = split(square)
        grad_query = grad_query + dot_nn(wide, jnp.concatenate([state_high, state_high], axis=0))
        grad_query = grad_query + dot_nn(high, state_low)
        grad_query = grad_query + jnp.where(first_wide, one, two) * total
        qkv[0, index, columns] = (grad_query * feature_slope(raw_query)).astype(BF16)
        grads[0, index, columns] = grad_key
        grads[1, index, columns] = grad_value

    def local_parts(start, count):
        def one(index, carry):
            local_part(start + index)
            return carry

        lax.fori_loop(0, count, one, 0)

    local_parts(0, 2)
    scan.middle()
    go((forward, down, 0), (forward, down, 1))
    up[1].begin()
    up[2].begin()
    local_parts(2, 8)
    go((forward, up, 0))
    local_parts(10, 6)
    settle(out_loads)
    swap = Swap(place, s["stage"], *s["swap"])
    land, cat = s["land"], s["pre_cat"]
    own, other = pl.ds(0, rows), pl.ds(rows, rows)
    swap.put(0, 0, qkv[0, :, half_tile(0, 1 - core)], land.at[0])
    mixed_load = load(gmixed_in, att)
    scan.finish(0)
    scan.finish(1)

    def incoming(unit):
        index, columns = unit_slices(unit, block)
        square, total = unpack_state(scan.result[unit])
        high, low = split(square)
        raw_key = qkv[1, index, columns].astype(F32)
        key, value = features(raw_key), qkv[2, index, columns]
        grad_key = grads[0, index, columns] + total
        grad_key = grad_key + dot_nt(
            jnp.concatenate([value, value], axis=1), jnp.concatenate([high, low], axis=1)
        )
        grad_value = grads[1, index, columns] + dot_nn(
            jnp.concatenate([key, key], axis=1), jnp.concatenate([high, low], axis=0)
        )
        qkv[1, index, columns] = (grad_key * feature_slope(raw_key)).astype(BF16)
        qkv[2, index, columns] = grad_value.astype(BF16)

    for_units(incoming, 2)
    for third in (1, 2):
        swap.put(third, third, qkv[third, :, half_tile(0, 1 - core)], land.at[third])
    go((proceed, down, 2), (proceed, down, 0), (proceed, down, 1))
    settle(late_loads)

    def back_norm(columns):
        total = 0.0
        for third in range(3):
            total = total + dot_nt(qkv[third], s["w"][columns, pl.ds(third * 1024, 1024)])
        gn[:, columns] = total

    for start in (0, 256, 512, 768):
        back_norm(pl.ds(start, 256))
        if start == 0:
            go((forward, up, 1), (forward, up, 2))
    for third in range(3):
        columns = pl.ds(third * TILE, TILE)
        cat[own, columns] = qkv[third, :, half_tile(0, core)]
        cat[other, columns] = swap.get(third, land.at[third])
    norm_load.wait()
    mixed_load.wait()
    def turn(k):
        up[k].finish(s["up_chunks"][k])
        up[k].drain()
        for step in (1, -1):
            pl.semaphore_signal(
                s["credit"].at[k],
                inc=1,
                device_id=place.neighbour(ORDERS[k][0], step),
                device_id_type=MESH,
            )
        narrow = (slice(None),) * 4 + (pl.ds(0, QKV_WIDTHS[k]),)
        data = slabs[k].at[narrow]
        stream_product(k, s["norm_cat"], cat, data, QKV_WIDTHS, 3 * TILE)
        pl.semaphore_wait(s["credit"].at[k], 2)
        phases = [[up_first[k][0].at[narrow], up_first[k][1].at[narrow], *s["qkv_sems"][k]]]
        qkv_sum[k] = Stream(place, data, ORDERS[k], phases + s["qkv_sum"][k])
        qkv_sum[k].begin()

    def store(index, values):
        gn[index, :] = values

    sums = s["sums"]
    norm_back_rows(s["x"], gn, att, gain, sums, store)
    leave = load(gn, grad_input)
    four = jnp.concatenate([sums[0:2, :], sums_two[0:2, :]], axis=0)
    eight = jnp.concatenate([four, four], axis=0)
    turned = jnp.transpose(jnp.concatenate([eight, jnp.zeros((120, 1024), F32)], axis=0))
    turned = turned.reshape(4, 2, 4, 4, 8, 128)
    lane = lax.broadcasted_iota(jnp.int32, (8, 128), 1)
    s["vec_slab"][...] = jnp.where(lane < 4, turned[:, 0], jnp.where(lane < 8, turned[:, 1], 0.0))
    for stream in out:
        stream.begin()
    turn(0)
    go((forward, out, 0))
    turn(1)
    go((forward, out, 2), (forward, out, 1))
    turn(2)
    go(
        (proceed, out, 2), (finish, down, 1), (finish, down, 2), (finish, down, 0), (begin, vec, 0),
        (forward, qkv_sum, 0), (forward, qkv_sum, 1), (forward, qkv_sum, 2), (begin, up, 0), (begin, up, 1),
        (begin, up, 2), (proceed, out, 1), (proceed, out, 0), (proceed, vec, 0), (proceed, qkv_sum, 1),
        (proceed, qkv_sum, 2), (proceed, qkv_sum, 0), (forward, up, 0), (forward, up, 1), (forward, up, 2),
        (forward, qkv_sum, 1), (forward, qkv_sum, 2), (forward, qkv_sum, 0), (proceed, out, 2), (proceed, vec, 0),
        (proceed, out, 0), (proceed, out, 1), (proceed, up, 0), (proceed, qkv_sum, 1), (proceed, qkv_sum, 2),
        (proceed, qkv_sum, 0), (proceed, up, 1), (proceed, up, 2), (finish, out, 2), (finish, out, 0),
        (finish, out, 1), (finish, vec, 0), (finish, up, 0), (finish, up, 1), (finish, up, 2),
    )
    for k in range(3):
        piece = down[k].data
        grad_down[pl.ds(8 * k, 8), :] = piece[:, pl.ds(0, 1024)]
        start, width_k = DOWN_CUTS[k]
        grad_down[pl.ds(24, 8), pl.ds(start, width_k)] = piece[:, pl.ds(1024, width_k)]
    swaps = []

    def swap_rows(streams, widths, columns, rows_land, slot):
        shared_rows(streams, widths, columns, rows_land[0])
        copy = row_swap(place, *rows_land, s["row_sems"].at[slot])
        copy.start()
        swaps.append(copy)

    swap_rows(up, UP_WIDTHS, 2048, s["up_rows"], 0)
    vec_tile = vec[0].data
    vec_copy = pltpu.make_async_remote_copy(
        src_ref=vec_tile,
        dst_ref=s["vec_land"],
        send_sem=s["vec_sems"].at[0],
        recv_sem=s["vec_sems"].at[1],
        device_id=place.partner(),
        device_id_type=MESH,
    )
    vec_copy.start()
    swap_rows(out, OUT_WIDTHS, TILE, s["out_rows"], 1)
    go((finish, qkv_sum, 1), (finish, qkv_sum, 0), (finish, qkv_sum, 2))
    swap_rows(qkv_sum, QKV_WIDTHS, 3 * TILE, s["qkv_rows"], 2)
    scan.drain()
    for number in range(3):
        swap.copy(number, number, land.at[number]).wait_send()
    for stream in (*down, *up, *out, *qkv_sum, *vec):
        stream.drain()
    vec_copy.wait()
    grad_gains[...] = vec_tile[...] + s["vec_land"][...]
    leave.wait()
    swaps[0].wait()
    lay_rows(place, *s["up_rows"], grad_up)
    swaps[1].wait()
    lay_rows(place, *s["out_rows"], grad_out)
    swaps[2].wait()
    lay_rows(place, *s["qkv_rows"], grad_qkv)


def last_part(qkv, att, terms, state, gn, gmixed, norm_one, norm_cat, pre_cat, down, out, x, weight, gain, sums_two, block):
    rows, width = x.shape

    def kernel(*refs):
        last_kernel(block, *refs)

    outs = [
        struct((rows, width)),
        struct((8, 4096)),
        struct((8, width)),
        struct((8, 3 * width)),
        struct((32, width)),
        struct((8, 128)),
    ]
    like = last_scratch(rows, width)
    scratch = [leaf for name in like for leaf in flatten(like[name])]
    out = out.reshape(4, 2, 4, 4, 8, TILE)
    operands = (
        qkv, att, terms, state, gn, gmixed, norm_one, norm_cat, pre_cat, *down, out, x, weight, gain, sums_two,
    )
    specs = [ANY_SPEC] * 15 + [VMEM_SPEC] * 2
    out_specs = [ANY_SPEC] + [VMEM_SPEC] * 5
    return call(kernel, outs, out_specs, operands, specs, scratch, 2)


def lay_out_kernel(gains, *refs):
    targets = refs[-4:]
    core = lax.rem(lax.axis_index("dp"), 2)
    turned = jnp.transpose(jnp.concatenate([gains[...], jnp.zeros((120, 128), F32)], axis=0))
    for k, target in enumerate(targets):
        target[...] = jnp.where(core == 0, turned[k : k + 1, :8], turned[4 + k : 5 + k, :8])


def lay_out(gains, *arrays):
    count = len(arrays)
    return pl.pallas_call(
        lay_out_kernel,
        out_shape=[struct(array.shape, array.dtype) for array in arrays] + [struct((1, 8))] * 4,
        in_specs=[VMEM_SPEC] + [ANY_SPEC] * count,
        out_specs=[ANY_SPEC] * count + [VMEM_SPEC] * 4,
        input_output_aliases={k + 1: k for k in range(count)},
        compiler_params=pltpu.CompilerParams(vmem_limit_bytes=62 * MIB),
    )(gains, *arrays)


def body(
    inputs,
    first_gain,
    first_shift,
    qkv_weight,
    out_weight,
    second_gain,
    second_shift,
    up_weight,
    down_weight,
    cotangent,
):
    sequences, block, width = inputs.shape
    rows = sequences * block
    x = inputs.reshape(rows, width)
    cot = cotangent.reshape(rows, width)
    gain_one, gain_two = first_gain.reshape(1, width), second_gain.reshape(1, width)
    shift_two = second_shift.reshape(1, width)
    norm_one, cot_cat, qkv, att, att_low, den, state = attention_forward(
        x, first_gain, first_shift, qkv_weight, cot, block
    )
    output, gmixed, gn, sums_two, norm_cat, pre_cat, out, terms, *down = feed_forward(
        x, att_low, gain_two, shift_two, cot_cat, out_weight, up_weight, down_weight, qkv, att, den, block
    )
    grads = last_part(
        qkv, att, terms, state, gn, gmixed, norm_one, norm_cat, pre_cat, down, out, x, qkv_weight,
        gain_one, sums_two, block,
    )
    *grads, gains = grads
    output, grad_input, grad_up, grad_out, grad_qkv, grad_down, *gains = lay_out(gains, output, *grads)
    return (
        output.reshape(inputs.shape),
        grad_input.reshape(inputs.shape),
        grad_qkv,
        grad_out,
        grad_up,
        grad_down,
        *[gain.reshape(8) for gain in gains],
    )


def solution(mesh):
    return jax.shard_map(
        body,
        mesh=mesh,
        in_specs=(
            P("dp", "seq", None),
            P(),
            P(),
            P(),
            P(),
            P(),
            P(),
            P(),
            P(),
            P("dp", "seq", None),
        ),
        out_specs=(
            P("dp", "seq", None),
            P("dp", "seq", None),
            P(("dp", "seq"), None),
            P(("dp", "seq"), None),
            P(("dp", "seq"), None),
            P(("dp", "seq"), None),
            P(("dp", "seq")),
            P(("dp", "seq")),
            P(("dp", "seq")),
            P(("dp", "seq")),
        ),
        check_vma=False,
    )
```

```python
import math

import jax
import jax.numpy as jnp
from jax import lax
from jax.experimental import pallas as pl
from jax.experimental.pallas import tpu as pltpu
from jax.sharding import PartitionSpec as P

MESH = pl.DeviceIdType.MESH
F32 = jnp.float32
BF16 = jnp.bfloat16
RING = 4
MIB = 2**20


class Place:
    def __init__(self):
        dp, seq = lax.axis_index("dp"), lax.axis_index("seq")
        self.core = lax.rem(dp, 2)
        self.at = (lax.div(dp, 2), lax.div(seq, RING), lax.rem(seq, RING))

    def id_of(self, x, y, z, core):
        return (x * 2 + core, y * RING + z)

    def ring(self, axis, step):
        return lax.rem(self.at[axis] + (step + RING), RING)

    def neighbour(self, axis, step):
        at = list(self.at)
        at[axis] = self.ring(axis, step)
        return self.id_of(*at, self.core)

    def partner(self):
        return self.id_of(*self.at, 1 - self.core)


def greet(others):
    barrier = pltpu.get_barrier_semaphore()
    for other in others:
        pl.semaphore_signal(barrier, inc=1, device_id=other, device_id_type=MESH)


def met(count):
    pl.semaphore_wait(pltpu.get_barrier_semaphore(), count)


def link_neighbours(place):
    others = [place.neighbour(axis, step) for axis in range(3) for step in (1, -1)]
    return [*others, place.partner()]


ORDERS = ((0, 1, 2), (1, 2, 0), (2, 0, 1))


def phase_scratch(remaining, length, messages=6):
    if remaining:
        half = (2, 2, *[4] * (remaining - 1), 8, length)
    else:
        half = (2, 8, (length // 128 + 1) // 2 * 128)
    return [
        pltpu.VMEM((2, *[4] * remaining, 8, length), F32),
        pltpu.VMEM(half, F32),
        pltpu.SemaphoreType.DMA((messages,)),
        pltpu.SemaphoreType.DMA((messages,)),
    ]


class Phase:
    def __init__(self, place, data, axes, axis, scratch):
        self.place, self.data, self.axis = place, data, axis
        self.where = axes.index(axis)
        self.full, self.half, self.sent, self.came = scratch
        self.flying = []
        self.flat = len(axes) == 1
        self.length = data.shape[-1]
        self.cut = (self.length // 128 + 1) // 2 * 128
        self.whole = self.flat and self.cut == self.length

    def empty(self, which):
        return self.whole and which == 1

    def chunk(self, target):
        index = [slice(None)] * self.where + [target]
        return self.data.at[tuple(index)]

    def part(self, ref, which):
        if not self.flat:
            return ref.at[pl.ds(2 * which, 2)]
        if which == 0:
            return ref.at[:, pl.ds(0, self.cut)]
        return ref.at[:, pl.ds(self.cut, self.length - self.cut)]

    def through(self, way):
        ref = self.half.at[way]
        if self.flat and way == 1:
            return ref.at[:, pl.ds(0, self.length - self.cut)]
        return ref

    def copy(self, kind, way, source, target):
        number = kind * 2 + way
        return pltpu.make_async_remote_copy(
            src_ref=source,
            dst_ref=target,
            send_sem=self.sent.at[number],
            recv_sem=self.came.at[number],
            device_id=self.place.neighbour(self.axis, 1 - 2 * way),
            device_id_type=MESH,
        )

    def send(self, kind, way, source, target):
        copy = self.copy(kind, way, source, target)
        copy.start()
        self.flying.append(copy)

    def beside(self, way):
        return self.chunk(self.place.ring(self.axis, 1 - 2 * way))

    def begin_far(self):
        opposite = self.chunk(self.place.ring(self.axis, 2))
        for way in range(2):
            if not self.empty(way):
                self.send(0, way, self.part(opposite, way), self.through(way))

    def begin_near(self, way):
        if not self.empty(1 - way):
            target = self.part(self.full.at[way], 1 - way)
            self.send(1, way, self.part(self.beside(way), 1 - way), target)

    def begin(self):
        self.begin_far()
        for way in range(2):
            self.begin_near(way)

    def forward(self):
        for way in range(2):
            if self.empty(way):
                continue
            came = self.through(way)
            self.copy(0, way, came, came).wait_recv()
            own = self.part(self.beside(way), way)
            add_into(own, own, came)
            self.send(2, way, own, self.part(self.full.at[way], way))

    def finish(self, out=None):
        own = self.chunk(self.place.at[self.axis])
        for way in range(2):
            for kind, which in ((1, 1 - way), (2, way)):
                if self.empty(which):
                    continue
                target = self.part(self.full.at[way], which)
                self.copy(kind, way, target, target).wait_recv()
        add_into(own if out is None else out, own, self.full.at[0], self.full.at[1])
        return own

    def drain(self):
        for copy in self.flying:
            copy.wait_send()


HALVES = ((2, 1), (3, 0))


class SplitPhase(Phase):
    def block(self, way, j):
        return self.place.ring(0, HALVES[way][j])

    def copy_block(self, kind, way, j, source, target):
        number = kind * 4 + way * 2 + j
        return pltpu.make_async_remote_copy(
            src_ref=source,
            dst_ref=target,
            send_sem=self.sent.at[number],
            recv_sem=self.came.at[number],
            device_id=self.place.neighbour(self.axis, 1 - 2 * way),
            device_id_type=MESH,
        )

    def send_far(self, way, j):
        source = self.chunk(self.place.ring(self.axis, 2)).at[self.block(way, j)]
        self.flying.append(self.copy_block(0, way, j, source, self.half.at[way, j]))
        self.flying[-1].start()

    def send_near(self, kind, way, j):
        block = self.block(way if kind == 2 else 1 - way, j)
        source, target = self.beside(way).at[block], self.full.at[way, block]
        self.flying.append(self.copy_block(kind, way, j, source, target))
        self.flying[-1].start()

    def begin_first(self):
        for j in range(2):
            self.send_far(0, j)
        self.send_near(1, 1, 0)

    def begin_second(self):
        for j in range(2):
            self.send_far(1, j)
        self.send_near(1, 1, 1)
        for j in range(2):
            self.send_near(1, 0, j)

    def forward(self):
        for way in range(2):
            for j in range(2):
                came = self.half.at[way, j]
                self.copy_block(0, way, j, came, came).wait_recv()
                own = self.beside(way).at[self.block(way, j)]
                add_into(own, own, came)
                self.send_near(2, way, j)

    def finish(self, out=None):
        own = self.chunk(self.place.at[self.axis])
        for way in range(2):
            for kind, part in ((1, 1 - way), (2, way)):
                for j in range(2):
                    target = self.full.at[way, self.block(part, j)]
                    self.copy_block(kind, way, j, target, target).wait_recv()
        add_into(own if out is None else out, own, self.full.at[0], self.full.at[1])
        return own


class Direct:
    def __init__(self, place, data, axes, axis, scratch):
        self.place, self.data, self.axis = place, data, axis
        self.where = axes.index(axis)
        self.full, self.sent, self.came = scratch
        self.flying = []

    def chunk(self, target):
        index = [slice(None)] * self.where + [target]
        return self.data.at[tuple(index)]

    def copy(self, step, source):
        return pltpu.make_async_remote_copy(
            src_ref=source,
            dst_ref=self.full.at[step - 1],
            send_sem=self.sent.at[step - 1],
            recv_sem=self.came.at[step - 1],
            device_id=self.place.neighbour(self.axis, step),
            device_id_type=MESH,
        )

    def begin(self):
        for step in (2, 1, 3):
            copy = self.copy(step, self.chunk(self.place.ring(self.axis, step)))
            copy.start()
            self.flying.append(copy)

    def forward(self):
        pass

    def finish(self, out=None):
        own = self.chunk(self.place.at[self.axis])
        for step in (1, 2, 3):
            self.copy(step, self.full.at[step - 1]).wait_recv()
        add_into(own if out is None else out, own, *[self.full.at[k] for k in range(3)])
        return own

    def drain(self):
        for copy in self.flying:
            copy.wait_send()


class Route:
    def __init__(self, place, data, axis, pieces, scratch, out):
        self.place, self.data, self.axis, self.pieces, self.out = place, data, axis, pieces, out
        self.scratch = scratch

    def send_each(self, act):
        core = self.place.core
        for (owner, _, width, at), (land, sent, came) in zip(self.pieces, self.scratch):

            def copy(step):
                position = list(self.place.at)
                position[self.axis] = self.place.ring(self.axis, step)
                return pltpu.make_async_remote_copy(
                    src_ref=self.data.at[self.place.ring(self.axis, step), :, pl.ds(at, width)],
                    dst_ref=land.at[core, step],
                    send_sem=sent.at[step],
                    recv_sem=came.at[core, step],
                    device_id=self.place.id_of(*position, owner),
                    device_id_type=MESH,
                )

            for step in (2, 1, 3):
                act(copy(step))

            @pl.when(core != owner)
            def _():
                act(copy(0))

    def begin(self):
        self.send_each(lambda copy: copy.start())

    def forward(self):
        pass

    def finish(self, out=None):
        core = self.place.core
        mine = self.place.at[self.axis]
        for (owner, start, width, at), (land, sent, came) in zip(self.pieces, self.scratch):

            @pl.when(core == owner)
            def _():
                for source, steps in ((core, (1, 2, 3)), (1 - core, (0, 1, 2, 3))):
                    for step in steps:
                        target = land.at[source, step]
                        pltpu.make_async_remote_copy(
                            src_ref=target,
                            dst_ref=target,
                            send_sem=sent.at[step],
                            recv_sem=came.at[source, step],
                            device_id=self.place.partner(),
                            device_id_type=MESH,
                        ).wait_recv()
                done = 0
                while done < width:
                    column = start + done
                    tile, within = column // TILE, column % TILE
                    step = min(TILE - within, width - done)
                    part = pl.ds(done, step)
                    ours = self.data[mine, :, pl.ds(at + done, step)]
                    for k in (1, 2, 3):
                        ours = ours + land[core, k, :, part]
                    theirs = land[1 - core, 0, :, part]
                    for k in (1, 2, 3):
                        theirs = theirs + land[1 - core, k, :, part]
                    for values, half in ((ours, core), (theirs, 1 - core)):
                        place = pl.multiple_of((2 * tile + half) * TILE + within, 128)
                        self.out[:, pl.ds(place, step)] = values
                    done += step

    def drain(self):
        self.send_each(lambda copy: copy.wait_send())


def route_scratch(stream, widths, columns):
    return [
        [
            pltpu.VMEM((2, 4, 8, width), F32),
            pltpu.SemaphoreType.DMA((4,)),
            pltpu.SemaphoreType.DMA((2, 4)),
        ]
        for _, _, width, _ in stream_pieces(stream, widths, columns)
    ]


class Stream:
    def __init__(self, place, data, order, scratch, first=None, last=None):
        self.place, self.data, self.scratch, self.first, self.last = place, data, scratch, first, last
        self.todo, self.old = [axis for axis in order], []
        self.axes = sorted(order)
        self.phase = None

    def prepare(self):
        scratch = self.scratch.pop(0)
        if self.last and len(self.todo) == 1:
            pieces, out = self.last
            self.phase = Route(self.place, self.data, self.todo[0], pieces, scratch, out)
            return self.phase
        kind = self.first or (Phase if len(scratch) == 4 else Direct)
        self.first = None
        self.phase = kind(self.place, self.data, self.axes, self.todo[0], scratch)
        return self.phase

    def begin(self):
        self.prepare().begin()

    def forward(self):
        self.phase.forward()

    def finish(self, out=None):
        own = self.phase.finish(out)
        self.data = own if out is None else out
        self.axes.remove(self.todo.pop(0))
        self.old.append(self.phase)

    def proceed(self):
        self.finish()
        self.begin()

    def drain(self):
        for phase in self.old:
            phase.drain()
        self.old = []


def direct_scratch(remaining, length):
    return [
        pltpu.VMEM((3, *[4] * remaining, 8, length), F32),
        pltpu.SemaphoreType.DMA((3,)),
        pltpu.SemaphoreType.DMA((3,)),
    ]


def stream_scratch(length, phases, direct=()):
    return [
        (direct_scratch if phase in direct else phase_scratch)(2 - phase, length)
        for phase in phases
    ]


class Taker:
    def __init__(self, refs):
        self.refs = list(refs)

    def __call__(self, like):
        if isinstance(like, list):
            return [self(item) for item in like]
        return self.refs.pop(0)


def flatten(items):
    if isinstance(items, list):
        return [leaf for item in items for leaf in flatten(item)]
    return [items]


def add_into(out, *terms):
    if len(out.shape) > 2:

        def row(index, carry):
            add_into(out.at[index], *[term.at[index] for term in terms])
            return carry

        if len(out.shape) == 4:
            lax.fori_loop(0, out.shape[0], row, 0)
        else:
            for index in range(out.shape[0]):
                row(index, 0)
        return
    total = terms[0][...]
    for term in terms[1:]:
        total = total + term[...]
    out[...] = total


def tn_dot(left, right):
    return lax.dot_general(left, right, (((0,), (0,)), ((), ())), preferred_element_type=F32)


TILE = 512


class Swap:
    def __init__(self, place, stage, sent, came):
        self.place, self.stage, self.sent, self.came = place, stage, sent, came

    def copy(self, number, slot, target):
        return pltpu.make_async_remote_copy(
            src_ref=self.stage.at[slot],
            dst_ref=target,
            send_sem=self.sent.at[number],
            recv_sem=self.came.at[number],
            device_id=self.place.partner(),
            device_id_type=MESH,
        )

    def put(self, number, slot, values, target, before=None):
        if before is not None:
            self.copy(before, slot, target).wait_send()
        self.stage[slot] = values.astype(F32)
        self.copy(number, slot, target).start()

    def get(self, number, target):
        self.copy(number, 0, target).wait_recv()
        return target[...].astype(BF16)

    def drain(self, numbers, target):
        for number in numbers:
            self.copy(number, number % 4, target).wait_send()


def half_columns(block, core, quarter):
    half = quarter // 2
    return pl.ds(pl.multiple_of(block * quarter + core * half, half), half)


def half_tile(index, core):
    return pl.ds(pl.multiple_of((2 * index + core) * TILE, TILE), TILE)


def core_product(left, core, right, start, width, slab, at):
    done = 0
    while done < width:
        step = min(TILE, width - done)
        product = tn_dot(left[core], right[:, pl.ds(start + done, step)])
        slab[:, :, :, :, pl.ds(at + done, step)] = product.reshape(4, 4, 4, 8, step)
        done += step


UP_WIDTHS = (1536, 1280, 1280)
OUT_WIDTHS = (512, 256, 256)
QKV_WIDTHS = (1152, 896, 1024)


def stream_pieces(stream, widths, columns):
    if stream < 2:
        return [(stream, 0, widths[stream], 0)]
    pieces, at = [], 0
    for core in range(2):
        width = columns - widths[core]
        if width:
            pieces.append((core, widths[core], width, at))
        at += width
    return pieces


def stream_product(stream, left, right, slab, widths, columns):
    for core, start, width, at in stream_pieces(stream, widths, columns):
        core_product(left, core, right, start, width, slab, at)


DOWN_CUTS = ((0, 384), (384, 384), (768, 256))
DOWN_WIDTHS = (1408, 1408, 1280)


SEQ = 16
PAIR = 128
NT = (((1,), (1,)), ((), ()))
TN = (((0,), (0,)), ((), ()))


def dot_nt(left, right):
    return lax.dot_general(left, right, NT, preferred_element_type=F32)


def dot_nn(left, right):
    return jnp.dot(left, right, preferred_element_type=F32)


def split(values):
    high = values.astype(BF16)
    return high, (values - high.astype(F32)).astype(BF16)


def features(raw):
    return jnp.where(raw > 0, raw + 1.0, jnp.exp(jnp.minimum(raw, 0.0))).astype(BF16)


def feature_slope(raw):
    return jnp.where(raw > 0, 1.0, jnp.exp(jnp.minimum(raw, 0.0)))


def head_masks():
    lane = lax.broadcasted_iota(jnp.int32, (1, PAIR), 1)
    first = jnp.where(lane < 64, 1.0, 0.0)
    return first.astype(BF16), (1.0 - first).astype(BF16)


def first_head(rows):
    return lax.broadcasted_iota(jnp.int32, (rows, PAIR), 1) < 64


def pack_state(square, total):
    blocks = jnp.where(first_head(64), square[:64], square[64:])
    return blocks, jnp.broadcast_to(total, (8, PAIR))


def unpack_state(packed):
    first = first_head(64)
    square = jnp.concatenate(
        [jnp.where(first, packed[:64], 0.0), jnp.where(first, 0.0, packed[:64])], axis=0
    )
    return square, packed[64:65]


def same_head():
    row = lax.broadcasted_iota(jnp.int32, (PAIR, PAIR), 0)
    lane = lax.broadcasted_iota(jnp.int32, (PAIR, PAIR), 1)
    return (row < 64) == (lane < 64)


def head_slopes(numer, attended, first_wide):
    product = numer * attended
    ours = jnp.sum(jnp.where(first_wide, product, 0.0), axis=1, keepdims=True)
    theirs = jnp.sum(jnp.where(first_wide, 0.0, product), axis=1, keepdims=True)
    return -ours, -theirs


def state_gradient(query, numer, attended, first_wide):
    one, two = head_slopes(numer, attended, first_wide)
    high, low = split(numer)
    wide = tn_dot(query, jnp.concatenate([high, low], axis=1))
    spread = jnp.where(first_wide, one, two)
    total = jnp.sum(query.astype(F32) * spread, axis=0, keepdims=True)
    return pack_state(wide[:, :PAIR] + wide[:, PAIR:], total)


OFFSETS = sorted(
    ((y, z) for y in range(RING) for z in range(RING) if y or z),
    key=lambda offset: -sum(min(step, RING - step) for step in offset),
)


class Scan:
    def __init__(self, terms, landed, sums, result, sems, reverse):
        self.terms, self.landed, self.sums, self.result = terms, landed, sums, result
        self.sems, self.reverse = sems, reverse
        self.dp, self.me = lax.axis_index("dp"), lax.axis_index("seq")
        self.y, self.z = lax.div(self.me, RING), lax.rem(self.me, RING)
        self.parity = lax.rem(self.y + self.z, 2)
        self.unit = self.unit_of(self.parity, self.me)

    def unit_of(self, parity, device):
        return parity * 8 + lax.div(device, 2)

    def at(self, y, z, sign=1):
        y = lax.rem(self.y + (sign * y + RING), RING)
        z = lax.rem(self.z + (sign * z + RING), RING)
        return y * RING + z

    def others(self):
        return [(self.dp, self.at(*offset)) for offset in OFFSETS]

    def half_offsets(self, half):
        for y in (2, 1, 3, 0):
            for step in (1, 0):
                yield y, 2 * step + lax.rem(self.parity + (y + half), 2)

    def copy(self, number, source, target, sems, other):
        return pltpu.make_async_remote_copy(
            src_ref=source,
            dst_ref=target,
            send_sem=sems[0].at[number],
            recv_sem=sems[1].at[number],
            device_id=(self.dp, other),
            device_id_type=MESH,
        )

    def start(self):
        for half in range(2):
            for y, z in self.half_offsets(half):
                other = self.at(y, z)
                source = self.terms.at[self.unit_of(half, other)]
                copy = self.copy(y * RING + z, source, self.landed.at[self.me], self.sems[:2], other)
                if y:
                    copy.start()
                else:
                    pl.when(z > 0)(copy.start)
        self.landed[self.me] = self.terms[self.unit]

    def middle(self):
        for y, z in OFFSETS:
            other = self.at(y, z, -1)
            came = self.landed.at[other]
            self.copy(y * RING + z, came, came, self.sems[:2], other).wait_recv()
        total = jnp.zeros(self.landed.shape[1:], F32)
        for k in range(SEQ):
            at = SEQ - 1 - k if self.reverse else k
            self.sums[at] = total
            total = total + self.landed[at]
        for y, z in OFFSETS:
            other = self.at(y, z)
            target = self.result.at[self.unit]
            self.copy(y * RING + z, self.sums.at[other], target, self.sems[2:], other).start()
        self.result[self.unit] = self.sums[self.me]

    def finish(self, half):
        for y, z in self.half_offsets(half):
            other = self.at(y, z, -1)
            came = self.result.at[self.unit_of(half, other)]
            copy = self.copy(y * RING + z, came, came, self.sems[2:], other)
            if y:
                copy.wait_recv()
            else:
                pl.when(z > 0)(copy.wait_recv)

    def drain(self):
        for y, z in OFFSETS:
            number, other = y * RING + z, self.at(y, z)
            self.copy(number, self.terms.at[0], self.landed.at[0], self.sems[:2], other).wait_send()
            self.copy(number, self.sums.at[0], self.result.at[0], self.sems[2:], other).wait_send()


SCAN_SCRATCH = [
    pltpu.VMEM((SEQ, 72, PAIR), F32),
    pltpu.VMEM((SEQ, 72, PAIR), F32),
    pltpu.VMEM((SEQ, 72, PAIR), F32),
    *[pltpu.SemaphoreType.DMA((SEQ,)) for _ in range(4)],
]


def unit_slices(unit, block):
    rows = pl.ds(pl.multiple_of(lax.div(unit, 8) * block, block), block)
    columns = pl.ds(pl.multiple_of(lax.rem(unit, 8) * PAIR, PAIR), PAIR)
    return rows, columns


def for_units(step, together):
    def several(index, carry):
        for offset in range(together):
            step(index * together + offset)
        return carry

    lax.fori_loop(0, SEQ // together, several, 0)


def causal_mask(block, transposed=False):
    row = lax.broadcasted_iota(jnp.int32, (block, block), 0)
    column = lax.broadcasted_iota(jnp.int32, (block, block), 1)
    return (row <= column) if transposed else (row >= column)


def norm_rows(values):
    center = jnp.mean(values, axis=-1, keepdims=True)
    centered = values - center
    variance = jnp.mean(centered * centered, axis=-1, keepdims=True)
    inverse = lax.rsqrt(variance + 1e-05)
    return centered * inverse, inverse


ROWS = 64


def for_rows(count, step):
    def one(index, carry):
        step(pl.ds(pl.multiple_of(index * ROWS, ROWS), ROWS))
        return carry

    lax.fori_loop(0, count // ROWS, one, 0)


def for_columns(count, width, step):
    def one(index, carry):
        step(pl.ds(pl.multiple_of(index * width, width), width))
        return carry

    lax.fori_loop(0, count // width, one, 0)


def attention_forward_kernel(
    block, x, gain, shift, weight, cot_in, cat_out, cot_out, qkv_out, att_out, att_low_out, den_out, state_out,
    w, cot, normed, qkv, att, att_low, den, cat, fq, fk, stage, land, state, terms, landed, sums, s0, s1, s2, s3,
    wsem, osem, swap_sent, swap_came,
):
    place = Place()
    rows_all = x.shape[0]
    own, other = pl.ds(0, rows_all), pl.ds(rows_all, rows_all)
    outs = []

    def leave(source, target):
        outs.append(pltpu.make_async_copy(source, target, osem.at[len(outs)]))
        outs[-1].start()

    scan = Scan(terms, landed, sums, state, (s0, s1, s2, s3), False)
    others = [*scan.others(), place.partner()]
    greet(others)
    loads = []
    cot_load = pltpu.make_async_copy(cot_in, cot.at[own], wsem.at[3])
    for slot, third in enumerate((1, 2, 0)):
        load = pltpu.make_async_copy(
            weight.at[:, pl.ds(third * 1024, 1024)], w.at[slot], wsem.at[slot]
        )
        load.start()
        loads.append(load)
    cot_load.start()

    def norm_step(rows):
        scaled, _ = norm_rows(x[rows, :].astype(F32))
        normed[rows, :] = (scaled * gain[...] + shift[...]).astype(BF16)

    for_rows(x.shape[0], norm_step)

    def project(slot, third, feature):
        loads[slot].wait()

        def step(columns):
            raw = dot_nn(normed[...], w[slot, :, columns]).astype(BF16)
            qkv[third, :, columns] = raw
            if feature is not None:
                feature[:, columns] = features(raw.astype(F32))

        for_columns(1024, 512, step)

    project(0, 1, fk)
    project(1, 2, None)

    def local_state(unit):
        rows, columns = unit_slices(unit, block)
        keys = fk[rows, columns]
        square = tn_dot(qkv[2, rows, columns], keys)
        total = jnp.sum(keys.astype(F32), axis=0, keepdims=True)
        blocks, row = pack_state(square, total)
        terms[unit, pl.ds(0, 64)] = blocks
        terms[unit, pl.ds(64, 8)] = row

    for_units(local_state, 4)
    met(len(others))
    scan.start()
    swap = Swap(place, stage, swap_sent, swap_came)
    for core in range(2):
        for block_x in range(4):
            columns = pl.ds(block_x * 256 + core * 128, 128)
            cat[core, own, pl.ds(block_x * 128, 128)] = normed[:, columns]
        swap.put(core, core, cat[core, own, :], land.at[core])
    cot_load.wait()
    for tile in range(2):
        swap.put(2 + tile, 2 + tile, cot[own, pl.ds(tile * TILE, TILE)], land.at[2 + tile])
    leave(qkv.at[pl.ds(1, 2)], qkv_out.at[pl.ds(1, 2)])
    project(2, 0, fq)
    leave(qkv.at[0], qkv_out.at[0])
    first, second = head_masks()
    causal = causal_mask(block)

    def local_part(unit):
        rows, columns = unit_slices(unit, block)
        query, key, value = fq[rows, columns], fk[rows, columns], qkv[2, rows, columns]
        scores = dot_nt(jnp.concatenate([query * first, query * second], axis=0), key)
        both = 0.0
        for head, mask in enumerate((first, second)):
            own = jnp.where(causal, scores[head * block : (head + 1) * block], 0.0).astype(BF16)
            right = jnp.concatenate([value * mask, jnp.broadcast_to(mask, value.shape)], axis=1)
            both = both + dot_nn(own, right)
        att[rows, columns] = both[:, :PAIR]
        den[rows, columns] = both[:, PAIR:]

    def local_parts(start, count):
        def two(index, carry):
            local_part(start + 2 * index)
            local_part(start + 2 * index + 1)
            return carry

        lax.fori_loop(0, count // 2, two, 0)

    local_parts(0, 10)
    scan.middle()
    local_parts(10, 6)
    for core in range(2):
        cat[core, other, :] = swap.get(core, land.at[core])
        cot[other, pl.ds(core * TILE, TILE)] = swap.get(2 + core, land.at[2 + core])
    leave(cat, cat_out)
    leave(cot, cot_out)
    together = same_head()

    def incoming(unit):
        rows, columns = unit_slices(unit, block)
        square, total = unpack_state(state[unit])
        totals = jnp.where(together, jnp.broadcast_to(total, (PAIR, PAIR)), 0.0)
        high, low = split(jnp.concatenate([square, totals], axis=0))
        query = fq[rows, columns]
        both = dot_nt(
            jnp.concatenate([query, query], axis=1), jnp.concatenate([high, low], axis=1)
        )
        denom = den[rows, columns] + both[:, PAIR:]
        den[rows, columns] = denom
        attended = (att[rows, columns] + both[:, :PAIR]) / denom
        att[rows, columns] = attended
        att_low[rows, columns] = attended.astype(BF16)

    for half in range(2):
        scan.finish(half)
        leave(state.at[pl.ds(half * 8, 8)], state_out.at[pl.ds(half * 8, 8)])

        def several(index, carry):
            incoming(half * 8 + 2 * index)
            incoming(half * 8 + 2 * index + 1)
            return carry

        lax.fori_loop(0, 4, several, 0)
        part = pl.ds(half * block, block)
        leave(att.at[part], att_out.at[part])
        leave(den.at[part], den_out.at[part])
        leave(att_low.at[part], att_low_out.at[part])
    scan.drain()
    swap.drain(range(4), land.at[0])
    for copy in outs:
        copy.wait()


def attention_forward(x, gain, shift, weight, cot, block):
    rows, width = x.shape
    vmem = pl.BlockSpec(memory_space=pltpu.VMEM)

    def kernel(*refs):
        attention_forward_kernel(block, *refs)

    return pl.pallas_call(
        kernel,
        out_shape=[
            struct((2, 2 * rows, width // 2), BF16),
            struct((2 * rows, width), BF16),
            struct((3, rows, width), BF16),
            struct((rows, width)),
            struct((rows, width), BF16),
            struct((rows, width)),
            struct((SEQ, 72, PAIR)),
        ],
        in_specs=[vmem, vmem, vmem, ANY_SPEC, ANY_SPEC],
        out_specs=[ANY_SPEC] * 7,
        scratch_shapes=[
            pltpu.VMEM((3, width, width), BF16),
            pltpu.VMEM((2 * rows, width), BF16),
            pltpu.VMEM((rows, width), BF16),
            pltpu.VMEM((3, rows, width), BF16),
            pltpu.VMEM((rows, width), F32),
            pltpu.VMEM((rows, width), BF16),
            pltpu.VMEM((rows, width), F32),
            pltpu.VMEM((2, 2 * rows, width // 2), BF16),
            pltpu.VMEM((rows, width), BF16),
            pltpu.VMEM((rows, width), BF16),
            pltpu.VMEM((4, rows, TILE), F32),
            pltpu.VMEM((4, rows, TILE), F32),
            SCAN_SCRATCH[0],
            *SCAN_SCRATCH,
            pltpu.SemaphoreType.DMA((4,)),
            pltpu.SemaphoreType.DMA((12,)),
            pltpu.SemaphoreType.DMA((4,)),
            pltpu.SemaphoreType.DMA((4,)),
        ],
        compiler_params=pltpu.CompilerParams(
            collective_id=5, has_side_effects=True, vmem_limit_bytes=62 * MIB
        ),
    )(x, gain.reshape(1, width), shift.reshape(1, width), weight, cot)


def gelu_both(pre):
    cumulative = 0.5 * (1.0 + lax.erf(pre * (1.0 / math.sqrt(2.0))))
    density = jnp.exp(-0.5 * pre * pre) * (1.0 / math.sqrt(2.0 * math.pi))
    return (pre * cumulative).astype(BF16), (cumulative + pre * density).astype(BF16)


def norm_back(grad, gain, scaled, inverse):
    spread = grad * gain
    first_mean = jnp.mean(spread, axis=-1, keepdims=True)
    second_mean = jnp.mean(spread * scaled, axis=-1, keepdims=True)
    return inverse * (spread - first_mean - scaled * second_mean)


def norm_back_rows(values, grad, base, gain, sums, store):
    sums[...] = jnp.zeros_like(sums)

    def step(rows):
        scaled, inverse = norm_rows(values[rows, :].astype(F32))
        part = grad[rows, :]
        sums[0:1, :] += jnp.sum(part * scaled, axis=0, keepdims=True)
        sums[1:2, :] += jnp.sum(part, axis=0, keepdims=True)
        store(rows, base[rows, :].astype(F32) + norm_back(part, gain[...], scaled, inverse))

    for_rows(grad.shape[0], step)


def feed_forward_kernel(
    block_rows, x, att_low, gain, shift, cot_in, w_out, w_up, w_down, qkv_in, att_in, den_in,
    output_out, gmixed_out, gn_out, sums, norm_out, pre_out, out_out, terms, down_a, down_b, down_c,
    wo, wu, wd, wsem, osem, output, gmixed, gatt, norm_cat, pre_cat, hidden, slope, cot_cat,
    stage, land, land_att, land_norm, swap_sent, swap_came, free, *scratch,
):
    take_scratch = Taker(scratch)
    slabs = take_scratch(slab_shapes(DOWN_WIDTHS))
    slab_a, slab_b, slab_c = slabs
    phases = take_scratch([[phase_scratch(2, length, 12)] for length in DOWN_WIDTHS])
    place = Place()
    core = place.core
    rows = x.shape[0]
    others = link_neighbours(place)
    greet(others)
    own, other = pl.ds(0, rows), pl.ds(rows, rows)
    mixed = gatt
    loads = []
    moves = ((w_out, wo), (w_up, wu), (w_down, wd), (cot_in, cot_cat))
    for slot in (0, 1, 3, 2):
        loads.append(pltpu.make_async_copy(*moves[slot], wsem.at[slot]))
        loads[-1].start()
    outs = []

    def leave(source, target):
        outs.append(pltpu.make_async_copy(source, target, osem.at[len(outs)]))
        outs[-1].start()

    cot = cot_cat.at[own]
    swap = Swap(place, stage, swap_sent, swap_came)
    loads[0].wait()

    def mix(columns):
        mixed[:, columns] = x[:, columns].astype(F32) + dot_nn(att_low[...], wo[:, columns])

    for_columns(1024, TILE, mix)

    def norm_step(index):
        scaled, _ = norm_rows(mixed[index, :])
        norm_cat[index, :] = (scaled * gain[...] + shift[...]).astype(BF16)

    for_rows(rows, norm_step)
    met(len(others))
    loads[1].wait()

    def up(columns):
        ours, ours_slope = gelu_both(dot_nn(norm_cat[own, :], wu[:, columns]))
        hidden[:, columns] = ours
        slope[:, columns] = ours_slope
        return ours

    def nth_block(index):
        return lax.rem(place.at[0] + jnp.where(index == 2, 3, jnp.maximum(2 - index, 0)), RING)

    def give(index, carry):
        theirs = up(half_columns(nth_block(index), 1 - core, 1024))
        swap.put(index, index, theirs, land.at[index])
        return carry

    lax.fori_loop(0, 4, give, 0)
    loads[2].wait()

    def take(index, carry):
        block = nth_block(index)
        ours = up(half_columns(block, core, 1024))
        both = jnp.concatenate([ours, swap.get(index, land.at[index])], axis=0)
        for half in range(2):
            columns = pl.ds(half * TILE, TILE)
            product = tn_dot(both, cot_cat[:, columns]).reshape(4, 4, 4, 8, TILE)
            for stream in range(3):
                slabs[stream][block, :, :, :, columns] = product[:, :, stream]
            last = product[:, :, 3]
            if half == 0:
                slab_a[block, :, :, :, pl.ds(1024, 384)] = last[..., :384]
                slab_b[block, :, :, :, pl.ds(1024, 128)] = last[..., 384:]
            else:
                slab_b[block, :, :, :, pl.ds(1152, 256)] = last[..., :256]
                slab_c[block, :, :, :, pl.ds(1024, 256)] = last[..., 256:]
        return carry

    kinds = (None, SplitPhase, SplitPhase)
    down = [Stream(place, slabs[k], ORDERS[k], phases[k], kinds[k]) for k in range(3)]
    first, *split = [stream.prepare() for stream in down]
    lax.fori_loop(0, 2, take, 0)
    first.begin_far()
    for phase in split:
        phase.begin_first()
    first.begin_near(0)
    lax.fori_loop(2, 4, take, 0)
    for phase in split:
        phase.begin_second()
    first.begin_near(1)
    pl.semaphore_signal(free, inc=1, device_id=place.partner(), device_id_type=MESH)
    for tile in range(2):
        columns = pl.ds(tile * TILE, TILE)
        swap.put(4 + tile, tile, norm_cat[own, columns], land_norm.at[tile], before=tile)
    loads[3].wait()

    def finish_forward(columns):
        output[:, columns] = (mixed[:, columns] + dot_nn(hidden[...], wd[:, columns])).astype(BF16)

    for_columns(1024, 256, finish_forward)
    leave(output, output_out)

    def back(columns):
        grad = dot_nt(cot[...], wd[columns, :]) * slope[:, columns].astype(F32)
        low = grad.astype(BF16)
        hidden[:, columns] = low
        return low

    pl.semaphore_wait(free, 1)

    def give_back(block, carry):
        theirs = back(half_columns(block, 1 - core, 1024))
        before = jnp.where(block < 2, 4 + block, block)
        swap.put(6 + block, block, theirs, land.at[block], before=before)
        return carry

    lax.fori_loop(0, 4, give_back, 0)

    def keep_back(block, carry):
        columns = pl.ds(pl.multiple_of(block * TILE, TILE), TILE)
        pre_cat[own, columns] = back(half_columns(block, core, 1024))
        return carry

    lax.fori_loop(0, 4, keep_back, 0)
    for stream in down:
        stream.forward()

    def back_up(columns):
        gmixed[:, columns] = dot_nt(hidden[...], wu[columns, :])

    for_columns(1024, 256, back_up)

    def take_back(block, carry):
        columns = pl.ds(pl.multiple_of(block * TILE, TILE), TILE)
        pre_cat[other, columns] = swap.get(6 + block, land.at[block])
        return carry

    lax.fori_loop(0, 4, take_back, 0)
    leave(pre_cat, pre_out)
    for tile in range(2):
        columns = pl.ds(tile * TILE, TILE)
        norm_cat[other, columns] = swap.get(4 + tile, land_norm.at[tile])
        swap.put(10 + tile, tile, att_low[:, columns], land_att.at[tile], before=6 + tile)
    leave(norm_cat, norm_out)
    query_load = pltpu.make_async_copy(qkv_in.at[0], slope.at[:, pl.ds(0, 1024)], wsem.at[4])
    query_load.start()
    pl.semaphore_signal(free, inc=1, device_id=place.partner(), device_id_type=MESH)
    def store(index, values):
        gmixed[index, :] = values
        hidden[index, pl.ds(0, 1024)] = values.astype(BF16)

    norm_back_rows(mixed, gmixed, cot, gain, sums, store)
    leave(gmixed, gmixed_out)
    pl.semaphore_wait(free, 1)
    swap.put(12, 2, hidden[:, half_tile(0, 1 - core)], land_norm.at[0], before=8)

    def back_out(columns):
        gatt[:, columns] = dot_nt(hidden[:, pl.ds(0, 1024)], wo[columns, :])

    state_loads = [query_load]

    def load_state(slots):
        for slot in slots:
            source = (att_in, den_in)[slot // 2].at[:, pl.ds(slot % 2 * TILE, TILE)]
            state_loads.append(pltpu.make_async_copy(source, stage.at[slot], wsem.at[5 + slot]))
            state_loads[-1].start()

    for number, slot in ((9, 3), (10, 0), (11, 1)):
        swap.copy(number, slot, land_norm.at[0]).wait_send()
    load_state((0, 1, 3))
    for_columns(1024, TILE, back_out)
    ours = hidden[:, half_tile(0, core)]
    swap.copy(12, 2, land_norm.at[0]).wait_send()
    load_state((2,))
    theirs = swap.get(12, land_norm.at[0])
    for tile in range(2):
        swap.copy(10 + tile, tile, land_att.at[tile]).wait_recv()
        for part, (start, width) in enumerate(((0, 384), (384, 128))):
            product = tn_dot(att_low[:, pl.ds(tile * TILE + start, width)], ours)
            theirs_att = land_att[tile, :, pl.ds(start, width)].astype(BF16)
            land[2 * tile + part, pl.ds(0, width), :] = product + tn_dot(theirs_att, theirs)
            leave(land.at[2 * tile + part, pl.ds(0, width)], out_out.at[pl.ds(tile * TILE + start, width)])
    for copy in state_loads:
        copy.wait()
    first_wide = first_head(block_rows)

    def local_state(unit):
        index, columns = unit_slices(unit, block_rows)
        pair = lax.rem(unit, 8)
        within = pl.ds(pl.multiple_of(lax.rem(pair, 4) * PAIR, PAIR), PAIR)
        tile = lax.div(pair, 4)
        numer = gatt[index, columns] / stage[2 + tile, index, within]
        gatt[index, columns] = numer
        query = features(slope[index, columns].astype(F32))
        blocks, row = state_gradient(query, numer, stage[tile, index, within], first_wide)
        terms[unit, pl.ds(0, 64)] = blocks
        terms[unit, pl.ds(64, 8)] = row

    for_units(local_state, 2)
    leave(gatt, gn_out)
    for stream, target in zip(down, (down_a, down_b, down_c)):
        stream.finish()
        leave(stream.data, target)
    for stream in down:
        stream.drain()
    for copy in outs:
        copy.wait()


def slab_shapes(widths):
    return [pltpu.VMEM((4, 4, 4, 8, width), F32) for width in widths]


def struct(shape, dtype=F32):
    return jax.ShapeDtypeStruct(shape, dtype)


VMEM_SPEC = pl.BlockSpec(memory_space=pltpu.VMEM)
ANY_SPEC = pl.BlockSpec(memory_space=pl.ANY)


def call(kernel, outs, out_specs, operands, in_specs, scratch, collective_id):
    return pl.pallas_call(
        kernel,
        out_shape=outs,
        in_specs=in_specs,
        out_specs=out_specs,
        scratch_shapes=scratch,
        compiler_params=pltpu.CompilerParams(
            collective_id=collective_id, has_side_effects=True, vmem_limit_bytes=63 * MIB
        ),
    )(*operands)


def feed_forward(x, att_low, gain, shift, cot_cat, w_out, w_up, w_down, qkv, att, den, block):
    rows, width = x.shape
    wide = w_up.shape[1]
    outs = [
        struct((rows, width), BF16),
        struct((rows, width)),
        struct((rows, width)),
        struct((8, width)),
        struct((2 * rows, width), BF16),
        struct((2 * rows, wide // 2), BF16),
        struct((width, TILE)),
        struct((SEQ, 72, PAIR)),
        *[struct((4, 4, 8, length)) for length in DOWN_WIDTHS],
    ]
    scratch = [
        pltpu.VMEM((width, width), BF16),
        pltpu.VMEM((width, wide), BF16),
        pltpu.VMEM((wide, width), BF16),
        pltpu.SemaphoreType.DMA((9,)),
        pltpu.SemaphoreType.DMA((12,)),
        pltpu.VMEM((rows, width), BF16),
        pltpu.VMEM((rows, width), F32),
        pltpu.VMEM((rows, width), F32),
        pltpu.VMEM((2 * rows, width), BF16),
        pltpu.VMEM((2 * rows, wide // 2), BF16),
        pltpu.VMEM((rows, wide), BF16),
        pltpu.VMEM((rows, wide), BF16),
        pltpu.VMEM((2 * rows, width), BF16),
        pltpu.VMEM((4, rows, TILE), F32),
        pltpu.VMEM((4, rows, TILE), F32),
        pltpu.VMEM((2, rows, TILE), F32),
        pltpu.VMEM((2, rows, TILE), F32),
        pltpu.SemaphoreType.DMA((13,)),
        pltpu.SemaphoreType.DMA((13,)),
        pltpu.SemaphoreType.REGULAR,
        *slab_shapes(DOWN_WIDTHS),
        *flatten([[phase_scratch(2, length, 12)] for length in DOWN_WIDTHS]),
    ]
    specs = [VMEM_SPEC] * 4 + [ANY_SPEC] * 7
    out_specs = [ANY_SPEC] * 3 + [VMEM_SPEC] + [ANY_SPEC] * 3 + [VMEM_SPEC] + [ANY_SPEC] * 3
    operands = (x, att_low, gain, shift, cot_cat, w_out, w_up, w_down, qkv, att, den)

    def kernel(*refs):
        feed_forward_kernel(block, *refs)

    return call(kernel, outs, out_specs, operands, specs, scratch, 1)


def last_scratch(rows, width):
    return {
        "qkv": pltpu.VMEM((3, rows, width), BF16),
        "att": pltpu.VMEM((rows, width), F32),
        "gn": pltpu.VMEM((rows, width), F32),
        "state": pltpu.VMEM((SEQ, 72, PAIR), F32),
        "x": pltpu.VMEM((rows, width), BF16),
        "grads": pltpu.VMEM((2, rows, width), F32),
        "scan": list(SCAN_SCRATCH[:3]) + [SCAN_SCRATCH[0]] + list(SCAN_SCRATCH[3:]),
        "norm_cat": pltpu.VMEM((2, 2 * rows, width // 2), BF16),
        "pre_cat": pltpu.VMEM((2 * rows, 2 * width), BF16),
        "w": pltpu.VMEM((width, 3 * width), BF16),
        "stage": pltpu.VMEM((3, rows, TILE), F32),
        "land": pltpu.VMEM((3, rows, TILE), F32),
        "swap": [pltpu.SemaphoreType.DMA((3,)), pltpu.SemaphoreType.DMA((3,))],
        "slabs": slab_shapes(UP_WIDTHS),
        "chunks": [pltpu.VMEM((4, 4, 8, length), F32) for length in DOWN_WIDTHS],
        "up_chunks": [pltpu.VMEM((4, 4, 8, length), F32) for length in UP_WIDTHS],
        "out_slabs": slab_shapes(OUT_WIDTHS),
        "vec_slab": pltpu.VMEM((4, 4, 4, 8, 128), F32),
        "sums": pltpu.VMEM((8, width), F32),
        "down": [stream_scratch(length, (1, 2), (2,)) for length in DOWN_WIDTHS],
        "up": [
            [*stream_scratch(length, (0, 1)), route_scratch(k, UP_WIDTHS, 2048)] for k, length in enumerate(UP_WIDTHS)
        ],
        "out": [
            [*stream_scratch(length, (0, 1), (1,)), route_scratch(k, OUT_WIDTHS, TILE)]
            for k, length in enumerate(OUT_WIDTHS)
        ],
        "qkv_sems": [[pltpu.SemaphoreType.DMA((6,))] * 2 for _ in QKV_WIDTHS],
        "qkv_sum": [
            [*stream_scratch(length, (1,)), route_scratch(k, QKV_WIDTHS, 3 * TILE)]
            for k, length in enumerate(QKV_WIDTHS)
        ],
        "vec": stream_scratch(128, (0, 1, 2), (0, 1, 2)),
        "vec_land": pltpu.VMEM((8, 128), F32),
        "vec_sems": pltpu.SemaphoreType.DMA((2,)),
        "credit": pltpu.SemaphoreType.REGULAR((3,)),
        "loads": pltpu.SemaphoreType.DMA((32,)),
    }


def last_kernel(
    block, qkv_in, att_in, terms_in, state_in, gn_in, gmixed_in, norm_one_in, norm_in, pre_in,
    down_in_a, down_in_b, down_in_c, out_in, x_in, weight, gain, sums_two,
    grad_input, grad_up, grad_out, grad_qkv, grad_down, grad_gains, *scratch,
):
    place = Place()
    core = place.core
    rows, width = att_in.shape
    like = last_scratch(rows, width)
    take = Taker(scratch)
    s = {name: take(like[name]) for name in like}
    qkv, att, gn, grads = s["qkv"], s["att"], s["gn"], s["grads"]
    slabs = s["slabs"]
    scan = Scan(*s["scan"][:4], s["scan"][4:], True)
    across = [place.neighbour(0, step) for step in (1, -1, 2)]
    beside = []
    for axis in range(3):
        for step in (1, 2, 3):
            position = list(place.at)
            position[axis] = place.ring(axis, step)
            beside.append(place.id_of(*position, 1 - core))
    others = [*across, place.partner(), *beside, *scan.others()]
    greet(others)
    loads = []

    def load(source, target):
        copy = pltpu.make_async_copy(source, target, s["loads"].at[len(loads)])
        copy.start()
        loads.append(copy)
        return copy

    started = load(terms_in, scan.terms)
    out_loads = []
    for k in (0, 2, 1):
        for which, start, length, at in stream_pieces(k, OUT_WIDTHS, TILE):
            source = out_in.at[:, which, :, :, :, pl.ds(start, length)]
            target = s["out_slabs"][k].at[:, :, :, :, pl.ds(at, length)]
            out_loads.append(load(source, target))
    up_loads = [load(pre_in, s["pre_cat"])]
    for which in range(2):
        for block_x in range(4):
            source = norm_in.at[:, pl.ds(block_x * 256 + which * 128, 128)]
            target = s["norm_cat"].at[which, :, pl.ds(block_x * 128, 128)]
            up_loads.append(load(source, target))
    down_in = (down_in_a, down_in_b, down_in_c)
    down_loads = [load(source, target) for source, target in zip(down_in, s["chunks"])]
    qkv_loads = [load(qkv_in, qkv), load(state_in, s["state"]), load(gn_in, gn), load(att_in, att)]
    late_loads = [load(weight, s["w"]), load(x_in, s["x"])]

    def settle(copies):
        for copy in copies:
            copy.wait()

    first, second = head_masks()
    first_wide = first_head(block)

    up_first = [phases[0] for phases in s["up"]]
    down = [Stream(place, s["chunks"][k], ORDERS[k][1:], s["down"][k]) for k in range(3)]
    up = [
        Stream(place, slabs[k], ORDERS[k], s["up"][k], None, (stream_pieces(k, UP_WIDTHS, 2048), grad_up))
        for k in range(3)
    ]
    out = [
        Stream(place, s["out_slabs"][k], ORDERS[k], s["out"][k], None, (stream_pieces(k, OUT_WIDTHS, TILE), grad_out))
        for k in range(3)
    ]
    qkv_sum = [None] * 3
    vec = [Stream(place, s["vec_slab"], ORDERS[0], s["vec"])]
    begin, forward, proceed, finish = Stream.begin, Stream.forward, Stream.proceed, Stream.finish

    def go(*steps):
        for step, streams, k in steps:
            step(streams[k])

    settle(out_loads)
    met(len(others))
    go((begin, out, 0))
    started.wait()
    scan.start()
    go((begin, out, 2))
    settle(up_loads)
    for k in range(3):
        stream_product(k, s["norm_cat"], s["pre_cat"], slabs[k], UP_WIDTHS, 2048)
        if k == 1:
            settle(down_loads)
            go((begin, down, 0), (begin, up, 0))
    go((begin, out, 1))
    norm_load = load(norm_one_in, s["norm_cat"])
    settle(qkv_loads)
    causal = causal_mask(block)
    causal_t = causal_mask(block, True)

    def local_part(unit):
        index, columns = unit_slices(unit, block)
        raw_query = qkv[0, index, columns].astype(F32)
        query, value = features(raw_query), qkv[2, index, columns]
        key = features(qkv[1, index, columns].astype(F32))
        numer = gn[index, columns]
        one, two = head_slopes(numer, att[index, columns], first_wide)
        high, low = split(numer)
        scores = dot_nt(jnp.concatenate([key * first, key * second], axis=0), query)
        wide = jnp.concatenate([high, low], axis=1)
        values = jnp.concatenate([value, value], axis=1)
        grad_query, grad_key, grad_value = 0.0, 0.0, 0.0
        for head, (mask, slope) in enumerate(((first, one), (second, two))):
            mask_wide = jnp.concatenate([mask, mask], axis=1)
            mixing = jnp.where(causal, dot_nt(wide * mask_wide, values) + slope, 0.0).astype(BF16)
            turned = jnp.where(causal_t, scores[head * block : (head + 1) * block], 0.0)
            grad_query = grad_query + dot_nn(mixing, key * mask)
            grad_key = grad_key + tn_dot(mixing, query * mask)
            grad_value = grad_value + dot_nn(turned.astype(BF16), high * mask)
        square, total = unpack_state(s["state"][unit])
        state_high, state_low = split(square)
        grad_query = grad_query + dot_nn(wide, jnp.concatenate([state_high, state_high], axis=0))
        grad_query = grad_query + dot_nn(high, state_low)
        grad_query = grad_query + jnp.where(first_wide, one, two) * total
        qkv[0, index, columns] = (grad_query * feature_slope(raw_query)).astype(BF16)
        grads[0, index, columns] = grad_key
        grads[1, index, columns] = grad_value

    def local_parts(start, count):
        def one(index, carry):
            local_part(start + index)
            return carry

        lax.fori_loop(0, count, one, 0)

    local_parts(0, 2)
    scan.middle()
    local_parts(2, 1)
    go((begin, up, 2), (forward, out, 2), (forward, out, 0))
    local_parts(3, 2)
    go((forward, out, 1))
    local_parts(5, 3)
    go((begin, up, 1))
    local_parts(8, 7)
    go((forward, up, 0))
    local_parts(15, 1)
    swap = Swap(place, s["stage"], *s["swap"])
    land, cat = s["land"], s["pre_cat"]
    own, other = pl.ds(0, rows), pl.ds(rows, rows)
    swap.put(0, 0, qkv[0, :, half_tile(0, 1 - core)], land.at[0])
    mixed_load = load(gmixed_in, att)
    scan.finish(0)
    scan.finish(1)
    go((begin, down, 2))

    def incoming(unit):
        index, columns = unit_slices(unit, block)
        square, total = unpack_state(scan.result[unit])
        high, low = split(square)
        raw_key = qkv[1, index, columns].astype(F32)
        key, value = features(raw_key), qkv[2, index, columns]
        grad_key = grads[0, index, columns] + total
        grad_key = grad_key + dot_nt(
            jnp.concatenate([value, value], axis=1), jnp.concatenate([high, low], axis=1)
        )
        grad_value = grads[1, index, columns] + dot_nn(
            jnp.concatenate([key, key], axis=1), jnp.concatenate([high, low], axis=0)
        )
        qkv[1, index, columns] = (grad_key * feature_slope(raw_key)).astype(BF16)
        qkv[2, index, columns] = grad_value.astype(BF16)

    for_units(incoming, 2)
    for third in (1, 2):
        swap.put(third, third, qkv[third, :, half_tile(0, 1 - core)], land.at[third])
    settle(late_loads)

    def back_norm(columns):
        total = 0.0
        for third in range(3):
            total = total + dot_nt(qkv[third], s["w"][columns, pl.ds(third * 1024, 1024)])
        gn[:, columns] = total

    for start in (0, 256, 512, 768):
        back_norm(pl.ds(start, 256))
    for third in range(3):
        columns = pl.ds(third * TILE, TILE)
        cat[own, columns] = qkv[third, :, half_tile(0, core)]
        cat[other, columns] = swap.get(third, land.at[third])
    go((forward, up, 2), (forward, up, 1))
    norm_load.wait()
    mixed_load.wait()
    def turn(k):
        up[k].finish(s["up_chunks"][k])
        up[k].drain()
        for step in (1, -1):
            pl.semaphore_signal(
                s["credit"].at[k],
                inc=1,
                device_id=place.neighbour(ORDERS[k][0], step),
                device_id_type=MESH,
            )
        narrow = (slice(None),) * 4 + (pl.ds(0, QKV_WIDTHS[k]),)
        data = slabs[k].at[narrow]
        stream_product(k, s["norm_cat"], cat, data, QKV_WIDTHS, 3 * TILE)
        pl.semaphore_wait(s["credit"].at[k], 2)
        phases = [[up_first[k][0].at[narrow], up_first[k][1].at[narrow], *s["qkv_sems"][k]]]
        last = (stream_pieces(k, QKV_WIDTHS, 3 * TILE), grad_qkv)
        qkv_sum[k] = Stream(place, data, ORDERS[k], phases + s["qkv_sum"][k], None, last)
        qkv_sum[k].begin()

    def store(index, values):
        gn[index, :] = values

    sums = s["sums"]
    norm_back_rows(s["x"], gn, att, gain, sums, store)
    leave = load(gn, grad_input)
    go((begin, down, 1), (proceed, out, 0))
    four = jnp.concatenate([sums[0:2, :], sums_two[0:2, :]], axis=0)
    eight = jnp.concatenate([four, four], axis=0)
    turned = jnp.transpose(jnp.concatenate([eight, jnp.zeros((120, 1024), F32)], axis=0))
    turned = turned.reshape(4, 2, 4, 4, 8, 128)
    lane = lax.broadcasted_iota(jnp.int32, (8, 128), 1)
    s["vec_slab"][...] = jnp.where(lane < 4, turned[:, 0], jnp.where(lane < 8, turned[:, 1], 0.0))
    go((begin, vec, 0), (proceed, out, 1))
    turn(0)
    turn(2)
    go((begin, up, 0))
    turn(1)
    go(
        (forward, qkv_sum, 0), (forward, qkv_sum, 2), (begin, up, 1), (forward, down, 2), (forward, down, 1),
        (begin, up, 2), (proceed, out, 0), (forward, qkv_sum, 1), (proceed, vec, 0), (proceed, qkv_sum, 2),
        (proceed, qkv_sum, 0), (proceed, qkv_sum, 1), (forward, down, 0), (forward, up, 0), (forward, up, 1),
        (proceed, out, 2), (proceed, vec, 0), (forward, qkv_sum, 2), (forward, up, 2), (proceed, down, 1),
        (forward, qkv_sum, 0), (forward, qkv_sum, 1), (proceed, down, 2), (proceed, down, 0), (proceed, qkv_sum, 2),
        (proceed, up, 0), (proceed, up, 1), (proceed, out, 2), (proceed, qkv_sum, 0), (proceed, up, 2),
        (proceed, out, 1), (proceed, qkv_sum, 1), (finish, down, 2), (finish, down, 1), (finish, down, 0),
        (finish, up, 1), (finish, vec, 0),
    )
    vec_tile = vec[0].data
    vec_copy = pltpu.make_async_remote_copy(
        src_ref=vec_tile,
        dst_ref=s["vec_land"],
        send_sem=s["vec_sems"].at[0],
        recv_sem=s["vec_sems"].at[1],
        device_id=place.partner(),
        device_id_type=MESH,
    )
    vec_copy.start()
    go(
        (finish, up, 0), (finish, qkv_sum, 0), (finish, qkv_sum, 2), (finish, out, 0), (finish, qkv_sum, 1),
        (finish, out, 2), (finish, out, 1), (finish, up, 2),
    )
    for k in range(3):
        piece = down[k].data
        grad_down[pl.ds(8 * k, 8), :] = piece[:, pl.ds(0, 1024)]
        start, width_k = DOWN_CUTS[k]
        grad_down[pl.ds(24, 8), pl.ds(start, width_k)] = piece[:, pl.ds(1024, width_k)]
    scan.drain()
    for number in range(3):
        swap.copy(number, number, land.at[number]).wait_send()
    for stream in (*down, *up, *out, *qkv_sum, *vec):
        stream.drain()
    vec_copy.wait()
    grad_gains[...] = vec_tile[...] + s["vec_land"][...]
    leave.wait()


def last_part(qkv, att, terms, state, gn, gmixed, norm_one, norm_cat, pre_cat, down, out, x, weight, gain, sums_two, block):
    rows, width = x.shape

    def kernel(*refs):
        last_kernel(block, *refs)

    outs = [
        struct((rows, width)),
        struct((8, 4096)),
        struct((8, width)),
        struct((8, 3 * width)),
        struct((32, width)),
        struct((8, 128)),
    ]
    like = last_scratch(rows, width)
    scratch = [leaf for name in like for leaf in flatten(like[name])]
    out = out.reshape(4, 2, 4, 4, 8, TILE)
    operands = (
        qkv, att, terms, state, gn, gmixed, norm_one, norm_cat, pre_cat, *down, out, x, weight, gain, sums_two,
    )
    specs = [ANY_SPEC] * 15 + [VMEM_SPEC] * 2
    out_specs = [ANY_SPEC] + [VMEM_SPEC] * 5
    return call(kernel, outs, out_specs, operands, specs, scratch, 2)


def lay_out_kernel(output, grad_input, up, out, qkv, down, gains, output_to, grad_to, up_to, out_to, qkv_to, down_to, a, b, c, d):
    pairs = (
        (output, output_to), (grad_input, grad_to), (up, up_to), (out, out_to), (qkv, qkv_to), (down, down_to),
    )
    for source, target in pairs:
        target[...] = source[...]
    core = lax.rem(lax.axis_index("dp"), 2)
    turned = jnp.transpose(jnp.concatenate([gains[...], jnp.zeros((120, 128), F32)], axis=0))
    for k, target in enumerate((a, b, c, d)):
        target[...] = jnp.where(core == 0, turned[k : k + 1, :8], turned[4 + k : 5 + k, :8])


def lay_out(output, *grads):
    arrays = (output, *grads[:-1])
    outs = [struct(array.shape, array.dtype) for array in arrays] + [struct((1, 8))] * 4
    return pl.pallas_call(
        lay_out_kernel,
        out_shape=outs,
        in_specs=[VMEM_SPEC] * 7,
        out_specs=[VMEM_SPEC] * 10,
        compiler_params=pltpu.CompilerParams(vmem_limit_bytes=62 * MIB),
    )(output, *grads)


def body(
    inputs,
    first_gain,
    first_shift,
    qkv_weight,
    out_weight,
    second_gain,
    second_shift,
    up_weight,
    down_weight,
    cotangent,
):
    sequences, block, width = inputs.shape
    rows = sequences * block
    x = inputs.reshape(rows, width)
    cot = cotangent.reshape(rows, width)
    gain_one, gain_two = first_gain.reshape(1, width), second_gain.reshape(1, width)
    shift_two = second_shift.reshape(1, width)
    norm_one, cot_cat, qkv, att, att_low, den, state = attention_forward(
        x, first_gain, first_shift, qkv_weight, cot, block
    )
    output, gmixed, gn, sums_two, norm_cat, pre_cat, out, terms, *down = feed_forward(
        x, att_low, gain_two, shift_two, cot_cat, out_weight, up_weight, down_weight, qkv, att, den, block
    )
    grads = last_part(
        qkv, att, terms, state, gn, gmixed, norm_one, norm_cat, pre_cat, down, out, x, qkv_weight,
        gain_one, sums_two, block,
    )
    output, grad_input, grad_up, grad_out, grad_qkv, grad_down, *gains = lay_out(output, *grads)
    return (
        output.reshape(inputs.shape),
        grad_input.reshape(inputs.shape),
        grad_qkv,
        grad_out,
        grad_up,
        grad_down,
        *[gain.reshape(8) for gain in gains],
    )


def solution(mesh):
    return jax.shard_map(
        body,
        mesh=mesh,
        in_specs=(
            P("dp", "seq", None),
            P(),
            P(),
            P(),
            P(),
            P(),
            P(),
            P(),
            P(),
            P("dp", "seq", None),
        ),
        out_specs=(
            P("dp", "seq", None),
            P("dp", "seq", None),
            P(("dp", "seq"), None),
            P(("dp", "seq"), None),
            P(("dp", "seq"), None),
            P(("dp", "seq"), None),
            P(("dp", "seq")),
            P(("dp", "seq")),
            P(("dp", "seq")),
            P(("dp", "seq")),
        ),
        check_vma=False,
    )
```

```python
import math

import jax
import jax.numpy as jnp
from jax import lax
from jax.experimental import pallas as pl
from jax.experimental.pallas import tpu as pltpu
from jax.sharding import PartitionSpec as P

MESH = pl.DeviceIdType.MESH
F32 = jnp.float32
BF16 = jnp.bfloat16
RING = 4
MIB = 2**20


class Place:
    def __init__(self):
        dp, seq = lax.axis_index("dp"), lax.axis_index("seq")
        self.core = lax.rem(dp, 2)
        self.at = (lax.div(dp, 2), lax.div(seq, RING), lax.rem(seq, RING))

    def id_of(self, x, y, z, core):
        return (x * 2 + core, y * RING + z)

    def ring(self, axis, step):
        return lax.rem(self.at[axis] + (step + RING), RING)

    def neighbour(self, axis, step):
        at = list(self.at)
        at[axis] = self.ring(axis, step)
        return self.id_of(*at, self.core)

    def partner(self):
        return self.id_of(*self.at, 1 - self.core)


def greet(others):
    barrier = pltpu.get_barrier_semaphore()
    for other in others:
        pl.semaphore_signal(barrier, inc=1, device_id=other, device_id_type=MESH)


def met(count):
    pl.semaphore_wait(pltpu.get_barrier_semaphore(), count)


def link_neighbours(place):
    others = [place.neighbour(axis, step) for axis in range(3) for step in (1, -1)]
    return [*others, place.partner()]


ORDERS = ((0, 1, 2), (1, 2, 0), (2, 0, 1))


def phase_scratch(remaining, length, messages=6):
    if remaining:
        half = (2, 2, *[4] * (remaining - 1), 8, length)
    else:
        half = (2, 8, (length // 128 + 1) // 2 * 128)
    return [
        pltpu.VMEM((2, *[4] * remaining, 8, length), F32),
        pltpu.VMEM(half, F32),
        pltpu.SemaphoreType.DMA((messages,)),
        pltpu.SemaphoreType.DMA((messages,)),
    ]


class Phase:
    def __init__(self, place, data, axes, axis, scratch):
        self.place, self.data, self.axis = place, data, axis
        self.where = axes.index(axis)
        self.full, self.half, self.sent, self.came = scratch
        self.flying = []
        self.flat = len(axes) == 1
        self.length = data.shape[-1]
        self.cut = (self.length // 128 + 1) // 2 * 128
        self.whole = self.flat and self.cut == self.length

    def empty(self, which):
        return self.whole and which == 1

    def chunk(self, target):
        index = [slice(None)] * self.where + [target]
        return self.data.at[tuple(index)]

    def part(self, ref, which):
        if not self.flat:
            return ref.at[pl.ds(2 * which, 2)]
        if which == 0:
            return ref.at[:, pl.ds(0, self.cut)]
        return ref.at[:, pl.ds(self.cut, self.length - self.cut)]

    def through(self, way):
        ref = self.half.at[way]
        if self.flat and way == 1:
            return ref.at[:, pl.ds(0, self.length - self.cut)]
        return ref

    def copy(self, kind, way, source, target):
        number = kind * 2 + way
        return pltpu.make_async_remote_copy(
            src_ref=source,
            dst_ref=target,
            send_sem=self.sent.at[number],
            recv_sem=self.came.at[number],
            device_id=self.place.neighbour(self.axis, 1 - 2 * way),
            device_id_type=MESH,
        )

    def send(self, kind, way, source, target):
        copy = self.copy(kind, way, source, target)
        copy.start()
        self.flying.append(copy)

    def beside(self, way):
        return self.chunk(self.place.ring(self.axis, 1 - 2 * way))

    def begin_far(self):
        opposite = self.chunk(self.place.ring(self.axis, 2))
        for way in range(2):
            if not self.empty(way):
                self.send(0, way, self.part(opposite, way), self.through(way))

    def begin_near(self, way):
        if not self.empty(1 - way):
            target = self.part(self.full.at[way], 1 - way)
            self.send(1, way, self.part(self.beside(way), 1 - way), target)

    def begin(self):
        self.begin_far()
        for way in range(2):
            self.begin_near(way)

    def forward(self):
        for way in range(2):
            if self.empty(way):
                continue
            came = self.through(way)
            self.copy(0, way, came, came).wait_recv()
            own = self.part(self.beside(way), way)
            add_into(own, own, came)
            self.send(2, way, own, self.part(self.full.at[way], way))

    def finish(self, out=None):
        own = self.chunk(self.place.at[self.axis])
        for way in range(2):
            for kind, which in ((1, 1 - way), (2, way)):
                if self.empty(which):
                    continue
                target = self.part(self.full.at[way], which)
                self.copy(kind, way, target, target).wait_recv()
        add_into(own if out is None else out, own, self.full.at[0], self.full.at[1])
        return own

    def drain(self):
        for copy in self.flying:
            copy.wait_send()


HALVES = ((2, 1), (3, 0))


class SplitPhase(Phase):
    def block(self, way, j):
        return self.place.ring(0, HALVES[way][j])

    def copy_block(self, kind, way, j, source, target):
        number = kind * 4 + way * 2 + j
        return pltpu.make_async_remote_copy(
            src_ref=source,
            dst_ref=target,
            send_sem=self.sent.at[number],
            recv_sem=self.came.at[number],
            device_id=self.place.neighbour(self.axis, 1 - 2 * way),
            device_id_type=MESH,
        )

    def send_far(self, way, j):
        source = self.chunk(self.place.ring(self.axis, 2)).at[self.block(way, j)]
        self.flying.append(self.copy_block(0, way, j, source, self.half.at[way, j]))
        self.flying[-1].start()

    def send_near(self, kind, way, j):
        block = self.block(way if kind == 2 else 1 - way, j)
        source, target = self.beside(way).at[block], self.full.at[way, block]
        self.flying.append(self.copy_block(kind, way, j, source, target))
        self.flying[-1].start()

    def begin_first(self):
        for j in range(2):
            self.send_far(0, j)
        self.send_near(1, 1, 0)

    def begin_second(self):
        for j in range(2):
            self.send_far(1, j)
        self.send_near(1, 1, 1)
        for j in range(2):
            self.send_near(1, 0, j)

    def forward(self):
        for way in range(2):
            for j in range(2):
                came = self.half.at[way, j]
                self.copy_block(0, way, j, came, came).wait_recv()
                own = self.beside(way).at[self.block(way, j)]
                add_into(own, own, came)
                self.send_near(2, way, j)

    def finish(self, out=None):
        own = self.chunk(self.place.at[self.axis])
        for way in range(2):
            for kind, part in ((1, 1 - way), (2, way)):
                for j in range(2):
                    target = self.full.at[way, self.block(part, j)]
                    self.copy_block(kind, way, j, target, target).wait_recv()
        add_into(own if out is None else out, own, self.full.at[0], self.full.at[1])
        return own


class Direct:
    def __init__(self, place, data, axes, axis, scratch):
        self.place, self.data, self.axis = place, data, axis
        self.where = axes.index(axis)
        self.full, self.sent, self.came = scratch
        self.flying = []

    def chunk(self, target):
        index = [slice(None)] * self.where + [target]
        return self.data.at[tuple(index)]

    def copy(self, step, source):
        return pltpu.make_async_remote_copy(
            src_ref=source,
            dst_ref=self.full.at[step - 1],
            send_sem=self.sent.at[step - 1],
            recv_sem=self.came.at[step - 1],
            device_id=self.place.neighbour(self.axis, step),
            device_id_type=MESH,
        )

    def begin(self):
        for step in (2, 1, 3):
            copy = self.copy(step, self.chunk(self.place.ring(self.axis, step)))
            copy.start()
            self.flying.append(copy)

    def forward(self):
        pass

    def finish(self, out=None):
        own = self.chunk(self.place.at[self.axis])
        for step in (1, 2, 3):
            self.copy(step, self.full.at[step - 1]).wait_recv()
        add_into(own if out is None else out, own, *[self.full.at[k] for k in range(3)])
        return own

    def drain(self):
        for copy in self.flying:
            copy.wait_send()


class Route:
    def __init__(self, place, data, axis, pieces, scratch, out):
        self.place, self.data, self.axis, self.pieces, self.out = place, data, axis, pieces, out
        self.scratch = scratch

    def send_each(self, act):
        core = self.place.core
        for (owner, _, width, at), (land, sent, came) in zip(self.pieces, self.scratch):

            def copy(step):
                position = list(self.place.at)
                position[self.axis] = self.place.ring(self.axis, step)
                return pltpu.make_async_remote_copy(
                    src_ref=self.data.at[self.place.ring(self.axis, step), :, pl.ds(at, width)],
                    dst_ref=land.at[core, step],
                    send_sem=sent.at[step],
                    recv_sem=came.at[core, step],
                    device_id=self.place.id_of(*position, owner),
                    device_id_type=MESH,
                )

            for step in (2, 1, 3):
                act(copy(step))

            @pl.when(core != owner)
            def _():
                act(copy(0))

    def begin(self):
        self.send_each(lambda copy: copy.start())

    def forward(self):
        pass

    def finish(self, out=None):
        core = self.place.core
        mine = self.place.at[self.axis]
        for (owner, start, width, at), (land, sent, came) in zip(self.pieces, self.scratch):

            @pl.when(core == owner)
            def _():
                for source, steps in ((core, (1, 2, 3)), (1 - core, (0, 1, 2, 3))):
                    for step in steps:
                        target = land.at[source, step]
                        pltpu.make_async_remote_copy(
                            src_ref=target,
                            dst_ref=target,
                            send_sem=sent.at[step],
                            recv_sem=came.at[source, step],
                            device_id=self.place.partner(),
                            device_id_type=MESH,
                        ).wait_recv()
                done = 0
                while done < width:
                    column = start + done
                    tile, within = column // TILE, column % TILE
                    step = min(TILE - within, width - done)
                    part = pl.ds(done, step)
                    ours = self.data[mine, :, pl.ds(at + done, step)]
                    for k in (1, 2, 3):
                        ours = ours + land[core, k, :, part]
                    theirs = land[1 - core, 0, :, part]
                    for k in (1, 2, 3):
                        theirs = theirs + land[1 - core, k, :, part]
                    for values, half in ((ours, core), (theirs, 1 - core)):
                        place = pl.multiple_of((2 * tile + half) * TILE + within, 128)
                        self.out[:, pl.ds(place, step)] = values
                    done += step

    def drain(self):
        self.send_each(lambda copy: copy.wait_send())


def route_scratch(stream, widths, columns):
    return [
        [
            pltpu.VMEM((2, 4, 8, width), F32),
            pltpu.SemaphoreType.DMA((4,)),
            pltpu.SemaphoreType.DMA((2, 4)),
        ]
        for _, _, width, _ in stream_pieces(stream, widths, columns)
    ]


class Stream:
    def __init__(self, place, data, order, scratch, first=None, last=None):
        self.place, self.data, self.scratch, self.first, self.last = place, data, scratch, first, last
        self.todo, self.old = [axis for axis in order], []
        self.axes = sorted(order)
        self.phase = None

    def prepare(self):
        scratch = self.scratch.pop(0)
        if self.last and len(self.todo) == 1:
            pieces, out = self.last
            self.phase = Route(self.place, self.data, self.todo[0], pieces, scratch, out)
            return self.phase
        kind = self.first or (Phase if len(scratch) == 4 else Direct)
        self.first = None
        self.phase = kind(self.place, self.data, self.axes, self.todo[0], scratch)
        return self.phase

    def begin(self):
        self.prepare().begin()

    def forward(self):
        self.phase.forward()

    def finish(self, out=None):
        own = self.phase.finish(out)
        self.data = own if out is None else out
        self.axes.remove(self.todo.pop(0))
        self.old.append(self.phase)

    def proceed(self):
        self.finish()
        self.begin()

    def drain(self):
        for phase in self.old:
            phase.drain()
        self.old = []


def direct_scratch(remaining, length):
    return [
        pltpu.VMEM((3, *[4] * remaining, 8, length), F32),
        pltpu.SemaphoreType.DMA((3,)),
        pltpu.SemaphoreType.DMA((3,)),
    ]


def stream_scratch(length, phases, direct=()):
    return [
        (direct_scratch if phase in direct else phase_scratch)(2 - phase, length)
        for phase in phases
    ]


class Taker:
    def __init__(self, refs):
        self.refs = list(refs)

    def __call__(self, like):
        if isinstance(like, list):
            return [self(item) for item in like]
        return self.refs.pop(0)


def flatten(items):
    if isinstance(items, list):
        return [leaf for item in items for leaf in flatten(item)]
    return [items]


def add_into(out, *terms):
    if len(out.shape) > 2:

        def row(index, carry):
            add_into(out.at[index], *[term.at[index] for term in terms])
            return carry

        if len(out.shape) == 4:
            lax.fori_loop(0, out.shape[0], row, 0)
        else:
            for index in range(out.shape[0]):
                row(index, 0)
        return
    total = terms[0][...]
    for term in terms[1:]:
        total = total + term[...]
    out[...] = total


def tn_dot(left, right):
    return lax.dot_general(left, right, (((0,), (0,)), ((), ())), preferred_element_type=F32)


TILE = 512


class Swap:
    def __init__(self, place, stage, sent, came):
        self.place, self.stage, self.sent, self.came = place, stage, sent, came

    def copy(self, number, slot, target):
        return pltpu.make_async_remote_copy(
            src_ref=self.stage.at[slot],
            dst_ref=target,
            send_sem=self.sent.at[number],
            recv_sem=self.came.at[number],
            device_id=self.place.partner(),
            device_id_type=MESH,
        )

    def put(self, number, slot, values, target, before=None):
        if before is not None:
            self.copy(before, slot, target).wait_send()
        self.stage[slot] = values.astype(F32)
        self.copy(number, slot, target).start()

    def get(self, number, target):
        self.copy(number, 0, target).wait_recv()
        return target[...].astype(BF16)

    def drain(self, numbers, target):
        for number in numbers:
            self.copy(number, number % 4, target).wait_send()


def half_columns(block, core, quarter):
    half = quarter // 2
    return pl.ds(pl.multiple_of(block * quarter + core * half, half), half)


def half_tile(index, core):
    return pl.ds(pl.multiple_of((2 * index + core) * TILE, TILE), TILE)


def core_product(left, core, right, start, width, slab, at):
    done = 0
    while done < width:
        step = min(TILE, width - done)
        product = tn_dot(left[core], right[:, pl.ds(start + done, step)])
        slab[:, :, :, :, pl.ds(at + done, step)] = product.reshape(4, 4, 4, 8, step)
        done += step


UP_WIDTHS = (1536, 1280, 1280)
OUT_WIDTHS = (512, 256, 256)
QKV_WIDTHS = (1152, 896, 1024)


def stream_pieces(stream, widths, columns):
    if stream < 2:
        return [(stream, 0, widths[stream], 0)]
    pieces, at = [], 0
    for core in range(2):
        width = columns - widths[core]
        if width:
            pieces.append((core, widths[core], width, at))
        at += width
    return pieces


def stream_product(stream, left, right, slab, widths, columns):
    for core, start, width, at in stream_pieces(stream, widths, columns):
        core_product(left, core, right, start, width, slab, at)


DOWN_CUTS = ((0, 384), (384, 384), (768, 256))
DOWN_WIDTHS = (1408, 1408, 1280)


SEQ = 16
PAIR = 128
NT = (((1,), (1,)), ((), ()))
TN = (((0,), (0,)), ((), ()))


def dot_nt(left, right):
    return lax.dot_general(left, right, NT, preferred_element_type=F32)


def dot_nn(left, right):
    return jnp.dot(left, right, preferred_element_type=F32)


def split(values):
    high = values.astype(BF16)
    return high, (values - high.astype(F32)).astype(BF16)


def features(raw):
    return jnp.where(raw > 0, raw + 1.0, jnp.exp(jnp.minimum(raw, 0.0))).astype(BF16)


def feature_slope(raw):
    return jnp.where(raw > 0, 1.0, jnp.exp(jnp.minimum(raw, 0.0)))


def head_masks():
    lane = lax.broadcasted_iota(jnp.int32, (1, PAIR), 1)
    first = jnp.where(lane < 64, 1.0, 0.0)
    return first.astype(BF16), (1.0 - first).astype(BF16)


def first_head(rows):
    return lax.broadcasted_iota(jnp.int32, (rows, PAIR), 1) < 64


def pack_state(square, total):
    blocks = jnp.where(first_head(64), square[:64], square[64:])
    return blocks, jnp.broadcast_to(total, (8, PAIR))


def unpack_state(packed):
    first = first_head(64)
    square = jnp.concatenate(
        [jnp.where(first, packed[:64], 0.0), jnp.where(first, 0.0, packed[:64])], axis=0
    )
    return square, packed[64:65]


def same_head():
    row = lax.broadcasted_iota(jnp.int32, (PAIR, PAIR), 0)
    lane = lax.broadcasted_iota(jnp.int32, (PAIR, PAIR), 1)
    return (row < 64) == (lane < 64)


def head_slopes(numer, attended, first_wide):
    product = numer * attended
    ours = jnp.sum(jnp.where(first_wide, product, 0.0), axis=1, keepdims=True)
    theirs = jnp.sum(jnp.where(first_wide, 0.0, product), axis=1, keepdims=True)
    return -ours, -theirs


def state_gradient(query, numer, attended, first_wide):
    one, two = head_slopes(numer, attended, first_wide)
    high, low = split(numer)
    wide = tn_dot(query, jnp.concatenate([high, low], axis=1))
    spread = jnp.where(first_wide, one, two)
    total = jnp.sum(query.astype(F32) * spread, axis=0, keepdims=True)
    return pack_state(wide[:, :PAIR] + wide[:, PAIR:], total)


OFFSETS = sorted(
    ((y, z) for y in range(RING) for z in range(RING) if y or z),
    key=lambda offset: -sum(min(step, RING - step) for step in offset),
)


class Units:
    def __init__(self, ref):
        self.ref = ref

    def at(self, unit):
        rows = pl.ds(pl.multiple_of(lax.div(lax.rem(unit, 8), 4) * 72, 8), 72)
        columns = pl.ds(pl.multiple_of(lax.rem(unit, 4) * PAIR, PAIR), PAIR)
        return self.ref.at[lax.div(unit, 8), rows, columns]


class Slots:
    def __init__(self, ref):
        self.ref = ref

    def at(self, unit):
        return self.ref.at[unit]


class Scan:
    def __init__(self, terms, landed, sums, result, sems, reverse):
        self.terms, self.landed, self.sums, self.result = terms, landed, sums, result
        self.sems, self.reverse = sems, reverse
        self.dp, self.me = lax.axis_index("dp"), lax.axis_index("seq")
        self.y, self.z = lax.div(self.me, RING), lax.rem(self.me, RING)
        self.parity = lax.rem(self.y + self.z, 2)
        self.unit = self.unit_of(self.parity, self.me)

    def unit_of(self, parity, device):
        return parity * 8 + lax.div(device, 2)

    def at(self, y, z, sign=1):
        y = lax.rem(self.y + (sign * y + RING), RING)
        z = lax.rem(self.z + (sign * z + RING), RING)
        return y * RING + z

    def others(self):
        return [(self.dp, self.at(*offset)) for offset in OFFSETS]

    def half_offsets(self, half):
        for y in (2, 1, 3, 0):
            for step in (1, 0):
                yield y, 2 * step + lax.rem(self.parity + (y + half), 2)

    def copy(self, number, source, target, sems, other):
        return pltpu.make_async_remote_copy(
            src_ref=source,
            dst_ref=target,
            send_sem=sems[0].at[number],
            recv_sem=sems[1].at[number],
            device_id=(self.dp, other),
            device_id_type=MESH,
        )

    def start(self):
        for half in range(2):
            for y, z in self.half_offsets(half):
                other = self.at(y, z)
                source = self.terms.at(self.unit_of(half, other))
                copy = self.copy(y * RING + z, source, self.landed.at(self.me), self.sems[:2], other)
                if y:
                    copy.start()
                else:
                    pl.when(z > 0)(copy.start)
        self.landed.at(self.me)[...] = self.terms.at(self.unit)[...]

    def middle(self):
        for y, z in OFFSETS:
            other = self.at(y, z, -1)
            came = self.landed.at(other)
            self.copy(y * RING + z, came, came, self.sems[:2], other).wait_recv()
        total = jnp.zeros((72, PAIR), F32)
        for k in range(SEQ):
            at = SEQ - 1 - k if self.reverse else k
            self.sums.at(at)[...] = total
            total = total + self.landed.at(at)[...]
        for y, z in OFFSETS:
            other = self.at(y, z)
            target = self.result.at(self.unit)
            self.copy(y * RING + z, self.sums.at(other), target, self.sems[2:], other).start()
        self.result.at(self.unit)[...] = self.sums.at(self.me)[...]

    def finish(self, half):
        for y, z in self.half_offsets(half):
            other = self.at(y, z, -1)
            came = self.result.at(self.unit_of(half, other))
            copy = self.copy(y * RING + z, came, came, self.sems[2:], other)
            if y:
                copy.wait_recv()
            else:
                pl.when(z > 0)(copy.wait_recv)

    def drain(self):
        for y, z in OFFSETS:
            number, other = y * RING + z, self.at(y, z)
            self.copy(number, self.terms.at(0), self.landed.at(0), self.sems[:2], other).wait_send()
            self.copy(number, self.sums.at(0), self.result.at(0), self.sems[2:], other).wait_send()


SCAN_SCRATCH = [
    pltpu.VMEM((SEQ, 72, PAIR), F32),
    pltpu.VMEM((SEQ, 72, PAIR), F32),
    pltpu.VMEM((SEQ, 72, PAIR), F32),
    *[pltpu.SemaphoreType.DMA((SEQ,)) for _ in range(4)],
]


def unit_slices(unit, block):
    rows = pl.ds(pl.multiple_of(lax.div(unit, 8) * block, block), block)
    columns = pl.ds(pl.multiple_of(lax.rem(unit, 8) * PAIR, PAIR), PAIR)
    return rows, columns


def for_units(step, together):
    def several(index, carry):
        for offset in range(together):
            step(index * together + offset)
        return carry

    lax.fori_loop(0, SEQ // together, several, 0)


def causal_mask(block, transposed=False):
    row = lax.broadcasted_iota(jnp.int32, (block, block), 0)
    column = lax.broadcasted_iota(jnp.int32, (block, block), 1)
    return (row <= column) if transposed else (row >= column)


def norm_rows(values):
    center = jnp.mean(values, axis=-1, keepdims=True)
    centered = values - center
    variance = jnp.mean(centered * centered, axis=-1, keepdims=True)
    inverse = lax.rsqrt(variance + 1e-05)
    return centered * inverse, inverse


ROWS = 64


def for_rows(count, step):
    def one(index, carry):
        step(pl.ds(pl.multiple_of(index * ROWS, ROWS), ROWS))
        return carry

    lax.fori_loop(0, count // ROWS, one, 0)


def for_columns(count, width, step):
    def one(index, carry):
        step(pl.ds(pl.multiple_of(index * width, width), width))
        return carry

    lax.fori_loop(0, count // width, one, 0)


SLOPE_SCALE = 28000.0


def gelu_both(pre):
    cumulative = 0.5 * (1.0 + lax.erf(pre * (1.0 / math.sqrt(2.0))))
    density = jnp.exp(-0.5 * pre * pre) * (1.0 / math.sqrt(2.0 * math.pi))
    slope = (cumulative + pre * density) * SLOPE_SCALE
    return (pre * cumulative).astype(BF16), jnp.round(slope).astype(jnp.int32).astype(jnp.int16)


def norm_back(grad, gain, scaled, inverse):
    spread = grad * gain
    first_mean = jnp.mean(spread, axis=-1, keepdims=True)
    second_mean = jnp.mean(spread * scaled, axis=-1, keepdims=True)
    return inverse * (spread - first_mean - scaled * second_mean)


def norm_back_rows(values, grad, base, gain, sums, store):
    sums[...] = jnp.zeros_like(sums)

    def step(rows):
        scaled, inverse = norm_rows(values[rows, :].astype(F32))
        part = grad[rows, :]
        sums[0:1, :] += jnp.sum(part * scaled, axis=0, keepdims=True)
        sums[1:2, :] += jnp.sum(part, axis=0, keepdims=True)
        store(rows, base[rows, :].astype(F32) + norm_back(part, gain[...], scaled, inverse))

    for_rows(grad.shape[0], step)


def front_kernel(
    block, x, gain_one, shift_one, gain, shift, w_qkv, cot_in, w_out, w_up, w_down,
    norm_one_out, qkv_out, att_out, den_out, state_out, output_out, gmixed_out, gn_out, sums, norm_out, pre_out,
    out_out, terms, down_a, down_b, down_c,
    wo, wu, wd, wsem, osem, att_low, state, output, gmixed, gatt, norm_cat, pre_cat, hidden, slope, cot_cat,
    stage, land, land_att, land_norm, swap_sent, swap_came, free, s0, s1, s2, s3, *scratch,
):
    take_scratch = Taker(scratch)
    slabs = take_scratch(slab_shapes(DOWN_WIDTHS))
    slab_a, slab_b, slab_c = slabs
    phases = take_scratch([[phase_scratch(2, length, 12)] for length in DOWN_WIDTHS])
    place = Place()
    core = place.core
    rows = x.shape[0]
    scan = Scan(Slots(terms), Units(land_att), Units(land_norm), Slots(state), (s0, s1, s2, s3), False)
    others = [place.neighbour(0, 1), place.neighbour(0, -1), place.partner(), *scan.others()]
    greet(others)
    own, other = pl.ds(0, rows), pl.ds(rows, rows)

    def load(source, target, slot):
        copy = pltpu.make_async_copy(source, target, wsem.at[slot])
        copy.start()
        return copy

    outs = []

    def leave(source, target):
        copy = pltpu.make_async_copy(source, target, osem.at[len(outs)])
        copy.start()
        outs.append(copy)
        return copy

    def settle(copies):
        for copy in copies:
            copy.wait()
            settled.append(id(copy))

    settled = []
    thirds = [
        load(w_qkv.at[:, pl.ds(third * 1024, 1024)], wu.at[:, pl.ds(slot * 1024, 1024)], slot)
        for slot, third in enumerate((1, 2, 0))
    ]
    cot_load = load(cot_in, cot_cat.at[own], 3)
    out_load = load(w_out, wo, 4)

    def norm_step(index):
        scaled, _ = norm_rows(x[index, :].astype(F32))
        hidden[index, pl.ds(0, 1024)] = (scaled * gain_one[...] + shift_one[...]).astype(BF16)

    for_rows(rows, norm_step)

    def shifted(columns, offset):
        return pl.ds(pl.multiple_of(columns.start + offset, PAIR), columns.size)

    def later_rows(index, offset):
        return pl.ds(pl.multiple_of(index.start + offset, 64), index.size)

    def project(slot, third, feature):
        thirds[slot].wait()

        def step(columns):
            raw = dot_nn(hidden[:, pl.ds(0, 1024)], wu[:, shifted(columns, slot * 1024)]).astype(BF16)
            hidden[:, shifted(columns, 1024 + third * 1024)] = raw
            if feature is not None:
                wd[pl.ds(feature * rows, rows), columns] = features(raw.astype(F32))

        for_columns(1024, TILE, step)

    project(0, 1, 1)
    project(1, 2, None)

    def local_state(unit):
        index, columns = unit_slices(unit, block)
        keys = wd[later_rows(index, rows), columns]
        square = tn_dot(hidden[index, shifted(columns, 3072)], keys)
        total = jnp.sum(keys.astype(F32), axis=0, keepdims=True)
        blocks, row = pack_state(square, total)
        terms[unit, pl.ds(0, 64)] = blocks
        terms[unit, pl.ds(64, 8)] = row

    for_units(local_state, 4)
    met(len(others))
    scan.start()
    swap = Swap(place, stage, swap_sent, swap_came)
    for which in range(2):
        for block_x in range(4):
            columns = pl.ds(block_x * 256 + which * 128, 128)
            pre_cat[own, pl.ds(which * TILE + block_x * 128, 128)] = hidden[:, columns]
        swap.put(which, which, pre_cat[own, pl.ds(which * TILE, TILE)], land.at[which])
    cot_load.wait()
    for tile in range(2):
        swap.put(2 + tile, 2 + tile, cot_cat[own, pl.ds(tile * TILE, TILE)], land.at[2 + tile])
    qkv_leaves = [leave(hidden.at[:, pl.ds(third * 1024 + 1024, 1024)], qkv_out.at[third]) for third in (1, 2)]
    project(2, 0, 0)
    qkv_leaves.append(leave(hidden.at[:, pl.ds(1024, 1024)], qkv_out.at[0]))
    up_load = load(w_up, wu, 6)
    first, second = head_masks()
    causal = causal_mask(block)

    def local_part(unit):
        index, columns = unit_slices(unit, block)
        query, key = wd[index, columns], wd[later_rows(index, rows), columns]
        value = hidden[index, shifted(columns, 3072)]
        scores = dot_nt(jnp.concatenate([query * first, query * second], axis=0), key)
        both = 0.0
        for head, mask in enumerate((first, second)):
            kept = jnp.where(causal, scores[head * block : (head + 1) * block], 0.0).astype(BF16)
            right = jnp.concatenate([value * mask, jnp.broadcast_to(mask, value.shape)], axis=1)
            both = both + dot_nn(kept, right)
        gmixed[index, columns] = both[:, :PAIR]
        gatt[index, columns] = both[:, PAIR:]

    def local_parts(start, count):
        def two(index, carry):
            local_part(start + 2 * index)
            local_part(start + 2 * index + 1)
            return carry

        lax.fori_loop(0, count // 2, two, 0)

    local_parts(0, 10)
    scan.middle()
    local_parts(10, 6)
    for which in range(2):
        pre_cat[other, pl.ds(which * TILE, TILE)] = swap.get(which, land.at[which])
        cot_cat[other, pl.ds(which * TILE, TILE)] = swap.get(2 + which, land.at[2 + which])
    cat_leaves = [leave(pre_cat.at[:, pl.ds(which * TILE, TILE)], norm_one_out.at[which]) for which in range(2)]
    together = same_head()

    def incoming(unit):
        index, columns = unit_slices(unit, block)
        square, total = unpack_state(state[unit])
        totals = jnp.where(together, jnp.broadcast_to(total, (PAIR, PAIR)), 0.0)
        high, low = split(jnp.concatenate([square, totals], axis=0))
        query = wd[index, columns]
        both = dot_nt(
            jnp.concatenate([query, query], axis=1), jnp.concatenate([high, low], axis=1)
        )
        denom = gatt[index, columns] + both[:, PAIR:]
        attended = (gmixed[index, columns] + both[:, :PAIR]) / denom
        tile, within = stage_place(unit)
        stage[tile, index, within] = attended
        stage[2 + tile, index, within] = denom
        att_low[index, columns] = attended.astype(BF16)

    def stage_place(unit):
        pair = lax.rem(unit, 8)
        return lax.div(pair, 4), pl.ds(pl.multiple_of(lax.rem(pair, 4) * PAIR, PAIR), PAIR)

    mixed = gatt

    def up(columns, index):
        ours, ours_slope = gelu_both(dot_nn(norm_cat[index, :], wu[:, columns]))
        hidden[index, columns] = ours
        slope[index, columns] = ours_slope

    settle(qkv_leaves)
    swap.drain(range(4), land.at[0])
    att_leaves = []
    for half in range(2):
        scan.finish(half)
        leave(state.at[pl.ds(half * 8, 8)], state_out.at[pl.ds(half * 8, 8)])

        def several(index, carry):
            incoming(half * 8 + 2 * index)
            incoming(half * 8 + 2 * index + 1)
            return carry

        lax.fori_loop(0, 4, several, 0)
        part = pl.ds(half * block, block)
        for slot in range(4):
            target = (att_out, den_out)[slot // 2].at[part, pl.ds(slot % 2 * TILE, TILE)]
            att_leaves.append(leave(stage.at[slot, part], target))
        if half == 0:
            out_load.wait()

        def mix(columns):
            mixed[part, columns] = x[part, columns].astype(F32) + dot_nn(att_low[part, :], wo[:, columns])

        mix(pl.ds(0, 1024))
        for start in range(0, block, ROWS):
            index = pl.ds(half * block + start, ROWS)
            scaled, _ = norm_rows(mixed[index, :])
            norm_cat[index, :] = (scaled * gain[...] + shift[...]).astype(BF16)
        if half == 0:
            up_load.wait()
            for_columns(4096, 1024, lambda columns: up(columns, part))
    down_load = load(w_down, wd, 5)
    late = pl.ds(block, block)
    scan.drain()
    pl.semaphore_signal(free, inc=1, device_id=place.partner(), device_id_type=MESH)
    settle(att_leaves)
    pl.semaphore_wait(free, 1)

    def nth_block(index):
        return lax.rem(place.at[0] + jnp.where(index == 2, 3, jnp.maximum(2 - index, 0)), RING)

    def give(index, carry):
        columns = half_columns(nth_block(index), 1 - core, 1024)
        up(columns, late)
        swap.put(4 + index, index, hidden[:, columns], land.at[index])
        return carry

    lax.fori_loop(0, 4, give, 0)

    def take(index, carry):
        block_x = nth_block(index)
        columns = half_columns(block_x, core, 1024)
        up(columns, late)
        both = jnp.concatenate([hidden[:, columns], swap.get(4 + index, land.at[index])], axis=0)
        for half in range(2):
            columns = pl.ds(half * TILE, TILE)
            product = tn_dot(both, cot_cat[:, columns]).reshape(4, 4, 4, 8, TILE)
            for stream in range(3):
                slabs[stream][block_x, :, :, :, columns] = product[:, :, stream]
            last = product[:, :, 3]
            if half == 0:
                slab_a[block_x, :, :, :, pl.ds(1024, 384)] = last[..., :384]
                slab_b[block_x, :, :, :, pl.ds(1024, 128)] = last[..., 384:]
            else:
                slab_b[block_x, :, :, :, pl.ds(1152, 256)] = last[..., :256]
                slab_c[block_x, :, :, :, pl.ds(1024, 256)] = last[..., 256:]
        return carry

    kinds = (None, SplitPhase, SplitPhase)
    down = [Stream(place, slabs[k], ORDERS[k], phases[k], kinds[k]) for k in range(3)]
    lead, *others_two = [stream.prepare() for stream in down]
    lax.fori_loop(0, 2, take, 0)
    lead.begin_far()
    for phase in others_two:
        phase.begin_first()
    lead.begin_near(0)
    lax.fori_loop(2, 4, take, 0)
    for phase in others_two:
        phase.begin_second()
    lead.begin_near(1)
    pl.semaphore_signal(free, inc=1, device_id=place.partner(), device_id_type=MESH)
    for tile in range(2):
        columns = pl.ds(tile * TILE, TILE)
        swap.put(8 + tile, tile, norm_cat[own, columns], land_norm.at[tile], before=4 + tile)
    down_load.wait()
    cot = cot_cat.at[own]

    def finish_forward(columns):
        output[:, columns] = (mixed[:, columns] + dot_nn(hidden[...], wd[:, columns])).astype(BF16)

    for_columns(1024, 256, finish_forward)
    leave(output, output_out)

    def back(columns):
        held = slope[:, columns].astype(jnp.int32).astype(F32) * (1.0 / SLOPE_SCALE)
        grad = dot_nt(cot[...], wd[columns, :]) * held
        low = grad.astype(BF16)
        hidden[:, columns] = low
        return low

    pl.semaphore_wait(free, 1)

    def give_back(block, carry):
        theirs = back(half_columns(block, 1 - core, 1024))
        before = jnp.where(block < 2, 8 + block, 4 + block)
        swap.put(10 + block, block, theirs, land.at[block], before=before)
        return carry

    lax.fori_loop(0, 4, give_back, 0)

    def keep_back(block, carry):
        columns = pl.ds(pl.multiple_of(block * TILE, TILE), TILE)
        pre_cat[own, columns] = back(half_columns(block, core, 1024))
        return carry

    settle(cat_leaves)
    lax.fori_loop(0, 4, keep_back, 0)
    for stream in down:
        stream.forward()

    def back_up(columns):
        gmixed[:, columns] = dot_nt(hidden[...], wu[columns, :])

    for_columns(1024, 256, back_up)

    def take_back(block, carry):
        columns = pl.ds(pl.multiple_of(block * TILE, TILE), TILE)
        pre_cat[other, columns] = swap.get(10 + block, land.at[block])
        return carry

    lax.fori_loop(0, 4, take_back, 0)
    leave(pre_cat, pre_out)
    for tile in range(2):
        columns = pl.ds(tile * TILE, TILE)
        norm_cat[other, columns] = swap.get(8 + tile, land_norm.at[tile])
        swap.put(14 + tile, tile, att_low[:, columns], land_att.at[tile], before=10 + tile)
    leave(norm_cat, norm_out)
    query_load = load(qkv_out.at[0], wd.at[own], 7)
    pl.semaphore_signal(free, inc=1, device_id=place.partner(), device_id_type=MESH)
    def store(index, values):
        gmixed[index, :] = values
        hidden[index, pl.ds(0, 1024)] = values.astype(BF16)

    norm_back_rows(mixed, gmixed, cot, gain, sums, store)
    leave(gmixed, gmixed_out)
    pl.semaphore_wait(free, 1)
    swap.put(16, 2, hidden[:, half_tile(0, 1 - core)], land_norm.at[0], before=12)

    def back_out(columns):
        gatt[:, columns] = dot_nt(hidden[:, pl.ds(0, 1024)], wo[columns, :])

    state_loads = [query_load]

    def load_state(slots):
        for slot in slots:
            source = (att_out, den_out)[slot // 2].at[:, pl.ds(slot % 2 * TILE, TILE)]
            state_loads.append(load(source, stage.at[slot], 8 + slot))

    for number, slot in ((13, 3), (14, 0), (15, 1)):
        swap.copy(number, slot, land_norm.at[0]).wait_send()
    load_state((0, 1, 3))
    for_columns(1024, TILE, back_out)
    ours = hidden[:, half_tile(0, core)]
    swap.copy(16, 2, land_norm.at[0]).wait_send()
    load_state((2,))
    theirs = swap.get(16, land_norm.at[0])
    for tile in range(2):
        swap.copy(14 + tile, tile, land_att.at[tile]).wait_recv()
        for part, (start, width) in enumerate(((0, 384), (384, 128))):
            product = tn_dot(att_low[:, pl.ds(tile * TILE + start, width)], ours)
            theirs_att = land_att[tile, :, pl.ds(start, width)].astype(BF16)
            land[2 * tile + part, pl.ds(0, width), :] = product + tn_dot(theirs_att, theirs)
            leave(land.at[2 * tile + part, pl.ds(0, width)], out_out.at[pl.ds(tile * TILE + start, width)])
    for copy in state_loads:
        copy.wait()
    first_wide = first_head(block)

    def state_back(unit):
        index, columns = unit_slices(unit, block)
        tile, within = stage_place(unit)
        numer = gatt[index, columns] / stage[2 + tile, index, within]
        gatt[index, columns] = numer
        query = features(wd[index, columns].astype(F32))
        blocks, row = state_gradient(query, numer, stage[tile, index, within], first_wide)
        terms[unit, pl.ds(0, 64)] = blocks
        terms[unit, pl.ds(64, 8)] = row

    for_units(state_back, 2)
    leave(gatt, gn_out)
    for stream, target in zip(down, (down_a, down_b, down_c)):
        stream.finish()
        leave(stream.data, target)
    for stream in down:
        stream.drain()
    for copy in outs:
        if id(copy) not in settled:
            copy.wait()


def slab_shapes(widths):
    return [pltpu.VMEM((4, 4, 4, 8, width), F32) for width in widths]


def struct(shape, dtype=F32):
    return jax.ShapeDtypeStruct(shape, dtype)


VMEM_SPEC = pl.BlockSpec(memory_space=pltpu.VMEM)
ANY_SPEC = pl.BlockSpec(memory_space=pl.ANY)


def call(kernel, outs, out_specs, operands, in_specs, scratch, collective_id):
    return pl.pallas_call(
        kernel,
        out_shape=outs,
        in_specs=in_specs,
        out_specs=out_specs,
        scratch_shapes=scratch,
        compiler_params=pltpu.CompilerParams(
            collective_id=collective_id, has_side_effects=True, vmem_limit_bytes=63 * MIB
        ),
    )(*operands)


def front(x, gain_one, shift_one, gain, shift, w_qkv, cot, w_out, w_up, w_down, block):
    rows, width = x.shape
    wide = w_up.shape[1]
    outs = [
        struct((2, 2 * rows, width // 2), BF16),
        struct((3, rows, width), BF16),
        struct((rows, width)),
        struct((rows, width)),
        struct((SEQ, 72, PAIR)),
        struct((rows, width), BF16),
        struct((rows, width)),
        struct((rows, width)),
        struct((8, width)),
        struct((2 * rows, width), BF16),
        struct((2 * rows, wide // 2), BF16),
        struct((width, TILE)),
        struct((SEQ, 72, PAIR)),
        *[struct((4, 4, 8, length)) for length in DOWN_WIDTHS],
    ]
    scratch = [
        pltpu.VMEM((width, width), BF16),
        pltpu.VMEM((width, wide), BF16),
        pltpu.VMEM((wide, width), BF16),
        pltpu.SemaphoreType.DMA((12,)),
        pltpu.SemaphoreType.DMA((28,)),
        pltpu.VMEM((rows, width), BF16),
        SCAN_SCRATCH[0],
        pltpu.VMEM((rows, width), BF16),
        pltpu.VMEM((rows, width), F32),
        pltpu.VMEM((rows, width), F32),
        pltpu.VMEM((2 * rows, width), BF16),
        pltpu.VMEM((2 * rows, wide // 2), BF16),
        pltpu.VMEM((rows, wide), BF16),
        pltpu.VMEM((rows, wide), jnp.int16),
        pltpu.VMEM((2 * rows, width), BF16),
        pltpu.VMEM((4, rows, TILE), F32),
        pltpu.VMEM((4, rows, TILE), F32),
        pltpu.VMEM((2, rows, TILE), F32),
        pltpu.VMEM((2, rows, TILE), F32),
        pltpu.SemaphoreType.DMA((17,)),
        pltpu.SemaphoreType.DMA((17,)),
        pltpu.SemaphoreType.REGULAR,
        *SCAN_SCRATCH[3:],
        *slab_shapes(DOWN_WIDTHS),
        *flatten([[phase_scratch(2, length, 12)] for length in DOWN_WIDTHS]),
    ]
    specs = [VMEM_SPEC] * 5 + [ANY_SPEC] * 5
    out_specs = [ANY_SPEC] * 8 + [VMEM_SPEC] + [ANY_SPEC] * 3 + [VMEM_SPEC] + [ANY_SPEC] * 3
    operands = (x, gain_one, shift_one, gain, shift, w_qkv, cot, w_out, w_up, w_down)

    def kernel(*refs):
        front_kernel(block, *refs)

    return call(kernel, outs, out_specs, operands, specs, scratch, 1)


def last_scratch(rows, width):
    return {
        "qkv": pltpu.VMEM((3, rows, width), BF16),
        "att": pltpu.VMEM((rows, width), F32),
        "gn": pltpu.VMEM((rows, width), F32),
        "state": pltpu.VMEM((SEQ, 72, PAIR), F32),
        "x": pltpu.VMEM((rows, width), BF16),
        "grads": pltpu.VMEM((2, rows, width), F32),
        "scan": list(SCAN_SCRATCH[:3]) + [SCAN_SCRATCH[0]] + list(SCAN_SCRATCH[3:]),
        "norm_cat": pltpu.VMEM((2, 2 * rows, width // 2), BF16),
        "pre_cat": pltpu.VMEM((2 * rows, 2 * width), BF16),
        "w": pltpu.VMEM((width, 3 * width), BF16),
        "stage": pltpu.VMEM((3, rows, TILE), F32),
        "land": pltpu.VMEM((3, rows, TILE), F32),
        "swap": [pltpu.SemaphoreType.DMA((3,)), pltpu.SemaphoreType.DMA((3,))],
        "slabs": slab_shapes(UP_WIDTHS),
        "chunks": [pltpu.VMEM((4, 4, 8, length), F32) for length in DOWN_WIDTHS],
        "up_chunks": [pltpu.VMEM((4, 4, 8, length), F32) for length in UP_WIDTHS],
        "out_slabs": slab_shapes(OUT_WIDTHS),
        "vec_slab": pltpu.VMEM((4, 4, 4, 8, 128), F32),
        "sums": pltpu.VMEM((8, width), F32),
        "down": [stream_scratch(length, (1, 2), (2,)) for length in DOWN_WIDTHS],
        "up": [
            [*stream_scratch(length, (0, 1)), route_scratch(k, UP_WIDTHS, 2048)] for k, length in enumerate(UP_WIDTHS)
        ],
        "out": [
            [*stream_scratch(length, (0, 1), (1,)), route_scratch(k, OUT_WIDTHS, TILE)]
            for k, length in enumerate(OUT_WIDTHS)
        ],
        "qkv_sems": [[pltpu.SemaphoreType.DMA((6,))] * 2 for _ in QKV_WIDTHS],
        "qkv_sum": [
            [*stream_scratch(length, (1,)), route_scratch(k, QKV_WIDTHS, 3 * TILE)]
            for k, length in enumerate(QKV_WIDTHS)
        ],
        "vec": stream_scratch(128, (0, 1, 2), (0, 1, 2)),
        "vec_land": pltpu.VMEM((8, 128), F32),
        "vec_sems": pltpu.SemaphoreType.DMA((2,)),
        "credit": pltpu.SemaphoreType.REGULAR((3,)),
        "loads": pltpu.SemaphoreType.DMA((32,)),
    }


def last_kernel(
    block, qkv_in, att_in, terms_in, state_in, gn_in, gmixed_in, norm_one_in, norm_in, pre_in,
    down_in_a, down_in_b, down_in_c, out_in, x_in, weight, gain, sums_two,
    grad_input, grad_up, grad_out, grad_qkv, grad_down, grad_gains, *scratch,
):
    place = Place()
    core = place.core
    rows, width = att_in.shape
    like = last_scratch(rows, width)
    take = Taker(scratch)
    s = {name: take(like[name]) for name in like}
    qkv, att, gn, grads = s["qkv"], s["att"], s["gn"], s["grads"]
    slabs = s["slabs"]
    scan = Scan(*[Slots(ref) for ref in s["scan"][:4]], s["scan"][4:], True)
    across = [place.neighbour(0, step) for step in (1, -1, 2)]
    beside = []
    for axis in range(3):
        for step in (1, 2, 3):
            position = list(place.at)
            position[axis] = place.ring(axis, step)
            beside.append(place.id_of(*position, 1 - core))
    others = [*across, place.partner(), *beside, *scan.others()]
    greet(others)
    loads = []

    def load(source, target):
        copy = pltpu.make_async_copy(source, target, s["loads"].at[len(loads)])
        copy.start()
        loads.append(copy)
        return copy

    started = load(terms_in, scan.terms.ref)
    out_loads = []
    for k in (0, 2, 1):
        for which, start, length, at in stream_pieces(k, OUT_WIDTHS, TILE):
            source = out_in.at[:, which, :, :, :, pl.ds(start, length)]
            target = s["out_slabs"][k].at[:, :, :, :, pl.ds(at, length)]
            out_loads.append(load(source, target))
    up_loads = [load(pre_in, s["pre_cat"])]
    for which in range(2):
        for block_x in range(4):
            source = norm_in.at[:, pl.ds(block_x * 256 + which * 128, 128)]
            target = s["norm_cat"].at[which, :, pl.ds(block_x * 128, 128)]
            up_loads.append(load(source, target))
    down_in = (down_in_a, down_in_b, down_in_c)
    down_loads = [load(source, target) for source, target in zip(down_in, s["chunks"])]
    qkv_loads = [load(qkv_in, qkv), load(state_in, s["state"]), load(gn_in, gn), load(att_in, att)]
    late_loads = [load(weight, s["w"]), load(x_in, s["x"])]

    def settle(copies):
        for copy in copies:
            copy.wait()

    first, second = head_masks()
    first_wide = first_head(block)

    up_first = [phases[0] for phases in s["up"]]
    down = [Stream(place, s["chunks"][k], ORDERS[k][1:], s["down"][k]) for k in range(3)]
    up = [
        Stream(place, slabs[k], ORDERS[k], s["up"][k], None, (stream_pieces(k, UP_WIDTHS, 2048), grad_up))
        for k in range(3)
    ]
    out = [
        Stream(place, s["out_slabs"][k], ORDERS[k], s["out"][k], None, (stream_pieces(k, OUT_WIDTHS, TILE), grad_out))
        for k in range(3)
    ]
    qkv_sum = [None] * 3
    vec = [Stream(place, s["vec_slab"], ORDERS[0], s["vec"])]
    begin, forward, proceed, finish = Stream.begin, Stream.forward, Stream.proceed, Stream.finish

    def go(*steps):
        for step, streams, k in steps:
            step(streams[k])

    settle(out_loads)
    met(len(others))
    go((begin, out, 0))
    started.wait()
    scan.start()
    go((begin, out, 2))
    settle(up_loads)
    for k in range(3):
        stream_product(k, s["norm_cat"], s["pre_cat"], slabs[k], UP_WIDTHS, 2048)
        if k == 1:
            settle(down_loads)
            go((begin, down, 0), (begin, up, 0))
    go((begin, out, 1))
    norm_load = load(norm_one_in, s["norm_cat"])
    settle(qkv_loads)
    causal = causal_mask(block)
    causal_t = causal_mask(block, True)

    def local_part(unit):
        index, columns = unit_slices(unit, block)
        raw_query = qkv[0, index, columns].astype(F32)
        query, value = features(raw_query), qkv[2, index, columns]
        key = features(qkv[1, index, columns].astype(F32))
        numer = gn[index, columns]
        one, two = head_slopes(numer, att[index, columns], first_wide)
        high, low = split(numer)
        scores = dot_nt(jnp.concatenate([key * first, key * second], axis=0), query)
        wide = jnp.concatenate([high, low], axis=1)
        values = jnp.concatenate([value, value], axis=1)
        grad_query, grad_key, grad_value = 0.0, 0.0, 0.0
        for head, (mask, slope) in enumerate(((first, one), (second, two))):
            mask_wide = jnp.concatenate([mask, mask], axis=1)
            mixing = jnp.where(causal, dot_nt(wide * mask_wide, values) + slope, 0.0).astype(BF16)
            turned = jnp.where(causal_t, scores[head * block : (head + 1) * block], 0.0)
            grad_query = grad_query + dot_nn(mixing, key * mask)
            grad_key = grad_key + tn_dot(mixing, query * mask)
            grad_value = grad_value + dot_nn(turned.astype(BF16), high * mask)
        square, total = unpack_state(s["state"][unit])
        state_high, state_low = split(square)
        grad_query = grad_query + dot_nn(wide, jnp.concatenate([state_high, state_high], axis=0))
        grad_query = grad_query + dot_nn(high, state_low)
        grad_query = grad_query + jnp.where(first_wide, one, two) * total
        qkv[0, index, columns] = (grad_query * feature_slope(raw_query)).astype(BF16)
        grads[0, index, columns] = grad_key
        grads[1, index, columns] = grad_value

    def local_parts(start, count):
        def one(index, carry):
            local_part(start + index)
            return carry

        lax.fori_loop(0, count, one, 0)

    local_parts(0, 2)
    scan.middle()
    local_parts(2, 1)
    go((begin, up, 2), (forward, out, 2), (forward, out, 0))
    local_parts(3, 2)
    go((forward, out, 1))
    local_parts(5, 3)
    go((begin, up, 1))
    local_parts(8, 7)
    go((forward, up, 0))
    local_parts(15, 1)
    swap = Swap(place, s["stage"], *s["swap"])
    land, cat = s["land"], s["pre_cat"]
    own, other = pl.ds(0, rows), pl.ds(rows, rows)
    swap.put(0, 0, qkv[0, :, half_tile(0, 1 - core)], land.at[0])
    mixed_load = load(gmixed_in, att)
    scan.finish(0)
    scan.finish(1)
    go((begin, down, 2))

    def incoming(unit):
        index, columns = unit_slices(unit, block)
        square, total = unpack_state(scan.result.ref[unit])
        high, low = split(square)
        raw_key = qkv[1, index, columns].astype(F32)
        key, value = features(raw_key), qkv[2, index, columns]
        grad_key = grads[0, index, columns] + total
        grad_key = grad_key + dot_nt(
            jnp.concatenate([value, value], axis=1), jnp.concatenate([high, low], axis=1)
        )
        grad_value = grads[1, index, columns] + dot_nn(
            jnp.concatenate([key, key], axis=1), jnp.concatenate([high, low], axis=0)
        )
        qkv[1, index, columns] = (grad_key * feature_slope(raw_key)).astype(BF16)
        qkv[2, index, columns] = grad_value.astype(BF16)

    for_units(incoming, 2)
    for third in (1, 2):
        swap.put(third, third, qkv[third, :, half_tile(0, 1 - core)], land.at[third])
    settle(late_loads)

    def back_norm(columns):
        total = 0.0
        for third in range(3):
            total = total + dot_nt(qkv[third], s["w"][columns, pl.ds(third * 1024, 1024)])
        gn[:, columns] = total

    for start in (0, 256, 512, 768):
        back_norm(pl.ds(start, 256))
    for third in range(3):
        columns = pl.ds(third * TILE, TILE)
        cat[own, columns] = qkv[third, :, half_tile(0, core)]
        cat[other, columns] = swap.get(third, land.at[third])
    go((forward, up, 2), (forward, up, 1))
    norm_load.wait()
    mixed_load.wait()
    def turn(k):
        up[k].finish(s["up_chunks"][k])
        up[k].drain()
        for step in (1, -1):
            pl.semaphore_signal(
                s["credit"].at[k],
                inc=1,
                device_id=place.neighbour(ORDERS[k][0], step),
                device_id_type=MESH,
            )
        narrow = (slice(None),) * 4 + (pl.ds(0, QKV_WIDTHS[k]),)
        data = slabs[k].at[narrow]
        stream_product(k, s["norm_cat"], cat, data, QKV_WIDTHS, 3 * TILE)
        pl.semaphore_wait(s["credit"].at[k], 2)
        phases = [[up_first[k][0].at[narrow], up_first[k][1].at[narrow], *s["qkv_sems"][k]]]
        last = (stream_pieces(k, QKV_WIDTHS, 3 * TILE), grad_qkv)
        qkv_sum[k] = Stream(place, data, ORDERS[k], phases + s["qkv_sum"][k], None, last)
        qkv_sum[k].begin()

    def store(index, values):
        gn[index, :] = values

    sums = s["sums"]
    norm_back_rows(s["x"], gn, att, gain, sums, store)
    leave = load(gn, grad_input)
    go((begin, down, 1), (proceed, out, 0))
    four = jnp.concatenate([sums[0:2, :], sums_two[0:2, :]], axis=0)
    eight = jnp.concatenate([four, four], axis=0)
    turned = jnp.transpose(jnp.concatenate([eight, jnp.zeros((120, 1024), F32)], axis=0))
    turned = turned.reshape(4, 2, 4, 4, 8, 128)
    lane = lax.broadcasted_iota(jnp.int32, (8, 128), 1)
    s["vec_slab"][...] = jnp.where(lane < 4, turned[:, 0], jnp.where(lane < 8, turned[:, 1], 0.0))
    go((begin, vec, 0), (proceed, out, 1))
    turn(0)
    turn(2)
    go((begin, up, 0))
    turn(1)
    go(
        (forward, qkv_sum, 0), (forward, qkv_sum, 2), (begin, up, 1), (forward, down, 2), (forward, down, 1),
        (begin, up, 2), (proceed, out, 0), (forward, qkv_sum, 1), (proceed, vec, 0), (proceed, qkv_sum, 2),
        (proceed, qkv_sum, 0), (proceed, qkv_sum, 1), (forward, down, 0), (forward, up, 0), (forward, up, 1),
        (proceed, out, 2), (proceed, vec, 0), (forward, qkv_sum, 2), (forward, up, 2), (proceed, down, 1),
        (forward, qkv_sum, 0), (forward, qkv_sum, 1), (proceed, down, 2), (proceed, down, 0), (proceed, qkv_sum, 2),
        (proceed, up, 0), (proceed, up, 1), (proceed, out, 2), (proceed, qkv_sum, 0), (proceed, up, 2),
        (proceed, out, 1), (proceed, qkv_sum, 1), (finish, down, 2), (finish, down, 1), (finish, down, 0),
        (finish, up, 1), (finish, vec, 0),
    )
    vec_tile = vec[0].data
    vec_copy = pltpu.make_async_remote_copy(
        src_ref=vec_tile,
        dst_ref=s["vec_land"],
        send_sem=s["vec_sems"].at[0],
        recv_sem=s["vec_sems"].at[1],
        device_id=place.partner(),
        device_id_type=MESH,
    )
    vec_copy.start()
    go(
        (finish, up, 0), (finish, qkv_sum, 0), (finish, qkv_sum, 2), (finish, out, 0), (finish, qkv_sum, 1),
        (finish, out, 2), (finish, out, 1), (finish, up, 2),
    )
    for k in range(3):
        piece = down[k].data
        grad_down[pl.ds(8 * k, 8), :] = piece[:, pl.ds(0, 1024)]
        start, width_k = DOWN_CUTS[k]
        grad_down[pl.ds(24, 8), pl.ds(start, width_k)] = piece[:, pl.ds(1024, width_k)]
    scan.drain()
    for number in range(3):
        swap.copy(number, number, land.at[number]).wait_send()
    for stream in (*down, *up, *out, *qkv_sum, *vec):
        stream.drain()
    vec_copy.wait()
    grad_gains[...] = vec_tile[...] + s["vec_land"][...]
    leave.wait()


def last_part(qkv, att, terms, state, gn, gmixed, norm_one, norm_cat, pre_cat, down, out, x, weight, gain, sums_two, block):
    rows, width = x.shape

    def kernel(*refs):
        last_kernel(block, *refs)

    outs = [
        struct((rows, width)),
        struct((8, 4096)),
        struct((8, width)),
        struct((8, 3 * width)),
        struct((32, width)),
        struct((8, 128)),
    ]
    like = last_scratch(rows, width)
    scratch = [leaf for name in like for leaf in flatten(like[name])]
    out = out.reshape(4, 2, 4, 4, 8, TILE)
    operands = (
        qkv, att, terms, state, gn, gmixed, norm_one, norm_cat, pre_cat, *down, out, x, weight, gain, sums_two,
    )
    specs = [ANY_SPEC] * 15 + [VMEM_SPEC] * 2
    out_specs = [ANY_SPEC] + [VMEM_SPEC] * 5
    return call(kernel, outs, out_specs, operands, specs, scratch, 2)


def lay_out_kernel(output, grad_input, up, out, qkv, down, gains, output_to, grad_to, up_to, out_to, qkv_to, down_to, a, b, c, d):
    pairs = (
        (output, output_to), (grad_input, grad_to), (up, up_to), (out, out_to), (qkv, qkv_to), (down, down_to),
    )
    for source, target in pairs:
        target[...] = source[...]
    core = lax.rem(lax.axis_index("dp"), 2)
    turned = jnp.transpose(jnp.concatenate([gains[...], jnp.zeros((120, 128), F32)], axis=0))
    for k, target in enumerate((a, b, c, d)):
        target[...] = jnp.where(core == 0, turned[k : k + 1, :8], turned[4 + k : 5 + k, :8])


def lay_out(output, *grads):
    arrays = (output, *grads[:-1])
    outs = [struct(array.shape, array.dtype) for array in arrays] + [struct((1, 8))] * 4
    return pl.pallas_call(
        lay_out_kernel,
        out_shape=outs,
        in_specs=[VMEM_SPEC] * 7,
        out_specs=[VMEM_SPEC] * 10,
        compiler_params=pltpu.CompilerParams(vmem_limit_bytes=62 * MIB),
    )(output, *grads)


def body(
    inputs,
    first_gain,
    first_shift,
    qkv_weight,
    out_weight,
    second_gain,
    second_shift,
    up_weight,
    down_weight,
    cotangent,
):
    sequences, block, width = inputs.shape
    rows = sequences * block
    x = inputs.reshape(rows, width)
    cot = cotangent.reshape(rows, width)
    gain_one, gain_two = first_gain.reshape(1, width), second_gain.reshape(1, width)
    shift_two = second_shift.reshape(1, width)
    shift_one = first_shift.reshape(1, width)
    norm_one, qkv, att, _, state, output, gmixed, gn, sums_two, norm_cat, pre_cat, out, terms, *down = front(
        x, gain_one, shift_one, gain_two, shift_two, qkv_weight, cot, out_weight, up_weight, down_weight, block
    )
    grads = last_part(
        qkv, att, terms, state, gn, gmixed, norm_one, norm_cat, pre_cat, down, out, x, qkv_weight,
        gain_one, sums_two, block,
    )
    output, grad_input, grad_up, grad_out, grad_qkv, grad_down, *gains = lay_out(output, *grads)
    return (
        output.reshape(inputs.shape),
        grad_input.reshape(inputs.shape),
        grad_qkv,
        grad_out,
        grad_up,
        grad_down,
        *[gain.reshape(8) for gain in gains],
    )


def solution(mesh):
    return jax.shard_map(
        body,
        mesh=mesh,
        in_specs=(
            P("dp", "seq", None),
            P(),
            P(),
            P(),
            P(),
            P(),
            P(),
            P(),
            P(),
            P("dp", "seq", None),
        ),
        out_specs=(
            P("dp", "seq", None),
            P("dp", "seq", None),
            P(("dp", "seq"), None),
            P(("dp", "seq"), None),
            P(("dp", "seq"), None),
            P(("dp", "seq"), None),
            P(("dp", "seq")),
            P(("dp", "seq")),
            P(("dp", "seq")),
            P(("dp", "seq")),
        ),
        check_vma=False,
    )
```

```python
import math

import jax
import jax.numpy as jnp
from jax import lax
from jax.experimental import pallas as pl
from jax.experimental.pallas import tpu as pltpu
from jax.sharding import PartitionSpec as P

MESH = pl.DeviceIdType.MESH
F32 = jnp.float32
BF16 = jnp.bfloat16
RING = 4
MIB = 2**20


class Place:
    def __init__(self):
        dp, seq = lax.axis_index("dp"), lax.axis_index("seq")
        self.core = lax.rem(dp, 2)
        self.at = (lax.div(dp, 2), lax.div(seq, RING), lax.rem(seq, RING))

    def id_of(self, x, y, z, core):
        return (x * 2 + core, y * RING + z)

    def ring(self, axis, step):
        return lax.rem(self.at[axis] + (step + RING), RING)

    def neighbour(self, axis, step):
        at = list(self.at)
        at[axis] = self.ring(axis, step)
        return self.id_of(*at, self.core)

    def partner(self):
        return self.id_of(*self.at, 1 - self.core)


def greet(others):
    barrier = pltpu.get_barrier_semaphore()
    for other in others:
        pl.semaphore_signal(barrier, inc=1, device_id=other, device_id_type=MESH)


def met(count):
    pl.semaphore_wait(pltpu.get_barrier_semaphore(), count)


def link_neighbours(place):
    others = [place.neighbour(axis, step) for axis in range(3) for step in (1, -1)]
    return [*others, place.partner()]


ORDERS = ((0, 1, 2), (1, 2, 0), (2, 0, 1))


def phase_scratch(remaining, length, messages=6):
    if remaining:
        half = (2, 2, *[4] * (remaining - 1), 8, length)
    else:
        half = (2, 8, (length // 128 + 1) // 2 * 128)
    return [
        pltpu.VMEM((2, *[4] * remaining, 8, length), F32),
        pltpu.VMEM(half, F32),
        pltpu.SemaphoreType.DMA((messages,)),
        pltpu.SemaphoreType.DMA((messages,)),
    ]


class Phase:
    def __init__(self, place, data, axes, axis, scratch):
        self.place, self.data, self.axis = place, data, axis
        self.where = axes.index(axis)
        self.full, self.half, self.sent, self.came = scratch
        self.flying = []
        self.flat = len(axes) == 1
        self.length = data.shape[-1]
        self.cut = (self.length // 128 + 1) // 2 * 128
        self.whole = self.flat and self.cut == self.length

    def empty(self, which):
        return self.whole and which == 1

    def chunk(self, target):
        index = [slice(None)] * self.where + [target]
        return self.data.at[tuple(index)]

    def part(self, ref, which):
        if not self.flat:
            return ref.at[pl.ds(2 * which, 2)]
        if which == 0:
            return ref.at[:, pl.ds(0, self.cut)]
        return ref.at[:, pl.ds(self.cut, self.length - self.cut)]

    def through(self, way):
        ref = self.half.at[way]
        if self.flat and way == 1:
            return ref.at[:, pl.ds(0, self.length - self.cut)]
        return ref

    def copy(self, kind, way, source, target):
        number = kind * 2 + way
        return pltpu.make_async_remote_copy(
            src_ref=source,
            dst_ref=target,
            send_sem=self.sent.at[number],
            recv_sem=self.came.at[number],
            device_id=self.place.neighbour(self.axis, 1 - 2 * way),
            device_id_type=MESH,
        )

    def send(self, kind, way, source, target):
        copy = self.copy(kind, way, source, target)
        copy.start()
        self.flying.append(copy)

    def beside(self, way):
        return self.chunk(self.place.ring(self.axis, 1 - 2 * way))

    def begin_far(self):
        opposite = self.chunk(self.place.ring(self.axis, 2))
        for way in range(2):
            if not self.empty(way):
                self.send(0, way, self.part(opposite, way), self.through(way))

    def begin_near(self, way):
        if not self.empty(1 - way):
            target = self.part(self.full.at[way], 1 - way)
            self.send(1, way, self.part(self.beside(way), 1 - way), target)

    def begin(self):
        self.begin_far()
        for way in range(2):
            self.begin_near(way)

    def forward(self):
        for way in range(2):
            if self.empty(way):
                continue
            came = self.through(way)
            self.copy(0, way, came, came).wait_recv()
            own = self.part(self.beside(way), way)
            add_into(own, own, came)
            self.send(2, way, own, self.part(self.full.at[way], way))

    def finish(self, out=None):
        own = self.chunk(self.place.at[self.axis])
        for way in range(2):
            for kind, which in ((1, 1 - way), (2, way)):
                if self.empty(which):
                    continue
                target = self.part(self.full.at[way], which)
                self.copy(kind, way, target, target).wait_recv()
        add_into(own if out is None else out, own, self.full.at[0], self.full.at[1])
        return own

    def drain(self):
        for copy in self.flying:
            copy.wait_send()


HALVES = ((2, 1), (3, 0))


class SplitPhase(Phase):
    def block(self, way, j):
        return self.place.ring(0, HALVES[way][j])

    def copy_block(self, kind, way, j, source, target):
        number = kind * 4 + way * 2 + j
        return pltpu.make_async_remote_copy(
            src_ref=source,
            dst_ref=target,
            send_sem=self.sent.at[number],
            recv_sem=self.came.at[number],
            device_id=self.place.neighbour(self.axis, 1 - 2 * way),
            device_id_type=MESH,
        )

    def send_far(self, way, j):
        source = self.chunk(self.place.ring(self.axis, 2)).at[self.block(way, j)]
        self.flying.append(self.copy_block(0, way, j, source, self.half.at[way, j]))
        self.flying[-1].start()

    def send_near(self, kind, way, j):
        block = self.block(way if kind == 2 else 1 - way, j)
        source, target = self.beside(way).at[block], self.full.at[way, block]
        self.flying.append(self.copy_block(kind, way, j, source, target))
        self.flying[-1].start()

    def begin_first(self):
        for j in range(2):
            self.send_far(0, j)
        self.send_near(1, 1, 0)

    def begin_second(self):
        for j in range(2):
            self.send_far(1, j)
        self.send_near(1, 1, 1)
        for j in range(2):
            self.send_near(1, 0, j)

    def forward(self):
        for way in range(2):
            for j in range(2):
                came = self.half.at[way, j]
                self.copy_block(0, way, j, came, came).wait_recv()
                own = self.beside(way).at[self.block(way, j)]
                add_into(own, own, came)
                self.send_near(2, way, j)

    def finish(self, out=None):
        own = self.chunk(self.place.at[self.axis])
        for way in range(2):
            for kind, part in ((1, 1 - way), (2, way)):
                for j in range(2):
                    target = self.full.at[way, self.block(part, j)]
                    self.copy_block(kind, way, j, target, target).wait_recv()
        add_into(own if out is None else out, own, self.full.at[0], self.full.at[1])
        return own


class Direct:
    def __init__(self, place, data, axes, axis, scratch):
        self.place, self.data, self.axis = place, data, axis
        self.where = axes.index(axis)
        self.full, self.sent, self.came = scratch
        self.flying = []

    def chunk(self, target):
        index = [slice(None)] * self.where + [target]
        return self.data.at[tuple(index)]

    def copy(self, step, source):
        return pltpu.make_async_remote_copy(
            src_ref=source,
            dst_ref=self.full.at[step - 1],
            send_sem=self.sent.at[step - 1],
            recv_sem=self.came.at[step - 1],
            device_id=self.place.neighbour(self.axis, step),
            device_id_type=MESH,
        )

    def begin(self):
        for step in (2, 1, 3):
            copy = self.copy(step, self.chunk(self.place.ring(self.axis, step)))
            copy.start()
            self.flying.append(copy)

    def forward(self):
        pass

    def finish(self, out=None):
        own = self.chunk(self.place.at[self.axis])
        for step in (1, 2, 3):
            self.copy(step, self.full.at[step - 1]).wait_recv()
        add_into(own if out is None else out, own, *[self.full.at[k] for k in range(3)])
        return own

    def drain(self):
        for copy in self.flying:
            copy.wait_send()


class Route:
    def __init__(self, place, data, axis, pieces, scratch, out):
        self.place, self.data, self.axis, self.pieces, self.out = place, data, axis, pieces, out
        self.scratch = scratch

    def send_each(self, act):
        core = self.place.core
        for (owner, _, width, at), (land, sent, came) in zip(self.pieces, self.scratch):

            def copy(step):
                position = list(self.place.at)
                position[self.axis] = self.place.ring(self.axis, step)
                return pltpu.make_async_remote_copy(
                    src_ref=self.data.at[self.place.ring(self.axis, step), :, pl.ds(at, width)],
                    dst_ref=land.at[core, step],
                    send_sem=sent.at[step],
                    recv_sem=came.at[core, step],
                    device_id=self.place.id_of(*position, owner),
                    device_id_type=MESH,
                )

            for step in (2, 1, 3):
                act(copy(step))

            @pl.when(core != owner)
            def _():
                act(copy(0))

    def begin(self):
        self.send_each(lambda copy: copy.start())

    def forward(self):
        pass

    def finish(self, out=None):
        core = self.place.core
        mine = self.place.at[self.axis]
        for (owner, start, width, at), (land, sent, came) in zip(self.pieces, self.scratch):

            @pl.when(core == owner)
            def _():
                for source, steps in ((core, (1, 2, 3)), (1 - core, (0, 1, 2, 3))):
                    for step in steps:
                        target = land.at[source, step]
                        pltpu.make_async_remote_copy(
                            src_ref=target,
                            dst_ref=target,
                            send_sem=sent.at[step],
                            recv_sem=came.at[source, step],
                            device_id=self.place.partner(),
                            device_id_type=MESH,
                        ).wait_recv()
                done = 0
                while done < width:
                    column = start + done
                    tile, within = column // TILE, column % TILE
                    step = min(TILE - within, width - done)
                    part = pl.ds(done, step)
                    ours = self.data[mine, :, pl.ds(at + done, step)]
                    for k in (1, 2, 3):
                        ours = ours + land[core, k, :, part]
                    theirs = land[1 - core, 0, :, part]
                    for k in (1, 2, 3):
                        theirs = theirs + land[1 - core, k, :, part]
                    for values, half in ((ours, core), (theirs, 1 - core)):
                        place = pl.multiple_of((2 * tile + half) * TILE + within, 128)
                        self.out[:, pl.ds(place, step)] = values
                    done += step

    def drain(self):
        self.send_each(lambda copy: copy.wait_send())


def route_scratch(stream, widths, columns):
    return [
        [
            pltpu.VMEM((2, 4, 8, width), F32),
            pltpu.SemaphoreType.DMA((4,)),
            pltpu.SemaphoreType.DMA((2, 4)),
        ]
        for _, _, width, _ in stream_pieces(stream, widths, columns)
    ]


class Stream:
    def __init__(self, place, data, order, scratch, first=None, last=None):
        self.place, self.data, self.scratch, self.first, self.last = place, data, scratch, first, last
        self.todo, self.old = [axis for axis in order], []
        self.axes = sorted(order)
        self.phase = None

    def prepare(self):
        scratch = self.scratch.pop(0)
        if self.last and len(self.todo) == 1:
            pieces, out = self.last
            self.phase = Route(self.place, self.data, self.todo[0], pieces, scratch, out)
            return self.phase
        kind = self.first or (Phase if len(scratch) == 4 else Direct)
        self.first = None
        self.phase = kind(self.place, self.data, self.axes, self.todo[0], scratch)
        return self.phase

    def begin(self):
        self.prepare().begin()

    def forward(self):
        self.phase.forward()

    def finish(self, out=None):
        own = self.phase.finish(out)
        self.data = own if out is None else out
        self.axes.remove(self.todo.pop(0))
        self.old.append(self.phase)

    def proceed(self):
        self.finish()
        self.begin()

    def drain(self):
        for phase in self.old:
            phase.drain()
        self.old = []


def direct_scratch(remaining, length):
    return [
        pltpu.VMEM((3, *[4] * remaining, 8, length), F32),
        pltpu.SemaphoreType.DMA((3,)),
        pltpu.SemaphoreType.DMA((3,)),
    ]


def stream_scratch(length, phases, direct=()):
    return [
        (direct_scratch if phase in direct else phase_scratch)(2 - phase, length)
        for phase in phases
    ]


class Taker:
    def __init__(self, refs):
        self.refs = list(refs)

    def __call__(self, like):
        if isinstance(like, list):
            return [self(item) for item in like]
        return self.refs.pop(0)


def flatten(items):
    if isinstance(items, list):
        return [leaf for item in items for leaf in flatten(item)]
    return [items]


def add_into(out, *terms):
    if len(out.shape) > 2:

        def row(index, carry):
            add_into(out.at[index], *[term.at[index] for term in terms])
            return carry

        if len(out.shape) == 4:
            lax.fori_loop(0, out.shape[0], row, 0)
        else:
            for index in range(out.shape[0]):
                row(index, 0)
        return
    total = terms[0][...]
    for term in terms[1:]:
        total = total + term[...]
    out[...] = total


def tn_dot(left, right):
    return lax.dot_general(left, right, (((0,), (0,)), ((), ())), preferred_element_type=F32)


TILE = 512


class Swap:
    def __init__(self, place, stage, sent, came):
        self.place, self.stage, self.sent, self.came = place, stage, sent, came

    def copy(self, number, slot, target):
        return pltpu.make_async_remote_copy(
            src_ref=self.stage.at[slot],
            dst_ref=target,
            send_sem=self.sent.at[number],
            recv_sem=self.came.at[number],
            device_id=self.place.partner(),
            device_id_type=MESH,
        )

    def put(self, number, slot, values, target, before=None):
        if before is not None:
            self.copy(before, slot, target).wait_send()
        self.stage[slot] = values.astype(F32)
        self.copy(number, slot, target).start()

    def get(self, number, target):
        self.copy(number, 0, target).wait_recv()
        return target[...].astype(BF16)

    def drain(self, numbers, target):
        for number in numbers:
            self.copy(number, number % 4, target).wait_send()


def half_columns(block, core, quarter):
    half = quarter // 2
    return pl.ds(pl.multiple_of(block * quarter + core * half, half), half)


def half_tile(index, core):
    return pl.ds(pl.multiple_of((2 * index + core) * TILE, TILE), TILE)


def core_product(left, core, right, start, width, slab, at):
    done = 0
    while done < width:
        step = min(TILE, width - done)
        product = tn_dot(left[core], right[:, pl.ds(start + done, step)])
        slab[:, :, :, :, pl.ds(at + done, step)] = product.reshape(4, 4, 4, 8, step)
        done += step


UP_WIDTHS = (1536, 1280, 1280)
OUT_WIDTHS = (512, 256, 256)
QKV_WIDTHS = (1152, 896, 1024)


def stream_pieces(stream, widths, columns):
    if stream < 2:
        return [(stream, 0, widths[stream], 0)]
    pieces, at = [], 0
    for core in range(2):
        width = columns - widths[core]
        if width:
            pieces.append((core, widths[core], width, at))
        at += width
    return pieces


def stream_product(stream, left, right, slab, widths, columns):
    for core, start, width, at in stream_pieces(stream, widths, columns):
        core_product(left, core, right, start, width, slab, at)


DOWN_CUTS = ((0, 384), (384, 384), (768, 256))
DOWN_WIDTHS = (1408, 1408, 1280)


SEQ = 16
PAIR = 128
NT = (((1,), (1,)), ((), ()))
TN = (((0,), (0,)), ((), ()))


def dot_nt(left, right):
    return lax.dot_general(left, right, NT, preferred_element_type=F32)


def dot_nn(left, right):
    return jnp.dot(left, right, preferred_element_type=F32)


def split(values):
    high = values.astype(BF16)
    return high, (values - high.astype(F32)).astype(BF16)


def features(raw):
    return jnp.where(raw > 0, raw + 1.0, jnp.exp(jnp.minimum(raw, 0.0))).astype(BF16)


def feature_slope(raw):
    return jnp.where(raw > 0, 1.0, jnp.exp(jnp.minimum(raw, 0.0)))


def head_masks():
    lane = lax.broadcasted_iota(jnp.int32, (1, PAIR), 1)
    first = jnp.where(lane < 64, 1.0, 0.0)
    return first.astype(BF16), (1.0 - first).astype(BF16)


def first_head(rows):
    return lax.broadcasted_iota(jnp.int32, (rows, PAIR), 1) < 64


def pack_state(square, total):
    blocks = jnp.where(first_head(64), square[:64], square[64:])
    return blocks, jnp.broadcast_to(total, (8, PAIR))


def unpack_state(packed):
    first = first_head(64)
    square = jnp.concatenate(
        [jnp.where(first, packed[:64], 0.0), jnp.where(first, 0.0, packed[:64])], axis=0
    )
    return square, packed[64:65]


def same_head():
    row = lax.broadcasted_iota(jnp.int32, (PAIR, PAIR), 0)
    lane = lax.broadcasted_iota(jnp.int32, (PAIR, PAIR), 1)
    return (row < 64) == (lane < 64)


def head_slopes(numer, attended, first_wide):
    product = numer * attended
    ours = jnp.sum(jnp.where(first_wide, product, 0.0), axis=1, keepdims=True)
    theirs = jnp.sum(jnp.where(first_wide, 0.0, product), axis=1, keepdims=True)
    return -ours, -theirs


def state_gradient(query, numer, attended, first_wide):
    one, two = head_slopes(numer, attended, first_wide)
    high, low = split(numer)
    wide = tn_dot(query, jnp.concatenate([high, low], axis=1))
    spread = jnp.where(first_wide, one, two)
    total = jnp.sum(query.astype(F32) * spread, axis=0, keepdims=True)
    return pack_state(wide[:, :PAIR] + wide[:, PAIR:], total)


OFFSETS = sorted(
    ((y, z) for y in range(RING) for z in range(RING) if y or z),
    key=lambda offset: -sum(min(step, RING - step) for step in offset),
)


class Units:
    def __init__(self, ref):
        self.ref = ref

    def at(self, unit):
        rows = pl.ds(pl.multiple_of(lax.div(lax.rem(unit, 8), 4) * 72, 8), 72)
        columns = pl.ds(pl.multiple_of(lax.rem(unit, 4) * PAIR, PAIR), PAIR)
        return self.ref.at[lax.div(unit, 8), rows, columns]


class Slots:
    def __init__(self, ref):
        self.ref = ref

    def at(self, unit):
        return self.ref.at[unit]


class Scan:
    def __init__(self, terms, landed, sums, result, sems, reverse):
        self.terms, self.landed, self.sums, self.result = terms, landed, sums, result
        self.sems, self.reverse = sems, reverse
        self.dp, self.me = lax.axis_index("dp"), lax.axis_index("seq")
        self.y, self.z = lax.div(self.me, RING), lax.rem(self.me, RING)
        self.parity = lax.rem(self.y + self.z, 2)
        self.unit = self.unit_of(self.parity, self.me)

    def unit_of(self, parity, device):
        return parity * 8 + lax.div(device, 2)

    def at(self, y, z, sign=1):
        y = lax.rem(self.y + (sign * y + RING), RING)
        z = lax.rem(self.z + (sign * z + RING), RING)
        return y * RING + z

    def others(self):
        return [(self.dp, self.at(*offset)) for offset in OFFSETS]

    def half_offsets(self, half):
        for y in (2, 1, 3, 0):
            for step in (1, 0):
                yield y, 2 * step + lax.rem(self.parity + (y + half), 2)

    def copy(self, number, source, target, sems, other):
        return pltpu.make_async_remote_copy(
            src_ref=source,
            dst_ref=target,
            send_sem=sems[0].at[number],
            recv_sem=sems[1].at[number],
            device_id=(self.dp, other),
            device_id_type=MESH,
        )

    def start(self, half):
        for y, z in self.half_offsets(half):
            other = self.at(y, z)
            source = self.terms.at(self.unit_of(half, other))
            copy = self.copy(y * RING + z, source, self.landed.at(self.me), self.sems[:2], other)
            if y:
                copy.start()
            else:
                pl.when(z > 0)(copy.start)

    def middle(self):
        for y, z in OFFSETS:
            other = self.at(y, z, -1)
            came = self.landed.at(other)
            self.copy(y * RING + z, came, came, self.sems[:2], other).wait_recv()
        self.landed.at(self.me)[...] = self.terms.at(self.unit)[...]
        total = jnp.zeros((72, PAIR), F32)
        for k in range(SEQ):
            at = SEQ - 1 - k if self.reverse else k
            self.sums.at(at)[...] = total
            total = total + self.landed.at(at)[...]
        for y, z in OFFSETS:
            other = self.at(y, z)
            target = self.result.at(self.unit)
            self.copy(y * RING + z, self.sums.at(other), target, self.sems[2:], other).start()
        self.result.at(self.unit)[...] = self.sums.at(self.me)[...]

    def finish(self, half):
        for y, z in self.half_offsets(half):
            other = self.at(y, z, -1)
            came = self.result.at(self.unit_of(half, other))
            copy = self.copy(y * RING + z, came, came, self.sems[2:], other)
            if y:
                copy.wait_recv()
            else:
                pl.when(z > 0)(copy.wait_recv)

    def drain(self):
        for y, z in OFFSETS:
            number, other = y * RING + z, self.at(y, z)
            self.copy(number, self.terms.at(0), self.landed.at(0), self.sems[:2], other).wait_send()
            self.copy(number, self.sums.at(0), self.result.at(0), self.sems[2:], other).wait_send()


SCAN_SCRATCH = [
    pltpu.VMEM((SEQ, 72, PAIR), F32),
    pltpu.VMEM((SEQ, 72, PAIR), F32),
    pltpu.VMEM((SEQ, 72, PAIR), F32),
    *[pltpu.SemaphoreType.DMA((SEQ,)) for _ in range(4)],
]


def unit_slices(unit, block):
    rows = pl.ds(pl.multiple_of(lax.div(unit, 8) * block, block), block)
    columns = pl.ds(pl.multiple_of(lax.rem(unit, 8) * PAIR, PAIR), PAIR)
    return rows, columns


def for_units(step, together):
    def several(index, carry):
        for offset in range(together):
            step(index * together + offset)
        return carry

    lax.fori_loop(0, SEQ // together, several, 0)


def causal_mask(block, transposed=False):
    row = lax.broadcasted_iota(jnp.int32, (block, block), 0)
    column = lax.broadcasted_iota(jnp.int32, (block, block), 1)
    return (row <= column) if transposed else (row >= column)


def norm_rows(values):
    center = jnp.mean(values, axis=-1, keepdims=True)
    centered = values - center
    variance = jnp.mean(centered * centered, axis=-1, keepdims=True)
    inverse = lax.rsqrt(variance + 1e-05)
    return centered * inverse, inverse


ROWS = 64


def for_rows(count, step):
    def one(index, carry):
        step(pl.ds(pl.multiple_of(index * ROWS, ROWS), ROWS))
        return carry

    lax.fori_loop(0, count // ROWS, one, 0)


def for_columns(count, width, step):
    def one(index, carry):
        step(pl.ds(pl.multiple_of(index * width, width), width))
        return carry

    lax.fori_loop(0, count // width, one, 0)


SLOPE_SCALE = 28000.0


def gelu_both(pre):
    cumulative = 0.5 * (1.0 + lax.erf(pre * (1.0 / math.sqrt(2.0))))
    density = jnp.exp(-0.5 * pre * pre) * (1.0 / math.sqrt(2.0 * math.pi))
    slope = (cumulative + pre * density) * SLOPE_SCALE
    return (pre * cumulative).astype(BF16), jnp.round(slope).astype(jnp.int32).astype(jnp.int16)


def norm_back(grad, gain, scaled, inverse):
    spread = grad * gain
    first_mean = jnp.mean(spread, axis=-1, keepdims=True)
    second_mean = jnp.mean(spread * scaled, axis=-1, keepdims=True)
    return inverse * (spread - first_mean - scaled * second_mean)


def norm_back_rows(values, grad, base, gain, sums, store):
    sums[...] = jnp.zeros_like(sums)

    def step(rows):
        scaled, inverse = norm_rows(values[rows, :].astype(F32))
        part = grad[rows, :]
        sums[0:1, :] += jnp.sum(part * scaled, axis=0, keepdims=True)
        sums[1:2, :] += jnp.sum(part, axis=0, keepdims=True)
        store(rows, base[rows, :].astype(F32) + norm_back(part, gain[...], scaled, inverse))

    for_rows(grad.shape[0], step)


def front_kernel(
    block, x, gain_one, shift_one, gain, shift, w_qkv, cot_in, w_out, w_up, w_down,
    norm_one_out, qkv_out, att_out, den_out, state_out, output_out, gmixed_out, gn_out, sums, norm_out, pre_out,
    out_out, terms, down_a, down_b, down_c,
    wo, wu, wd, wsem, osem, att_low, state, output, gmixed, gatt, norm_cat, pre_cat, hidden, slope, cot_cat,
    stage, land, land_att, land_norm, swap_sent, swap_came, free, s0, s1, s2, s3, *scratch,
):
    take_scratch = Taker(scratch)
    slabs = take_scratch(slab_shapes(DOWN_WIDTHS))
    slab_a, slab_b, slab_c = slabs
    phases = take_scratch([[phase_scratch(2, length, 12)] for length in DOWN_WIDTHS])
    place = Place()
    core = place.core
    rows = x.shape[0]
    scan = Scan(Slots(terms), Units(land_att), Units(land_norm), Slots(state), (s0, s1, s2, s3), False)
    others = [place.neighbour(0, 1), place.neighbour(0, -1), place.partner(), *scan.others()]
    greet(others)
    own, other = pl.ds(0, rows), pl.ds(rows, rows)

    def load(source, target, slot):
        copy = pltpu.make_async_copy(source, target, wsem.at[slot])
        copy.start()
        return copy

    outs = []

    def leave(source, target):
        copy = pltpu.make_async_copy(source, target, osem.at[len(outs)])
        copy.start()
        outs.append(copy)
        return copy

    def settle(copies):
        for copy in copies:
            copy.wait()
            settled.append(id(copy))

    settled = []
    thirds = [
        load(w_qkv.at[:, pl.ds(third * 1024, 1024)], wu.at[:, pl.ds(slot * 1024, 1024)], slot)
        for slot, third in enumerate((1, 2, 0))
    ]
    cot_load = load(cot_in, cot_cat.at[own], 3)
    out_load = load(w_out, wo, 4)

    def norm_step(index):
        scaled, _ = norm_rows(x[index, :].astype(F32))
        hidden[index, pl.ds(0, 1024)] = (scaled * gain_one[...] + shift_one[...]).astype(BF16)

    for_rows(rows, norm_step)

    def shifted(columns, offset):
        return pl.ds(pl.multiple_of(columns.start + offset, PAIR), columns.size)

    def later_rows(index, offset):
        return pl.ds(pl.multiple_of(index.start + offset, 64), index.size)

    def project(slot, third, feature):
        thirds[slot].wait()

        def step(columns):
            raw = dot_nn(hidden[:, pl.ds(0, 1024)], wu[:, shifted(columns, slot * 1024)]).astype(BF16)
            hidden[:, shifted(columns, 1024 + third * 1024)] = raw
            if feature is not None:
                wd[pl.ds(feature * rows, rows), columns] = features(raw.astype(F32))

        for_columns(1024, TILE, step)

    project(0, 1, 1)
    project(1, 2, None)

    def local_state(unit):
        index, columns = unit_slices(unit, block)
        keys = wd[later_rows(index, rows), columns]
        square = tn_dot(hidden[index, shifted(columns, 3072)], keys)
        total = jnp.sum(keys.astype(F32), axis=0, keepdims=True)
        blocks, row = pack_state(square, total)
        terms[unit, pl.ds(0, 64)] = blocks
        terms[unit, pl.ds(64, 8)] = row

    def local_states(half):
        def four(index, carry):
            for offset in range(4):
                local_state(half * 8 + index * 4 + offset)
            return carry

        lax.fori_loop(0, 2, four, 0)

    local_states(0)
    met(len(others))
    scan.start(0)
    local_states(1)
    scan.start(1)
    swap = Swap(place, stage, swap_sent, swap_came)
    for which in range(2):
        for block_x in range(4):
            columns = pl.ds(block_x * 256 + which * 128, 128)
            pre_cat[own, pl.ds(which * TILE + block_x * 128, 128)] = hidden[:, columns]
        swap.put(which, which, pre_cat[own, pl.ds(which * TILE, TILE)], land.at[which])
    cot_load.wait()
    for tile in range(2):
        swap.put(2 + tile, 2 + tile, cot_cat[own, pl.ds(tile * TILE, TILE)], land.at[2 + tile])
    qkv_leaves = [leave(hidden.at[:, pl.ds(third * 1024 + 1024, 1024)], qkv_out.at[third]) for third in (1, 2)]
    project(2, 0, 0)
    qkv_leaves.append(leave(hidden.at[:, pl.ds(1024, 1024)], qkv_out.at[0]))
    up_load = load(w_up, wu, 6)
    first, second = head_masks()
    causal = causal_mask(block)

    def local_part(unit):
        index, columns = unit_slices(unit, block)
        query, key = wd[index, columns], wd[later_rows(index, rows), columns]
        value = hidden[index, shifted(columns, 3072)]
        scores = dot_nt(jnp.concatenate([query * first, query * second], axis=0), key)
        both = 0.0
        for head, mask in enumerate((first, second)):
            kept = jnp.where(causal, scores[head * block : (head + 1) * block], 0.0).astype(BF16)
            right = jnp.concatenate([value * mask, jnp.broadcast_to(mask, value.shape)], axis=1)
            both = both + dot_nn(kept, right)
        gmixed[index, columns] = both[:, :PAIR]
        gatt[index, columns] = both[:, PAIR:]

    def local_parts(start, count):
        def two(index, carry):
            local_part(start + 2 * index)
            local_part(start + 2 * index + 1)
            return carry

        lax.fori_loop(0, count // 2, two, 0)

    local_parts(0, 10)
    scan.middle()
    local_parts(10, 6)
    for which in range(2):
        pre_cat[other, pl.ds(which * TILE, TILE)] = swap.get(which, land.at[which])
        cot_cat[other, pl.ds(which * TILE, TILE)] = swap.get(2 + which, land.at[2 + which])
    cat_leaves = [leave(pre_cat.at[:, pl.ds(which * TILE, TILE)], norm_one_out.at[which]) for which in range(2)]
    together = same_head()

    def incoming(unit):
        index, columns = unit_slices(unit, block)
        square, total = unpack_state(state[unit])
        totals = jnp.where(together, jnp.broadcast_to(total, (PAIR, PAIR)), 0.0)
        high, low = split(jnp.concatenate([square, totals], axis=0))
        query = wd[index, columns]
        both = dot_nt(
            jnp.concatenate([query, query], axis=1), jnp.concatenate([high, low], axis=1)
        )
        denom = gatt[index, columns] + both[:, PAIR:]
        attended = (gmixed[index, columns] + both[:, :PAIR]) / denom
        tile, within = stage_place(unit)
        stage[tile, index, within] = attended
        stage[2 + tile, index, within] = denom
        att_low[index, columns] = attended.astype(BF16)

    def stage_place(unit):
        pair = lax.rem(unit, 8)
        return lax.div(pair, 4), pl.ds(pl.multiple_of(lax.rem(pair, 4) * PAIR, PAIR), PAIR)

    mixed = gatt

    def up(columns, index):
        ours, ours_slope = gelu_both(dot_nn(norm_cat[index, :], wu[:, columns]))
        hidden[index, columns] = ours
        slope[index, columns] = ours_slope

    settle(qkv_leaves)
    swap.drain(range(4), land.at[0])
    att_leaves = []
    for half in range(2):
        scan.finish(half)
        leave(state.at[pl.ds(half * 8, 8)], state_out.at[pl.ds(half * 8, 8)])

        def several(index, carry):
            incoming(half * 8 + 2 * index)
            incoming(half * 8 + 2 * index + 1)
            return carry

        lax.fori_loop(0, 4, several, 0)
        part = pl.ds(half * block, block)
        for slot in range(4):
            target = (att_out, den_out)[slot // 2].at[part, pl.ds(slot % 2 * TILE, TILE)]
            att_leaves.append(leave(stage.at[slot, part], target))
        if half == 0:
            out_load.wait()

        def mix(columns):
            mixed[part, columns] = x[part, columns].astype(F32) + dot_nn(att_low[part, :], wo[:, columns])

        mix(pl.ds(0, 1024))
        for start in range(0, block, ROWS):
            index = pl.ds(half * block + start, ROWS)
            scaled, _ = norm_rows(mixed[index, :])
            norm_cat[index, :] = (scaled * gain[...] + shift[...]).astype(BF16)
        if half == 0:
            up_load.wait()
    down_load = load(w_down, wd, 5)
    scan.drain()
    pl.semaphore_signal(free, inc=1, device_id=place.partner(), device_id_type=MESH)
    settle(att_leaves)
    pl.semaphore_wait(free, 1)

    def nth_block(index):
        return lax.rem(place.at[0] + jnp.where(index == 2, 3, jnp.maximum(2 - index, 0)), RING)

    def give(index, carry):
        columns = half_columns(nth_block(index), 1 - core, 1024)
        up(columns, own)
        swap.put(4 + index, index, hidden[:, columns], land.at[index])
        return carry

    lax.fori_loop(0, 4, give, 0)

    def take(index, carry):
        block_x = nth_block(index)
        columns = half_columns(block_x, core, 1024)
        up(columns, own)
        both = jnp.concatenate([hidden[:, columns], swap.get(4 + index, land.at[index])], axis=0)
        for half in range(2):
            columns = pl.ds(half * TILE, TILE)
            product = tn_dot(both, cot_cat[:, columns]).reshape(4, 4, 4, 8, TILE)
            for stream in range(3):
                slabs[stream][block_x, :, :, :, columns] = product[:, :, stream]
            last = product[:, :, 3]
            if half == 0:
                slab_a[block_x, :, :, :, pl.ds(1024, 384)] = last[..., :384]
                slab_b[block_x, :, :, :, pl.ds(1024, 128)] = last[..., 384:]
            else:
                slab_b[block_x, :, :, :, pl.ds(1152, 256)] = last[..., :256]
                slab_c[block_x, :, :, :, pl.ds(1024, 256)] = last[..., 256:]
        return carry

    kinds = (None, SplitPhase, SplitPhase)
    down = [Stream(place, slabs[k], ORDERS[k], phases[k], kinds[k]) for k in range(3)]
    lead, *others_two = [stream.prepare() for stream in down]
    lax.fori_loop(0, 2, take, 0)
    lead.begin_far()
    for phase in others_two:
        phase.begin_first()
    lead.begin_near(0)
    lax.fori_loop(2, 4, take, 0)
    for phase in others_two:
        phase.begin_second()
    lead.begin_near(1)
    pl.semaphore_signal(free, inc=1, device_id=place.partner(), device_id_type=MESH)
    for tile in range(2):
        columns = pl.ds(tile * TILE, TILE)
        swap.put(8 + tile, tile, norm_cat[own, columns], land_norm.at[tile], before=4 + tile)
    down_load.wait()
    cot = cot_cat.at[own]

    def finish_forward(columns):
        output[:, columns] = (mixed[:, columns] + dot_nn(hidden[...], wd[:, columns])).astype(BF16)

    for_columns(1024, 256, finish_forward)
    leave(output, output_out)

    def back(columns):
        held = slope[:, columns].astype(jnp.int32).astype(F32) * (1.0 / SLOPE_SCALE)
        grad = dot_nt(cot[...], wd[columns, :]) * held
        low = grad.astype(BF16)
        hidden[:, columns] = low
        return low

    pl.semaphore_wait(free, 1)

    def give_back(block, carry):
        theirs = back(half_columns(block, 1 - core, 1024))
        before = jnp.where(block < 2, 8 + block, 4 + block)
        swap.put(10 + block, block, theirs, land.at[block], before=before)
        return carry

    lax.fori_loop(0, 4, give_back, 0)

    def keep_back(block, carry):
        columns = pl.ds(pl.multiple_of(block * TILE, TILE), TILE)
        pre_cat[own, columns] = back(half_columns(block, core, 1024))
        return carry

    settle(cat_leaves)
    lax.fori_loop(0, 4, keep_back, 0)
    for stream in down:
        stream.forward()

    def back_up(columns):
        gmixed[:, columns] = dot_nt(hidden[...], wu[columns, :])

    for_columns(1024, 256, back_up)

    def take_back(block, carry):
        columns = pl.ds(pl.multiple_of(block * TILE, TILE), TILE)
        pre_cat[other, columns] = swap.get(10 + block, land.at[block])
        return carry

    lax.fori_loop(0, 4, take_back, 0)
    leave(pre_cat, pre_out)
    for tile in range(2):
        columns = pl.ds(tile * TILE, TILE)
        norm_cat[other, columns] = swap.get(8 + tile, land_norm.at[tile])
        swap.put(14 + tile, tile, att_low[:, columns], land_att.at[tile], before=10 + tile)
    leave(norm_cat, norm_out)
    query_load = load(qkv_out.at[0], wd.at[own], 7)
    pl.semaphore_signal(free, inc=1, device_id=place.partner(), device_id_type=MESH)
    def store(index, values):
        gmixed[index, :] = values
        hidden[index, pl.ds(0, 1024)] = values.astype(BF16)

    norm_back_rows(mixed, gmixed, cot, gain, sums, store)
    leave(gmixed, gmixed_out)
    pl.semaphore_wait(free, 1)
    swap.put(16, 2, hidden[:, half_tile(0, 1 - core)], land_norm.at[0], before=12)

    def back_out(columns):
        gatt[:, columns] = dot_nt(hidden[:, pl.ds(0, 1024)], wo[columns, :])

    state_loads = [query_load]

    def load_state(slots):
        for slot in slots:
            source = (att_out, den_out)[slot // 2].at[:, pl.ds(slot % 2 * TILE, TILE)]
            state_loads.append(load(source, stage.at[slot], 8 + slot))

    for number, slot in ((13, 3), (14, 0), (15, 1)):
        swap.copy(number, slot, land_norm.at[0]).wait_send()
    load_state((0, 1, 3))
    for_columns(1024, TILE, back_out)
    ours = hidden[:, half_tile(0, core)]
    swap.copy(16, 2, land_norm.at[0]).wait_send()
    load_state((2,))
    theirs = swap.get(16, land_norm.at[0])
    for tile in range(2):
        swap.copy(14 + tile, tile, land_att.at[tile]).wait_recv()
        for part, (start, width) in enumerate(((0, 384), (384, 128))):
            product = tn_dot(att_low[:, pl.ds(tile * TILE + start, width)], ours)
            theirs_att = land_att[tile, :, pl.ds(start, width)].astype(BF16)
            land[2 * tile + part, pl.ds(0, width), :] = product + tn_dot(theirs_att, theirs)
            leave(land.at[2 * tile + part, pl.ds(0, width)], out_out.at[pl.ds(tile * TILE + start, width)])
    for copy in state_loads:
        copy.wait()
    first_wide = first_head(block)

    def state_back(unit):
        index, columns = unit_slices(unit, block)
        tile, within = stage_place(unit)
        numer = gatt[index, columns] / stage[2 + tile, index, within]
        gatt[index, columns] = numer
        query = features(wd[index, columns].astype(F32))
        blocks, row = state_gradient(query, numer, stage[tile, index, within], first_wide)
        terms[unit, pl.ds(0, 64)] = blocks
        terms[unit, pl.ds(64, 8)] = row

    for_units(state_back, 2)
    leave(gatt, gn_out)
    for stream, target in zip(down, (down_a, down_b, down_c)):
        stream.finish()
        leave(stream.data, target)
    for stream in down:
        stream.drain()
    for copy in outs:
        if id(copy) not in settled:
            copy.wait()


def slab_shapes(widths):
    return [pltpu.VMEM((4, 4, 4, 8, width), F32) for width in widths]


def struct(shape, dtype=F32):
    return jax.ShapeDtypeStruct(shape, dtype)


VMEM_SPEC = pl.BlockSpec(memory_space=pltpu.VMEM)
ANY_SPEC = pl.BlockSpec(memory_space=pl.ANY)


def call(kernel, outs, out_specs, operands, in_specs, scratch, collective_id):
    return pl.pallas_call(
        kernel,
        out_shape=outs,
        in_specs=in_specs,
        out_specs=out_specs,
        scratch_shapes=scratch,
        compiler_params=pltpu.CompilerParams(
            collective_id=collective_id, has_side_effects=True, vmem_limit_bytes=63 * MIB
        ),
    )(*operands)


def front(x, gain_one, shift_one, gain, shift, w_qkv, cot, w_out, w_up, w_down, block):
    rows, width = x.shape
    wide = w_up.shape[1]
    outs = [
        struct((2, 2 * rows, width // 2), BF16),
        struct((3, rows, width), BF16),
        struct((rows, width)),
        struct((rows, width)),
        struct((SEQ, 72, PAIR)),
        struct((rows, width), BF16),
        struct((rows, width)),
        struct((rows, width)),
        struct((8, width)),
        struct((2 * rows, width), BF16),
        struct((2 * rows, wide // 2), BF16),
        struct((width, TILE)),
        struct((SEQ, 72, PAIR)),
        *[struct((4, 4, 8, length)) for length in DOWN_WIDTHS],
    ]
    scratch = [
        pltpu.VMEM((width, width), BF16),
        pltpu.VMEM((width, wide), BF16),
        pltpu.VMEM((wide, width), BF16),
        pltpu.SemaphoreType.DMA((12,)),
        pltpu.SemaphoreType.DMA((28,)),
        pltpu.VMEM((rows, width), BF16),
        SCAN_SCRATCH[0],
        pltpu.VMEM((rows, width), BF16),
        pltpu.VMEM((rows, width), F32),
        pltpu.VMEM((rows, width), F32),
        pltpu.VMEM((2 * rows, width), BF16),
        pltpu.VMEM((2 * rows, wide // 2), BF16),
        pltpu.VMEM((rows, wide), BF16),
        pltpu.VMEM((rows, wide), jnp.int16),
        pltpu.VMEM((2 * rows, width), BF16),
        pltpu.VMEM((4, rows, TILE), F32),
        pltpu.VMEM((4, rows, TILE), F32),
        pltpu.VMEM((2, rows, TILE), F32),
        pltpu.VMEM((2, rows, TILE), F32),
        pltpu.SemaphoreType.DMA((17,)),
        pltpu.SemaphoreType.DMA((17,)),
        pltpu.SemaphoreType.REGULAR,
        *SCAN_SCRATCH[3:],
        *slab_shapes(DOWN_WIDTHS),
        *flatten([[phase_scratch(2, length, 12)] for length in DOWN_WIDTHS]),
    ]
    specs = [VMEM_SPEC] * 5 + [ANY_SPEC] * 5
    out_specs = [ANY_SPEC] * 8 + [VMEM_SPEC] + [ANY_SPEC] * 3 + [VMEM_SPEC] + [ANY_SPEC] * 3
    operands = (x, gain_one, shift_one, gain, shift, w_qkv, cot, w_out, w_up, w_down)

    def kernel(*refs):
        front_kernel(block, *refs)

    return call(kernel, outs, out_specs, operands, specs, scratch, 1)


def last_scratch(rows, width):
    return {
        "qkv": pltpu.VMEM((3, rows, width), BF16),
        "att": pltpu.VMEM((rows, width), F32),
        "gn": pltpu.VMEM((rows, width), F32),
        "state": pltpu.VMEM((SEQ, 72, PAIR), F32),
        "x": pltpu.VMEM((rows, width), BF16),
        "grads": pltpu.VMEM((2, rows, width), F32),
        "scan": list(SCAN_SCRATCH[:3]) + [SCAN_SCRATCH[0]] + list(SCAN_SCRATCH[3:]),
        "norm_cat": pltpu.VMEM((2, 2 * rows, width // 2), BF16),
        "pre_cat": pltpu.VMEM((2 * rows, 2 * width), BF16),
        "w": pltpu.VMEM((width, 3 * width), BF16),
        "stage": pltpu.VMEM((3, rows, TILE), F32),
        "land": pltpu.VMEM((3, rows, TILE), F32),
        "swap": [pltpu.SemaphoreType.DMA((3,)), pltpu.SemaphoreType.DMA((3,))],
        "slabs": slab_shapes(UP_WIDTHS),
        "chunks": [pltpu.VMEM((4, 4, 8, length), F32) for length in DOWN_WIDTHS],
        "up_chunks": [pltpu.VMEM((4, 4, 8, length), F32) for length in UP_WIDTHS],
        "out_slabs": slab_shapes(OUT_WIDTHS),
        "vec_slab": pltpu.VMEM((4, 4, 4, 8, 128), F32),
        "sums": pltpu.VMEM((8, width), F32),
        "down": [stream_scratch(length, (1, 2), (2,)) for length in DOWN_WIDTHS],
        "up": [
            [*stream_scratch(length, (0, 1)), route_scratch(k, UP_WIDTHS, 2048)] for k, length in enumerate(UP_WIDTHS)
        ],
        "out": [
            [*stream_scratch(length, (0, 1), (1,)), route_scratch(k, OUT_WIDTHS, TILE)]
            for k, length in enumerate(OUT_WIDTHS)
        ],
        "qkv_sems": [[pltpu.SemaphoreType.DMA((6,))] * 2 for _ in QKV_WIDTHS],
        "qkv_sum": [
            [*stream_scratch(length, (1,)), route_scratch(k, QKV_WIDTHS, 3 * TILE)]
            for k, length in enumerate(QKV_WIDTHS)
        ],
        "vec": stream_scratch(128, (0, 1, 2), (0, 1, 2)),
        "vec_land": pltpu.VMEM((8, 128), F32),
        "vec_sems": pltpu.SemaphoreType.DMA((2,)),
        "credit": pltpu.SemaphoreType.REGULAR((3,)),
        "loads": pltpu.SemaphoreType.DMA((32,)),
    }


def last_kernel(
    block, qkv_in, att_in, terms_in, state_in, gn_in, gmixed_in, norm_one_in, norm_in, pre_in,
    down_in_a, down_in_b, down_in_c, out_in, x_in, weight, gain, sums_two,
    grad_input, grad_up, grad_out, grad_qkv, grad_down, grad_gains, *scratch,
):
    place = Place()
    core = place.core
    rows, width = att_in.shape
    like = last_scratch(rows, width)
    take = Taker(scratch)
    s = {name: take(like[name]) for name in like}
    qkv, att, gn, grads = s["qkv"], s["att"], s["gn"], s["grads"]
    slabs = s["slabs"]
    scan = Scan(*[Slots(ref) for ref in s["scan"][:4]], s["scan"][4:], True)
    across = [place.neighbour(0, step) for step in (1, -1, 2)]
    beside = []
    for axis in range(3):
        for step in (1, 2, 3):
            position = list(place.at)
            position[axis] = place.ring(axis, step)
            beside.append(place.id_of(*position, 1 - core))
    others = [*across, place.partner(), *beside, *scan.others()]
    greet(others)
    loads = []

    def load(source, target):
        copy = pltpu.make_async_copy(source, target, s["loads"].at[len(loads)])
        copy.start()
        loads.append(copy)
        return copy

    started = load(terms_in, scan.terms.ref)
    out_loads = []
    for k in (0, 2, 1):
        for which, start, length, at in stream_pieces(k, OUT_WIDTHS, TILE):
            source = out_in.at[:, which, :, :, :, pl.ds(start, length)]
            target = s["out_slabs"][k].at[:, :, :, :, pl.ds(at, length)]
            out_loads.append(load(source, target))
    up_loads = [load(pre_in, s["pre_cat"])]
    for which in range(2):
        for block_x in range(4):
            source = norm_in.at[:, pl.ds(block_x * 256 + which * 128, 128)]
            target = s["norm_cat"].at[which, :, pl.ds(block_x * 128, 128)]
            up_loads.append(load(source, target))
    down_in = (down_in_a, down_in_b, down_in_c)
    down_loads = [load(source, target) for source, target in zip(down_in, s["chunks"])]
    qkv_loads = [load(qkv_in, qkv), load(state_in, s["state"]), load(gn_in, gn), load(att_in, att)]
    late_loads = [load(weight, s["w"]), load(x_in, s["x"])]

    def settle(copies):
        for copy in copies:
            copy.wait()

    first, second = head_masks()
    first_wide = first_head(block)

    up_first = [phases[0] for phases in s["up"]]
    down = [Stream(place, s["chunks"][k], ORDERS[k][1:], s["down"][k]) for k in range(3)]
    up = [
        Stream(place, slabs[k], ORDERS[k], s["up"][k], None, (stream_pieces(k, UP_WIDTHS, 2048), grad_up))
        for k in range(3)
    ]
    out = [
        Stream(place, s["out_slabs"][k], ORDERS[k], s["out"][k], None, (stream_pieces(k, OUT_WIDTHS, TILE), grad_out))
        for k in range(3)
    ]
    qkv_sum = [None] * 3
    vec = [Stream(place, s["vec_slab"], ORDERS[0], s["vec"])]
    begin, forward, proceed, finish = Stream.begin, Stream.forward, Stream.proceed, Stream.finish

    def go(*steps):
        for step, streams, k in steps:
            step(streams[k])

    settle(out_loads)
    met(len(others))
    go((begin, out, 0))
    started.wait()
    scan.start(0)
    scan.start(1)
    go((begin, out, 2))
    settle(up_loads)
    for k in range(3):
        stream_product(k, s["norm_cat"], s["pre_cat"], slabs[k], UP_WIDTHS, 2048)
        if k == 1:
            settle(down_loads)
            go((begin, down, 0), (begin, up, 0))
    go((begin, out, 1))
    norm_load = load(norm_one_in, s["norm_cat"])
    settle(qkv_loads)
    causal = causal_mask(block)
    causal_t = causal_mask(block, True)

    def local_part(unit):
        index, columns = unit_slices(unit, block)
        raw_query = qkv[0, index, columns].astype(F32)
        query, value = features(raw_query), qkv[2, index, columns]
        key = features(qkv[1, index, columns].astype(F32))
        numer = gn[index, columns]
        one, two = head_slopes(numer, att[index, columns], first_wide)
        high, low = split(numer)
        scores = dot_nt(jnp.concatenate([key * first, key * second], axis=0), query)
        wide = jnp.concatenate([high, low], axis=1)
        values = jnp.concatenate([value, value], axis=1)
        grad_query, grad_key, grad_value = 0.0, 0.0, 0.0
        for head, (mask, slope) in enumerate(((first, one), (second, two))):
            mask_wide = jnp.concatenate([mask, mask], axis=1)
            mixing = split(jnp.where(causal, dot_nt(wide * mask_wide, values) + slope, 0.0))
            turned = jnp.where(causal_t, scores[head * block : (head + 1) * block], 0.0)
            for part in mixing:
                grad_query = grad_query + dot_nn(part, key * mask)
                grad_key = grad_key + tn_dot(part, query * mask)
            both = dot_nn(turned.astype(BF16), wide * mask_wide)
            grad_value = grad_value + both[:, :PAIR] + both[:, PAIR:]
        square, total = unpack_state(s["state"][unit])
        state_high, state_low = split(square)
        grad_query = grad_query + dot_nn(wide, jnp.concatenate([state_high, state_high], axis=0))
        grad_query = grad_query + dot_nn(high, state_low)
        grad_query = grad_query + jnp.where(first_wide, one, two) * total
        qkv[0, index, columns] = (grad_query * feature_slope(raw_query)).astype(BF16)
        grads[0, index, columns] = grad_key
        grads[1, index, columns] = grad_value

    def local_parts(start, count):
        def one(index, carry):
            local_part(start + index)
            return carry

        lax.fori_loop(0, count, one, 0)

    local_parts(0, 2)
    scan.middle()
    local_parts(2, 1)
    go((begin, up, 2), (forward, out, 2), (forward, out, 0))
    local_parts(3, 2)
    go((forward, out, 1))
    local_parts(5, 3)
    go((begin, up, 1))
    local_parts(8, 7)
    go((forward, up, 0))
    local_parts(15, 1)
    swap = Swap(place, s["stage"], *s["swap"])
    land, cat = s["land"], s["pre_cat"]
    own, other = pl.ds(0, rows), pl.ds(rows, rows)
    swap.put(0, 0, qkv[0, :, half_tile(0, 1 - core)], land.at[0])
    mixed_load = load(gmixed_in, att)
    scan.finish(0)
    scan.finish(1)
    go((begin, down, 2))

    def incoming(unit):
        index, columns = unit_slices(unit, block)
        square, total = unpack_state(scan.result.ref[unit])
        high, low = split(square)
        raw_key = qkv[1, index, columns].astype(F32)
        key, value = features(raw_key), qkv[2, index, columns]
        grad_key = grads[0, index, columns] + total
        grad_key = grad_key + dot_nt(
            jnp.concatenate([value, value], axis=1), jnp.concatenate([high, low], axis=1)
        )
        grad_value = grads[1, index, columns] + dot_nn(
            jnp.concatenate([key, key], axis=1), jnp.concatenate([high, low], axis=0)
        )
        qkv[1, index, columns] = (grad_key * feature_slope(raw_key)).astype(BF16)
        qkv[2, index, columns] = grad_value.astype(BF16)

    for_units(incoming, 2)
    for third in (1, 2):
        swap.put(third, third, qkv[third, :, half_tile(0, 1 - core)], land.at[third])
    settle(late_loads)

    def back_norm(columns):
        total = 0.0
        for third in range(3):
            total = total + dot_nt(qkv[third], s["w"][columns, pl.ds(third * 1024, 1024)])
        gn[:, columns] = total

    for start in (0, 256, 512, 768):
        back_norm(pl.ds(start, 256))
    for third in range(3):
        columns = pl.ds(third * TILE, TILE)
        cat[own, columns] = qkv[third, :, half_tile(0, core)]
        cat[other, columns] = swap.get(third, land.at[third])
    go((forward, up, 2), (forward, up, 1))
    norm_load.wait()
    mixed_load.wait()
    def turn(k):
        up[k].finish(s["up_chunks"][k])
        up[k].drain()
        for step in (1, -1):
            pl.semaphore_signal(
                s["credit"].at[k],
                inc=1,
                device_id=place.neighbour(ORDERS[k][0], step),
                device_id_type=MESH,
            )
        narrow = (slice(None),) * 4 + (pl.ds(0, QKV_WIDTHS[k]),)
        data = slabs[k].at[narrow]
        stream_product(k, s["norm_cat"], cat, data, QKV_WIDTHS, 3 * TILE)
        pl.semaphore_wait(s["credit"].at[k], 2)
        phases = [[up_first[k][0].at[narrow], up_first[k][1].at[narrow], *s["qkv_sems"][k]]]
        last = (stream_pieces(k, QKV_WIDTHS, 3 * TILE), grad_qkv)
        qkv_sum[k] = Stream(place, data, ORDERS[k], phases + s["qkv_sum"][k], None, last)
        qkv_sum[k].begin()

    def store(index, values):
        gn[index, :] = values

    sums = s["sums"]
    norm_back_rows(s["x"], gn, att, gain, sums, store)
    leave = load(gn, grad_input)
    go((begin, down, 1), (proceed, out, 0))
    four = jnp.concatenate([sums[0:2, :], sums_two[0:2, :]], axis=0)
    eight = jnp.concatenate([four, four], axis=0)
    turned = jnp.transpose(jnp.concatenate([eight, jnp.zeros((120, 1024), F32)], axis=0))
    turned = turned.reshape(4, 2, 4, 4, 8, 128)
    lane = lax.broadcasted_iota(jnp.int32, (8, 128), 1)
    s["vec_slab"][...] = jnp.where(lane < 4, turned[:, 0], jnp.where(lane < 8, turned[:, 1], 0.0))
    go((begin, vec, 0), (proceed, out, 1))
    turn(0)
    turn(2)
    go((begin, up, 0))
    turn(1)
    go(
        (forward, qkv_sum, 0), (forward, qkv_sum, 2), (begin, up, 1), (forward, down, 2), (forward, down, 1),
        (begin, up, 2), (proceed, out, 0), (forward, qkv_sum, 1), (proceed, vec, 0), (proceed, qkv_sum, 2),
        (proceed, qkv_sum, 0), (proceed, qkv_sum, 1), (forward, down, 0), (forward, up, 0), (forward, up, 1),
        (proceed, out, 2), (proceed, vec, 0), (forward, qkv_sum, 2), (forward, up, 2), (proceed, down, 1),
        (forward, qkv_sum, 0), (forward, qkv_sum, 1), (proceed, down, 2), (proceed, down, 0), (proceed, qkv_sum, 2),
        (proceed, up, 0), (proceed, up, 1), (proceed, out, 2), (proceed, qkv_sum, 0), (proceed, up, 2),
        (proceed, out, 1), (proceed, qkv_sum, 1), (finish, down, 2), (finish, down, 1), (finish, down, 0),
        (finish, up, 1), (finish, vec, 0),
    )
    vec_tile = vec[0].data
    vec_copy = pltpu.make_async_remote_copy(
        src_ref=vec_tile,
        dst_ref=s["vec_land"],
        send_sem=s["vec_sems"].at[0],
        recv_sem=s["vec_sems"].at[1],
        device_id=place.partner(),
        device_id_type=MESH,
    )
    vec_copy.start()
    go(
        (finish, up, 0), (finish, qkv_sum, 0), (finish, qkv_sum, 2), (finish, out, 0), (finish, qkv_sum, 1),
        (finish, out, 2), (finish, out, 1), (finish, up, 2),
    )
    for k in range(3):
        piece = down[k].data
        grad_down[pl.ds(8 * k, 8), :] = piece[:, pl.ds(0, 1024)]
        start, width_k = DOWN_CUTS[k]
        grad_down[pl.ds(24, 8), pl.ds(start, width_k)] = piece[:, pl.ds(1024, width_k)]
    scan.drain()
    for number in range(3):
        swap.copy(number, number, land.at[number]).wait_send()
    for stream in (*down, *up, *out, *qkv_sum, *vec):
        stream.drain()
    vec_copy.wait()
    grad_gains[...] = vec_tile[...] + s["vec_land"][...]
    leave.wait()


def last_part(qkv, att, terms, state, gn, gmixed, norm_one, norm_cat, pre_cat, down, out, x, weight, gain, sums_two, block):
    rows, width = x.shape

    def kernel(*refs):
        last_kernel(block, *refs)

    outs = [
        struct((rows, width)),
        struct((8, 4096)),
        struct((8, width)),
        struct((8, 3 * width)),
        struct((32, width)),
        struct((8, 128)),
    ]
    like = last_scratch(rows, width)
    scratch = [leaf for name in like for leaf in flatten(like[name])]
    out = out.reshape(4, 2, 4, 4, 8, TILE)
    operands = (
        qkv, att, terms, state, gn, gmixed, norm_one, norm_cat, pre_cat, *down, out, x, weight, gain, sums_two,
    )
    specs = [ANY_SPEC] * 15 + [VMEM_SPEC] * 2
    out_specs = [ANY_SPEC] + [VMEM_SPEC] * 5
    return call(kernel, outs, out_specs, operands, specs, scratch, 2)


def lay_out_kernel(output, grad_input, up, out, qkv, down, gains, output_to, grad_to, up_to, out_to, qkv_to, down_to, a, b, c, d):
    pairs = (
        (output, output_to), (grad_input, grad_to), (up, up_to), (out, out_to), (qkv, qkv_to), (down, down_to),
    )
    for source, target in pairs:
        target[...] = source[...]
    core = lax.rem(lax.axis_index("dp"), 2)
    turned = jnp.transpose(jnp.concatenate([gains[...], jnp.zeros((120, 128), F32)], axis=0))
    for k, target in enumerate((a, b, c, d)):
        target[...] = jnp.where(core == 0, turned[k : k + 1, :8], turned[4 + k : 5 + k, :8])


def lay_out(output, *grads):
    arrays = (output, *grads[:-1])
    outs = [struct(array.shape, array.dtype) for array in arrays] + [struct((1, 8))] * 4
    return pl.pallas_call(
        lay_out_kernel,
        out_shape=outs,
        in_specs=[VMEM_SPEC] * 7,
        out_specs=[VMEM_SPEC] * 10,
        compiler_params=pltpu.CompilerParams(vmem_limit_bytes=62 * MIB),
    )(output, *grads)


def body(
    inputs,
    first_gain,
    first_shift,
    qkv_weight,
    out_weight,
    second_gain,
    second_shift,
    up_weight,
    down_weight,
    cotangent,
):
    sequences, block, width = inputs.shape
    rows = sequences * block
    x = inputs.reshape(rows, width)
    cot = cotangent.reshape(rows, width)
    gain_one, gain_two = first_gain.reshape(1, width), second_gain.reshape(1, width)
    shift_two = second_shift.reshape(1, width)
    shift_one = first_shift.reshape(1, width)
    norm_one, qkv, att, _, state, output, gmixed, gn, sums_two, norm_cat, pre_cat, out, terms, *down = front(
        x, gain_one, shift_one, gain_two, shift_two, qkv_weight, cot, out_weight, up_weight, down_weight, block
    )
    grads = last_part(
        qkv, att, terms, state, gn, gmixed, norm_one, norm_cat, pre_cat, down, out, x, qkv_weight,
        gain_one, sums_two, block,
    )
    output, grad_input, grad_up, grad_out, grad_qkv, grad_down, *gains = lay_out(output, *grads)
    return (
        output.reshape(inputs.shape),
        grad_input.reshape(inputs.shape),
        grad_qkv,
        grad_out,
        grad_up,
        grad_down,
        *[gain.reshape(8) for gain in gains],
    )


def solution(mesh):
    return jax.shard_map(
        body,
        mesh=mesh,
        in_specs=(
            P("dp", "seq", None),
            P(),
            P(),
            P(),
            P(),
            P(),
            P(),
            P(),
            P(),
            P("dp", "seq", None),
        ),
        out_specs=(
            P("dp", "seq", None),
            P("dp", "seq", None),
            P(("dp", "seq"), None),
            P(("dp", "seq"), None),
            P(("dp", "seq"), None),
            P(("dp", "seq"), None),
            P(("dp", "seq")),
            P(("dp", "seq")),
            P(("dp", "seq")),
            P(("dp", "seq")),
        ),
        check_vma=False,
    )
```

```python
import math

import jax
import jax.numpy as jnp
from jax import lax
from jax.experimental import pallas as pl
from jax.experimental.pallas import tpu as pltpu
from jax.sharding import PartitionSpec as P

MESH = pl.DeviceIdType.MESH
F32 = jnp.float32
BF16 = jnp.bfloat16
RING = 4
MIB = 2**20


class Place:
    def __init__(self):
        dp, seq = lax.axis_index("dp"), lax.axis_index("seq")
        self.core = lax.rem(dp, 2)
        self.at = (lax.div(dp, 2), lax.div(seq, RING), lax.rem(seq, RING))

    def id_of(self, x, y, z, core):
        return (x * 2 + core, y * RING + z)

    def ring(self, axis, step):
        return lax.rem(self.at[axis] + (step + RING), RING)

    def neighbour(self, axis, step):
        at = list(self.at)
        at[axis] = self.ring(axis, step)
        return self.id_of(*at, self.core)

    def partner(self):
        return self.id_of(*self.at, 1 - self.core)


def greet(others):
    barrier = pltpu.get_barrier_semaphore()
    for other in others:
        pl.semaphore_signal(barrier, inc=1, device_id=other, device_id_type=MESH)


def met(count):
    pl.semaphore_wait(pltpu.get_barrier_semaphore(), count)


def link_neighbours(place):
    others = [place.neighbour(axis, step) for axis in range(3) for step in (1, -1)]
    return [*others, place.partner()]


ORDERS = ((0, 1, 2), (1, 2, 0), (2, 0, 1))


def phase_scratch(remaining, length, messages=6):
    if remaining:
        half = (2, 2, *[4] * (remaining - 1), 8, length)
    else:
        half = (2, 8, (length // 128 + 1) // 2 * 128)
    return [
        pltpu.VMEM((2, *[4] * remaining, 8, length), F32),
        pltpu.VMEM(half, F32),
        pltpu.SemaphoreType.DMA((messages,)),
        pltpu.SemaphoreType.DMA((messages,)),
    ]


class Phase:
    def __init__(self, place, data, axes, axis, scratch):
        self.place, self.data, self.axis = place, data, axis
        self.where = axes.index(axis)
        self.full, self.half, self.sent, self.came = scratch
        self.flying = []
        self.flat = len(axes) == 1
        self.length = data.shape[-1]
        self.cut = (self.length // 128 + 1) // 2 * 128
        self.whole = self.flat and self.cut == self.length

    def empty(self, which):
        return self.whole and which == 1

    def chunk(self, target):
        index = [slice(None)] * self.where + [target]
        return self.data.at[tuple(index)]

    def part(self, ref, which):
        if not self.flat:
            return ref.at[pl.ds(2 * which, 2)]
        if which == 0:
            return ref.at[:, pl.ds(0, self.cut)]
        return ref.at[:, pl.ds(self.cut, self.length - self.cut)]

    def through(self, way):
        ref = self.half.at[way]
        if self.flat and way == 1:
            return ref.at[:, pl.ds(0, self.length - self.cut)]
        return ref

    def copy(self, kind, way, source, target):
        number = kind * 2 + way
        return pltpu.make_async_remote_copy(
            src_ref=source,
            dst_ref=target,
            send_sem=self.sent.at[number],
            recv_sem=self.came.at[number],
            device_id=self.place.neighbour(self.axis, 1 - 2 * way),
            device_id_type=MESH,
        )

    def send(self, kind, way, source, target):
        copy = self.copy(kind, way, source, target)
        copy.start()
        self.flying.append(copy)

    def beside(self, way):
        return self.chunk(self.place.ring(self.axis, 1 - 2 * way))

    def begin_far(self):
        opposite = self.chunk(self.place.ring(self.axis, 2))
        for way in range(2):
            if not self.empty(way):
                self.send(0, way, self.part(opposite, way), self.through(way))

    def begin_near(self, way):
        if not self.empty(1 - way):
            target = self.part(self.full.at[way], 1 - way)
            self.send(1, way, self.part(self.beside(way), 1 - way), target)

    def begin(self):
        self.begin_far()
        for way in range(2):
            self.begin_near(way)

    def forward(self):
        for way in range(2):
            if self.empty(way):
                continue
            came = self.through(way)
            self.copy(0, way, came, came).wait_recv()
            own = self.part(self.beside(way), way)
            add_into(own, own, came)
            self.send(2, way, own, self.part(self.full.at[way], way))

    def finish(self, out=None):
        own = self.chunk(self.place.at[self.axis])
        for way in range(2):
            for kind, which in ((1, 1 - way), (2, way)):
                if self.empty(which):
                    continue
                target = self.part(self.full.at[way], which)
                self.copy(kind, way, target, target).wait_recv()
        add_into(own if out is None else out, own, self.full.at[0], self.full.at[1])
        return own

    def drain(self):
        for copy in self.flying:
            copy.wait_send()


HALVES = ((2, 1), (3, 0))


class SplitPhase(Phase):
    def block(self, way, j):
        return self.place.ring(0, HALVES[way][j])

    def copy_block(self, kind, way, j, source, target):
        number = kind * 4 + way * 2 + j
        return pltpu.make_async_remote_copy(
            src_ref=source,
            dst_ref=target,
            send_sem=self.sent.at[number],
            recv_sem=self.came.at[number],
            device_id=self.place.neighbour(self.axis, 1 - 2 * way),
            device_id_type=MESH,
        )

    def send_far(self, way, j):
        source = self.chunk(self.place.ring(self.axis, 2)).at[self.block(way, j)]
        self.flying.append(self.copy_block(0, way, j, source, self.half.at[way, j]))
        self.flying[-1].start()

    def send_near(self, kind, way, j):
        block = self.block(way if kind == 2 else 1 - way, j)
        source, target = self.beside(way).at[block], self.full.at[way, block]
        self.flying.append(self.copy_block(kind, way, j, source, target))
        self.flying[-1].start()

    def begin_first(self):
        for j in range(2):
            self.send_far(0, j)
        self.send_near(1, 1, 0)

    def begin_second(self):
        for j in range(2):
            self.send_far(1, j)
        self.send_near(1, 1, 1)
        for j in range(2):
            self.send_near(1, 0, j)

    def forward(self):
        for way in range(2):
            for j in range(2):
                came = self.half.at[way, j]
                self.copy_block(0, way, j, came, came).wait_recv()
                own = self.beside(way).at[self.block(way, j)]
                add_into(own, own, came)
                self.send_near(2, way, j)

    def finish(self, out=None):
        own = self.chunk(self.place.at[self.axis])
        for way in range(2):
            for kind, part in ((1, 1 - way), (2, way)):
                for j in range(2):
                    target = self.full.at[way, self.block(part, j)]
                    self.copy_block(kind, way, j, target, target).wait_recv()
        add_into(own if out is None else out, own, self.full.at[0], self.full.at[1])
        return own


class Direct:
    def __init__(self, place, data, axes, axis, scratch):
        self.place, self.data, self.axis = place, data, axis
        self.where = axes.index(axis)
        self.full, self.sent, self.came = scratch
        self.flying = []

    def chunk(self, target):
        index = [slice(None)] * self.where + [target]
        return self.data.at[tuple(index)]

    def copy(self, step, source):
        return pltpu.make_async_remote_copy(
            src_ref=source,
            dst_ref=self.full.at[step - 1],
            send_sem=self.sent.at[step - 1],
            recv_sem=self.came.at[step - 1],
            device_id=self.place.neighbour(self.axis, step),
            device_id_type=MESH,
        )

    def begin(self):
        for step in (2, 1, 3):
            copy = self.copy(step, self.chunk(self.place.ring(self.axis, step)))
            copy.start()
            self.flying.append(copy)

    def forward(self):
        pass

    def finish(self, out=None):
        own = self.chunk(self.place.at[self.axis])
        for step in (1, 2, 3):
            self.copy(step, self.full.at[step - 1]).wait_recv()
        add_into(own if out is None else out, own, *[self.full.at[k] for k in range(3)])
        return own

    def drain(self):
        for copy in self.flying:
            copy.wait_send()


class Route:
    def __init__(self, place, data, axis, pieces, scratch, out):
        self.place, self.data, self.axis, self.pieces, self.out = place, data, axis, pieces, out
        self.scratch = scratch

    def send_each(self, act):
        core = self.place.core
        for (owner, _, width, at), (land, sent, came) in zip(self.pieces, self.scratch):

            def copy(step):
                position = list(self.place.at)
                position[self.axis] = self.place.ring(self.axis, step)
                return pltpu.make_async_remote_copy(
                    src_ref=self.data.at[self.place.ring(self.axis, step), :, pl.ds(at, width)],
                    dst_ref=land.at[core, step],
                    send_sem=sent.at[step],
                    recv_sem=came.at[core, step],
                    device_id=self.place.id_of(*position, owner),
                    device_id_type=MESH,
                )

            for step in (2, 1, 3):
                act(copy(step))

            @pl.when(core != owner)
            def _():
                act(copy(0))

    def begin(self):
        self.send_each(lambda copy: copy.start())

    def forward(self):
        pass

    def finish(self, out=None):
        core = self.place.core
        mine = self.place.at[self.axis]
        for (owner, start, width, at), (land, sent, came) in zip(self.pieces, self.scratch):

            @pl.when(core == owner)
            def _():
                for source, steps in ((core, (1, 2, 3)), (1 - core, (0, 1, 2, 3))):
                    for step in steps:
                        target = land.at[source, step]
                        pltpu.make_async_remote_copy(
                            src_ref=target,
                            dst_ref=target,
                            send_sem=sent.at[step],
                            recv_sem=came.at[source, step],
                            device_id=self.place.partner(),
                            device_id_type=MESH,
                        ).wait_recv()
                done = 0
                while done < width:
                    column = start + done
                    tile, within = column // TILE, column % TILE
                    step = min(TILE - within, width - done)
                    part = pl.ds(done, step)
                    ours = self.data[mine, :, pl.ds(at + done, step)]
                    for k in (1, 2, 3):
                        ours = ours + land[core, k, :, part]
                    theirs = land[1 - core, 0, :, part]
                    for k in (1, 2, 3):
                        theirs = theirs + land[1 - core, k, :, part]
                    for values, half in ((ours, core), (theirs, 1 - core)):
                        place = pl.multiple_of((2 * tile + half) * TILE + within, 128)
                        self.out[:, pl.ds(place, step)] = values
                    done += step

    def drain(self):
        self.send_each(lambda copy: copy.wait_send())


def route_scratch(stream, widths, columns):
    return [
        [
            pltpu.VMEM((2, 4, 8, width), F32),
            pltpu.SemaphoreType.DMA((4,)),
            pltpu.SemaphoreType.DMA((2, 4)),
        ]
        for _, _, width, _ in stream_pieces(stream, widths, columns)
    ]


class Stream:
    def __init__(self, place, data, order, scratch, first=None, last=None):
        self.place, self.data, self.scratch, self.first, self.last = place, data, scratch, first, last
        self.todo, self.old = [axis for axis in order], []
        self.axes = sorted(order)
        self.phase = None

    def prepare(self):
        scratch = self.scratch.pop(0)
        if self.last and len(self.todo) == 1:
            pieces, out = self.last
            self.phase = Route(self.place, self.data, self.todo[0], pieces, scratch, out)
            return self.phase
        kind = self.first or (Phase if len(scratch) == 4 else Direct)
        self.first = None
        self.phase = kind(self.place, self.data, self.axes, self.todo[0], scratch)
        return self.phase

    def begin(self):
        self.prepare().begin()

    def forward(self):
        self.phase.forward()

    def finish(self, out=None):
        own = self.phase.finish(out)
        self.data = own if out is None else out
        self.axes.remove(self.todo.pop(0))
        self.old.append(self.phase)

    def proceed(self):
        self.finish()
        self.begin()

    def drain(self):
        for phase in self.old:
            phase.drain()
        self.old = []


def direct_scratch(remaining, length):
    return [
        pltpu.VMEM((3, *[4] * remaining, 8, length), F32),
        pltpu.SemaphoreType.DMA((3,)),
        pltpu.SemaphoreType.DMA((3,)),
    ]


def stream_scratch(length, phases, direct=()):
    return [
        (direct_scratch if phase in direct else phase_scratch)(2 - phase, length)
        for phase in phases
    ]


class Taker:
    def __init__(self, refs):
        self.refs = list(refs)

    def __call__(self, like):
        if isinstance(like, list):
            return [self(item) for item in like]
        return self.refs.pop(0)


def flatten(items):
    if isinstance(items, list):
        return [leaf for item in items for leaf in flatten(item)]
    return [items]


def add_into(out, *terms):
    if len(out.shape) > 2:

        def row(index, carry):
            add_into(out.at[index], *[term.at[index] for term in terms])
            return carry

        if len(out.shape) == 4:
            lax.fori_loop(0, out.shape[0], row, 0)
        else:
            for index in range(out.shape[0]):
                row(index, 0)
        return
    total = terms[0][...]
    for term in terms[1:]:
        total = total + term[...]
    out[...] = total


def tn_dot(left, right):
    return lax.dot_general(left, right, (((0,), (0,)), ((), ())), preferred_element_type=F32)


TILE = 512


class Swap:
    def __init__(self, place, stage, sent, came):
        self.place, self.stage, self.sent, self.came = place, stage, sent, came

    def copy(self, number, slot, target):
        return pltpu.make_async_remote_copy(
            src_ref=self.stage.at[slot],
            dst_ref=target,
            send_sem=self.sent.at[number],
            recv_sem=self.came.at[number],
            device_id=self.place.partner(),
            device_id_type=MESH,
        )

    def put(self, number, slot, values, target, before=None):
        if before is not None:
            self.copy(before, slot, target).wait_send()
        self.stage[slot] = values.astype(F32)
        self.copy(number, slot, target).start()

    def get(self, number, target):
        self.copy(number, 0, target).wait_recv()
        return target[...].astype(BF16)

    def drain(self, numbers, target):
        for number in numbers:
            self.copy(number, number % 4, target).wait_send()


def half_columns(block, core, quarter):
    half = quarter // 2
    return pl.ds(pl.multiple_of(block * quarter + core * half, half), half)


def half_tile(index, core):
    return pl.ds(pl.multiple_of((2 * index + core) * TILE, TILE), TILE)


def core_product(left, core, right, start, width, slab, at):
    done = 0
    while done < width:
        step = min(TILE, width - done)
        product = tn_dot(left[core], right[:, pl.ds(start + done, step)])
        slab[:, :, :, :, pl.ds(at + done, step)] = product.reshape(4, 4, 4, 8, step)
        done += step


UP_WIDTHS = (1536, 1280, 1280)
OUT_WIDTHS = (512, 256, 256)
QKV_WIDTHS = (1152, 896, 1024)


def stream_pieces(stream, widths, columns):
    if stream < 2:
        return [(stream, 0, widths[stream], 0)]
    pieces, at = [], 0
    for core in range(2):
        width = columns - widths[core]
        if width:
            pieces.append((core, widths[core], width, at))
        at += width
    return pieces


def stream_product(stream, left, right, slab, widths, columns):
    for core, start, width, at in stream_pieces(stream, widths, columns):
        core_product(left, core, right, start, width, slab, at)


DOWN_CUTS = ((0, 384), (384, 384), (768, 256))
DOWN_WIDTHS = (1408, 1408, 1280)


SEQ = 16
PAIR = 128
NT = (((1,), (1,)), ((), ()))
TN = (((0,), (0,)), ((), ()))


def dot_nt(left, right):
    return lax.dot_general(left, right, NT, preferred_element_type=F32)


def dot_nn(left, right):
    return jnp.dot(left, right, preferred_element_type=F32)


def split(values):
    high = values.astype(BF16)
    return high, (values - high.astype(F32)).astype(BF16)


def features(raw):
    return jnp.where(raw > 0, raw + 1.0, jnp.exp(jnp.minimum(raw, 0.0))).astype(BF16)


def feature_slope(raw):
    return jnp.where(raw > 0, 1.0, jnp.exp(jnp.minimum(raw, 0.0)))


def head_masks():
    lane = lax.broadcasted_iota(jnp.int32, (1, PAIR), 1)
    first = jnp.where(lane < 64, 1.0, 0.0)
    return first.astype(BF16), (1.0 - first).astype(BF16)


def first_head(rows):
    return lax.broadcasted_iota(jnp.int32, (rows, PAIR), 1) < 64


def pack_state(square, total):
    blocks = jnp.where(first_head(64), square[:64], square[64:])
    return blocks, jnp.broadcast_to(total, (8, PAIR))


def unpack_state(packed):
    first = first_head(64)
    square = jnp.concatenate(
        [jnp.where(first, packed[:64], 0.0), jnp.where(first, 0.0, packed[:64])], axis=0
    )
    return square, packed[64:65]


def same_head():
    row = lax.broadcasted_iota(jnp.int32, (PAIR, PAIR), 0)
    lane = lax.broadcasted_iota(jnp.int32, (PAIR, PAIR), 1)
    return (row < 64) == (lane < 64)


def head_slopes(numer, attended, first_wide):
    product = numer * attended
    ours = jnp.sum(jnp.where(first_wide, product, 0.0), axis=1, keepdims=True)
    theirs = jnp.sum(jnp.where(first_wide, 0.0, product), axis=1, keepdims=True)
    return -ours, -theirs


def state_gradient(query, numer, attended, first_wide):
    one, two = head_slopes(numer, attended, first_wide)
    high, low = split(numer)
    wide = tn_dot(query, jnp.concatenate([high, low], axis=1))
    spread = jnp.where(first_wide, one, two)
    total = jnp.sum(query.astype(F32) * spread, axis=0, keepdims=True)
    return pack_state(wide[:, :PAIR] + wide[:, PAIR:], total)


OFFSETS = sorted(
    ((y, z) for y in range(RING) for z in range(RING) if y or z),
    key=lambda offset: -sum(min(step, RING - step) for step in offset),
)


class Units:
    def __init__(self, ref):
        self.ref = ref

    def at(self, unit):
        rows = pl.ds(pl.multiple_of(lax.div(lax.rem(unit, 8), 4) * 72, 8), 72)
        columns = pl.ds(pl.multiple_of(lax.rem(unit, 4) * PAIR, PAIR), PAIR)
        return self.ref.at[lax.div(unit, 8), rows, columns]


class Slots:
    def __init__(self, ref):
        self.ref = ref

    def at(self, unit):
        return self.ref.at[unit]


class Scan:
    def __init__(self, terms, landed, sums, result, sems, reverse):
        self.terms, self.landed, self.sums, self.result = terms, landed, sums, result
        self.sems, self.reverse = sems, reverse
        self.dp, self.me = lax.axis_index("dp"), lax.axis_index("seq")
        self.y, self.z = lax.div(self.me, RING), lax.rem(self.me, RING)
        self.parity = lax.rem(self.y + self.z, 2)
        self.unit = self.unit_of(self.parity, self.me)

    def unit_of(self, parity, device):
        return parity * 8 + lax.div(device, 2)

    def at(self, y, z, sign=1):
        y = lax.rem(self.y + (sign * y + RING), RING)
        z = lax.rem(self.z + (sign * z + RING), RING)
        return y * RING + z

    def others(self):
        return [(self.dp, self.at(*offset)) for offset in OFFSETS]

    def half_offsets(self, half):
        for y in (2, 1, 3, 0):
            for step in (1, 0):
                yield y, 2 * step + lax.rem(self.parity + (y + half), 2)

    def copy(self, number, source, target, sems, other):
        return pltpu.make_async_remote_copy(
            src_ref=source,
            dst_ref=target,
            send_sem=sems[0].at[number],
            recv_sem=sems[1].at[number],
            device_id=(self.dp, other),
            device_id_type=MESH,
        )

    def start(self, half):
        for y, z in self.half_offsets(half):
            other = self.at(y, z)
            source = self.terms.at(self.unit_of(half, other))
            copy = self.copy(y * RING + z, source, self.landed.at(self.me), self.sems[:2], other)
            if y:
                copy.start()
            else:
                pl.when(z > 0)(copy.start)

    def middle(self):
        for y, z in OFFSETS:
            other = self.at(y, z, -1)
            came = self.landed.at(other)
            self.copy(y * RING + z, came, came, self.sems[:2], other).wait_recv()
        self.landed.at(self.me)[...] = self.terms.at(self.unit)[...]
        total = jnp.zeros((72, PAIR), F32)
        for k in range(SEQ):
            at = SEQ - 1 - k if self.reverse else k
            self.sums.at(at)[...] = total
            total = total + self.landed.at(at)[...]
        for y, z in OFFSETS:
            other = self.at(y, z)
            target = self.result.at(self.unit)
            self.copy(y * RING + z, self.sums.at(other), target, self.sems[2:], other).start()
        self.result.at(self.unit)[...] = self.sums.at(self.me)[...]

    def finish(self, half):
        for y, z in self.half_offsets(half):
            other = self.at(y, z, -1)
            came = self.result.at(self.unit_of(half, other))
            copy = self.copy(y * RING + z, came, came, self.sems[2:], other)
            if y:
                copy.wait_recv()
            else:
                pl.when(z > 0)(copy.wait_recv)

    def drain(self):
        for y, z in OFFSETS:
            number, other = y * RING + z, self.at(y, z)
            self.copy(number, self.terms.at(0), self.landed.at(0), self.sems[:2], other).wait_send()
            self.copy(number, self.sums.at(0), self.result.at(0), self.sems[2:], other).wait_send()


SCAN_SCRATCH = [
    pltpu.VMEM((SEQ, 72, PAIR), F32),
    pltpu.VMEM((SEQ, 72, PAIR), F32),
    pltpu.VMEM((SEQ, 72, PAIR), F32),
    *[pltpu.SemaphoreType.DMA((SEQ,)) for _ in range(4)],
]


def unit_slices(unit, block):
    rows = pl.ds(pl.multiple_of(lax.div(unit, 8) * block, block), block)
    columns = pl.ds(pl.multiple_of(lax.rem(unit, 8) * PAIR, PAIR), PAIR)
    return rows, columns


def for_units(step, together):
    def several(index, carry):
        for offset in range(together):
            step(index * together + offset)
        return carry

    lax.fori_loop(0, SEQ // together, several, 0)


def causal_mask(block, transposed=False):
    row = lax.broadcasted_iota(jnp.int32, (block, block), 0)
    column = lax.broadcasted_iota(jnp.int32, (block, block), 1)
    return (row <= column) if transposed else (row >= column)


def norm_rows(values):
    center = jnp.mean(values, axis=-1, keepdims=True)
    centered = values - center
    variance = jnp.mean(centered * centered, axis=-1, keepdims=True)
    inverse = lax.rsqrt(variance + 1e-05)
    return centered * inverse, inverse


ROWS = 64


def for_rows(count, step):
    def one(index, carry):
        step(pl.ds(pl.multiple_of(index * ROWS, ROWS), ROWS))
        return carry

    lax.fori_loop(0, count // ROWS, one, 0)


def for_columns(count, width, step):
    def one(index, carry):
        step(pl.ds(pl.multiple_of(index * width, width), width))
        return carry

    lax.fori_loop(0, count // width, one, 0)


SLOPE_SCALE = 28000.0


def gelu_both(pre):
    cumulative = 0.5 * (1.0 + lax.erf(pre * (1.0 / math.sqrt(2.0))))
    density = jnp.exp(-0.5 * pre * pre) * (1.0 / math.sqrt(2.0 * math.pi))
    slope = (cumulative + pre * density) * SLOPE_SCALE
    return (pre * cumulative).astype(BF16), slope.astype(jnp.int32).astype(jnp.int16)


def norm_back(grad, gain, scaled, inverse):
    spread = grad * gain
    first_mean = jnp.mean(spread, axis=-1, keepdims=True)
    second_mean = jnp.mean(spread * scaled, axis=-1, keepdims=True)
    return inverse * (spread - first_mean - scaled * second_mean)


def norm_back_rows(values, grad, base, gain, sums, store):
    sums[...] = jnp.zeros_like(sums)

    def step(rows):
        scaled, inverse = norm_rows(values[rows, :].astype(F32))
        part = grad[rows, :]
        sums[0:1, :] += jnp.sum(part * scaled, axis=0, keepdims=True)
        sums[1:2, :] += jnp.sum(part, axis=0, keepdims=True)
        store(rows, base[rows, :].astype(F32) + norm_back(part, gain[...], scaled, inverse))

    for_rows(grad.shape[0], step)


def front_kernel(
    block, x, gain_one, shift_one, gain, shift, w_qkv, cot_in, w_out, w_up, w_down,
    norm_one_out, qkv_out, att_out, den_out, state_out, output_out, gmixed_out, gn_out, sums, norm_out, pre_out,
    out_out, terms, down_a, down_b, down_c,
    wo, wu, wd, wsem, osem, att_low, state, output, gmixed, gatt, norm_cat, pre_cat, hidden, slope, cot_cat,
    stage, land, land_att, land_norm, swap_sent, swap_came, free, s0, s1, s2, s3, *scratch,
):
    take_scratch = Taker(scratch)
    slabs = take_scratch(slab_shapes(DOWN_WIDTHS))
    slab_a, slab_b, slab_c = slabs
    phases = take_scratch([[phase_scratch(2, length, 12)] for length in DOWN_WIDTHS])
    place = Place()
    core = place.core
    rows = x.shape[0]
    scan = Scan(Slots(terms), Units(land_att), Units(land_norm), Slots(state), (s0, s1, s2, s3), False)
    others = [place.neighbour(0, 1), place.neighbour(0, -1), place.partner(), *scan.others()]
    greet(others)
    own, other = pl.ds(0, rows), pl.ds(rows, rows)

    def load(source, target, slot):
        copy = pltpu.make_async_copy(source, target, wsem.at[slot])
        copy.start()
        return copy

    outs = []

    def leave(source, target):
        copy = pltpu.make_async_copy(source, target, osem.at[len(outs)])
        copy.start()
        outs.append(copy)
        return copy

    def settle(copies):
        for copy in copies:
            copy.wait()
            settled.append(id(copy))

    settled = []
    thirds = [
        load(w_qkv.at[:, pl.ds(third * 1024, 1024)], wu.at[:, pl.ds(slot * 1024, 1024)], slot)
        for slot, third in enumerate((1, 2, 0))
    ]
    cot_load = load(cot_in, cot_cat.at[own], 3)
    out_load = load(w_out, wo, 4)

    def norm_step(index):
        scaled, _ = norm_rows(x[index, :].astype(F32))
        hidden[index, pl.ds(0, 1024)] = (scaled * gain_one[...] + shift_one[...]).astype(BF16)

    for_rows(rows, norm_step)

    def shifted(columns, offset):
        return pl.ds(pl.multiple_of(columns.start + offset, PAIR), columns.size)

    def later_rows(index, offset):
        return pl.ds(pl.multiple_of(index.start + offset, 64), index.size)

    def project(slot, third, feature):
        thirds[slot].wait()

        def step(columns):
            raw = dot_nn(hidden[:, pl.ds(0, 1024)], wu[:, shifted(columns, slot * 1024)]).astype(BF16)
            hidden[:, shifted(columns, 1024 + third * 1024)] = raw
            if feature is not None:
                wd[pl.ds(feature * rows, rows), columns] = features(raw.astype(F32))

        for_columns(1024, TILE, step)

    project(0, 1, 1)
    project(1, 2, None)

    def local_state(unit):
        index, columns = unit_slices(unit, block)
        keys = wd[later_rows(index, rows), columns]
        square = tn_dot(hidden[index, shifted(columns, 3072)], keys)
        total = jnp.sum(keys.astype(F32), axis=0, keepdims=True)
        blocks, row = pack_state(square, total)
        terms[unit, pl.ds(0, 64)] = blocks
        terms[unit, pl.ds(64, 8)] = row

    def local_states(half):
        def four(index, carry):
            for offset in range(4):
                local_state(half * 8 + index * 4 + offset)
            return carry

        lax.fori_loop(0, 2, four, 0)

    local_states(0)
    met(len(others))
    scan.start(0)
    local_states(1)
    scan.start(1)
    swap = Swap(place, stage, swap_sent, swap_came)
    for which in range(2):
        for block_x in range(4):
            columns = pl.ds(block_x * 256 + which * 128, 128)
            pre_cat[own, pl.ds(which * TILE + block_x * 128, 128)] = hidden[:, columns]
        swap.put(which, which, pre_cat[own, pl.ds(which * TILE, TILE)], land.at[which])
    cot_load.wait()
    for tile in range(2):
        swap.put(2 + tile, 2 + tile, cot_cat[own, pl.ds(tile * TILE, TILE)], land.at[2 + tile])
    qkv_leaves = [leave(hidden.at[:, pl.ds(third * 1024 + 1024, 1024)], qkv_out.at[third]) for third in (1, 2)]
    project(2, 0, 0)
    qkv_leaves.append(leave(hidden.at[:, pl.ds(1024, 1024)], qkv_out.at[0]))
    up_load = load(w_up, wu, 6)
    first, second = head_masks()
    causal = causal_mask(block)

    def local_part(unit):
        index, columns = unit_slices(unit, block)
        query, key = wd[index, columns], wd[later_rows(index, rows), columns]
        value = hidden[index, shifted(columns, 3072)]
        scores = dot_nt(jnp.concatenate([query * first, query * second], axis=0), key)
        both = 0.0
        for head, mask in enumerate((first, second)):
            kept = jnp.where(causal, scores[head * block : (head + 1) * block], 0.0).astype(BF16)
            right = jnp.concatenate([value * mask, jnp.broadcast_to(mask, value.shape)], axis=1)
            both = both + dot_nn(kept, right)
        gmixed[index, columns] = both[:, :PAIR]
        gatt[index, columns] = both[:, PAIR:]

    def local_parts(start, count):
        def two(index, carry):
            local_part(start + 2 * index)
            local_part(start + 2 * index + 1)
            return carry

        lax.fori_loop(0, count // 2, two, 0)

    local_parts(0, 10)
    scan.middle()
    local_parts(10, 6)
    for which in range(2):
        pre_cat[other, pl.ds(which * TILE, TILE)] = swap.get(which, land.at[which])
        cot_cat[other, pl.ds(which * TILE, TILE)] = swap.get(2 + which, land.at[2 + which])
    cat_leaves = [leave(pre_cat.at[:, pl.ds(which * TILE, TILE)], norm_one_out.at[which]) for which in range(2)]
    together = same_head()

    def incoming(unit):
        index, columns = unit_slices(unit, block)
        square, total = unpack_state(state[unit])
        totals = jnp.where(together, jnp.broadcast_to(total, (PAIR, PAIR)), 0.0)
        high, low = split(jnp.concatenate([square, totals], axis=0))
        query = wd[index, columns]
        both = dot_nt(
            jnp.concatenate([query, query], axis=1), jnp.concatenate([high, low], axis=1)
        )
        denom = gatt[index, columns] + both[:, PAIR:]
        attended = (gmixed[index, columns] + both[:, :PAIR]) / denom
        tile, within = stage_place(unit)
        stage[tile, index, within] = attended
        stage[2 + tile, index, within] = denom
        att_low[index, columns] = attended.astype(BF16)

    def stage_place(unit):
        pair = lax.rem(unit, 8)
        return lax.div(pair, 4), pl.ds(pl.multiple_of(lax.rem(pair, 4) * PAIR, PAIR), PAIR)

    mixed = gatt

    def up(columns, index):
        ours, ours_slope = gelu_both(dot_nn(norm_cat[index, :], wu[:, columns]))
        hidden[index, columns] = ours
        slope[index, columns] = ours_slope

    settle(qkv_leaves)
    swap.drain(range(4), land.at[0])
    att_leaves = []
    for half in range(2):
        scan.finish(half)
        leave(state.at[pl.ds(half * 8, 8)], state_out.at[pl.ds(half * 8, 8)])

        def several(index, carry):
            for offset in range(4):
                incoming(half * 8 + 4 * index + offset)
            return carry

        lax.fori_loop(0, 2, several, 0)
        part = pl.ds(half * block, block)
        for slot in range(4):
            target = (att_out, den_out)[slot // 2].at[part, pl.ds(slot % 2 * TILE, TILE)]
            att_leaves.append(leave(stage.at[slot, part], target))
        if half == 0:
            out_load.wait()

        def mix(columns):
            mixed[part, columns] = x[part, columns].astype(F32) + dot_nn(att_low[part, :], wo[:, columns])

        mix(pl.ds(0, 1024))
        for start in range(0, block, ROWS):
            index = pl.ds(half * block + start, ROWS)
            scaled, _ = norm_rows(mixed[index, :])
            norm_cat[index, :] = (scaled * gain[...] + shift[...]).astype(BF16)
        if half == 0:
            up_load.wait()
    down_load = load(w_down, wd, 5)
    scan.drain()
    pl.semaphore_signal(free, inc=1, device_id=place.partner(), device_id_type=MESH)
    settle(att_leaves)
    pl.semaphore_wait(free, 1)

    def nth_block(index):
        return lax.rem(place.at[0] + jnp.where(index == 2, 3, jnp.maximum(2 - index, 0)), RING)

    def give(index, carry):
        columns = half_columns(nth_block(index), 1 - core, 1024)
        up(columns, own)
        swap.put(4 + index, index, hidden[:, columns], land.at[index])
        return carry

    lax.fori_loop(0, 4, give, 0)

    def take(index, carry):
        block_x = nth_block(index)
        columns = half_columns(block_x, core, 1024)
        up(columns, own)
        both = jnp.concatenate([hidden[:, columns], swap.get(4 + index, land.at[index])], axis=0)
        for half in range(2):
            columns = pl.ds(half * TILE, TILE)
            product = tn_dot(both, cot_cat[:, columns]).reshape(4, 4, 4, 8, TILE)
            for stream in range(3):
                slabs[stream][block_x, :, :, :, columns] = product[:, :, stream]
            last = product[:, :, 3]
            if half == 0:
                slab_a[block_x, :, :, :, pl.ds(1024, 384)] = last[..., :384]
                slab_b[block_x, :, :, :, pl.ds(1024, 128)] = last[..., 384:]
            else:
                slab_b[block_x, :, :, :, pl.ds(1152, 256)] = last[..., :256]
                slab_c[block_x, :, :, :, pl.ds(1024, 256)] = last[..., 256:]
        return carry

    kinds = (None, SplitPhase, SplitPhase)
    down = [Stream(place, slabs[k], ORDERS[k], phases[k], kinds[k]) for k in range(3)]
    lead, *others_two = [stream.prepare() for stream in down]
    lax.fori_loop(0, 2, take, 0)
    lead.begin_far()
    for phase in others_two:
        phase.begin_first()
    lead.begin_near(0)
    lax.fori_loop(2, 4, take, 0)
    for phase in others_two:
        phase.begin_second()
    lead.begin_near(1)
    pl.semaphore_signal(free, inc=1, device_id=place.partner(), device_id_type=MESH)
    for tile in range(2):
        columns = pl.ds(tile * TILE, TILE)
        swap.put(8 + tile, tile, norm_cat[own, columns], land_norm.at[tile], before=4 + tile)
    down_load.wait()
    cot = cot_cat.at[own]

    def finish_forward(columns):
        output[:, columns] = (mixed[:, columns] + dot_nn(hidden[...], wd[:, columns])).astype(BF16)

    for_columns(1024, 256, finish_forward)
    leave(output, output_out)

    def back(columns):
        held = slope[:, columns].astype(jnp.int32).astype(F32) * (1.0 / SLOPE_SCALE)
        grad = dot_nt(cot[...], wd[columns, :]) * held
        low = grad.astype(BF16)
        hidden[:, columns] = low
        return low

    pl.semaphore_wait(free, 1)

    def give_back(block, carry):
        theirs = back(half_columns(block, 1 - core, 1024))
        before = jnp.where(block < 2, 8 + block, 4 + block)
        swap.put(10 + block, block, theirs, land.at[block], before=before)
        return carry

    lax.fori_loop(0, 4, give_back, 0)

    def keep_back(block, carry):
        columns = pl.ds(pl.multiple_of(block * TILE, TILE), TILE)
        pre_cat[own, columns] = back(half_columns(block, core, 1024))
        return carry

    settle(cat_leaves)
    lax.fori_loop(0, 4, keep_back, 0)
    for stream in down:
        stream.forward()

    def back_up(columns):
        gmixed[:, columns] = dot_nt(hidden[...], wu[columns, :])

    for_columns(1024, 256, back_up)

    def take_back(block, carry):
        columns = pl.ds(pl.multiple_of(block * TILE, TILE), TILE)
        pre_cat[other, columns] = swap.get(10 + block, land.at[block])
        return carry

    lax.fori_loop(0, 4, take_back, 0)
    leave(pre_cat, pre_out)
    for tile in range(2):
        columns = pl.ds(tile * TILE, TILE)
        norm_cat[other, columns] = swap.get(8 + tile, land_norm.at[tile])
        swap.put(14 + tile, tile, att_low[:, columns], land_att.at[tile], before=10 + tile)
    leave(norm_cat, norm_out)
    query_load = load(qkv_out.at[0], wd.at[own], 7)
    pl.semaphore_signal(free, inc=1, device_id=place.partner(), device_id_type=MESH)
    def store(index, values):
        gmixed[index, :] = values
        hidden[index, pl.ds(0, 1024)] = values.astype(BF16)

    norm_back_rows(mixed, gmixed, cot, gain, sums, store)
    leave(gmixed, gmixed_out)
    pl.semaphore_wait(free, 1)
    swap.put(16, 2, hidden[:, half_tile(0, 1 - core)], land_norm.at[0], before=12)

    def back_out(columns):
        gatt[:, columns] = dot_nt(hidden[:, pl.ds(0, 1024)], wo[columns, :])

    state_loads = [query_load]

    def load_state(slots):
        for slot in slots:
            source = (att_out, den_out)[slot // 2].at[:, pl.ds(slot % 2 * TILE, TILE)]
            state_loads.append(load(source, stage.at[slot], 8 + slot))

    for number, slot in ((13, 3), (14, 0), (15, 1)):
        swap.copy(number, slot, land_norm.at[0]).wait_send()
    load_state((0, 1, 3))
    for_columns(1024, TILE, back_out)
    ours = hidden[:, half_tile(0, core)]
    swap.copy(16, 2, land_norm.at[0]).wait_send()
    load_state((2,))
    theirs = swap.get(16, land_norm.at[0])
    for tile in range(2):
        swap.copy(14 + tile, tile, land_att.at[tile]).wait_recv()
        for part, (start, width) in enumerate(((0, 384), (384, 128))):
            product = tn_dot(att_low[:, pl.ds(tile * TILE + start, width)], ours)
            theirs_att = land_att[tile, :, pl.ds(start, width)].astype(BF16)
            land[2 * tile + part, pl.ds(0, width), :] = product + tn_dot(theirs_att, theirs)
            leave(land.at[2 * tile + part, pl.ds(0, width)], out_out.at[pl.ds(tile * TILE + start, width)])
    for copy in state_loads:
        copy.wait()
    first_wide = first_head(block)

    def state_back(unit):
        index, columns = unit_slices(unit, block)
        tile, within = stage_place(unit)
        numer = gatt[index, columns] / stage[2 + tile, index, within]
        gatt[index, columns] = numer
        query = features(wd[index, columns].astype(F32))
        blocks, row = state_gradient(query, numer, stage[tile, index, within], first_wide)
        terms[unit, pl.ds(0, 64)] = blocks
        terms[unit, pl.ds(64, 8)] = row

    for_units(state_back, 2)
    leave(gatt, gn_out)
    for stream, target in zip(down, (down_a, down_b, down_c)):
        stream.finish()
        leave(stream.data, target)
    for stream in down:
        stream.drain()
    for copy in outs:
        if id(copy) not in settled:
            copy.wait()


def slab_shapes(widths):
    return [pltpu.VMEM((4, 4, 4, 8, width), F32) for width in widths]


def struct(shape, dtype=F32):
    return jax.ShapeDtypeStruct(shape, dtype)


VMEM_SPEC = pl.BlockSpec(memory_space=pltpu.VMEM)
ANY_SPEC = pl.BlockSpec(memory_space=pl.ANY)


def call(kernel, outs, out_specs, operands, in_specs, scratch, collective_id):
    return pl.pallas_call(
        kernel,
        out_shape=outs,
        in_specs=in_specs,
        out_specs=out_specs,
        scratch_shapes=scratch,
        compiler_params=pltpu.CompilerParams(
            collective_id=collective_id, has_side_effects=True, vmem_limit_bytes=63 * MIB
        ),
    )(*operands)


def front(x, gain_one, shift_one, gain, shift, w_qkv, cot, w_out, w_up, w_down, block):
    rows, width = x.shape
    wide = w_up.shape[1]
    outs = [
        struct((2, 2 * rows, width // 2), BF16),
        struct((3, rows, width), BF16),
        struct((rows, width)),
        struct((rows, width)),
        struct((SEQ, 72, PAIR)),
        struct((rows, width), BF16),
        struct((rows, width)),
        struct((rows, width)),
        struct((8, width)),
        struct((2 * rows, width), BF16),
        struct((2 * rows, wide // 2), BF16),
        struct((width, TILE)),
        struct((SEQ, 72, PAIR)),
        *[struct((4, 4, 8, length)) for length in DOWN_WIDTHS],
    ]
    scratch = [
        pltpu.VMEM((width, width), BF16),
        pltpu.VMEM((width, wide), BF16),
        pltpu.VMEM((wide, width), BF16),
        pltpu.SemaphoreType.DMA((12,)),
        pltpu.SemaphoreType.DMA((28,)),
        pltpu.VMEM((rows, width), BF16),
        SCAN_SCRATCH[0],
        pltpu.VMEM((rows, width), BF16),
        pltpu.VMEM((rows, width), F32),
        pltpu.VMEM((rows, width), F32),
        pltpu.VMEM((2 * rows, width), BF16),
        pltpu.VMEM((2 * rows, wide // 2), BF16),
        pltpu.VMEM((rows, wide), BF16),
        pltpu.VMEM((rows, wide), jnp.int16),
        pltpu.VMEM((2 * rows, width), BF16),
        pltpu.VMEM((4, rows, TILE), F32),
        pltpu.VMEM((4, rows, TILE), F32),
        pltpu.VMEM((2, rows, TILE), F32),
        pltpu.VMEM((2, rows, TILE), F32),
        pltpu.SemaphoreType.DMA((17,)),
        pltpu.SemaphoreType.DMA((17,)),
        pltpu.SemaphoreType.REGULAR,
        *SCAN_SCRATCH[3:],
        *slab_shapes(DOWN_WIDTHS),
        *flatten([[phase_scratch(2, length, 12)] for length in DOWN_WIDTHS]),
    ]
    specs = [VMEM_SPEC] * 5 + [ANY_SPEC] * 5
    out_specs = [ANY_SPEC] * 8 + [VMEM_SPEC] + [ANY_SPEC] * 3 + [VMEM_SPEC] + [ANY_SPEC] * 3
    operands = (x, gain_one, shift_one, gain, shift, w_qkv, cot, w_out, w_up, w_down)

    def kernel(*refs):
        front_kernel(block, *refs)

    return call(kernel, outs, out_specs, operands, specs, scratch, 1)


def last_scratch(rows, width):
    return {
        "qkv": pltpu.VMEM((3, rows, width), BF16),
        "att": pltpu.VMEM((rows, width), F32),
        "gn": pltpu.VMEM((rows, width), F32),
        "state": pltpu.VMEM((SEQ, 72, PAIR), F32),
        "x": pltpu.VMEM((rows, width), BF16),
        "grads": pltpu.VMEM((2, rows, width), F32),
        "scan": list(SCAN_SCRATCH[:3]) + [SCAN_SCRATCH[0]] + list(SCAN_SCRATCH[3:]),
        "norm_cat": pltpu.VMEM((2, 2 * rows, width // 2), BF16),
        "pre_cat": pltpu.VMEM((2 * rows, 2 * width), BF16),
        "w": pltpu.VMEM((width, 3 * width), BF16),
        "stage": pltpu.VMEM((3, rows, TILE), F32),
        "land": pltpu.VMEM((3, rows, TILE), F32),
        "swap": [pltpu.SemaphoreType.DMA((3,)), pltpu.SemaphoreType.DMA((3,))],
        "slabs": slab_shapes(UP_WIDTHS),
        "chunks": [pltpu.VMEM((4, 4, 8, length), F32) for length in DOWN_WIDTHS],
        "up_chunks": [pltpu.VMEM((4, 4, 8, length), F32) for length in UP_WIDTHS],
        "out_slabs": slab_shapes(OUT_WIDTHS),
        "vec_slab": pltpu.VMEM((4, 4, 4, 8, 128), F32),
        "sums": pltpu.VMEM((8, width), F32),
        "down": [stream_scratch(length, (1, 2), (2,)) for length in DOWN_WIDTHS],
        "up": [
            [*stream_scratch(length, (0, 1)), route_scratch(k, UP_WIDTHS, 2048)] for k, length in enumerate(UP_WIDTHS)
        ],
        "out": [
            [*stream_scratch(length, (0, 1), (1,)), route_scratch(k, OUT_WIDTHS, TILE)]
            for k, length in enumerate(OUT_WIDTHS)
        ],
        "qkv_sems": [[pltpu.SemaphoreType.DMA((6,))] * 2 for _ in QKV_WIDTHS],
        "qkv_sum": [
            [*stream_scratch(length, (1,)), route_scratch(k, QKV_WIDTHS, 3 * TILE)]
            for k, length in enumerate(QKV_WIDTHS)
        ],
        "vec": stream_scratch(128, (0, 1, 2), (0, 1, 2)),
        "vec_land": pltpu.VMEM((8, 128), F32),
        "vec_sems": pltpu.SemaphoreType.DMA((2,)),
        "credit": pltpu.SemaphoreType.REGULAR((3,)),
        "loads": pltpu.SemaphoreType.DMA((32,)),
    }


def last_kernel(
    block, qkv_in, att_in, terms_in, state_in, gn_in, gmixed_in, norm_one_in, norm_in, pre_in,
    down_in_a, down_in_b, down_in_c, out_in, x_in, weight, gain, sums_two,
    grad_input, grad_up, grad_out, grad_qkv, grad_down, grad_gains, *scratch,
):
    place = Place()
    core = place.core
    rows, width = att_in.shape
    like = last_scratch(rows, width)
    take = Taker(scratch)
    s = {name: take(like[name]) for name in like}
    qkv, att, gn, grads = s["qkv"], s["att"], s["gn"], s["grads"]
    slabs = s["slabs"]
    scan = Scan(*[Slots(ref) for ref in s["scan"][:4]], s["scan"][4:], True)
    across = [place.neighbour(0, step) for step in (1, -1, 2)]
    beside = []
    for axis in range(3):
        for step in (1, 2, 3):
            position = list(place.at)
            position[axis] = place.ring(axis, step)
            beside.append(place.id_of(*position, 1 - core))
    others = [*across, place.partner(), *beside, *scan.others()]
    greet(others)
    loads = []

    def load(source, target):
        copy = pltpu.make_async_copy(source, target, s["loads"].at[len(loads)])
        copy.start()
        loads.append(copy)
        return copy

    started = load(terms_in, scan.terms.ref)
    out_loads = []
    for k in (0, 2, 1):
        for which, start, length, at in stream_pieces(k, OUT_WIDTHS, TILE):
            source = out_in.at[:, which, :, :, :, pl.ds(start, length)]
            target = s["out_slabs"][k].at[:, :, :, :, pl.ds(at, length)]
            out_loads.append(load(source, target))
    up_loads = [load(pre_in, s["pre_cat"])]
    for which in range(2):
        for block_x in range(4):
            source = norm_in.at[:, pl.ds(block_x * 256 + which * 128, 128)]
            target = s["norm_cat"].at[which, :, pl.ds(block_x * 128, 128)]
            up_loads.append(load(source, target))
    down_in = (down_in_a, down_in_b, down_in_c)
    down_loads = [load(source, target) for source, target in zip(down_in, s["chunks"])]
    qkv_loads = [load(qkv_in, qkv), load(state_in, s["state"]), load(gn_in, gn), load(att_in, att)]
    late_loads = [load(weight, s["w"]), load(x_in, s["x"])]

    def settle(copies):
        for copy in copies:
            copy.wait()

    first, second = head_masks()
    first_wide = first_head(block)

    up_first = [phases[0] for phases in s["up"]]
    down = [Stream(place, s["chunks"][k], ORDERS[k][1:], s["down"][k]) for k in range(3)]
    up = [
        Stream(place, slabs[k], ORDERS[k], s["up"][k], None, (stream_pieces(k, UP_WIDTHS, 2048), grad_up))
        for k in range(3)
    ]
    out = [
        Stream(place, s["out_slabs"][k], ORDERS[k], s["out"][k], None, (stream_pieces(k, OUT_WIDTHS, TILE), grad_out))
        for k in range(3)
    ]
    qkv_sum = [None] * 3
    vec = [Stream(place, s["vec_slab"], ORDERS[0], s["vec"])]
    begin, forward, proceed, finish = Stream.begin, Stream.forward, Stream.proceed, Stream.finish

    def go(*steps):
        for step, streams, k in steps:
            step(streams[k])

    settle(out_loads)
    met(len(others))
    go((begin, out, 0))
    started.wait()
    scan.start(0)
    scan.start(1)
    go((begin, out, 2))
    settle(up_loads)
    for k in range(3):
        stream_product(k, s["norm_cat"], s["pre_cat"], slabs[k], UP_WIDTHS, 2048)
        if k == 1:
            settle(down_loads)
            go((begin, down, 0), (begin, up, 0))
    go((begin, out, 1))
    norm_load = load(norm_one_in, s["norm_cat"])
    settle(qkv_loads)
    causal = causal_mask(block)
    causal_t = causal_mask(block, True)

    def local_part(unit):
        index, columns = unit_slices(unit, block)
        raw_query = qkv[0, index, columns].astype(F32)
        query, value = features(raw_query), qkv[2, index, columns]
        key = features(qkv[1, index, columns].astype(F32))
        numer = gn[index, columns]
        one, two = head_slopes(numer, att[index, columns], first_wide)
        high, low = split(numer)
        scores = dot_nt(jnp.concatenate([key * first, key * second], axis=0), query)
        wide = jnp.concatenate([high, low], axis=1)
        values = jnp.concatenate([value, value], axis=1)
        grad_query, grad_key, grad_value = 0.0, 0.0, 0.0
        for head, (mask, slope) in enumerate(((first, one), (second, two))):
            mask_wide = jnp.concatenate([mask, mask], axis=1)
            mixing = split(jnp.where(causal, dot_nt(wide * mask_wide, values) + slope, 0.0))
            turned = jnp.where(causal_t, scores[head * block : (head + 1) * block], 0.0)
            for part in mixing:
                grad_query = grad_query + dot_nn(part, key * mask)
                grad_key = grad_key + tn_dot(part, query * mask)
            both = dot_nn(turned.astype(BF16), wide * mask_wide)
            grad_value = grad_value + both[:, :PAIR] + both[:, PAIR:]
        square, total = unpack_state(s["state"][unit])
        state_high, state_low = split(square)
        grad_query = grad_query + dot_nn(wide, jnp.concatenate([state_high, state_high], axis=0))
        grad_query = grad_query + dot_nn(high, state_low)
        grad_query = grad_query + jnp.where(first_wide, one, two) * total
        qkv[0, index, columns] = (grad_query * feature_slope(raw_query)).astype(BF16)
        grads[0, index, columns] = grad_key
        grads[1, index, columns] = grad_value

    def local_parts(start, count):
        def one(index, carry):
            local_part(start + index)
            return carry

        lax.fori_loop(0, count, one, 0)

    local_parts(0, 2)
    scan.middle()
    local_parts(2, 1)
    go((begin, up, 2), (forward, out, 2), (forward, out, 0))
    local_parts(3, 2)
    go((forward, out, 1))
    local_parts(5, 3)
    go((begin, up, 1))
    local_parts(8, 7)
    go((forward, up, 0))
    local_parts(15, 1)
    swap = Swap(place, s["stage"], *s["swap"])
    land, cat = s["land"], s["pre_cat"]
    own, other = pl.ds(0, rows), pl.ds(rows, rows)
    swap.put(0, 0, qkv[0, :, half_tile(0, 1 - core)], land.at[0])
    mixed_load = load(gmixed_in, att)
    scan.finish(0)
    scan.finish(1)
    go((begin, down, 2))

    def incoming(unit):
        index, columns = unit_slices(unit, block)
        square, total = unpack_state(scan.result.ref[unit])
        high, low = split(square)
        raw_key = qkv[1, index, columns].astype(F32)
        key, value = features(raw_key), qkv[2, index, columns]
        grad_key = grads[0, index, columns] + total
        grad_key = grad_key + dot_nt(
            jnp.concatenate([value, value], axis=1), jnp.concatenate([high, low], axis=1)
        )
        grad_value = grads[1, index, columns] + dot_nn(
            jnp.concatenate([key, key], axis=1), jnp.concatenate([high, low], axis=0)
        )
        qkv[1, index, columns] = (grad_key * feature_slope(raw_key)).astype(BF16)
        qkv[2, index, columns] = grad_value.astype(BF16)

    for_units(incoming, 2)
    for third in (1, 2):
        swap.put(third, third, qkv[third, :, half_tile(0, 1 - core)], land.at[third])
    settle(late_loads)

    def back_norm(columns):
        total = 0.0
        for third in range(3):
            total = total + dot_nt(qkv[third], s["w"][columns, pl.ds(third * 1024, 1024)])
        gn[:, columns] = total

    for start in (0, 256, 512, 768):
        back_norm(pl.ds(start, 256))
    for third in range(3):
        columns = pl.ds(third * TILE, TILE)
        cat[own, columns] = qkv[third, :, half_tile(0, core)]
        cat[other, columns] = swap.get(third, land.at[third])
    go((forward, up, 2), (forward, up, 1))
    norm_load.wait()
    mixed_load.wait()
    def turn(k):
        up[k].finish(s["up_chunks"][k])
        up[k].drain()
        for step in (1, -1):
            pl.semaphore_signal(
                s["credit"].at[k],
                inc=1,
                device_id=place.neighbour(ORDERS[k][0], step),
                device_id_type=MESH,
            )
        narrow = (slice(None),) * 4 + (pl.ds(0, QKV_WIDTHS[k]),)
        data = slabs[k].at[narrow]
        stream_product(k, s["norm_cat"], cat, data, QKV_WIDTHS, 3 * TILE)
        pl.semaphore_wait(s["credit"].at[k], 2)
        phases = [[up_first[k][0].at[narrow], up_first[k][1].at[narrow], *s["qkv_sems"][k]]]
        last = (stream_pieces(k, QKV_WIDTHS, 3 * TILE), grad_qkv)
        qkv_sum[k] = Stream(place, data, ORDERS[k], phases + s["qkv_sum"][k], None, last)
        qkv_sum[k].begin()

    def store(index, values):
        gn[index, :] = values

    sums = s["sums"]
    norm_back_rows(s["x"], gn, att, gain, sums, store)
    leave = load(gn, grad_input)
    go((begin, down, 1), (proceed, out, 0))
    four = jnp.concatenate([sums[0:2, :], sums_two[0:2, :]], axis=0)
    eight = jnp.concatenate([four, four], axis=0)
    turned = jnp.transpose(jnp.concatenate([eight, jnp.zeros((120, 1024), F32)], axis=0))
    turned = turned.reshape(4, 2, 4, 4, 8, 128)
    lane = lax.broadcasted_iota(jnp.int32, (8, 128), 1)
    s["vec_slab"][...] = jnp.where(lane < 4, turned[:, 0], jnp.where(lane < 8, turned[:, 1], 0.0))
    go((begin, vec, 0), (proceed, out, 1))
    turn(0)
    turn(2)
    go((begin, up, 0))
    turn(1)
    go(
        (forward, qkv_sum, 0), (forward, qkv_sum, 2), (begin, up, 1), (forward, down, 2), (forward, down, 1),
        (begin, up, 2), (proceed, out, 0), (forward, qkv_sum, 1), (proceed, vec, 0), (proceed, qkv_sum, 2),
        (proceed, qkv_sum, 0), (proceed, qkv_sum, 1), (forward, down, 0), (forward, up, 0), (forward, up, 1),
        (proceed, out, 2), (proceed, vec, 0), (forward, qkv_sum, 2), (forward, up, 2), (proceed, down, 1),
        (forward, qkv_sum, 0), (forward, qkv_sum, 1), (proceed, down, 2), (proceed, down, 0), (proceed, qkv_sum, 2),
        (proceed, up, 0), (proceed, up, 1), (proceed, out, 2), (proceed, qkv_sum, 0), (proceed, up, 2),
        (proceed, out, 1), (proceed, qkv_sum, 1), (finish, down, 2), (finish, down, 1), (finish, down, 0),
        (finish, up, 1), (finish, vec, 0),
    )
    vec_tile = vec[0].data
    vec_copy = pltpu.make_async_remote_copy(
        src_ref=vec_tile,
        dst_ref=s["vec_land"],
        send_sem=s["vec_sems"].at[0],
        recv_sem=s["vec_sems"].at[1],
        device_id=place.partner(),
        device_id_type=MESH,
    )
    vec_copy.start()
    go(
        (finish, up, 0), (finish, qkv_sum, 0), (finish, qkv_sum, 2), (finish, out, 0), (finish, qkv_sum, 1),
        (finish, out, 2), (finish, out, 1), (finish, up, 2),
    )
    for k in range(3):
        piece = down[k].data
        grad_down[pl.ds(8 * k, 8), :] = piece[:, pl.ds(0, 1024)]
        start, width_k = DOWN_CUTS[k]
        grad_down[pl.ds(24, 8), pl.ds(start, width_k)] = piece[:, pl.ds(1024, width_k)]
    scan.drain()
    for number in range(3):
        swap.copy(number, number, land.at[number]).wait_send()
    for stream in (*down, *up, *out, *qkv_sum, *vec):
        stream.drain()
    vec_copy.wait()
    grad_gains[...] = vec_tile[...] + s["vec_land"][...]
    leave.wait()


def last_part(qkv, att, terms, state, gn, gmixed, norm_one, norm_cat, pre_cat, down, out, x, weight, gain, sums_two, block):
    rows, width = x.shape

    def kernel(*refs):
        last_kernel(block, *refs)

    outs = [
        struct((rows, width)),
        struct((8, 4096)),
        struct((8, width)),
        struct((8, 3 * width)),
        struct((32, width)),
        struct((8, 128)),
    ]
    like = last_scratch(rows, width)
    scratch = [leaf for name in like for leaf in flatten(like[name])]
    out = out.reshape(4, 2, 4, 4, 8, TILE)
    operands = (
        qkv, att, terms, state, gn, gmixed, norm_one, norm_cat, pre_cat, *down, out, x, weight, gain, sums_two,
    )
    specs = [ANY_SPEC] * 15 + [VMEM_SPEC] * 2
    out_specs = [ANY_SPEC] + [VMEM_SPEC] * 5
    return call(kernel, outs, out_specs, operands, specs, scratch, 2)


PARTS = (4, 4, 1, 1, 1, 1)


def lay_out_kernel(core_gains, *refs):
    count = len(PARTS)
    sources, targets, gains = refs[:count], refs[count : 2 * count], refs[2 * count : 2 * count + 4]
    held, (into, out_of) = refs[2 * count + 4 : 3 * count + 4], refs[3 * count + 4 :]
    moves = []
    for k in (1, 0, 2, 3, 4, 5):
        rows = sources[k].shape[0] // PARTS[k]
        for part in range(PARTS[k]):
            index, number = pl.ds(part * rows, rows), len(moves)
            load = pltpu.make_async_copy(sources[k].at[index], held[k].at[index], into.at[number])
            leave = pltpu.make_async_copy(held[k].at[index], targets[k].at[index], out_of.at[number])
            load.start()
            moves.append((load, leave))
    for load, leave in moves:
        load.wait()
        leave.start()
    core = lax.rem(lax.axis_index("dp"), 2)
    turned = jnp.transpose(jnp.concatenate([core_gains[...], jnp.zeros((120, 128), F32)], axis=0))
    for k, target in enumerate(gains):
        target[...] = jnp.where(core == 0, turned[k : k + 1, :8], turned[4 + k : 5 + k, :8])
    for _, leave in moves:
        leave.wait()


def lay_out(gains, *arrays):
    return pl.pallas_call(
        lay_out_kernel,
        out_shape=[struct(array.shape, array.dtype) for array in arrays] + [struct((1, 8))] * 4,
        in_specs=[VMEM_SPEC] + [ANY_SPEC] * len(PARTS),
        out_specs=[ANY_SPEC] * len(PARTS) + [VMEM_SPEC] * 4,
        scratch_shapes=[
            *[pltpu.VMEM(array.shape, array.dtype) for array in arrays],
            pltpu.SemaphoreType.DMA((sum(PARTS),)),
            pltpu.SemaphoreType.DMA((sum(PARTS),)),
        ],
        compiler_params=pltpu.CompilerParams(vmem_limit_bytes=62 * MIB),
    )(gains, *arrays)


def body(
    inputs,
    first_gain,
    first_shift,
    qkv_weight,
    out_weight,
    second_gain,
    second_shift,
    up_weight,
    down_weight,
    cotangent,
):
    sequences, block, width = inputs.shape
    rows = sequences * block
    x = inputs.reshape(rows, width)
    cot = cotangent.reshape(rows, width)
    gain_one, gain_two = first_gain.reshape(1, width), second_gain.reshape(1, width)
    shift_two = second_shift.reshape(1, width)
    shift_one = first_shift.reshape(1, width)
    norm_one, qkv, att, _, state, output, gmixed, gn, sums_two, norm_cat, pre_cat, out, terms, *down = front(
        x, gain_one, shift_one, gain_two, shift_two, qkv_weight, cot, out_weight, up_weight, down_weight, block
    )
    grads = last_part(
        qkv, att, terms, state, gn, gmixed, norm_one, norm_cat, pre_cat, down, out, x, qkv_weight,
        gain_one, sums_two, block,
    )
    *grads, gains = grads
    output, grad_input, grad_up, grad_out, grad_qkv, grad_down, *gains = lay_out(gains, output, *grads)
    return (
        output.reshape(inputs.shape),
        grad_input.reshape(inputs.shape),
        grad_qkv,
        grad_out,
        grad_up,
        grad_down,
        *[gain.reshape(8) for gain in gains],
    )


def solution(mesh):
    return jax.shard_map(
        body,
        mesh=mesh,
        in_specs=(
            P("dp", "seq", None),
            P(),
            P(),
            P(),
            P(),
            P(),
            P(),
            P(),
            P(),
            P("dp", "seq", None),
        ),
        out_specs=(
            P("dp", "seq", None),
            P("dp", "seq", None),
            P(("dp", "seq"), None),
            P(("dp", "seq"), None),
            P(("dp", "seq"), None),
            P(("dp", "seq"), None),
            P(("dp", "seq")),
            P(("dp", "seq")),
            P(("dp", "seq")),
            P(("dp", "seq")),
        ),
        check_vma=False,
    )
```

```python
import math

import jax
import jax.numpy as jnp
from jax import lax
from jax.experimental import pallas as pl
from jax.experimental.pallas import tpu as pltpu
from jax.sharding import PartitionSpec as P

MESH = pl.DeviceIdType.MESH
F32 = jnp.float32
BF16 = jnp.bfloat16
RING = 4
MIB = 2**20


class Place:
    def __init__(self):
        dp, seq = lax.axis_index("dp"), lax.axis_index("seq")
        self.core = lax.rem(dp, 2)
        self.at = (lax.div(dp, 2), lax.div(seq, RING), lax.rem(seq, RING))

    def id_of(self, x, y, z, core):
        return (x * 2 + core, y * RING + z)

    def ring(self, axis, step):
        return lax.rem(self.at[axis] + (step + RING), RING)

    def neighbour(self, axis, step):
        at = list(self.at)
        at[axis] = self.ring(axis, step)
        return self.id_of(*at, self.core)

    def partner(self):
        return self.id_of(*self.at, 1 - self.core)


def greet(others):
    barrier = pltpu.get_barrier_semaphore()
    for other in others:
        pl.semaphore_signal(barrier, inc=1, device_id=other, device_id_type=MESH)


def met(count):
    pl.semaphore_wait(pltpu.get_barrier_semaphore(), count)


def link_neighbours(place):
    others = [place.neighbour(axis, step) for axis in range(3) for step in (1, -1)]
    return [*others, place.partner()]


ORDERS = ((0, 1, 2), (1, 2, 0), (2, 0, 1))


def phase_scratch(remaining, length, messages=6):
    if remaining:
        half = (2, 2, *[4] * (remaining - 1), 8, length)
    else:
        half = (2, 8, (length // 128 + 1) // 2 * 128)
    return [
        pltpu.VMEM((2, *[4] * remaining, 8, length), F32),
        pltpu.VMEM(half, F32),
        pltpu.SemaphoreType.DMA((messages,)),
        pltpu.SemaphoreType.DMA((messages,)),
    ]


class Phase:
    def __init__(self, place, data, axes, axis, scratch):
        self.place, self.data, self.axis = place, data, axis
        self.where = axes.index(axis)
        self.full, self.half, self.sent, self.came = scratch
        self.flying = []
        self.flat = len(axes) == 1
        self.length = data.shape[-1]
        self.cut = (self.length // 128 + 1) // 2 * 128
        self.whole = self.flat and self.cut == self.length

    def empty(self, which):
        return self.whole and which == 1

    def chunk(self, target):
        index = [slice(None)] * self.where + [target]
        return self.data.at[tuple(index)]

    def part(self, ref, which):
        if not self.flat:
            return ref.at[pl.ds(2 * which, 2)]
        if which == 0:
            return ref.at[:, pl.ds(0, self.cut)]
        return ref.at[:, pl.ds(self.cut, self.length - self.cut)]

    def through(self, way):
        ref = self.half.at[way]
        if self.flat and way == 1:
            return ref.at[:, pl.ds(0, self.length - self.cut)]
        return ref

    def copy(self, kind, way, source, target):
        number = kind * 2 + way
        return pltpu.make_async_remote_copy(
            src_ref=source,
            dst_ref=target,
            send_sem=self.sent.at[number],
            recv_sem=self.came.at[number],
            device_id=self.place.neighbour(self.axis, 1 - 2 * way),
            device_id_type=MESH,
        )

    def send(self, kind, way, source, target):
        copy = self.copy(kind, way, source, target)
        copy.start()
        self.flying.append(copy)

    def beside(self, way):
        return self.chunk(self.place.ring(self.axis, 1 - 2 * way))

    def begin_far(self):
        opposite = self.chunk(self.place.ring(self.axis, 2))
        for way in range(2):
            if not self.empty(way):
                self.send(0, way, self.part(opposite, way), self.through(way))

    def begin_near(self, way):
        if not self.empty(1 - way):
            target = self.part(self.full.at[way], 1 - way)
            self.send(1, way, self.part(self.beside(way), 1 - way), target)

    def begin(self):
        self.begin_far()
        for way in range(2):
            self.begin_near(way)

    def forward(self):
        for way in range(2):
            if self.empty(way):
                continue
            came = self.through(way)
            self.copy(0, way, came, came).wait_recv()
            own = self.part(self.beside(way), way)
            add_into(own, own, came)
            self.send(2, way, own, self.part(self.full.at[way], way))

    def finish(self, out=None):
        own = self.chunk(self.place.at[self.axis])
        for way in range(2):
            for kind, which in ((1, 1 - way), (2, way)):
                if self.empty(which):
                    continue
                target = self.part(self.full.at[way], which)
                self.copy(kind, way, target, target).wait_recv()
        add_into(own if out is None else out, own, self.full.at[0], self.full.at[1])
        return own

    def drain(self):
        for copy in self.flying:
            copy.wait_send()


HALVES = ((2, 1), (3, 0))


class SplitPhase(Phase):
    def block(self, way, j):
        return self.place.ring(0, HALVES[way][j])

    def copy_block(self, kind, way, j, source, target):
        number = kind * 4 + way * 2 + j
        return pltpu.make_async_remote_copy(
            src_ref=source,
            dst_ref=target,
            send_sem=self.sent.at[number],
            recv_sem=self.came.at[number],
            device_id=self.place.neighbour(self.axis, 1 - 2 * way),
            device_id_type=MESH,
        )

    def send_far(self, way, j):
        source = self.chunk(self.place.ring(self.axis, 2)).at[self.block(way, j)]
        self.flying.append(self.copy_block(0, way, j, source, self.half.at[way, j]))
        self.flying[-1].start()

    def send_near(self, kind, way, j):
        block = self.block(way if kind == 2 else 1 - way, j)
        source, target = self.beside(way).at[block], self.full.at[way, block]
        self.flying.append(self.copy_block(kind, way, j, source, target))
        self.flying[-1].start()

    def begin_first(self):
        for j in range(2):
            self.send_far(0, j)
        self.send_near(1, 1, 0)

    def begin_second(self):
        for j in range(2):
            self.send_far(1, j)
        self.send_near(1, 1, 1)
        for j in range(2):
            self.send_near(1, 0, j)

    def forward(self):
        for way in range(2):
            for j in range(2):
                came = self.half.at[way, j]
                self.copy_block(0, way, j, came, came).wait_recv()
                own = self.beside(way).at[self.block(way, j)]
                add_into(own, own, came)
                self.send_near(2, way, j)

    def finish(self, out=None):
        own = self.chunk(self.place.at[self.axis])
        for way in range(2):
            for kind, part in ((1, 1 - way), (2, way)):
                for j in range(2):
                    target = self.full.at[way, self.block(part, j)]
                    self.copy_block(kind, way, j, target, target).wait_recv()
        add_into(own if out is None else out, own, self.full.at[0], self.full.at[1])
        return own


class Direct:
    def __init__(self, place, data, axes, axis, scratch):
        self.place, self.data, self.axis = place, data, axis
        self.where = axes.index(axis)
        self.full, self.sent, self.came = scratch
        self.flying = []

    def chunk(self, target):
        index = [slice(None)] * self.where + [target]
        return self.data.at[tuple(index)]

    def copy(self, step, source):
        return pltpu.make_async_remote_copy(
            src_ref=source,
            dst_ref=self.full.at[step - 1],
            send_sem=self.sent.at[step - 1],
            recv_sem=self.came.at[step - 1],
            device_id=self.place.neighbour(self.axis, step),
            device_id_type=MESH,
        )

    def begin(self):
        for step in (2, 1, 3):
            copy = self.copy(step, self.chunk(self.place.ring(self.axis, step)))
            copy.start()
            self.flying.append(copy)

    def forward(self):
        pass

    def finish(self, out=None):
        own = self.chunk(self.place.at[self.axis])
        for step in (1, 2, 3):
            self.copy(step, self.full.at[step - 1]).wait_recv()
        add_into(own if out is None else out, own, *[self.full.at[k] for k in range(3)])
        return own

    def drain(self):
        for copy in self.flying:
            copy.wait_send()


class Route:
    def __init__(self, place, data, axis, pieces, scratch, out):
        self.place, self.data, self.axis, self.pieces, self.out = place, data, axis, pieces, out
        self.scratch = scratch

    def send_each(self, act):
        core = self.place.core
        for (owner, _, width, at), (land, sent, came) in zip(self.pieces, self.scratch):

            def copy(step):
                position = list(self.place.at)
                position[self.axis] = self.place.ring(self.axis, step)
                return pltpu.make_async_remote_copy(
                    src_ref=self.data.at[self.place.ring(self.axis, step), :, pl.ds(at, width)],
                    dst_ref=land.at[core, step],
                    send_sem=sent.at[step],
                    recv_sem=came.at[core, step],
                    device_id=self.place.id_of(*position, owner),
                    device_id_type=MESH,
                )

            for step in (2, 1, 3):
                act(copy(step))

            @pl.when(core != owner)
            def _():
                act(copy(0))

    def begin(self):
        self.send_each(lambda copy: copy.start())

    def forward(self):
        pass

    def finish(self, out=None):
        core = self.place.core
        mine = self.place.at[self.axis]
        for (owner, start, width, at), (land, sent, came) in zip(self.pieces, self.scratch):

            @pl.when(core == owner)
            def _():
                for source, steps in ((core, (1, 2, 3)), (1 - core, (0, 1, 2, 3))):
                    for step in steps:
                        target = land.at[source, step]
                        pltpu.make_async_remote_copy(
                            src_ref=target,
                            dst_ref=target,
                            send_sem=sent.at[step],
                            recv_sem=came.at[source, step],
                            device_id=self.place.partner(),
                            device_id_type=MESH,
                        ).wait_recv()
                done = 0
                while done < width:
                    column = start + done
                    tile, within = column // TILE, column % TILE
                    step = min(TILE - within, width - done)
                    part = pl.ds(done, step)
                    ours = self.data[mine, :, pl.ds(at + done, step)]
                    for k in (1, 2, 3):
                        ours = ours + land[core, k, :, part]
                    theirs = land[1 - core, 0, :, part]
                    for k in (1, 2, 3):
                        theirs = theirs + land[1 - core, k, :, part]
                    for values, half in ((ours, core), (theirs, 1 - core)):
                        place = pl.multiple_of((2 * tile + half) * TILE + within, 128)
                        self.out[:, pl.ds(place, step)] = values
                    done += step

    def drain(self):
        self.send_each(lambda copy: copy.wait_send())


def route_scratch(stream, widths, columns):
    return [
        [
            pltpu.VMEM((2, 4, 8, width), F32),
            pltpu.SemaphoreType.DMA((4,)),
            pltpu.SemaphoreType.DMA((2, 4)),
        ]
        for _, _, width, _ in stream_pieces(stream, widths, columns)
    ]


class Stream:
    def __init__(self, place, data, order, scratch, first=None, last=None):
        self.place, self.data, self.scratch, self.first, self.last = place, data, scratch, first, last
        self.todo, self.old = [axis for axis in order], []
        self.axes = sorted(order)
        self.phase = None

    def prepare(self):
        scratch = self.scratch.pop(0)
        if self.last and len(self.todo) == 1:
            pieces, out = self.last
            self.phase = Route(self.place, self.data, self.todo[0], pieces, scratch, out)
            return self.phase
        kind = self.first or (Phase if len(scratch) == 4 else Direct)
        self.first = None
        self.phase = kind(self.place, self.data, self.axes, self.todo[0], scratch)
        return self.phase

    def begin(self):
        self.prepare().begin()

    def forward(self):
        self.phase.forward()

    def finish(self, out=None):
        own = self.phase.finish(out)
        self.data = own if out is None else out
        self.axes.remove(self.todo.pop(0))
        self.old.append(self.phase)

    def proceed(self):
        self.finish()
        self.begin()

    def drain(self):
        for phase in self.old:
            phase.drain()
        self.old = []


def direct_scratch(remaining, length):
    return [
        pltpu.VMEM((3, *[4] * remaining, 8, length), F32),
        pltpu.SemaphoreType.DMA((3,)),
        pltpu.SemaphoreType.DMA((3,)),
    ]


def stream_scratch(length, phases, direct=()):
    return [
        (direct_scratch if phase in direct else phase_scratch)(2 - phase, length)
        for phase in phases
    ]


class Taker:
    def __init__(self, refs):
        self.refs = list(refs)

    def __call__(self, like):
        if isinstance(like, list):
            return [self(item) for item in like]
        return self.refs.pop(0)


def flatten(items):
    if isinstance(items, list):
        return [leaf for item in items for leaf in flatten(item)]
    return [items]


def add_into(out, *terms):
    if len(out.shape) > 2:

        def row(index, carry):
            add_into(out.at[index], *[term.at[index] for term in terms])
            return carry

        if len(out.shape) == 4:
            lax.fori_loop(0, out.shape[0], row, 0)
        else:
            for index in range(out.shape[0]):
                row(index, 0)
        return
    total = terms[0][...]
    for term in terms[1:]:
        total = total + term[...]
    out[...] = total


def tn_dot(left, right):
    return lax.dot_general(left, right, (((0,), (0,)), ((), ())), preferred_element_type=F32)


TILE = 512


class Swap:
    def __init__(self, place, stage, sent, came):
        self.place, self.stage, self.sent, self.came = place, stage, sent, came

    def copy(self, number, slot, target):
        return pltpu.make_async_remote_copy(
            src_ref=self.stage.at[slot],
            dst_ref=target,
            send_sem=self.sent.at[number],
            recv_sem=self.came.at[number],
            device_id=self.place.partner(),
            device_id_type=MESH,
        )

    def put(self, number, slot, values, target, before=None):
        if before is not None:
            self.copy(before, slot, target).wait_send()
        self.stage[slot] = values.astype(F32)
        self.copy(number, slot, target).start()

    def get(self, number, target):
        self.copy(number, 0, target).wait_recv()
        return target[...].astype(BF16)

    def drain(self, numbers, target):
        for number in numbers:
            self.copy(number, number % 4, target).wait_send()


def half_columns(block, core, quarter):
    half = quarter // 2
    return pl.ds(pl.multiple_of(block * quarter + core * half, half), half)


def half_tile(index, core):
    return pl.ds(pl.multiple_of((2 * index + core) * TILE, TILE), TILE)


def core_product(left, core, right, start, width, slab, at):
    done = 0
    while done < width:
        step = min(TILE, width - done)
        product = tn_dot(left[core], right[:, pl.ds(start + done, step)])
        slab[:, :, :, :, pl.ds(at + done, step)] = product.reshape(4, 4, 4, 8, step)
        done += step


UP_WIDTHS = (1536, 1280, 1280)
OUT_WIDTHS = (512, 256, 256)
QKV_WIDTHS = (1152, 896, 1024)


def stream_pieces(stream, widths, columns):
    if stream < 2:
        return [(stream, 0, widths[stream], 0)]
    pieces, at = [], 0
    for core in range(2):
        width = columns - widths[core]
        if width:
            pieces.append((core, widths[core], width, at))
        at += width
    return pieces


def stream_product(stream, left, right, slab, widths, columns):
    for core, start, width, at in stream_pieces(stream, widths, columns):
        core_product(left, core, right, start, width, slab, at)


DOWN_CUTS = ((0, 384), (384, 384), (768, 256))
DOWN_WIDTHS = (1408, 1408, 1280)


SEQ = 16
PAIR = 128
NT = (((1,), (1,)), ((), ()))
TN = (((0,), (0,)), ((), ()))


def dot_nt(left, right):
    return lax.dot_general(left, right, NT, preferred_element_type=F32)


def dot_nn(left, right):
    return jnp.dot(left, right, preferred_element_type=F32)


def split(values):
    high = values.astype(BF16)
    return high, (values - high.astype(F32)).astype(BF16)


def features(raw):
    return jnp.where(raw > 0, raw + 1.0, jnp.exp(jnp.minimum(raw, 0.0))).astype(BF16)


def feature_slope(raw):
    return jnp.where(raw > 0, 1.0, jnp.exp(jnp.minimum(raw, 0.0)))


def head_masks():
    lane = lax.broadcasted_iota(jnp.int32, (1, PAIR), 1)
    first = jnp.where(lane < 64, 1.0, 0.0)
    return first.astype(BF16), (1.0 - first).astype(BF16)


def first_head(rows):
    return lax.broadcasted_iota(jnp.int32, (rows, PAIR), 1) < 64


def pack_state(square, total):
    blocks = jnp.where(first_head(64), square[:64], square[64:])
    return blocks, jnp.broadcast_to(total, (8, PAIR))


def unpack_state(packed):
    first = first_head(64)
    square = jnp.concatenate(
        [jnp.where(first, packed[:64], 0.0), jnp.where(first, 0.0, packed[:64])], axis=0
    )
    return square, packed[64:65]


def same_head():
    row = lax.broadcasted_iota(jnp.int32, (PAIR, PAIR), 0)
    lane = lax.broadcasted_iota(jnp.int32, (PAIR, PAIR), 1)
    return (row < 64) == (lane < 64)


def head_slopes(numer, attended, first_wide):
    product = numer * attended
    ours = jnp.sum(jnp.where(first_wide, product, 0.0), axis=1, keepdims=True)
    theirs = jnp.sum(jnp.where(first_wide, 0.0, product), axis=1, keepdims=True)
    return -ours, -theirs


def state_gradient(query, numer, attended, first_wide):
    one, two = head_slopes(numer, attended, first_wide)
    high, low = split(numer)
    wide = tn_dot(query, jnp.concatenate([high, low], axis=1))
    spread = jnp.where(first_wide, one, two)
    total = jnp.sum(query.astype(F32) * spread, axis=0, keepdims=True)
    return pack_state(wide[:, :PAIR] + wide[:, PAIR:], total)


OFFSETS = sorted(
    ((y, z) for y in range(RING) for z in range(RING) if y or z),
    key=lambda offset: -sum(min(step, RING - step) for step in offset),
)


class Units:
    def __init__(self, ref):
        self.ref = ref

    def at(self, unit):
        rows = pl.ds(pl.multiple_of(lax.div(lax.rem(unit, 8), 4) * 72, 8), 72)
        columns = pl.ds(pl.multiple_of(lax.rem(unit, 4) * PAIR, PAIR), PAIR)
        return self.ref.at[lax.div(unit, 8), rows, columns]


class Slots:
    def __init__(self, ref):
        self.ref = ref

    def at(self, unit):
        return self.ref.at[unit]


class Scan:
    def __init__(self, terms, landed, sums, result, sems, reverse):
        self.terms, self.landed, self.sums, self.result = terms, landed, sums, result
        self.sems, self.reverse = sems, reverse
        self.dp, self.me = lax.axis_index("dp"), lax.axis_index("seq")
        self.y, self.z = lax.div(self.me, RING), lax.rem(self.me, RING)
        self.parity = lax.rem(self.y + self.z, 2)
        self.unit = self.unit_of(self.parity, self.me)

    def unit_of(self, parity, device):
        return parity * 8 + lax.div(device, 2)

    def at(self, y, z, sign=1):
        y = lax.rem(self.y + (sign * y + RING), RING)
        z = lax.rem(self.z + (sign * z + RING), RING)
        return y * RING + z

    def others(self):
        return [(self.dp, self.at(*offset)) for offset in OFFSETS]

    def half_offsets(self, half):
        for y in (2, 1, 3, 0):
            for step in (1, 0):
                yield y, 2 * step + lax.rem(self.parity + (y + half), 2)

    def copy(self, number, source, target, sems, other):
        return pltpu.make_async_remote_copy(
            src_ref=source,
            dst_ref=target,
            send_sem=sems[0].at[number],
            recv_sem=sems[1].at[number],
            device_id=(self.dp, other),
            device_id_type=MESH,
        )

    def start(self, half):
        for y, z in self.half_offsets(half):
            other = self.at(y, z)
            source = self.terms.at(self.unit_of(half, other))
            copy = self.copy(y * RING + z, source, self.landed.at(self.me), self.sems[:2], other)
            if y:
                copy.start()
            else:
                pl.when(z > 0)(copy.start)

    def middle(self):
        for y, z in OFFSETS:
            other = self.at(y, z, -1)
            came = self.landed.at(other)
            self.copy(y * RING + z, came, came, self.sems[:2], other).wait_recv()
        self.landed.at(self.me)[...] = self.terms.at(self.unit)[...]
        total = jnp.zeros((72, PAIR), F32)
        for k in range(SEQ):
            at = SEQ - 1 - k if self.reverse else k
            self.sums.at(at)[...] = total
            total = total + self.landed.at(at)[...]
        for y, z in OFFSETS:
            other = self.at(y, z)
            target = self.result.at(self.unit)
            self.copy(y * RING + z, self.sums.at(other), target, self.sems[2:], other).start()
        self.result.at(self.unit)[...] = self.sums.at(self.me)[...]

    def finish(self, half):
        for y, z in self.half_offsets(half):
            other = self.at(y, z, -1)
            came = self.result.at(self.unit_of(half, other))
            copy = self.copy(y * RING + z, came, came, self.sems[2:], other)
            if y:
                copy.wait_recv()
            else:
                pl.when(z > 0)(copy.wait_recv)

    def drain(self):
        for y, z in OFFSETS:
            number, other = y * RING + z, self.at(y, z)
            self.copy(number, self.terms.at(0), self.landed.at(0), self.sems[:2], other).wait_send()
            self.copy(number, self.sums.at(0), self.result.at(0), self.sems[2:], other).wait_send()


SCAN_SCRATCH = [
    pltpu.VMEM((SEQ, 72, PAIR), F32),
    pltpu.VMEM((SEQ, 72, PAIR), F32),
    pltpu.VMEM((SEQ, 72, PAIR), F32),
    *[pltpu.SemaphoreType.DMA((SEQ,)) for _ in range(4)],
]


def unit_slices(unit, block):
    rows = pl.ds(pl.multiple_of(lax.div(unit, 8) * block, block), block)
    columns = pl.ds(pl.multiple_of(lax.rem(unit, 8) * PAIR, PAIR), PAIR)
    return rows, columns


def for_units(step, together):
    def several(index, carry):
        for offset in range(together):
            step(index * together + offset)
        return carry

    lax.fori_loop(0, SEQ // together, several, 0)


def causal_mask(block, transposed=False):
    row = lax.broadcasted_iota(jnp.int32, (block, block), 0)
    column = lax.broadcasted_iota(jnp.int32, (block, block), 1)
    return (row <= column) if transposed else (row >= column)


def norm_rows(values):
    center = jnp.mean(values, axis=-1, keepdims=True)
    centered = values - center
    variance = jnp.mean(centered * centered, axis=-1, keepdims=True)
    inverse = lax.rsqrt(variance + 1e-05)
    return centered * inverse, inverse


ROWS = 64


def for_rows(count, step):
    def one(index, carry):
        step(pl.ds(pl.multiple_of(index * ROWS, ROWS), ROWS))
        return carry

    lax.fori_loop(0, count // ROWS, one, 0)


def for_columns(count, width, step):
    def one(index, carry):
        step(pl.ds(pl.multiple_of(index * width, width), width))
        return carry

    lax.fori_loop(0, count // width, one, 0)


SLOPE_SCALE = 28000.0


def gelu_both(pre):
    cumulative = 0.5 * (1.0 + lax.erf(pre * (1.0 / math.sqrt(2.0))))
    density = jnp.exp(-0.5 * pre * pre) * (1.0 / math.sqrt(2.0 * math.pi))
    slope = (cumulative + pre * density) * SLOPE_SCALE
    return (pre * cumulative).astype(BF16), slope.astype(jnp.int32).astype(jnp.int16)


def norm_back(grad, gain, scaled, inverse):
    spread = grad * gain
    first_mean = jnp.mean(spread, axis=-1, keepdims=True)
    second_mean = jnp.mean(spread * scaled, axis=-1, keepdims=True)
    return inverse * (spread - first_mean - scaled * second_mean)


def norm_back_rows(values, grad, base, gain, sums, store):
    sums[...] = jnp.zeros_like(sums)

    def step(rows):
        scaled, inverse = norm_rows(values[rows, :].astype(F32))
        part = grad[rows, :]
        sums[0:1, :] += jnp.sum(part * scaled, axis=0, keepdims=True)
        sums[1:2, :] += jnp.sum(part, axis=0, keepdims=True)
        store(rows, base[rows, :].astype(F32) + norm_back(part, gain[...], scaled, inverse))

    for_rows(grad.shape[0], step)


def front_kernel(
    block, x, gain_one, shift_one, gain, shift, w_qkv, cot_in, w_out, w_up, w_down,
    norm_one_out, qkv_out, att_out, den_out, state_out, output_out, gmixed_out, gn_out, sums, norm_out, pre_out,
    out_out, terms, down_a, down_b, down_c,
    wo, wu, wd, wsem, osem, att_low, state, output, gmixed, gatt, norm_cat, pre_cat, hidden, slope, cot_cat,
    stage, land, land_att, land_norm, swap_sent, swap_came, free, s0, s1, s2, s3, *scratch,
):
    take_scratch = Taker(scratch)
    slabs = take_scratch(slab_shapes(DOWN_WIDTHS))
    slab_a, slab_b, slab_c = slabs
    phases = take_scratch([[phase_scratch(2, length, 12)] for length in DOWN_WIDTHS])
    place = Place()
    core = place.core
    rows = x.shape[0]
    scan = Scan(Slots(terms), Units(land_att), Units(land_norm), Slots(state), (s0, s1, s2, s3), False)
    others = [place.neighbour(0, 1), place.neighbour(0, -1), place.partner(), *scan.others()]
    greet(others)
    own, other = pl.ds(0, rows), pl.ds(rows, rows)

    def load(source, target, slot):
        copy = pltpu.make_async_copy(source, target, wsem.at[slot])
        copy.start()
        return copy

    outs = []

    def leave(source, target):
        copy = pltpu.make_async_copy(source, target, osem.at[len(outs)])
        copy.start()
        outs.append(copy)
        return copy

    def settle(copies):
        for copy in copies:
            copy.wait()
            settled.append(id(copy))

    settled = []
    thirds = [
        load(w_qkv.at[:, pl.ds(third * 1024, 1024)], wu.at[:, pl.ds(slot * 1024, 1024)], slot)
        for slot, third in enumerate((1, 2, 0))
    ]
    cot_load = load(cot_in, cot_cat.at[own], 3)
    out_load = load(w_out, wo, 4)

    def norm_step(index):
        scaled, _ = norm_rows(x[index, :].astype(F32))
        hidden[index, pl.ds(0, 1024)] = (scaled * gain_one[...] + shift_one[...]).astype(BF16)

    for_rows(rows, norm_step)

    def shifted(columns, offset):
        return pl.ds(pl.multiple_of(columns.start + offset, PAIR), columns.size)

    def later_rows(index, offset):
        return pl.ds(pl.multiple_of(index.start + offset, 64), index.size)

    def project(slot, third, feature):
        thirds[slot].wait()

        def step(columns):
            raw = dot_nn(hidden[:, pl.ds(0, 1024)], wu[:, shifted(columns, slot * 1024)]).astype(BF16)
            hidden[:, shifted(columns, 1024 + third * 1024)] = raw
            if feature is not None:
                wd[pl.ds(feature * rows, rows), columns] = features(raw.astype(F32))

        for_columns(1024, TILE, step)

    project(0, 1, 1)
    project(1, 2, None)

    def local_state(unit):
        index, columns = unit_slices(unit, block)
        keys = wd[later_rows(index, rows), columns]
        square = tn_dot(hidden[index, shifted(columns, 3072)], keys)
        total = jnp.sum(keys.astype(F32), axis=0, keepdims=True)
        blocks, row = pack_state(square, total)
        terms[unit, pl.ds(0, 64)] = blocks
        terms[unit, pl.ds(64, 8)] = row

    def local_states(half):
        def four(index, carry):
            for offset in range(4):
                local_state(half * 8 + index * 4 + offset)
            return carry

        lax.fori_loop(0, 2, four, 0)

    local_states(0)
    met(len(others))
    scan.start(0)
    local_states(1)
    scan.start(1)
    swap = Swap(place, stage, swap_sent, swap_came)
    for which in range(2):
        for block_x in range(4):
            columns = pl.ds(block_x * 256 + which * 128, 128)
            pre_cat[own, pl.ds(which * TILE + block_x * 128, 128)] = hidden[:, columns]
        swap.put(which, which, pre_cat[own, pl.ds(which * TILE, TILE)], land.at[which])
    cot_load.wait()
    for tile in range(2):
        swap.put(2 + tile, 2 + tile, cot_cat[own, pl.ds(tile * TILE, TILE)], land.at[2 + tile])
    qkv_leaves = [leave(hidden.at[:, pl.ds(third * 1024 + 1024, 1024)], qkv_out.at[third]) for third in (1, 2)]
    project(2, 0, 0)
    qkv_leaves.append(leave(hidden.at[:, pl.ds(1024, 1024)], qkv_out.at[0]))
    up_load = load(w_up, wu, 6)
    first, second = head_masks()
    causal = causal_mask(block)

    def local_part(unit):
        index, columns = unit_slices(unit, block)
        query, key = wd[index, columns], wd[later_rows(index, rows), columns]
        value = hidden[index, shifted(columns, 3072)]
        scores = dot_nt(jnp.concatenate([query * first, query * second], axis=0), key)
        both = 0.0
        for head, mask in enumerate((first, second)):
            kept = jnp.where(causal, scores[head * block : (head + 1) * block], 0.0).astype(BF16)
            right = jnp.concatenate([value * mask, jnp.broadcast_to(mask, value.shape)], axis=1)
            both = both + dot_nn(kept, right)
        gmixed[index, columns] = both[:, :PAIR]
        gatt[index, columns] = both[:, PAIR:]

    def local_parts(start, count):
        def two(index, carry):
            local_part(start + 2 * index)
            local_part(start + 2 * index + 1)
            return carry

        lax.fori_loop(0, count // 2, two, 0)

    local_parts(0, 10)
    scan.middle()
    local_parts(10, 6)
    for which in range(2):
        pre_cat[other, pl.ds(which * TILE, TILE)] = swap.get(which, land.at[which])
        cot_cat[other, pl.ds(which * TILE, TILE)] = swap.get(2 + which, land.at[2 + which])
    cat_leaves = [leave(pre_cat.at[:, pl.ds(which * TILE, TILE)], norm_one_out.at[which]) for which in range(2)]
    together = same_head()

    def incoming(unit):
        index, columns = unit_slices(unit, block)
        square, total = unpack_state(state[unit])
        totals = jnp.where(together, jnp.broadcast_to(total, (PAIR, PAIR)), 0.0)
        high, low = split(jnp.concatenate([square, totals], axis=0))
        query = wd[index, columns]
        both = dot_nt(
            jnp.concatenate([query, query], axis=1), jnp.concatenate([high, low], axis=1)
        )
        denom = gatt[index, columns] + both[:, PAIR:]
        attended = (gmixed[index, columns] + both[:, :PAIR]) / denom
        tile, within = stage_place(unit)
        stage[tile, index, within] = attended
        stage[2 + tile, index, within] = denom
        att_low[index, columns] = attended.astype(BF16)

    def stage_place(unit):
        pair = lax.rem(unit, 8)
        return lax.div(pair, 4), pl.ds(pl.multiple_of(lax.rem(pair, 4) * PAIR, PAIR), PAIR)

    mixed = gatt

    def up(columns, index):
        ours, ours_slope = gelu_both(dot_nn(norm_cat[index, :], wu[:, columns]))
        hidden[index, columns] = ours
        slope[index, columns] = ours_slope

    settle(qkv_leaves)
    swap.drain(range(4), land.at[0])
    att_leaves = []
    for half in range(2):
        scan.finish(half)
        leave(state.at[pl.ds(half * 8, 8)], state_out.at[pl.ds(half * 8, 8)])

        def several(index, carry):
            for offset in range(4):
                incoming(half * 8 + 4 * index + offset)
            return carry

        lax.fori_loop(0, 2, several, 0)
        part = pl.ds(half * block, block)
        for slot in range(4):
            target = (att_out, den_out)[slot // 2].at[part, pl.ds(slot % 2 * TILE, TILE)]
            att_leaves.append(leave(stage.at[slot, part], target))
        if half == 0:
            out_load.wait()

        def mix(columns):
            mixed[part, columns] = x[part, columns].astype(F32) + dot_nn(att_low[part, :], wo[:, columns])

        mix(pl.ds(0, 1024))
        for start in range(0, block, ROWS):
            index = pl.ds(half * block + start, ROWS)
            scaled, _ = norm_rows(mixed[index, :])
            norm_cat[index, :] = (scaled * gain[...] + shift[...]).astype(BF16)
        if half == 0:
            up_load.wait()
    down_load = load(w_down, wd, 5)
    scan.drain()
    pl.semaphore_signal(free, inc=1, device_id=place.partner(), device_id_type=MESH)
    settle(att_leaves)
    pl.semaphore_wait(free, 1)

    def nth_block(index):
        return lax.rem(place.at[0] + jnp.where(index == 2, 3, jnp.maximum(2 - index, 0)), RING)

    def give(index, carry):
        columns = half_columns(nth_block(index), 1 - core, 1024)
        up(columns, own)
        swap.put(4 + index, index, hidden[:, columns], land.at[index])
        return carry

    lax.fori_loop(0, 4, give, 0)

    def take(index, carry):
        block_x = nth_block(index)
        columns = half_columns(block_x, core, 1024)
        up(columns, own)
        both = jnp.concatenate([hidden[:, columns], swap.get(4 + index, land.at[index])], axis=0)
        for half in range(2):
            columns = pl.ds(half * TILE, TILE)
            product = tn_dot(both, cot_cat[:, columns]).reshape(4, 4, 4, 8, TILE)
            for stream in range(3):
                slabs[stream][block_x, :, :, :, columns] = product[:, :, stream]
            last = product[:, :, 3]
            if half == 0:
                slab_a[block_x, :, :, :, pl.ds(1024, 384)] = last[..., :384]
                slab_b[block_x, :, :, :, pl.ds(1024, 128)] = last[..., 384:]
            else:
                slab_b[block_x, :, :, :, pl.ds(1152, 256)] = last[..., :256]
                slab_c[block_x, :, :, :, pl.ds(1024, 256)] = last[..., 256:]
        return carry

    kinds = (None, SplitPhase, SplitPhase)
    down = [Stream(place, slabs[k], ORDERS[k], phases[k], kinds[k]) for k in range(3)]
    lead, *others_two = [stream.prepare() for stream in down]
    lax.fori_loop(0, 2, take, 0)
    lead.begin_far()
    for phase in others_two:
        phase.begin_first()
    lead.begin_near(0)
    lax.fori_loop(2, 4, take, 0)
    for phase in others_two:
        phase.begin_second()
    lead.begin_near(1)
    pl.semaphore_signal(free, inc=1, device_id=place.partner(), device_id_type=MESH)
    for tile in range(2):
        columns = pl.ds(tile * TILE, TILE)
        swap.put(8 + tile, tile, norm_cat[own, columns], land_norm.at[tile], before=4 + tile)
    down_load.wait()
    cot = cot_cat.at[own]

    def finish_forward(columns):
        output[:, columns] = (mixed[:, columns] + dot_nn(hidden[...], wd[:, columns])).astype(BF16)

    for_columns(1024, 256, finish_forward)
    leave(output, output_out)

    def back(columns):
        held = slope[:, columns].astype(jnp.int32).astype(F32) * (1.0 / SLOPE_SCALE)
        grad = dot_nt(cot[...], wd[columns, :]) * held
        low = grad.astype(BF16)
        hidden[:, columns] = low
        return low

    pl.semaphore_wait(free, 1)

    def give_back(block, carry):
        theirs = back(half_columns(block, 1 - core, 1024))
        before = jnp.where(block < 2, 8 + block, 4 + block)
        swap.put(10 + block, block, theirs, land.at[block], before=before)
        return carry

    lax.fori_loop(0, 4, give_back, 0)

    def keep_back(block, carry):
        columns = pl.ds(pl.multiple_of(block * TILE, TILE), TILE)
        pre_cat[own, columns] = back(half_columns(block, core, 1024))
        return carry

    settle(cat_leaves)
    lax.fori_loop(0, 4, keep_back, 0)
    for stream in down:
        stream.forward()

    def back_up(columns):
        gmixed[:, columns] = dot_nt(hidden[...], wu[columns, :])

    for_columns(1024, 256, back_up)

    def take_back(block, carry):
        columns = pl.ds(pl.multiple_of(block * TILE, TILE), TILE)
        pre_cat[other, columns] = swap.get(10 + block, land.at[block])
        return carry

    lax.fori_loop(0, 4, take_back, 0)
    leave(pre_cat, pre_out)
    for tile in range(2):
        columns = pl.ds(tile * TILE, TILE)
        norm_cat[other, columns] = swap.get(8 + tile, land_norm.at[tile])
        swap.put(14 + tile, tile, att_low[:, columns], land_att.at[tile], before=10 + tile)
    leave(norm_cat, norm_out)
    query_load = load(qkv_out.at[0], wd.at[own], 7)
    pl.semaphore_signal(free, inc=1, device_id=place.partner(), device_id_type=MESH)
    def store(index, values):
        gmixed[index, :] = values
        hidden[index, pl.ds(0, 1024)] = values.astype(BF16)

    norm_back_rows(mixed, gmixed, cot, gain, sums, store)
    leave(gmixed, gmixed_out)
    pl.semaphore_wait(free, 1)
    swap.put(16, 2, hidden[:, half_tile(0, 1 - core)], land_norm.at[0], before=12)

    def back_out(columns):
        gatt[:, columns] = dot_nt(hidden[:, pl.ds(0, 1024)], wo[columns, :])

    state_loads = [query_load]

    def load_state(slots):
        for slot in slots:
            source = (att_out, den_out)[slot // 2].at[:, pl.ds(slot % 2 * TILE, TILE)]
            state_loads.append(load(source, stage.at[slot], 8 + slot))

    for number, slot in ((13, 3), (14, 0), (15, 1)):
        swap.copy(number, slot, land_norm.at[0]).wait_send()
    load_state((0, 1, 3))
    for_columns(1024, TILE, back_out)
    ours = hidden[:, half_tile(0, core)]
    swap.copy(16, 2, land_norm.at[0]).wait_send()
    load_state((2,))
    theirs = swap.get(16, land_norm.at[0])
    for tile in range(2):
        swap.copy(14 + tile, tile, land_att.at[tile]).wait_recv()
        for part, (start, width) in enumerate(((0, 384), (384, 128))):
            product = tn_dot(att_low[:, pl.ds(tile * TILE + start, width)], ours)
            theirs_att = land_att[tile, :, pl.ds(start, width)].astype(BF16)
            land[2 * tile + part, pl.ds(0, width), :] = product + tn_dot(theirs_att, theirs)
            leave(land.at[2 * tile + part, pl.ds(0, width)], out_out.at[pl.ds(tile * TILE + start, width)])
    for copy in state_loads:
        copy.wait()
    first_wide = first_head(block)

    def state_back(unit):
        index, columns = unit_slices(unit, block)
        tile, within = stage_place(unit)
        numer = gatt[index, columns] / stage[2 + tile, index, within]
        gatt[index, columns] = numer
        query = features(wd[index, columns].astype(F32))
        blocks, row = state_gradient(query, numer, stage[tile, index, within], first_wide)
        terms[unit, pl.ds(0, 64)] = blocks
        terms[unit, pl.ds(64, 8)] = row

    for_units(state_back, 2)
    leave(gatt, gn_out)
    for stream, target in zip(down, (down_a, down_b, down_c)):
        stream.finish()
        leave(stream.data, target)
    for stream in down:
        stream.drain()
    for copy in outs:
        if id(copy) not in settled:
            copy.wait()


def slab_shapes(widths):
    return [pltpu.VMEM((4, 4, 4, 8, width), F32) for width in widths]


def struct(shape, dtype=F32):
    return jax.ShapeDtypeStruct(shape, dtype)


VMEM_SPEC = pl.BlockSpec(memory_space=pltpu.VMEM)
ANY_SPEC = pl.BlockSpec(memory_space=pl.ANY)


def call(kernel, outs, out_specs, operands, in_specs, scratch, collective_id):
    return pl.pallas_call(
        kernel,
        out_shape=outs,
        in_specs=in_specs,
        out_specs=out_specs,
        scratch_shapes=scratch,
        compiler_params=pltpu.CompilerParams(
            collective_id=collective_id, has_side_effects=True, vmem_limit_bytes=63 * MIB
        ),
    )(*operands)


def front(x, gain_one, shift_one, gain, shift, w_qkv, cot, w_out, w_up, w_down, block):
    rows, width = x.shape
    wide = w_up.shape[1]
    outs = [
        struct((2, 2 * rows, width // 2), BF16),
        struct((3, rows, width), BF16),
        struct((rows, width)),
        struct((rows, width)),
        struct((SEQ, 72, PAIR)),
        struct((rows, width), BF16),
        struct((rows, width)),
        struct((rows, width)),
        struct((8, width)),
        struct((2 * rows, width), BF16),
        struct((2 * rows, wide // 2), BF16),
        struct((width, TILE)),
        struct((SEQ, 72, PAIR)),
        *[struct((4, 4, 8, length)) for length in DOWN_WIDTHS],
    ]
    scratch = [
        pltpu.VMEM((width, width), BF16),
        pltpu.VMEM((width, wide), BF16),
        pltpu.VMEM((wide, width), BF16),
        pltpu.SemaphoreType.DMA((12,)),
        pltpu.SemaphoreType.DMA((28,)),
        pltpu.VMEM((rows, width), BF16),
        SCAN_SCRATCH[0],
        pltpu.VMEM((rows, width), BF16),
        pltpu.VMEM((rows, width), F32),
        pltpu.VMEM((rows, width), F32),
        pltpu.VMEM((2 * rows, width), BF16),
        pltpu.VMEM((2 * rows, wide // 2), BF16),
        pltpu.VMEM((rows, wide), BF16),
        pltpu.VMEM((rows, wide), jnp.int16),
        pltpu.VMEM((2 * rows, width), BF16),
        pltpu.VMEM((4, rows, TILE), F32),
        pltpu.VMEM((4, rows, TILE), F32),
        pltpu.VMEM((2, rows, TILE), F32),
        pltpu.VMEM((2, rows, TILE), F32),
        pltpu.SemaphoreType.DMA((17,)),
        pltpu.SemaphoreType.DMA((17,)),
        pltpu.SemaphoreType.REGULAR,
        *SCAN_SCRATCH[3:],
        *slab_shapes(DOWN_WIDTHS),
        *flatten([[phase_scratch(2, length, 12)] for length in DOWN_WIDTHS]),
    ]
    specs = [VMEM_SPEC] * 5 + [ANY_SPEC] * 5
    out_specs = [ANY_SPEC] * 8 + [VMEM_SPEC] + [ANY_SPEC] * 3 + [VMEM_SPEC] + [ANY_SPEC] * 3
    operands = (x, gain_one, shift_one, gain, shift, w_qkv, cot, w_out, w_up, w_down)

    def kernel(*refs):
        front_kernel(block, *refs)

    return call(kernel, outs, out_specs, operands, specs, scratch, 1)


def last_scratch(rows, width):
    return {
        "qkv": pltpu.VMEM((3, rows, width), BF16),
        "att": pltpu.VMEM((rows, width), F32),
        "gn": pltpu.VMEM((rows, width), F32),
        "state": pltpu.VMEM((SEQ, 72, PAIR), F32),
        "x": pltpu.VMEM((rows, width), BF16),
        "grads": pltpu.VMEM((2, rows, width), F32),
        "scan": list(SCAN_SCRATCH[:3]) + [SCAN_SCRATCH[0]] + list(SCAN_SCRATCH[3:]),
        "norm_cat": pltpu.VMEM((2, 2 * rows, width // 2), BF16),
        "pre_cat": pltpu.VMEM((2 * rows, 2 * width), BF16),
        "w": pltpu.VMEM((width, 3 * width), BF16),
        "stage": pltpu.VMEM((3, rows, TILE), F32),
        "land": pltpu.VMEM((3, rows, TILE), F32),
        "swap": [pltpu.SemaphoreType.DMA((3,)), pltpu.SemaphoreType.DMA((3,))],
        "slabs": slab_shapes(UP_WIDTHS),
        "chunks": [pltpu.VMEM((4, 4, 8, length), F32) for length in DOWN_WIDTHS],
        "up_chunks": [pltpu.VMEM((4, 4, 8, length), F32) for length in UP_WIDTHS],
        "out_slabs": slab_shapes(OUT_WIDTHS),
        "vec_slab": pltpu.VMEM((4, 4, 4, 8, 128), F32),
        "sums": pltpu.VMEM((8, width), F32),
        "down": [stream_scratch(length, (1, 2), (2,)) for length in DOWN_WIDTHS],
        "up": [
            [*stream_scratch(length, (0, 1)), route_scratch(k, UP_WIDTHS, 2048)] for k, length in enumerate(UP_WIDTHS)
        ],
        "out": [
            [*stream_scratch(length, (0, 1), (1,)), route_scratch(k, OUT_WIDTHS, TILE)]
            for k, length in enumerate(OUT_WIDTHS)
        ],
        "qkv_sems": [[pltpu.SemaphoreType.DMA((6,))] * 2 for _ in QKV_WIDTHS],
        "qkv_sum": [
            [*stream_scratch(length, (1,)), route_scratch(k, QKV_WIDTHS, 3 * TILE)]
            for k, length in enumerate(QKV_WIDTHS)
        ],
        "vec": stream_scratch(128, (0, 1, 2), (0, 1, 2)),
        "vec_land": pltpu.VMEM((8, 128), F32),
        "vec_sems": pltpu.SemaphoreType.DMA((2,)),
        "credit": pltpu.SemaphoreType.REGULAR((3,)),
        "loads": pltpu.SemaphoreType.DMA((32,)),
    }


def last_kernel(
    block, qkv_in, att_in, terms_in, state_in, gn_in, gmixed_in, norm_one_in, norm_in, pre_in,
    down_in_a, down_in_b, down_in_c, out_in, x_in, weight, gain, sums_two,
    grad_input, grad_up, grad_out, grad_qkv, grad_down, grad_gains, *scratch,
):
    place = Place()
    core = place.core
    rows, width = att_in.shape
    like = last_scratch(rows, width)
    take = Taker(scratch)
    s = {name: take(like[name]) for name in like}
    qkv, att, gn, grads = s["qkv"], s["att"], s["gn"], s["grads"]
    slabs = s["slabs"]
    scan = Scan(*[Slots(ref) for ref in s["scan"][:4]], s["scan"][4:], True)
    across = [place.neighbour(0, step) for step in (1, -1, 2)]
    beside = []
    for axis in range(3):
        for step in (1, 2, 3):
            position = list(place.at)
            position[axis] = place.ring(axis, step)
            beside.append(place.id_of(*position, 1 - core))
    others = [*across, place.partner(), *beside, *scan.others()]
    greet(others)
    loads = []

    def load(source, target):
        copy = pltpu.make_async_copy(source, target, s["loads"].at[len(loads)])
        copy.start()
        loads.append(copy)
        return copy

    started = load(terms_in, scan.terms.ref)
    out_loads = []
    for k in (0, 2, 1):
        for which, start, length, at in stream_pieces(k, OUT_WIDTHS, TILE):
            source = out_in.at[:, which, :, :, :, pl.ds(start, length)]
            target = s["out_slabs"][k].at[:, :, :, :, pl.ds(at, length)]
            out_loads.append(load(source, target))
    up_loads = [load(pre_in, s["pre_cat"])]
    for which in range(2):
        for block_x in range(4):
            source = norm_in.at[:, pl.ds(block_x * 256 + which * 128, 128)]
            target = s["norm_cat"].at[which, :, pl.ds(block_x * 128, 128)]
            up_loads.append(load(source, target))
    down_in = (down_in_a, down_in_b, down_in_c)
    down_loads = [load(source, target) for source, target in zip(down_in, s["chunks"])]
    qkv_loads = [load(qkv_in, qkv), load(state_in, s["state"]), load(gn_in, gn), load(att_in, att)]
    late_loads = [load(weight, s["w"]), load(x_in, s["x"])]

    def settle(copies):
        for copy in copies:
            copy.wait()

    first, second = head_masks()
    first_wide = first_head(block)

    up_first = [phases[0] for phases in s["up"]]
    down = [Stream(place, s["chunks"][k], ORDERS[k][1:], s["down"][k]) for k in range(3)]
    up = [
        Stream(place, slabs[k], ORDERS[k], s["up"][k], None, (stream_pieces(k, UP_WIDTHS, 2048), grad_up))
        for k in range(3)
    ]
    out = [
        Stream(place, s["out_slabs"][k], ORDERS[k], s["out"][k], None, (stream_pieces(k, OUT_WIDTHS, TILE), grad_out))
        for k in range(3)
    ]
    qkv_sum = [None] * 3
    vec = [Stream(place, s["vec_slab"], ORDERS[0], s["vec"])]
    begin, forward, proceed, finish = Stream.begin, Stream.forward, Stream.proceed, Stream.finish

    def go(*steps):
        for step, streams, k in steps:
            step(streams[k])

    settle(out_loads)
    met(len(others))
    go((begin, out, 0))
    started.wait()
    scan.start(0)
    scan.start(1)
    go((begin, out, 2))
    settle(up_loads)
    for k in range(3):
        stream_product(k, s["norm_cat"], s["pre_cat"], slabs[k], UP_WIDTHS, 2048)
        if k == 1:
            settle(down_loads)
            go((begin, down, 0), (begin, up, 0))
    go((begin, out, 1))
    norm_load = load(norm_one_in, s["norm_cat"])
    settle(qkv_loads)
    causal = causal_mask(block)
    causal_t = causal_mask(block, True)

    def local_part(unit):
        index, columns = unit_slices(unit, block)
        raw_query = qkv[0, index, columns].astype(F32)
        query, value = features(raw_query), qkv[2, index, columns]
        key = features(qkv[1, index, columns].astype(F32))
        numer = gn[index, columns]
        one, two = head_slopes(numer, att[index, columns], first_wide)
        high, low = split(numer)
        scores = dot_nt(jnp.concatenate([key * first, key * second], axis=0), query)
        wide = jnp.concatenate([high, low], axis=1)
        values = jnp.concatenate([value, value], axis=1)
        grad_query, grad_key, grad_value = 0.0, 0.0, 0.0
        for head, (mask, slope) in enumerate(((first, one), (second, two))):
            mask_wide = jnp.concatenate([mask, mask], axis=1)
            mixing = split(jnp.where(causal, dot_nt(wide * mask_wide, values) + slope, 0.0))
            turned = jnp.where(causal_t, scores[head * block : (head + 1) * block], 0.0)
            for part in mixing:
                grad_query = grad_query + dot_nn(part, key * mask)
                grad_key = grad_key + tn_dot(part, query * mask)
            both = dot_nn(turned.astype(BF16), wide * mask_wide)
            grad_value = grad_value + both[:, :PAIR] + both[:, PAIR:]
        square, total = unpack_state(s["state"][unit])
        state_high, state_low = split(square)
        grad_query = grad_query + dot_nn(wide, jnp.concatenate([state_high, state_high], axis=0))
        grad_query = grad_query + dot_nn(high, state_low)
        grad_query = grad_query + jnp.where(first_wide, one, two) * total
        qkv[0, index, columns] = (grad_query * feature_slope(raw_query)).astype(BF16)
        grads[0, index, columns] = grad_key
        grads[1, index, columns] = grad_value

    def local_parts(start, count):
        def one(index, carry):
            local_part(start + index)
            return carry

        lax.fori_loop(0, count, one, 0)

    local_parts(0, 2)
    scan.middle()
    local_parts(2, 1)
    go((begin, up, 2), (forward, out, 2), (forward, out, 0))
    local_parts(3, 2)
    go((forward, out, 1))
    local_parts(5, 3)
    go((begin, up, 1))
    local_parts(8, 7)
    go((forward, up, 0))
    local_parts(15, 1)
    swap = Swap(place, s["stage"], *s["swap"])
    land, cat = s["land"], s["pre_cat"]
    own, other = pl.ds(0, rows), pl.ds(rows, rows)
    swap.put(0, 0, qkv[0, :, half_tile(0, 1 - core)], land.at[0])
    mixed_load = load(gmixed_in, att)
    scan.finish(0)
    scan.finish(1)
    go((begin, down, 2))

    def incoming(unit):
        index, columns = unit_slices(unit, block)
        square, total = unpack_state(scan.result.ref[unit])
        high, low = split(square)
        raw_key = qkv[1, index, columns].astype(F32)
        key, value = features(raw_key), qkv[2, index, columns]
        grad_key = grads[0, index, columns] + total
        grad_key = grad_key + dot_nt(
            jnp.concatenate([value, value], axis=1), jnp.concatenate([high, low], axis=1)
        )
        grad_value = grads[1, index, columns] + dot_nn(
            jnp.concatenate([key, key], axis=1), jnp.concatenate([high, low], axis=0)
        )
        qkv[1, index, columns] = (grad_key * feature_slope(raw_key)).astype(BF16)
        qkv[2, index, columns] = grad_value.astype(BF16)

    for_units(incoming, 2)
    for third in (1, 2):
        swap.put(third, third, qkv[third, :, half_tile(0, 1 - core)], land.at[third])
    settle(late_loads)

    def back_norm(columns):
        total = 0.0
        for third in range(3):
            total = total + dot_nt(qkv[third], s["w"][columns, pl.ds(third * 1024, 1024)])
        gn[:, columns] = total

    for start in (0, 256, 512, 768):
        back_norm(pl.ds(start, 256))
    for third in range(3):
        columns = pl.ds(third * TILE, TILE)
        cat[own, columns] = qkv[third, :, half_tile(0, core)]
        cat[other, columns] = swap.get(third, land.at[third])
    go((forward, up, 2), (forward, up, 1))
    norm_load.wait()
    mixed_load.wait()
    def turn(k):
        up[k].finish(s["up_chunks"][k])
        up[k].drain()
        for step in (1, -1):
            pl.semaphore_signal(
                s["credit"].at[k],
                inc=1,
                device_id=place.neighbour(ORDERS[k][0], step),
                device_id_type=MESH,
            )
        narrow = (slice(None),) * 4 + (pl.ds(0, QKV_WIDTHS[k]),)
        data = slabs[k].at[narrow]
        stream_product(k, s["norm_cat"], cat, data, QKV_WIDTHS, 3 * TILE)
        pl.semaphore_wait(s["credit"].at[k], 2)
        phases = [[up_first[k][0].at[narrow], up_first[k][1].at[narrow], *s["qkv_sems"][k]]]
        last = (stream_pieces(k, QKV_WIDTHS, 3 * TILE), grad_qkv)
        qkv_sum[k] = Stream(place, data, ORDERS[k], phases + s["qkv_sum"][k], None, last)
        qkv_sum[k].begin()

    def store(index, values):
        gn[index, :] = values

    sums = s["sums"]
    norm_back_rows(s["x"], gn, att, gain, sums, store)
    leave = load(gn, grad_input)
    go((begin, down, 1), (proceed, out, 0))
    four = jnp.concatenate([sums[0:2, :], sums_two[0:2, :]], axis=0)
    eight = jnp.concatenate([four, four], axis=0)
    turned = jnp.transpose(jnp.concatenate([eight, jnp.zeros((120, 1024), F32)], axis=0))
    turned = turned.reshape(4, 2, 4, 4, 8, 128)
    lane = lax.broadcasted_iota(jnp.int32, (8, 128), 1)
    s["vec_slab"][...] = jnp.where(lane < 4, turned[:, 0], jnp.where(lane < 8, turned[:, 1], 0.0))
    go((begin, vec, 0), (proceed, out, 1))
    turn(0)
    turn(2)
    go((begin, up, 0))
    turn(1)
    go(
        (forward, qkv_sum, 0), (forward, qkv_sum, 2), (begin, up, 1), (forward, down, 2), (forward, down, 1),
        (begin, up, 2), (proceed, out, 0), (forward, qkv_sum, 1), (proceed, vec, 0), (proceed, qkv_sum, 2),
        (proceed, qkv_sum, 0), (proceed, qkv_sum, 1), (forward, down, 0), (forward, up, 0), (forward, up, 1),
        (proceed, out, 2), (proceed, vec, 0), (forward, qkv_sum, 2), (forward, up, 2), (proceed, down, 1),
        (forward, qkv_sum, 0), (forward, qkv_sum, 1), (proceed, down, 2), (proceed, down, 0), (proceed, qkv_sum, 2),
        (proceed, up, 0), (proceed, up, 1), (proceed, out, 2), (proceed, qkv_sum, 0), (proceed, up, 2),
        (proceed, out, 1), (proceed, qkv_sum, 1), (finish, down, 2), (finish, down, 1), (finish, down, 0),
        (finish, up, 1), (finish, vec, 0),
    )
    vec_tile = vec[0].data
    vec_copy = pltpu.make_async_remote_copy(
        src_ref=vec_tile,
        dst_ref=s["vec_land"],
        send_sem=s["vec_sems"].at[0],
        recv_sem=s["vec_sems"].at[1],
        device_id=place.partner(),
        device_id_type=MESH,
    )
    vec_copy.start()
    go(
        (finish, up, 0), (finish, qkv_sum, 0), (finish, qkv_sum, 2), (finish, out, 0), (finish, qkv_sum, 1),
        (finish, out, 2), (finish, out, 1), (finish, up, 2),
    )
    for k in range(3):
        piece = down[k].data
        grad_down[pl.ds(8 * k, 8), :] = piece[:, pl.ds(0, 1024)]
        start, width_k = DOWN_CUTS[k]
        grad_down[pl.ds(24, 8), pl.ds(start, width_k)] = piece[:, pl.ds(1024, width_k)]
    scan.drain()
    for number in range(3):
        swap.copy(number, number, land.at[number]).wait_send()
    for stream in (*down, *up, *out, *qkv_sum, *vec):
        stream.drain()
    vec_copy.wait()
    grad_gains[...] = vec_tile[...] + s["vec_land"][...]
    leave.wait()


def last_part(qkv, att, terms, state, gn, gmixed, norm_one, norm_cat, pre_cat, down, out, x, weight, gain, sums_two, block):
    rows, width = x.shape

    def kernel(*refs):
        last_kernel(block, *refs)

    outs = [
        struct((rows, width)),
        struct((8, 4096)),
        struct((8, width)),
        struct((8, 3 * width)),
        struct((32, width)),
        struct((8, 128)),
    ]
    like = last_scratch(rows, width)
    scratch = [leaf for name in like for leaf in flatten(like[name])]
    out = out.reshape(4, 2, 4, 4, 8, TILE)
    operands = (
        qkv, att, terms, state, gn, gmixed, norm_one, norm_cat, pre_cat, *down, out, x, weight, gain, sums_two,
    )
    specs = [ANY_SPEC] * 15 + [VMEM_SPEC] * 2
    out_specs = [ANY_SPEC] + [VMEM_SPEC] * 5
    return call(kernel, outs, out_specs, operands, specs, scratch, 2)


def lay_out_kernel(output, grad_input, up, out, qkv, down, gains, output_to, grad_to, up_to, out_to, qkv_to, down_to, a, b, c, d):
    pairs = (
        (output, output_to), (grad_input, grad_to), (up, up_to), (out, out_to), (qkv, qkv_to), (down, down_to),
    )
    for source, target in pairs:
        target[...] = source[...]
    core = lax.rem(lax.axis_index("dp"), 2)
    turned = jnp.transpose(jnp.concatenate([gains[...], jnp.zeros((120, 128), F32)], axis=0))
    for k, target in enumerate((a, b, c, d)):
        target[...] = jnp.where(core == 0, turned[k : k + 1, :8], turned[4 + k : 5 + k, :8])


def lay_out(output, *grads):
    arrays = (output, *grads[:-1])
    outs = [struct(array.shape, array.dtype) for array in arrays] + [struct((1, 8))] * 4
    return pl.pallas_call(
        lay_out_kernel,
        out_shape=outs,
        in_specs=[VMEM_SPEC] * 7,
        out_specs=[VMEM_SPEC] * 10,
        compiler_params=pltpu.CompilerParams(vmem_limit_bytes=62 * MIB),
    )(output, *grads)


def body(
    inputs,
    first_gain,
    first_shift,
    qkv_weight,
    out_weight,
    second_gain,
    second_shift,
    up_weight,
    down_weight,
    cotangent,
):
    sequences, block, width = inputs.shape
    rows = sequences * block
    x = inputs.reshape(rows, width)
    cot = cotangent.reshape(rows, width)
    gain_one, gain_two = first_gain.reshape(1, width), second_gain.reshape(1, width)
    shift_two = second_shift.reshape(1, width)
    shift_one = first_shift.reshape(1, width)
    norm_one, qkv, att, _, state, output, gmixed, gn, sums_two, norm_cat, pre_cat, out, terms, *down = front(
        x, gain_one, shift_one, gain_two, shift_two, qkv_weight, cot, out_weight, up_weight, down_weight, block
    )
    grads = last_part(
        qkv, att, terms, state, gn, gmixed, norm_one, norm_cat, pre_cat, down, out, x, qkv_weight,
        gain_one, sums_two, block,
    )
    output, grad_input, grad_up, grad_out, grad_qkv, grad_down, *gains = lay_out(output, *grads)
    return (
        output.reshape(inputs.shape),
        grad_input.reshape(inputs.shape),
        grad_qkv,
        grad_out,
        grad_up,
        grad_down,
        *[gain.reshape(8) for gain in gains],
    )


def solution(mesh):
    return jax.shard_map(
        body,
        mesh=mesh,
        in_specs=(
            P("dp", "seq", None),
            P(),
            P(),
            P(),
            P(),
            P(),
            P(),
            P(),
            P(),
            P("dp", "seq", None),
        ),
        out_specs=(
            P("dp", "seq", None),
            P("dp", "seq", None),
            P(("dp", "seq"), None),
            P(("dp", "seq"), None),
            P(("dp", "seq"), None),
            P(("dp", "seq"), None),
            P(("dp", "seq")),
            P(("dp", "seq")),
            P(("dp", "seq")),
            P(("dp", "seq")),
        ),
        check_vma=False,
    )
```
